32 devices in a mesh: runs: 2 (over x), space: 16 (over z, y, core).
Axes of the slice: x: 2, y: 2, z: 4, core: 2. Of those that a mesh axis runs over, the one named last changes fastest.
Arguments:
- fields: float32 [128, 512], P(('runs', 'space')), parts along dimension 0, may hold values from -3 to 3
- end_weights: bfloat16 [256, 128, 512], P(None, ('runs', 'space')), parts along dimension 1, may hold values from 0.5 to 1.5
- directions: float32 [3, 256], replicated, may hold values from -1 to 1
- analysis: bfloat16 [256, 256], replicated, may hold values from -0.375 to 0.375
- synthesis: bfloat16 [256, 256], replicated, may hold values from -0.375 to 0.375
- decay_rates: float32 [256], replicated, may hold values from 0.1 to 1
Outputs:
- density: float32 [128, 512], P(('runs', 'space')), parts along dimension 0
The draws below stay inside these ranges and needn't reach their ends.
There are 2 independent parts, one for each index of `runs`. The reference program is written for one: setup_inputs(seed, part) draws one part's arguments, and reference() takes and returns one part's arrays. A program takes and returns all parts, laid end to end along the dimension named above; an argument that names none is the same for every part. Nothing has to cross between parts.
All inputs are finite; a program needn't handle non-finite values.
Results may differ from the reference program's by a relative error of at most 0.003.
Values may be sent and summed in bfloat16 or wider, within the bound.
No kernel may reach another device: no remote copies, remote signals or barrier semaphores. Data moves between devices by JAX's collectives and lax.ppermute only.
A program may use at most 64 MiB of HBM per device.

```python
import math
import jax
import jax.numpy as jnp

ORIENT = 256
HARM = 256
SX = 4
NY = 32
NZ = 16
STEPS = 4
NX = 32


def steps_of(key, dims, cuts, low, top_value):
    gain = 1.0
    for axis_at, parts in cuts:
        draws = jax.random.uniform(jax.random.fold_in(jax.random.fold_in(key, 6), axis_at), (parts,), jnp.float32, low / len(cuts), top_value / len(cuts))
        gain = gain * jnp.repeat(jnp.exp(draws), dims[axis_at] // parts).reshape((-1,) + (1,) * (len(dims) - 1 - axis_at))
    return gain


def centred(stream_key, extent, spread, most, shards=(), kind=jnp.bfloat16):
    result = jax.random.normal(stream_key, extent, jnp.float32) * spread
    if len(shards) > 0:
        result = steps_of(stream_key, extent, shards, -0.22, 0.18) * result
    return jnp.clip(result, min=-most, max=most).astype(kind)


def setup_inputs(seed: int = 0, part: int = 0) -> dict:
    seeds = jax.random.split(jax.random.key(seed), 7)
    own_keys = jax.random.split(jax.random.fold_in(seeds[6], part), 7)
    return {
        "fields": centred(own_keys[0], (2 * NX, NY * NZ), 0.5, 3.0, ((0, 16),), jnp.float32),
        "end_weights": jnp.clip(0.5 + 1.0 * jax.random.uniform(own_keys[1], (ORIENT, 2 * NX, NY * NZ), jnp.float32) ** steps_of(own_keys[1], (ORIENT, 2 * NX, NY * NZ), ((1, 16),), -0.2, 0.2), 0.5, 1.5).astype(jnp.bfloat16),
        "directions": jnp.clip(jax.random.uniform(seeds[2], (3, ORIENT), jnp.float32, -1.0, 1.0), -1.0, 1.0),
        "analysis": centred(seeds[3], (HARM, ORIENT), ORIENT ** -0.5, 0.375),
        "synthesis": centred(seeds[4], (ORIENT, HARM), HARM ** -0.5, 0.375),
        "decay_rates": jnp.clip(jnp.exp(jax.random.uniform(seeds[5], (HARM,), jnp.float32, math.log(0.1), math.log(1.0))), 0.1, 1.0),
    }


courant = 0.3
slope = 0.6


def advance(current, field, velocity, analysis, synthesis, decay_rates):
    factor = jnp.exp(-0.5 * field)[None]
    shaped = (factor * current.astype(jnp.float32)).astype(jnp.bfloat16)
    center = shaped.astype(jnp.float32)
    drift_sum = jnp.zeros_like(center)
    for component in range(3):
        upwind_pos = jnp.maximum(velocity[component], 0.0)[:, None, None, None]
        upwind_neg = jnp.minimum(velocity[component], 0.0)[:, None, None, None]
        prev_cells = jnp.roll(center, 1, axis=component + 1)
        next_cells = jnp.roll(center, -1, axis=component + 1)
        drift_sum = drift_sum + upwind_pos * (center - prev_cells) + upwind_neg * (next_cells - center)
    moved_cells = (center - courant * drift_sum).astype(jnp.bfloat16)
    flattened = moved_cells.reshape(ORIENT, -1)
    harmonics = (decay_rates[:, None] * jnp.dot(analysis, flattened, preferred_element_type=jnp.float32)).astype(jnp.bfloat16)
    rotated = jnp.mean(flattened.astype(jnp.float32), axis=0, keepdims=True) + jnp.dot(synthesis, harmonics, preferred_element_type=jnp.float32)
    return (factor * rotated.reshape(current.shape)).astype(jnp.bfloat16)


def propagate(start, first_field, second_field, velocity, analysis, synthesis, decay_rates):
    slices = [start]
    current = start
    for step_index in range(STEPS):
        field = first_field if step_index < STEPS // 2 else second_field
        current = advance(current, field, velocity, analysis, synthesis, decay_rates)
        slices.append(current)
    return slices


def pair_sum(own_slices, partner_slices):
    half_steps = STEPS // 2
    running = jnp.zeros(own_slices[0].shape[1:], jnp.float32)
    for position in range(half_steps + 1):
        weight = 0.5 if position in (0, half_steps) else 1.0
        running = running + weight * jnp.mean(own_slices[position].astype(jnp.float32) * partner_slices[STEPS - position].astype(jnp.float32), axis=0)
    return running


def reference(fields, end_weights, directions, analysis, synthesis, decay_rates):
    slabs = NX // SX
    ramp = (slope * jnp.arange(NX).astype(jnp.float32) / NX)[:, None, None]
    split_fields = fields.reshape(slabs, 2, SX, NY, NZ)
    field_a = split_fields[:, 0].reshape(NX, NY, NZ) + ramp
    field_b = split_fields[:, 1].reshape(NX, NY, NZ) + ramp
    split_ends = end_weights.reshape(ORIENT, slabs, 2, SX, NY, NZ)
    start_a = split_ends[:, :, 0].reshape(ORIENT, NX, NY, NZ)
    start_b = split_ends[:, :, 1].reshape(ORIENT, NX, NY, NZ)
    forward_slices = propagate(start_a, field_a, field_b, directions, analysis, synthesis, decay_rates)
    backward_slices = propagate(start_b, field_b, field_a, -directions, analysis, synthesis, decay_rates)
    half_steps = STEPS // 2
    partition = jnp.mean(jnp.mean(forward_slices[half_steps].astype(jnp.float32) * backward_slices[half_steps].astype(jnp.float32), axis=0))
    density_a = pair_sum(forward_slices, backward_slices) / partition
    density_b = pair_sum(backward_slices, forward_slices) / partition
    stacked = jnp.stack([density_a.reshape(slabs, SX, NY * NZ), density_b.reshape(slabs, SX, NY * NZ)], axis=1)
    return stacked.reshape(2 * NX, NY * NZ)
```

```python
import functools

import jax
import jax.numpy as jnp
from jax import lax
from jax.experimental import pallas as pl
from jax.experimental.pallas import tpu as pltpu
from jax.sharding import PartitionSpec as P

NZ = 16
STEPS = 4
LANES = 128
ROWS = 64

courant = 0.3
slope = 0.6

BF16 = jnp.bfloat16
F32 = jnp.float32


def swap_species(block):
    count = lax.axis_size("space")
    return lax.ppermute(block, "space", [(i ^ 1, i) for i in range(count)])


def to_next_slab(block):
    count = lax.axis_size("space")
    return lax.ppermute(block, "space", [(i, (i + (2 if i % 2 == 0 else -2)) % count) for i in range(count)])


def rows_of(index):
    return pl.ds(pl.multiple_of(index * ROWS, ROWS), ROWS)


def columns(tile):
    return slice(LANES * tile, LANES * (tile + 1))


def geometry(v_ref, rows):
    lane = lax.broadcasted_iota(jnp.int32, (ROWS, LANES), 1)
    vx, vy, vz = (v_ref[c, rows, :] for c in range(3))
    plus_x, plus_y, plus_z = vx > 0, vy > 0, vz > 0
    rate_x, rate_y, rate_z = (courant * jnp.abs(t) for t in (vx, vy, vz))
    stay = 1.0 - (rate_x + rate_y + rate_z)
    z_from = (lane & (LANES - NZ)) | (jnp.where(plus_z, lane - 1, lane + 1) & (NZ - 1))
    y_from = jnp.where(plus_y, lane - NZ, lane + NZ) & (LANES - 1)
    y_edge = jnp.where(plus_y, lane, LANES - 1 - lane) < NZ
    return plus_x, plus_y, stay, rate_x, rate_y, rate_z, z_from, y_from, y_edge


def pick(tile, index):
    return jnp.take_along_axis(tile, index, axis=1)


def load_plane(ref, plane, rows):
    return [ref[plane, rows, columns(t)].astype(F32) for t in range(ref.shape[2] // LANES)]


def drift(center, before, after, geo):
    plus_x, plus_y, stay, rate_x, rate_y, rate_z, z_from, y_from, y_edge = geo
    tiles = len(center)
    turned = [pick(tile, y_from) for tile in center]
    moved = []
    for t in range(tiles):
        total = stay * center[t]
        if before is not None and after is not None:
            total = total + rate_x * jnp.where(plus_x, before[t], after[t])
        elif before is not None:
            total = total + jnp.where(plus_x, rate_x, 0.0) * before[t]
        elif after is not None:
            total = total + jnp.where(plus_x, 0.0, rate_x) * after[t]
        over = jnp.where(plus_y, turned[t - 1], turned[(t + 1) % tiles])
        total = total + rate_y * jnp.where(y_edge, over, turned[t])
        total = total + rate_z * pick(center[t], z_from)
        moved.append(total)
    return moved


def store_plane(ref, plane, rows, tiles):
    for t, tile in enumerate(tiles):
        ref[plane, rows, columns(t)] = tile.astype(ref.dtype)


def mix(matrix, moved):
    return jnp.dot(matrix, moved, preferred_element_type=F32)


def boltzmann(field):
    return jnp.exp(-0.5 * field)


def alone_kernel(start_ref, first_ref, second_ref, v_ref, m_ref, out_ref, edges_ref, held, moved):
    planes, orient, _ = start_ref.shape
    first = boltzmann(first_ref[...])
    second = boltzmann(second_ref[...])

    def write_edge(step, loaded, rows, plus_x):
        for t in range(len(loaded[0])):
            edges_ref[step, rows, columns(t)] = jnp.where(plus_x, loaded[-1][t], loaded[0][t]).astype(BF16)

    for p in range(planes):
        held[p] = (first[p : p + 1] * start_ref[p].astype(F32)).astype(BF16)

    def advance(step, targets, factor):
        @pl.loop(0, orient // ROWS)
        def _(index):
            rows = rows_of(index)
            geo = geometry(v_ref, rows)
            loaded = [load_plane(held, p, rows) for p in range(planes)]
            if step > 0:
                write_edge(step - 1, loaded, rows, geo[0])
            for p in targets:
                before = loaded[p - 1] if p > 0 else None
                after = loaded[p + 1] if p < planes - 1 else None
                store_plane(moved, p, rows, drift(loaded[p], before, after, geo))

        for p in targets:
            held[p] = (factor[p : p + 1] * mix(m_ref[...], moved[p])).astype(BF16)

    advance(0, range(planes), first * first)
    out_ref[...] = held[...]
    advance(1, range(planes), first * second)
    advance(2, (0, planes - 1), second * second)

    @pl.loop(0, orient // ROWS)
    def _(index):
        rows = rows_of(index)
        faces = [load_plane(held, p, rows) for p in (0, planes - 1)]
        write_edge(2, faces, rows, v_ref[0, rows, :] > 0)


def face_parts(v_ref, rows):
    vx = v_ref[0, rows, :]
    rate = courant * jnp.abs(vx)
    return v_ref[3, rows, :] > 0, jnp.where(vx > 0, rate, 0.0), jnp.where(vx > 0, 0.0, rate)


def face_drifts(v_ref, mine_ref, other_ref, moved, slots):
    @pl.loop(0, v_ref.shape[1] // ROWS)
    def _(index):
        rows = rows_of(index)
        ahead, rate_plus, rate_minus = face_parts(v_ref, rows)
        for t in range(mine_ref.shape[1] // LANES):
            mine = mine_ref[rows, columns(t)].astype(F32)
            other = other_ref[rows, columns(t)].astype(F32)
            face = jnp.where(ahead, mine, other)
            moved[slots[0], rows, columns(t)] = (rate_plus * face).astype(BF16)
            moved[slots[1], rows, columns(t)] = (rate_minus * face).astype(BF16)


def second_step_kernel(
    alone_ref, edge_ref, mine_ref, other_ref, first_ref, second_ref, beyond_ref, v_ref, m_ref, out_ref, next_ref, held, moved
):
    planes, orient, _ = alone_ref.shape
    matrix = m_ref[...]
    first, second = boltzmann(first_ref[...]), boltzmann(second_ref[...])
    beyond = boltzmann(beyond_ref[...])
    face_drifts(v_ref, mine_ref, other_ref, moved, (0, 1))

    @pl.loop(0, orient // ROWS)
    def _(index):
        rows = rows_of(index)
        _, rate_plus, rate_minus = face_parts(v_ref, rows)
        for t in range(edge_ref.shape[1] // LANES):
            edge = edge_ref[rows, columns(t)].astype(F32)
            moved[2, rows, columns(t)] = (rate_minus * edge).astype(BF16)
            moved[3, rows, columns(t)] = (rate_plus * edge).astype(BF16)

    squared = first * first
    for p in range(planes):
        kept = alone_ref[p]
        if p in (0, planes - 1):
            arrived = squared[p : p + 1] * mix(matrix, moved[min(p, 1)])
            kept = (kept.astype(F32) + arrived).astype(BF16)
        held[p + 1] = kept
        out_ref[p] = kept
    held[0] = (beyond[0:1] * beyond[0:1] * mix(matrix, moved[2])).astype(BF16)
    held[planes + 1] = (beyond[2:3] * beyond[2:3] * mix(matrix, moved[3])).astype(BF16)
    count = planes + 2

    @pl.loop(0, orient // ROWS)
    def _(index):
        rows = rows_of(index)
        geo = geometry(v_ref, rows)
        _, rate_plus, rate_minus = face_parts(v_ref, rows)
        loaded = [load_plane(held, p, rows) for p in range(count)]
        for p in range(count):
            before = loaded[p - 1] if p > 0 else None
            after = loaded[p + 1] if p < count - 1 else None
            store_plane(moved, p + 1, rows, drift(loaded[p], before, after, geo))
        store_plane(moved, 0, rows, [rate_minus * tile for tile in loaded[0]])
        store_plane(moved, count + 1, rows, [rate_plus * tile for tile in loaded[-1]])

    cross = first * second
    factors = [beyond[1:2] * beyond[5:6], beyond[0:1] * beyond[4:5]]
    factors += [cross[p : p + 1] for p in range(planes)]
    factors += [beyond[2:3] * beyond[6:7], beyond[3:4] * beyond[7:8]]
    for p, factor in enumerate(factors):
        next_ref[p] = (factor * mix(matrix, moved[p])).astype(BF16)


def third_step_kernel(
    held_ref, mine_ref, other_ref, first_ref, second_ref, beyond_ref, v_ref, m_ref, out_ref, next_ref, held, moved
):
    planes, orient, _ = out_ref.shape
    matrix = m_ref[...]
    first, second = boltzmann(first_ref[...]), boltzmann(second_ref[...])
    beyond = boltzmann(beyond_ref[...])
    face_drifts(v_ref, mine_ref, other_ref, moved, (0, 1))
    cross = first * second
    for p in range(planes):
        kept = held_ref[p + 2]
        if p in (0, planes - 1):
            arrived = cross[p : p + 1] * mix(matrix, moved[min(p, 1)])
            kept = (kept.astype(F32) + arrived).astype(BF16)
        held[p] = kept
        out_ref[p] = kept

    @pl.loop(0, orient // ROWS)
    def _(index):
        rows = rows_of(index)
        geo = geometry(v_ref, rows)
        loaded = [load_plane(held_ref, p, rows) for p in (0, 1)]
        loaded += [load_plane(held, p, rows) for p in range(planes)]
        loaded += [load_plane(held_ref, p, rows) for p in (planes + 2, planes + 3)]
        for p in range(planes + 2):
            store_plane(moved, p, rows, drift(loaded[p + 1], loaded[p], loaded[p + 2], geo))

    squared = second * second
    factors = [beyond[4:5] * beyond[4:5]] + [squared[p : p + 1] for p in range(planes)] + [beyond[6:7] * beyond[6:7]]
    for p, factor in enumerate(factors):
        next_ref[p] = (factor * mix(matrix, moved[p])).astype(BF16)


def pairing_kernel(
    held_ref, mine_ref, other_ref, second_ref, v_ref, m_ref, weight_ref, partner_ref, out_ref, held, moved
):
    planes, orient, cells = partner_ref.shape
    second = boltzmann(second_ref[...])
    squared = second * second
    face_drifts(v_ref, mine_ref, other_ref, moved, (0, 1))
    for p in range(planes):
        kept = held_ref[p + 1]
        if p in (0, planes - 1):
            arrived = squared[p : p + 1] * mix(m_ref[...], moved[min(p, 1)])
            kept = (kept.astype(F32) + arrived).astype(BF16)
        held[p] = kept

    tiles = cells // LANES

    def fold(value):
        return jnp.sum(value.reshape(ROWS // 8, 8, LANES), axis=0)

    def body(index, sums):
        rows = rows_of(index)
        geo = geometry(v_ref, rows)
        loaded = [load_plane(held_ref, 0, rows)]
        loaded += [load_plane(held, p, rows) for p in range(planes)]
        loaded += [load_plane(held_ref, planes + 1, rows)]
        new = []
        for p in range(planes):
            moved_tiles = drift(loaded[p + 1], loaded[p], loaded[p + 2], geo)
            weights = load_plane(weight_ref, p, rows)
            partner = load_plane(partner_ref, p, rows)
            for t in range(tiles):
                last, third = sums[2 * (p * tiles + t)], sums[2 * (p * tiles + t) + 1]
                new.append(last + fold(moved_tiles[t] * weights[t]))
                new.append(third + fold(loaded[p + 1][t] * partner[t]))
        return tuple(new)

    zero = jnp.zeros((8, LANES), F32)
    sums = lax.fori_loop(0, orient // ROWS, body, (zero,) * (2 * planes * tiles))
    for p in range(planes):
        for t in range(tiles):
            last = jnp.sum(sums[2 * (p * tiles + t)], axis=0, keepdims=True)
            third = jnp.sum(sums[2 * (p * tiles + t) + 1], axis=0, keepdims=True)
            factor = second[p : p + 1, columns(t)]
            out_ref[p : p + 1, columns(t)] = (0.5 * factor * last + third / (factor * factor)) / orient


def kernel_call(kernel, outs, scratch, args):
    vmem = pl.BlockSpec(memory_space=pltpu.VMEM)
    return pl.pallas_call(
        kernel,
        out_shape=outs,
        in_specs=[vmem] * len(args),
        out_specs=jax.tree.map(lambda _: vmem, outs),
        scratch_shapes=[pltpu.VMEM(shape, BF16) for shape in scratch],
        compiler_params=pltpu.CompilerParams(vmem_limit_bytes=24 << 20),
    )(*args)


def shards(fields, end_weights, directions, analysis, synthesis, decay_rates):
    device = lax.axis_index("space")
    core = device % 2
    is_first = core == 0
    planes, cells = fields.shape
    orient = end_weights.shape[0]
    plane_index = device // 2 * planes + lax.broadcasted_iota(jnp.int32, (planes, 1), 0)
    ramp = slope * plane_index.astype(F32) / (planes * lax.axis_size("space") // 2)
    own = fields + ramp
    partner = swap_species(fields) + ramp

    velocity = jnp.where(is_first, 1.0, -1.0) * directions
    ahead = (directions[0] > 0)[:, None]
    plus_x = (velocity[0] > 0)[:, None]
    spread = jnp.concatenate([velocity, directions[:1]])[:, :, None]
    spread = jnp.broadcast_to(spread, (4, orient, LANES))

    def message(mine, other):
        return jnp.where(ahead, mine, other)

    faces = jnp.where(plus_x, boltzmann(own[-1]) * end_weights[:, -1].astype(F32), boltzmann(own[0]) * end_weights[:, 0].astype(F32))
    edge0 = faces.astype(BF16)
    near = jnp.where(is_first, jnp.stack([own[-1], own[-2]]), own[:2])
    near_other = jnp.where(is_first, jnp.stack([partner[-1], partner[-2]]), partner[:2])
    field_rows = jnp.concatenate([near, near_other])
    high = lax.reduce_precision(field_rows, 8, 7)
    coded = jnp.concatenate([high, field_rows - high, jnp.zeros((8, cells), F32)]).astype(BF16)
    arrived0 = to_next_slab(jnp.concatenate([message(edge0, swap_species(edge0)), coded]))
    crossed0 = swap_species(arrived0)

    scaled = synthesis.astype(F32) * decay_rates[None]
    mixing = jnp.dot(scaled, analysis.astype(F32), precision=lax.Precision.HIGHEST) + 1.0 / orient
    matrix = mixing.astype(BF16)

    start = jnp.transpose(end_weights, (1, 0, 2))
    slab = jax.ShapeDtypeStruct((planes, orient, cells), BF16)
    wide = lambda extra: jax.ShapeDtypeStruct((planes + extra, orient, cells), BF16)
    alone, edges = kernel_call(
        alone_kernel,
        (slab, jax.ShapeDtypeStruct((STEPS - 1, orient, cells), BF16)),
        (slab.shape, slab.shape),
        (start, own, partner, spread, matrix),
    )
    swapped_edges = swap_species(edges)
    arrived = [to_next_slab(message(edges[s], swapped_edges[s])) for s in range(STEPS - 1)]
    crossed = [swap_species(block) for block in arrived[:-1]]

    def near_fields(block):
        rows = block[orient : orient + 4].astype(F32) + block[orient + 4 : orient + 8].astype(F32)
        return rows[:2], rows[2:]

    mine_first, mine_second = near_fields(arrived0)
    other_second, other_first = near_fields(crossed0)
    low_first = jnp.where(is_first, mine_first, other_first)
    high_first = jnp.where(is_first, other_first, mine_first)
    low_second = jnp.where(is_first, mine_second, other_second)
    high_second = jnp.where(is_first, other_second, mine_second)
    beyond = jnp.concatenate([low_first, high_first, low_second, high_second])

    first_state, second_state = kernel_call(
        second_step_kernel,
        (slab, wide(4)),
        (wide(2).shape, wide(4).shape),
        (alone, edge0, arrived0[:orient], crossed0[:orient], own, partner, beyond, spread, matrix),
    )
    middle, third_state = kernel_call(
        third_step_kernel,
        (slab, wide(2)),
        (slab.shape, wide(2).shape),
        (second_state, arrived[0], crossed[0], own, partner, beyond, spread, matrix),
    )

    half = planes // 2
    sent_middle = jnp.where(is_first, middle[half:], middle[:half])
    kept_middle = jnp.where(is_first, middle[:half], middle[half:])
    met = jnp.sum(kept_middle.astype(F32) * swap_species(sent_middle).astype(F32), axis=1) / orient
    own_half = lax.dynamic_slice_in_dim(own, core * half, half, 0)
    partner_half = lax.dynamic_slice_in_dim(partner, core * half, half, 0)
    met = met / (boltzmann(own_half) * boltzmann(partner_half))
    count = lax.axis_size("space")
    sums = lax.all_to_all(jnp.broadcast_to(jnp.sum(met), (count, 1, LANES)), "space", 0, 0)
    partition = jnp.sum(sums[:, 0, 0]) / (count // 2 * planes * cells)
    met = lax.dynamic_update_slice_in_dim(jnp.zeros((planes, cells), F32), 0.5 * met, core * half, 0)

    partner_start = swap_species(start)
    weights = jnp.einsum("vu,vpc->puc", matrix, jnp.transpose(partner_start, (1, 0, 2)), preferred_element_type=F32)
    face = core * (planes - 1)
    own_face = lax.dynamic_index_in_dim(start, face, 0, False)
    own_weight = jnp.einsum("vu,vc->uc", matrix, own_face, preferred_element_type=F32)
    partner_weight = lax.dynamic_index_in_dim(weights, face, 0, False)
    rate_x = (courant * jnp.abs(directions[0]))[:, None]
    last_weight = rate_x * jnp.where(ahead, partner_weight, own_weight)

    shared = kernel_call(
        pairing_kernel,
        jax.ShapeDtypeStruct((planes, cells), F32),
        (slab.shape, (2, orient, cells)),
        (third_state, arrived[1], crossed[1], partner, spread, matrix, weights.astype(BF16), swap_species(first_state)),
    )
    product = last_weight * arrived[2].astype(F32)
    sent_face = 0.5 * jnp.sum(jnp.where(ahead, product, 0.0), axis=0) / orient
    kept_face = 0.5 * jnp.sum(jnp.where(ahead, 0.0, product), axis=0) / orient
    on_face = lax.broadcasted_iota(jnp.int32, (planes, 1), 0) == face
    sent = shared + met + jnp.where(on_face, boltzmann(partner) * sent_face, 0.0)
    kept = met + jnp.where(on_face, boltzmann(own) * kept_face, 0.0)
    return (kept + swap_species(sent)) / partition


def solution(mesh):
    return jax.shard_map(
        shards,
        mesh=mesh,
        in_specs=(P(("runs", "space"), None), P(None, ("runs", "space"), None), P(), P(), P(), P()),
        out_specs=P(("runs", "space"), None),
        check_vma=False,
    )
```

```python
import functools

import jax
import jax.numpy as jnp
from jax import lax
from jax.experimental import pallas as pl
from jax.experimental.pallas import tpu as pltpu
from jax.sharding import PartitionSpec as P

NZ = 16
STEPS = 4
LANES = 128
ROWS = 64

courant = 0.3
slope = 0.6

BF16 = jnp.bfloat16
F32 = jnp.float32


def swap_species(block):
    count = lax.axis_size("space")
    return lax.ppermute(block, "space", [(i ^ 1, i) for i in range(count)])


def to_next_slab(block):
    count = lax.axis_size("space")
    return lax.ppermute(block, "space", [(i, (i + (2 if i % 2 == 0 else -2)) % count) for i in range(count)])


def rows_of(index):
    return pl.ds(pl.multiple_of(index * ROWS, ROWS), ROWS)


def columns(tile):
    return slice(LANES * tile, LANES * (tile + 1))


def geometry(v_ref, rows):
    lane = lax.broadcasted_iota(jnp.int32, (ROWS, LANES), 1)
    vx, vy, vz = (v_ref[c, rows, :] for c in range(3))
    plus_x, plus_y, plus_z = vx > 0, vy > 0, vz > 0
    rate_x, rate_y, rate_z = (courant * jnp.abs(t) for t in (vx, vy, vz))
    stay = 1.0 - (rate_x + rate_y + rate_z)
    z_from = (lane & (LANES - NZ)) | (jnp.where(plus_z, lane - 1, lane + 1) & (NZ - 1))
    y_from = jnp.where(plus_y, lane - NZ, lane + NZ) & (LANES - 1)
    y_edge = jnp.where(plus_y, lane, LANES - 1 - lane) < NZ
    return plus_x, plus_y, stay, rate_x, rate_y, rate_z, z_from, y_from, y_edge


def pick(tile, index):
    return jnp.take_along_axis(tile, index, axis=1)


def load_plane(ref, plane, rows):
    return [ref[plane, rows, columns(t)].astype(F32) for t in range(ref.shape[2] // LANES)]


def drift(center, before, after, geo):
    plus_x, plus_y, stay, rate_x, rate_y, rate_z, z_from, y_from, y_edge = geo
    tiles = len(center)
    turned = [pick(tile, y_from) for tile in center]
    moved = []
    for t in range(tiles):
        total = stay * center[t]
        if before is not None and after is not None:
            total = total + rate_x * jnp.where(plus_x, before[t], after[t])
        elif before is not None:
            total = total + jnp.where(plus_x, rate_x, 0.0) * before[t]
        elif after is not None:
            total = total + jnp.where(plus_x, 0.0, rate_x) * after[t]
        over = jnp.where(plus_y, turned[t - 1], turned[(t + 1) % tiles])
        total = total + rate_y * jnp.where(y_edge, over, turned[t])
        total = total + rate_z * pick(center[t], z_from)
        moved.append(total)
    return moved


def store_plane(ref, plane, rows, tiles):
    for t, tile in enumerate(tiles):
        ref[plane, rows, columns(t)] = tile.astype(ref.dtype)


def mix(matrix, moved):
    return jnp.dot(matrix, moved, preferred_element_type=F32)


def boltzmann(field):
    return jnp.exp(-0.5 * field)


def alone_kernel(start_ref, first_ref, second_ref, v_ref, m_ref, out_ref, edges_ref, held, moved):
    planes, orient, _ = start_ref.shape
    first = boltzmann(first_ref[...])
    second = boltzmann(second_ref[...])

    def write_edge(step, loaded, rows, plus_x):
        for t in range(len(loaded[0])):
            edges_ref[step, rows, columns(t)] = jnp.where(plus_x, loaded[-1][t], loaded[0][t]).astype(BF16)

    for p in range(planes):
        held[p] = (first[p : p + 1] * start_ref[p].astype(F32)).astype(BF16)

    def advance(step, targets, factor):
        @pl.loop(0, orient // ROWS)
        def _(index):
            rows = rows_of(index)
            geo = geometry(v_ref, rows)
            loaded = [load_plane(held, p, rows) for p in range(planes)]
            if step > 0:
                write_edge(step - 1, loaded, rows, geo[0])
            for p in targets:
                before = loaded[p - 1] if p > 0 else None
                after = loaded[p + 1] if p < planes - 1 else None
                store_plane(moved, p, rows, drift(loaded[p], before, after, geo))

        for p in targets:
            held[p] = (factor[p : p + 1] * mix(m_ref[...], moved[p])).astype(BF16)

    advance(0, range(planes), first * first)
    out_ref[...] = held[...]
    advance(1, range(planes), first * second)
    advance(2, (0, planes - 1), second * second)

    @pl.loop(0, orient // ROWS)
    def _(index):
        rows = rows_of(index)
        faces = [load_plane(held, p, rows) for p in (0, planes - 1)]
        write_edge(2, faces, rows, v_ref[0, rows, :] > 0)


def face_parts(v_ref, rows):
    vx = v_ref[0, rows, :]
    rate = courant * jnp.abs(vx)
    return v_ref[3, rows, :] > 0, jnp.where(vx > 0, rate, 0.0), jnp.where(vx > 0, 0.0, rate)


def face_drifts(v_ref, mine_ref, other_ref, moved, slots):
    @pl.loop(0, v_ref.shape[1] // ROWS)
    def _(index):
        rows = rows_of(index)
        ahead, rate_plus, rate_minus = face_parts(v_ref, rows)
        for t in range(mine_ref.shape[1] // LANES):
            mine = mine_ref[rows, columns(t)].astype(F32)
            other = other_ref[rows, columns(t)].astype(F32)
            face = jnp.where(ahead, mine, other)
            moved[slots[0], rows, columns(t)] = (rate_plus * face).astype(BF16)
            moved[slots[1], rows, columns(t)] = (rate_minus * face).astype(BF16)


def second_step_kernel(
    alone_ref, edge_ref, mine_ref, other_ref, first_ref, second_ref, beyond_ref, v_ref, m_ref, out_ref, next_ref, held, moved
):
    planes, orient, _ = alone_ref.shape
    matrix = m_ref[...]
    first, second = boltzmann(first_ref[...]), boltzmann(second_ref[...])
    beyond = boltzmann(beyond_ref[...])
    face_drifts(v_ref, mine_ref, other_ref, moved, (0, 1))

    @pl.loop(0, orient // ROWS)
    def _(index):
        rows = rows_of(index)
        _, rate_plus, rate_minus = face_parts(v_ref, rows)
        for t in range(edge_ref.shape[1] // LANES):
            edge = edge_ref[rows, columns(t)].astype(F32)
            moved[2, rows, columns(t)] = (rate_minus * edge).astype(BF16)
            moved[3, rows, columns(t)] = (rate_plus * edge).astype(BF16)

    squared = first * first
    for p in range(planes):
        kept = alone_ref[p]
        if p in (0, planes - 1):
            arrived = squared[p : p + 1] * mix(matrix, moved[min(p, 1)])
            kept = (kept.astype(F32) + arrived).astype(BF16)
        held[p + 1] = kept
        out_ref[p] = kept
    held[0] = (beyond[0:1] * beyond[0:1] * mix(matrix, moved[2])).astype(BF16)
    held[planes + 1] = (beyond[2:3] * beyond[2:3] * mix(matrix, moved[3])).astype(BF16)
    count = planes + 2

    @pl.loop(0, orient // ROWS)
    def _(index):
        rows = rows_of(index)
        geo = geometry(v_ref, rows)
        _, rate_plus, rate_minus = face_parts(v_ref, rows)
        loaded = [load_plane(held, p, rows) for p in range(count)]
        for p in range(count):
            before = loaded[p - 1] if p > 0 else None
            after = loaded[p + 1] if p < count - 1 else None
            store_plane(moved, p + 1, rows, drift(loaded[p], before, after, geo))
        store_plane(moved, 0, rows, [rate_minus * tile for tile in loaded[0]])
        store_plane(moved, count + 1, rows, [rate_plus * tile for tile in loaded[-1]])

    cross = first * second
    factors = [beyond[1:2] * beyond[5:6], beyond[0:1] * beyond[4:5]]
    factors += [cross[p : p + 1] for p in range(planes)]
    factors += [beyond[2:3] * beyond[6:7], beyond[3:4] * beyond[7:8]]
    for p, factor in enumerate(factors):
        next_ref[p] = (factor * mix(matrix, moved[p])).astype(BF16)


def middle_kernel(own_ref, partner_ref, message_ref, first_ref, second_ref, v_ref, m_ref, out_ref, moved):
    orient, cells = message_ref.shape
    cross = boltzmann(first_ref[...]) * boltzmann(second_ref[...])

    @pl.loop(0, orient // ROWS)
    def _(index):
        rows = rows_of(index)
        ahead, rate_plus, rate_minus = face_parts(v_ref, rows)
        rate = rate_plus + rate_minus
        for t in range(cells // LANES):
            gained = rate * message_ref[rows, columns(t)].astype(F32)
            moved[0, rows, columns(t)] = jnp.where(ahead, gained, 0.0).astype(BF16)
            moved[1, rows, columns(t)] = jnp.where(ahead, 0.0, gained).astype(BF16)

    own_face = own_ref[0].astype(F32) + cross[0:1] * mix(m_ref[...], moved[0])
    partner_face = partner_ref[0].astype(F32) + cross[0:1] * mix(m_ref[...], moved[1])
    face = jnp.sum(own_face * partner_face, axis=0, keepdims=True)
    inner = jnp.sum(own_ref[1].astype(F32) * partner_ref[1].astype(F32), axis=0, keepdims=True)
    out_ref[0:1] = face / (orient * cross[0:1])
    out_ref[1:2] = inner / (orient * cross[1:2])


def third_step_kernel(
    held_ref, mine_ref, other_ref, first_ref, second_ref, beyond_ref, v_ref, m_ref, next_ref, held, moved
):
    planes, orient, _ = held.shape
    matrix = m_ref[...]
    first, second = boltzmann(first_ref[...]), boltzmann(second_ref[...])
    beyond = boltzmann(beyond_ref[...])
    face_drifts(v_ref, mine_ref, other_ref, moved, (0, 1))
    cross = first * second
    for p in range(planes):
        kept = held_ref[p + 2]
        if p in (0, planes - 1):
            arrived = cross[p : p + 1] * mix(matrix, moved[min(p, 1)])
            kept = (kept.astype(F32) + arrived).astype(BF16)
        held[p] = kept

    @pl.loop(0, orient // ROWS)
    def _(index):
        rows = rows_of(index)
        geo = geometry(v_ref, rows)
        loaded = [load_plane(held_ref, p, rows) for p in (0, 1)]
        loaded += [load_plane(held, p, rows) for p in range(planes)]
        loaded += [load_plane(held_ref, p, rows) for p in (planes + 2, planes + 3)]
        for p in range(planes + 2):
            store_plane(moved, p, rows, drift(loaded[p + 1], loaded[p], loaded[p + 2], geo))

    squared = second * second
    factors = [beyond[4:5] * beyond[4:5]] + [squared[p : p + 1] for p in range(planes)] + [beyond[6:7] * beyond[6:7]]
    for p, factor in enumerate(factors):
        next_ref[p] = (factor * mix(matrix, moved[p])).astype(BF16)


def weight_kernel(partner_ref, face_ref, m_ref, weight_ref, own_ref):
    turned = m_ref[...].T
    for p in range(partner_ref.shape[0]):
        weight_ref[p] = mix(turned, partner_ref[p]).astype(BF16)
    own_ref[...] = mix(turned, face_ref[...]).astype(BF16)


def pairing_kernel(
    held_ref, mine_ref, other_ref, second_ref, v_ref, m_ref, weight_ref, partner_ref, out_ref, held, moved
):
    planes, orient, cells = partner_ref.shape
    second = boltzmann(second_ref[...])
    squared = second * second
    face_drifts(v_ref, mine_ref, other_ref, moved, (0, 1))
    for p in range(planes):
        kept = held_ref[p + 1]
        if p in (0, planes - 1):
            arrived = squared[p : p + 1] * mix(m_ref[...], moved[min(p, 1)])
            kept = (kept.astype(F32) + arrived).astype(BF16)
        held[p] = kept

    tiles = cells // LANES

    def fold(value):
        return jnp.sum(value.reshape(ROWS // 8, 8, LANES), axis=0)

    def body(index, sums):
        rows = rows_of(index)
        geo = geometry(v_ref, rows)
        loaded = [load_plane(held_ref, 0, rows)]
        loaded += [load_plane(held, p, rows) for p in range(planes)]
        loaded += [load_plane(held_ref, planes + 1, rows)]
        new = []
        for p in range(planes):
            moved_tiles = drift(loaded[p + 1], loaded[p], loaded[p + 2], geo)
            weights = load_plane(weight_ref, p, rows)
            partner = load_plane(partner_ref, p, rows)
            for t in range(tiles):
                last, third = sums[2 * (p * tiles + t)], sums[2 * (p * tiles + t) + 1]
                new.append(last + fold(moved_tiles[t] * weights[t]))
                new.append(third + fold(loaded[p + 1][t] * partner[t]))
        return tuple(new)

    zero = jnp.zeros((8, LANES), F32)
    sums = lax.fori_loop(0, orient // ROWS, body, (zero,) * (2 * planes * tiles))
    for p in range(planes):
        for t in range(tiles):
            last = jnp.sum(sums[2 * (p * tiles + t)], axis=0, keepdims=True)
            third = jnp.sum(sums[2 * (p * tiles + t) + 1], axis=0, keepdims=True)
            factor = second[p : p + 1, columns(t)]
            out_ref[p : p + 1, columns(t)] = (0.5 * factor * last + third / (factor * factor)) / orient


def kernel_call(kernel, outs, scratch, args):
    vmem = pl.BlockSpec(memory_space=pltpu.VMEM)
    return pl.pallas_call(
        kernel,
        out_shape=outs,
        in_specs=[vmem] * len(args),
        out_specs=jax.tree.map(lambda _: vmem, outs),
        scratch_shapes=[pltpu.VMEM(shape, BF16) for shape in scratch],
        compiler_params=pltpu.CompilerParams(vmem_limit_bytes=24 << 20),
        cost_estimate=pl.CostEstimate(flops=0, bytes_accessed=0, transcendentals=0),
    )(*args)


def shards(fields, end_weights, directions, analysis, synthesis, decay_rates):
    device = lax.axis_index("space")
    core = device % 2
    is_first = core == 0
    planes, cells = fields.shape
    orient = end_weights.shape[0]
    plane_index = device // 2 * planes + lax.broadcasted_iota(jnp.int32, (planes, 1), 0)
    ramp = slope * plane_index.astype(F32) / (planes * lax.axis_size("space") // 2)
    own = fields + ramp
    partner = swap_species(fields) + ramp

    velocity = jnp.where(is_first, 1.0, -1.0) * directions
    ahead = (directions[0] > 0)[:, None]
    plus_x = (velocity[0] > 0)[:, None]
    spread = jnp.concatenate([velocity, directions[:1]])[:, :, None]
    spread = jnp.broadcast_to(spread, (4, orient, LANES))

    def message(mine, other):
        return jnp.where(ahead, mine, other)

    faces = jnp.where(plus_x, boltzmann(own[-1]) * end_weights[:, -1].astype(F32), boltzmann(own[0]) * end_weights[:, 0].astype(F32))
    edge0 = faces.astype(BF16)
    near = jnp.where(is_first, jnp.stack([own[-1], own[-2]]), own[:2])
    near_other = jnp.where(is_first, jnp.stack([partner[-1], partner[-2]]), partner[:2])
    field_rows = jnp.concatenate([near, near_other])
    high = lax.reduce_precision(field_rows, 8, 7)
    coded = jnp.concatenate([high, field_rows - high, jnp.zeros((8, cells), F32)]).astype(BF16)
    message0 = jnp.concatenate([message(edge0, swap_species(edge0)), coded])

    scaled = synthesis.astype(F32) * decay_rates[None]
    mixing = jnp.dot(scaled, analysis.astype(F32), precision=lax.Precision.HIGHEST) + 1.0 / orient
    matrix = mixing.astype(BF16)

    start, _ = lax.optimization_barrier((jnp.transpose(end_weights, (1, 0, 2)), message0))
    arrived0 = to_next_slab(message0)
    slab = jax.ShapeDtypeStruct((planes, orient, cells), BF16)
    wide = lambda extra: jax.ShapeDtypeStruct((planes + extra, orient, cells), BF16)
    alone, edges = kernel_call(
        alone_kernel,
        (slab, jax.ShapeDtypeStruct((STEPS - 1, orient, cells), BF16)),
        (slab.shape, slab.shape),
        (start, own, partner, spread, matrix),
    )
    swapped_edges = swap_species(edges)
    messages = [message(edges[s], swapped_edges[s]) for s in range(STEPS - 1)]
    arrived = [to_next_slab(block) for block in messages]
    arrived0, _ = lax.optimization_barrier((arrived0, edges))
    crossed0 = swap_species(arrived0)

    def near_fields(block):
        rows = block[orient : orient + 4].astype(F32) + block[orient + 4 : orient + 8].astype(F32)
        return rows[:2], rows[2:]

    mine_first, mine_second = near_fields(arrived0)
    other_second, other_first = near_fields(crossed0)
    low_first = jnp.where(is_first, mine_first, other_first)
    high_first = jnp.where(is_first, other_first, mine_first)
    low_second = jnp.where(is_first, mine_second, other_second)
    high_second = jnp.where(is_first, other_second, mine_second)
    beyond = jnp.concatenate([low_first, high_first, low_second, high_second])

    alone, *_ = lax.optimization_barrier((alone, *messages))
    first_state, second_state = kernel_call(
        second_step_kernel,
        (slab, wide(4)),
        (wide(2).shape, wide(4).shape),
        (alone, edge0, arrived0[:orient], crossed0[:orient], own, partner, beyond, spread, matrix),
    )

    half = planes // 2
    low_half, high_half = second_state[2 : 2 + half], second_state[2 + half : 2 + planes][::-1]
    kept_half = jnp.where(is_first, low_half, high_half)
    partner_half = swap_species(jnp.where(is_first, high_half, low_half))
    arrived1, second_state = lax.optimization_barrier((arrived[0], second_state))
    own_half_field = jnp.where(is_first, own[:half], own[half:][::-1])
    partner_half_field = jnp.where(is_first, partner[:half], partner[half:][::-1])
    met = kernel_call(
        middle_kernel,
        jax.ShapeDtypeStruct((half, cells), F32),
        ((2, orient, cells),),
        (kept_half, partner_half, arrived1, own_half_field, partner_half_field, spread, matrix),
    )
    count = lax.axis_size("space")
    partition = jnp.broadcast_to(jnp.sum(met), (8, LANES))
    distance = 1
    while distance < count:
        partition = partition + lax.ppermute(partition, "space", [(i, i ^ distance) for i in range(count)])
        distance *= 2
    partition = partition[0, 0] / (count // 2 * planes * cells)

    crossed1 = swap_species(arrived1)
    third_state = kernel_call(
        third_step_kernel,
        wide(2),
        (slab.shape, wide(2).shape),
        (second_state, arrived1, crossed1, own, partner, beyond, spread, matrix),
    )
    arrived2, third_state = lax.optimization_barrier((arrived[1], third_state))
    crossed2 = swap_species(arrived2)
    empty = jnp.zeros_like(met)
    met = 0.5 * jnp.where(is_first, jnp.concatenate([met, empty]), jnp.concatenate([empty, met[::-1]]))

    face = core * (planes - 1)
    weights, own_weight = kernel_call(
        weight_kernel,
        (slab, jax.ShapeDtypeStruct((orient, cells), BF16)),
        (),
        (swap_species(start), jnp.where(is_first, start[0], start[-1]), matrix),
    )
    partner_weight = jnp.where(is_first, weights[0], weights[-1]).astype(F32)
    rate_x = (courant * jnp.abs(directions[0]))[:, None]
    last_weight = rate_x * jnp.where(ahead, partner_weight, own_weight.astype(F32))

    shared = kernel_call(
        pairing_kernel,
        jax.ShapeDtypeStruct((planes, cells), F32),
        (slab.shape, (2, orient, cells)),
        (third_state, arrived2, crossed2, partner, spread, matrix, weights, swap_species(first_state)),
    )
    arrived3, shared = lax.optimization_barrier((arrived[2], shared))
    product = last_weight * arrived3.astype(F32)
    sent_face = 0.5 * jnp.sum(jnp.where(ahead, product, 0.0), axis=0) / orient
    kept_face = 0.5 * jnp.sum(jnp.where(ahead, 0.0, product), axis=0) / orient
    on_face = lax.broadcasted_iota(jnp.int32, (planes, 1), 0) == face
    sent = shared + met + jnp.where(on_face, boltzmann(partner) * sent_face, 0.0)
    kept = met + jnp.where(on_face, boltzmann(own) * kept_face, 0.0)
    return (kept + swap_species(sent)) / partition


def solution(mesh):
    return jax.shard_map(
        shards,
        mesh=mesh,
        in_specs=(P(("runs", "space"), None), P(None, ("runs", "space"), None), P(), P(), P(), P()),
        out_specs=P(("runs", "space"), None),
        check_vma=False,
    )
```

```python
import functools

import jax
import jax.numpy as jnp
from jax import lax
from jax.experimental import pallas as pl
from jax.experimental.pallas import tpu as pltpu
from jax.sharding import PartitionSpec as P

NZ = 16
STEPS = 4
LANES = 128
ROWS = 64

courant = 0.3
slope = 0.6

BF16 = jnp.bfloat16
F32 = jnp.float32


def swap_species(block):
    count = lax.axis_size("space")
    return lax.ppermute(block, "space", [(i ^ 1, i) for i in range(count)])


def swap_parts(block, parts):
    size = block.shape[0] // parts
    return jnp.concatenate([swap_species(block[p * size : (p + 1) * size]) for p in range(parts)])


def to_next_slab(block):
    count = lax.axis_size("space")
    return lax.ppermute(block, "space", [(i, (i + (2 if i % 2 == 0 else -2)) % count) for i in range(count)])


def rows_of(index):
    return pl.ds(pl.multiple_of(index * ROWS, ROWS), ROWS)


def columns(tile):
    return slice(LANES * tile, LANES * (tile + 1))


def geometry(v_ref, rows):
    lane = lax.broadcasted_iota(jnp.int32, (ROWS, LANES), 1)
    vx, vy, vz = (v_ref[c, rows, :] for c in range(3))
    plus_x, plus_y, plus_z = vx > 0, vy > 0, vz > 0
    rate_x, rate_y, rate_z = (courant * jnp.abs(t) for t in (vx, vy, vz))
    stay = 1.0 - (rate_x + rate_y + rate_z)
    z_from = (lane & (LANES - NZ)) | (jnp.where(plus_z, lane - 1, lane + 1) & (NZ - 1))
    y_from = jnp.where(plus_y, lane - NZ, lane + NZ) & (LANES - 1)
    y_edge = jnp.where(plus_y, lane, LANES - 1 - lane) < NZ
    return plus_x, plus_y, stay, rate_x, rate_y, rate_z, z_from, y_from, y_edge


def pick(tile, index):
    return jnp.take_along_axis(tile, index, axis=1)


def load_plane(ref, plane, rows):
    return [ref[plane, rows, columns(t)].astype(F32) for t in range(ref.shape[2] // LANES)]


def drift(center, before, after, geo):
    plus_x, plus_y, stay, rate_x, rate_y, rate_z, z_from, y_from, y_edge = geo
    tiles = len(center)
    turned = [pick(tile, y_from) for tile in center]
    moved = []
    for t in range(tiles):
        total = stay * center[t]
        if before is not None and after is not None:
            total = total + rate_x * jnp.where(plus_x, before[t], after[t])
        elif before is not None:
            total = total + jnp.where(plus_x, rate_x, 0.0) * before[t]
        elif after is not None:
            total = total + jnp.where(plus_x, 0.0, rate_x) * after[t]
        over = jnp.where(plus_y, turned[t - 1], turned[(t + 1) % tiles])
        total = total + rate_y * jnp.where(y_edge, over, turned[t])
        total = total + rate_z * pick(center[t], z_from)
        moved.append(total)
    return moved


def store_plane(ref, plane, rows, tiles):
    for t, tile in enumerate(tiles):
        ref[plane, rows, columns(t)] = tile.astype(ref.dtype)


def mix(matrix, moved):
    return jnp.dot(matrix, moved, preferred_element_type=F32)


def boltzmann(field):
    return jnp.exp(-0.5 * field)


def alone_kernel(start_ref, first_ref, second_ref, v_ref, m_ref, out_ref, edges_ref, held, moved):
    planes, orient, _ = start_ref.shape
    first = boltzmann(first_ref[...])
    second = boltzmann(second_ref[...])

    def write_edge(step, loaded, rows, plus_x):
        for t in range(len(loaded[0])):
            edges_ref[step, rows, columns(t)] = jnp.where(plus_x, loaded[-1][t], loaded[0][t]).astype(BF16)

    for p in range(planes):
        held[p] = (first[p : p + 1] * start_ref[p].astype(F32)).astype(BF16)

    def advance(step, targets, factor):
        @pl.loop(0, orient // ROWS)
        def _(index):
            rows = rows_of(index)
            geo = geometry(v_ref, rows)
            loaded = [load_plane(held, p, rows) for p in range(planes)]
            if step > 0:
                write_edge(step - 1, loaded, rows, geo[0])
            for p in targets:
                before = loaded[p - 1] if p > 0 else None
                after = loaded[p + 1] if p < planes - 1 else None
                store_plane(moved, p, rows, drift(loaded[p], before, after, geo))

        for p in targets:
            held[p] = (factor[p : p + 1] * mix(m_ref[...], moved[p])).astype(BF16)

    advance(0, range(planes), first * first)
    out_ref[...] = held[...]
    advance(1, range(planes), first * second)
    advance(2, (0, planes - 1), second * second)

    @pl.loop(0, orient // ROWS)
    def _(index):
        rows = rows_of(index)
        faces = [load_plane(held, p, rows) for p in (0, planes - 1)]
        write_edge(2, faces, rows, v_ref[0, rows, :] > 0)


def face_parts(v_ref, rows):
    vx = v_ref[0, rows, :]
    rate = courant * jnp.abs(vx)
    return v_ref[3, rows, :] > 0, jnp.where(vx > 0, rate, 0.0), jnp.where(vx > 0, 0.0, rate)


def face_drifts(v_ref, mine_ref, other_ref, moved, slots):
    @pl.loop(0, v_ref.shape[1] // ROWS)
    def _(index):
        rows = rows_of(index)
        ahead, rate_plus, rate_minus = face_parts(v_ref, rows)
        for t in range(mine_ref.shape[1] // LANES):
            mine = mine_ref[rows, columns(t)].astype(F32)
            other = other_ref[rows, columns(t)].astype(F32)
            face = jnp.where(ahead, mine, other)
            moved[slots[0], rows, columns(t)] = (rate_plus * face).astype(BF16)
            moved[slots[1], rows, columns(t)] = (rate_minus * face).astype(BF16)


def second_step_kernel(
    alone_ref, edge_ref, mine_ref, other_ref, first_ref, second_ref, beyond_ref, v_ref, m_ref, out_ref, next_ref, held, moved
):
    planes, orient, _ = alone_ref.shape
    matrix = m_ref[...]
    first, second = boltzmann(first_ref[...]), boltzmann(second_ref[...])
    beyond = boltzmann(beyond_ref[...])
    face_drifts(v_ref, mine_ref, other_ref, moved, (0, 1))

    @pl.loop(0, orient // ROWS)
    def _(index):
        rows = rows_of(index)
        _, rate_plus, rate_minus = face_parts(v_ref, rows)
        for t in range(edge_ref.shape[1] // LANES):
            edge = edge_ref[rows, columns(t)].astype(F32)
            moved[2, rows, columns(t)] = (rate_minus * edge).astype(BF16)
            moved[3, rows, columns(t)] = (rate_plus * edge).astype(BF16)

    squared = first * first
    for p in range(planes):
        kept = alone_ref[p]
        if p in (0, planes - 1):
            arrived = squared[p : p + 1] * mix(matrix, moved[min(p, 1)])
            kept = (kept.astype(F32) + arrived).astype(BF16)
        held[p + 1] = kept
        out_ref[p] = kept
    held[0] = (beyond[0:1] * beyond[0:1] * mix(matrix, moved[2])).astype(BF16)
    held[planes + 1] = (beyond[2:3] * beyond[2:3] * mix(matrix, moved[3])).astype(BF16)
    count = planes + 2

    @pl.loop(0, orient // ROWS)
    def _(index):
        rows = rows_of(index)
        geo = geometry(v_ref, rows)
        _, rate_plus, rate_minus = face_parts(v_ref, rows)
        loaded = [load_plane(held, p, rows) for p in range(count)]
        for p in range(count):
            before = loaded[p - 1] if p > 0 else None
            after = loaded[p + 1] if p < count - 1 else None
            store_plane(moved, p + 1, rows, drift(loaded[p], before, after, geo))
        store_plane(moved, 0, rows, [rate_minus * tile for tile in loaded[0]])
        store_plane(moved, count + 1, rows, [rate_plus * tile for tile in loaded[-1]])

    cross = first * second
    factors = [beyond[1:2] * beyond[5:6], beyond[0:1] * beyond[4:5]]
    factors += [cross[p : p + 1] for p in range(planes)]
    factors += [beyond[2:3] * beyond[6:7], beyond[3:4] * beyond[7:8]]
    for p, factor in enumerate(factors):
        next_ref[p] = (factor * mix(matrix, moved[p])).astype(BF16)


def middle_kernel(own_ref, partner_ref, message_ref, first_ref, second_ref, v_ref, m_ref, out_ref, moved):
    orient, cells = message_ref.shape
    cross = boltzmann(first_ref[...]) * boltzmann(second_ref[...])

    @pl.loop(0, orient // ROWS)
    def _(index):
        rows = rows_of(index)
        ahead, rate_plus, rate_minus = face_parts(v_ref, rows)
        rate = rate_plus + rate_minus
        for t in range(cells // LANES):
            gained = rate * message_ref[rows, columns(t)].astype(F32)
            moved[0, rows, columns(t)] = jnp.where(ahead, gained, 0.0).astype(BF16)
            moved[1, rows, columns(t)] = jnp.where(ahead, 0.0, gained).astype(BF16)

    own_face = own_ref[0].astype(F32) + cross[0:1] * mix(m_ref[...], moved[0])
    partner_face = partner_ref[0].astype(F32) + cross[0:1] * mix(m_ref[...], moved[1])
    face = jnp.sum(own_face * partner_face, axis=0, keepdims=True)
    inner = jnp.sum(own_ref[1].astype(F32) * partner_ref[1].astype(F32), axis=0, keepdims=True)
    out_ref[0:1] = face / (orient * cross[0:1])
    out_ref[1:2] = inner / (orient * cross[1:2])


def third_step_kernel(
    held_ref, mine_ref, other_ref, first_ref, second_ref, beyond_ref, v_ref, m_ref, next_ref, held, moved
):
    planes, orient, _ = held.shape
    matrix = m_ref[...]
    first, second = boltzmann(first_ref[...]), boltzmann(second_ref[...])
    beyond = boltzmann(beyond_ref[...])
    face_drifts(v_ref, mine_ref, other_ref, moved, (0, 1))
    cross = first * second
    for p in range(planes):
        kept = held_ref[p + 2]
        if p in (0, planes - 1):
            arrived = cross[p : p + 1] * mix(matrix, moved[min(p, 1)])
            kept = (kept.astype(F32) + arrived).astype(BF16)
        held[p] = kept

    @pl.loop(0, orient // ROWS)
    def _(index):
        rows = rows_of(index)
        geo = geometry(v_ref, rows)
        loaded = [load_plane(held_ref, p, rows) for p in (0, 1)]
        loaded += [load_plane(held, p, rows) for p in range(planes)]
        loaded += [load_plane(held_ref, p, rows) for p in (planes + 2, planes + 3)]
        for p in range(planes + 2):
            store_plane(moved, p, rows, drift(loaded[p + 1], loaded[p], loaded[p + 2], geo))

    squared = second * second
    factors = [beyond[4:5] * beyond[4:5]] + [squared[p : p + 1] for p in range(planes)] + [beyond[6:7] * beyond[6:7]]
    for p, factor in enumerate(factors):
        next_ref[p] = (factor * mix(matrix, moved[p])).astype(BF16)


def weight_kernel(partner_ref, face_ref, m_ref, weight_ref, own_ref):
    turned = m_ref[...].T
    for p in range(partner_ref.shape[0]):
        weight_ref[p] = mix(turned, partner_ref[p]).astype(BF16)
    own_ref[...] = mix(turned, face_ref[...]).astype(BF16)


def pairing_kernel(
    held_ref, mine_ref, other_ref, second_ref, v_ref, m_ref, weight_ref, partner_ref, out_ref, held, moved
):
    planes, orient, cells = partner_ref.shape
    second = boltzmann(second_ref[...])
    squared = second * second
    face_drifts(v_ref, mine_ref, other_ref, moved, (0, 1))
    for p in range(planes):
        kept = held_ref[p + 1]
        if p in (0, planes - 1):
            arrived = squared[p : p + 1] * mix(m_ref[...], moved[min(p, 1)])
            kept = (kept.astype(F32) + arrived).astype(BF16)
        held[p] = kept

    tiles = cells // LANES

    def fold(value):
        return jnp.sum(value.reshape(ROWS // 8, 8, LANES), axis=0)

    def body(index, sums):
        rows = rows_of(index)
        geo = geometry(v_ref, rows)
        loaded = [load_plane(held_ref, 0, rows)]
        loaded += [load_plane(held, p, rows) for p in range(planes)]
        loaded += [load_plane(held_ref, planes + 1, rows)]
        new = []
        for p in range(planes):
            moved_tiles = drift(loaded[p + 1], loaded[p], loaded[p + 2], geo)
            weights = load_plane(weight_ref, p, rows)
            partner = load_plane(partner_ref, p, rows)
            for t in range(tiles):
                last, third = sums[2 * (p * tiles + t)], sums[2 * (p * tiles + t) + 1]
                new.append(last + fold(moved_tiles[t] * weights[t]))
                new.append(third + fold(loaded[p + 1][t] * partner[t]))
        return tuple(new)

    zero = jnp.zeros((8, LANES), F32)
    sums = lax.fori_loop(0, orient // ROWS, body, (zero,) * (2 * planes * tiles))
    for p in range(planes):
        for t in range(tiles):
            last = jnp.sum(sums[2 * (p * tiles + t)], axis=0, keepdims=True)
            third = jnp.sum(sums[2 * (p * tiles + t) + 1], axis=0, keepdims=True)
            factor = second[p : p + 1, columns(t)]
            out_ref[p : p + 1, columns(t)] = (0.5 * factor * last + third / (factor * factor)) / orient


def kernel_call(kernel, outs, scratch, args):
    vmem = pl.BlockSpec(memory_space=pltpu.VMEM)
    return pl.pallas_call(
        kernel,
        out_shape=outs,
        in_specs=[vmem] * len(args),
        out_specs=jax.tree.map(lambda _: vmem, outs),
        scratch_shapes=[pltpu.VMEM(shape, BF16) for shape in scratch],
        compiler_params=pltpu.CompilerParams(vmem_limit_bytes=24 << 20),
        cost_estimate=pl.CostEstimate(flops=0, bytes_accessed=0, transcendentals=0),
    )(*args)


def shards(fields, end_weights, directions, analysis, synthesis, decay_rates):
    device = lax.axis_index("space")
    core = device % 2
    is_first = core == 0
    planes, cells = fields.shape
    orient = end_weights.shape[0]
    plane_index = device // 2 * planes + lax.broadcasted_iota(jnp.int32, (planes, 1), 0)
    ramp = slope * plane_index.astype(F32) / (planes * lax.axis_size("space") // 2)
    own = fields + ramp
    partner = swap_species(fields) + ramp

    signs = jnp.concatenate([jnp.where(is_first, 1.0, -1.0) * jnp.ones((3, 1), F32), jnp.ones((1, 1), F32)])
    spread = signs[:, :, None] * jnp.concatenate([directions, directions[:1]])[:, :, None]
    spread = lax.optimization_barrier(jnp.broadcast_to(spread, (4, orient, LANES)))
    ahead = spread[3, :, :1] > 0
    plus_x = spread[0, :, :1] > 0

    def message(mine, other):
        return jnp.where(ahead, mine, other)

    faces = jnp.where(plus_x, boltzmann(own[-1]) * end_weights[:, -1].astype(F32), boltzmann(own[0]) * end_weights[:, 0].astype(F32))
    edge0 = faces.astype(BF16)
    near = jnp.where(is_first, jnp.stack([own[-1], own[-2]]), own[:2])
    near_other = jnp.where(is_first, jnp.stack([partner[-1], partner[-2]]), partner[:2])
    field_rows = jnp.concatenate([near, near_other])
    high = lax.reduce_precision(field_rows, 8, 7)
    coded = jnp.concatenate([high, field_rows - high, jnp.zeros((8, cells), F32)]).astype(BF16)
    message0 = jnp.concatenate([message(edge0, swap_species(edge0)), coded])

    scaled = synthesis.astype(F32) * decay_rates[None]
    mixing = jnp.dot(scaled, analysis.astype(F32), precision=lax.Precision.HIGHEST) + 1.0 / orient
    matrix = mixing.astype(BF16)

    start, _ = lax.optimization_barrier((jnp.transpose(end_weights, (1, 0, 2)), message0))
    arrived0 = to_next_slab(message0)
    slab = jax.ShapeDtypeStruct((planes, orient, cells), BF16)
    wide = lambda extra: jax.ShapeDtypeStruct((planes + extra, orient, cells), BF16)
    alone, edges = kernel_call(
        alone_kernel,
        (slab, jax.ShapeDtypeStruct((STEPS - 1, orient, cells), BF16)),
        (slab.shape, slab.shape),
        (start, own, partner, spread, matrix),
    )
    swapped_edges = swap_species(edges)
    messages = [message(edges[s], swapped_edges[s]) for s in range(STEPS - 1)]
    arrived = [to_next_slab(block) for block in messages]
    arrived0, _ = lax.optimization_barrier((arrived0, edges))
    crossed0 = swap_species(arrived0)

    def near_fields(block):
        rows = block[orient : orient + 4].astype(F32) + block[orient + 4 : orient + 8].astype(F32)
        return rows[:2], rows[2:]

    mine_first, mine_second = near_fields(arrived0)
    other_second, other_first = near_fields(crossed0)
    low_first = jnp.where(is_first, mine_first, other_first)
    high_first = jnp.where(is_first, other_first, mine_first)
    low_second = jnp.where(is_first, mine_second, other_second)
    high_second = jnp.where(is_first, other_second, mine_second)
    beyond = jnp.concatenate([low_first, high_first, low_second, high_second])

    alone, *_ = lax.optimization_barrier((alone, *messages))
    first_state, second_state = kernel_call(
        second_step_kernel,
        (slab, wide(4)),
        (wide(2).shape, wide(4).shape),
        (alone, edge0, arrived0[:orient], crossed0[:orient], own, partner, beyond, spread, matrix),
    )

    half = planes // 2
    low_half, high_half = second_state[2 : 2 + half], second_state[2 + half : 2 + planes][::-1]
    kept_half = jnp.where(is_first, low_half, high_half)
    arrived1, second_state = lax.optimization_barrier((arrived[0], second_state))
    sent_half, _ = lax.optimization_barrier((jnp.where(is_first, high_half, low_half), arrived1))
    partner_half = swap_species(sent_half)
    own_half_field = jnp.where(is_first, own[:half], own[half:][::-1])
    partner_half_field = jnp.where(is_first, partner[:half], partner[half:][::-1])
    met = kernel_call(
        middle_kernel,
        jax.ShapeDtypeStruct((half, cells), F32),
        ((2, orient, cells),),
        (kept_half, partner_half, arrived1, own_half_field, partner_half_field, spread, matrix),
    )
    count = lax.axis_size("space")
    partition = jnp.broadcast_to(jnp.sum(met), (8, LANES))
    distance = 1
    while distance < count:
        partition = partition + lax.ppermute(partition, "space", [(i, i ^ distance) for i in range(count)])
        distance *= 2
    partition = partition[0, 0] / (count // 2 * planes * cells)

    crossed1 = swap_parts(arrived1, 2)
    third_state = kernel_call(
        third_step_kernel,
        wide(2),
        (slab.shape, wide(2).shape),
        (second_state, arrived1, crossed1, own, partner, beyond, spread, matrix),
    )
    arrived2, third_state = lax.optimization_barrier((arrived[1], third_state))
    crossed2 = swap_parts(arrived2, 2)
    empty = jnp.zeros_like(met)
    met = 0.5 * jnp.where(is_first, jnp.concatenate([met, empty]), jnp.concatenate([empty, met[::-1]]))

    face = core * (planes - 1)
    weights, own_weight = kernel_call(
        weight_kernel,
        (slab, jax.ShapeDtypeStruct((orient, cells), BF16)),
        (),
        (swap_species(start), jnp.where(is_first, start[0], start[-1]), matrix),
    )
    partner_weight = jnp.where(is_first, weights[0], weights[-1]).astype(F32)
    rate_x = courant * jnp.abs(spread[3, :, :1])
    last_weight = rate_x * jnp.where(ahead, partner_weight, own_weight.astype(F32))

    shared = kernel_call(
        pairing_kernel,
        jax.ShapeDtypeStruct((planes, cells), F32),
        (slab.shape, (2, orient, cells)),
        (third_state, arrived2, crossed2, partner, spread, matrix, weights, swap_species(first_state)),
    )
    arrived3, shared = lax.optimization_barrier((arrived[2], shared))
    product = last_weight * arrived3.astype(F32)
    sent_face = 0.5 * jnp.sum(jnp.where(ahead, product, 0.0), axis=0) / orient
    kept_face = 0.5 * jnp.sum(jnp.where(ahead, 0.0, product), axis=0) / orient
    on_face = lax.broadcasted_iota(jnp.int32, (planes, 1), 0) == face
    sent = shared + met + jnp.where(on_face, boltzmann(partner) * sent_face, 0.0)
    kept = met + jnp.where(on_face, boltzmann(own) * kept_face, 0.0)
    return (kept + swap_species(sent)) / partition


def solution(mesh):
    return jax.shard_map(
        shards,
        mesh=mesh,
        in_specs=(P(("runs", "space"), None), P(None, ("runs", "space"), None), P(), P(), P(), P()),
        out_specs=P(("runs", "space"), None),
        check_vma=False,
    )
```

```python
import functools

import jax
import jax.numpy as jnp
from jax import lax
from jax.experimental import pallas as pl
from jax.experimental.pallas import tpu as pltpu
from jax.sharding import PartitionSpec as P

NZ = 16
STEPS = 4
LANES = 128
ROWS = 16
UNROLL = 4

courant = 0.3
slope = 0.6

BF16 = jnp.bfloat16
F32 = jnp.float32


def swap_species(block):
    count = lax.axis_size("space")
    return lax.ppermute(block, "space", [(i ^ 1, i) for i in range(count)])


def to_next_slab(block):
    count = lax.axis_size("space")
    return lax.ppermute(block, "space", [(i, (i + (2 if i % 2 == 0 else -2)) % count) for i in range(count)])


def rows_of(index):
    return pl.ds(pl.multiple_of(index * ROWS, ROWS), ROWS)


def each_row_block(orient):
    def run(body):
        def step(index, carry):
            body(index)
            return carry

        lax.fori_loop(0, orient // ROWS, step, 0, unroll=UNROLL)

    return run


def columns(tile):
    return slice(LANES * tile, LANES * (tile + 1))


def geometry(v_ref, rows):
    lane = lax.broadcasted_iota(jnp.int32, (ROWS, LANES), 1)
    vx, vy, vz = (v_ref[c, rows, :] for c in range(3))
    narrow = vx.astype(BF16)
    plus_x, narrow_plus, plus_y, plus_z = vx > 0, narrow > jnp.zeros_like(narrow), vy > 0, vz > 0
    rate_x, rate_y, rate_z = (courant * jnp.abs(t) for t in (vx, vy, vz))
    stay = 1.0 - (rate_x + rate_y + rate_z)
    z_from = (lane & (LANES - NZ)) | (jnp.where(plus_z, lane - 1, lane + 1) & (NZ - 1))
    y_from = jnp.where(plus_y, lane - NZ, lane + NZ) & (LANES - 1)
    y_edge = jnp.where(plus_y, lane, LANES - 1 - lane) < NZ
    return plus_x, narrow_plus, plus_y, stay, rate_x, rate_y, rate_z, z_from, y_from, y_edge


def pick(tile, index):
    return jnp.take_along_axis(tile, index, axis=1, mode="promise_in_bounds")


def load_plane(ref, plane, rows):
    return [ref[plane, rows, columns(t)] for t in range(ref.shape[2] // LANES)]


def drift(center, before, after, geo):
    plus_x, narrow_plus, plus_y, stay, rate_x, rate_y, rate_z, z_from, y_from, y_edge = geo
    tiles = len(center)
    center = [tile.astype(F32) for tile in center]
    turned = [pick(tile, y_from) for tile in center]
    moved = []
    for t in range(tiles):
        total = stay * center[t]
        if before is not None and after is not None:
            total = total + rate_x * jnp.where(narrow_plus, before[t], after[t]).astype(F32)
        elif before is not None:
            total = total + jnp.where(plus_x, rate_x, 0.0) * before[t].astype(F32)
        elif after is not None:
            total = total + jnp.where(plus_x, 0.0, rate_x) * after[t].astype(F32)
        over = jnp.where(plus_y, turned[t - 1], turned[(t + 1) % tiles])
        total = total + rate_y * jnp.where(y_edge, over, turned[t])
        total = total + rate_z * pick(center[t], z_from)
        moved.append(total)
    return moved


def store_plane(ref, plane, rows, tiles):
    for t, tile in enumerate(tiles):
        ref[plane, rows, columns(t)] = tile.astype(ref.dtype)


def mix(matrix, moved):
    return jnp.dot(matrix, moved, preferred_element_type=F32)


def boltzmann(field):
    return jnp.exp(-0.5 * field)


def alone_kernel(start_ref, first_ref, second_ref, v_ref, m_ref, out_ref, edges_ref, held, moved):
    planes, orient, _ = start_ref.shape
    first = boltzmann(first_ref[...])
    second = boltzmann(second_ref[...])

    def write_edge(step, loaded, rows, plus_x):
        for t in range(len(loaded[0])):
            edges_ref[step, rows, columns(t)] = jnp.where(plus_x, loaded[-1][t], loaded[0][t])

    for p in range(planes):
        held[p] = (first[p : p + 1] * start_ref[p].astype(F32)).astype(BF16)

    def advance(step, targets, factor):
        @each_row_block(orient)
        def _(index):
            rows = rows_of(index)
            geo = geometry(v_ref, rows)
            loaded = [load_plane(held, p, rows) for p in range(planes)]
            if step > 0:
                write_edge(step - 1, loaded, rows, geo[1])
            for p in targets:
                before = loaded[p - 1] if p > 0 else None
                after = loaded[p + 1] if p < planes - 1 else None
                store_plane(moved, p, rows, drift(loaded[p], before, after, geo))

        for p in targets:
            held[p] = (factor[p : p + 1] * mix(m_ref[...], moved[p])).astype(BF16)

    advance(0, range(planes), first * first)
    out_ref[...] = held[...]
    advance(1, range(planes), first * second)
    advance(2, (0, planes - 1), second * second)

    @each_row_block(orient)
    def _(index):
        rows = rows_of(index)
        faces = [load_plane(held, p, rows) for p in (0, planes - 1)]
        narrow = v_ref[0, rows, :].astype(BF16)
        write_edge(2, faces, rows, narrow > jnp.zeros_like(narrow))


def face_parts(v_ref, rows):
    vx = v_ref[0, rows, :]
    rate = courant * jnp.abs(vx)
    return v_ref[3, rows, :] > 0, jnp.where(vx > 0, rate, 0.0), jnp.where(vx > 0, 0.0, rate)


def face_drifts(v_ref, mine_ref, other_ref, moved, slots):
    @each_row_block(v_ref.shape[1])
    def _(index):
        rows = rows_of(index)
        ahead, rate_plus, rate_minus = face_parts(v_ref, rows)
        for t in range(mine_ref.shape[1] // LANES):
            mine = mine_ref[rows, columns(t)].astype(F32)
            other = other_ref[rows, columns(t)].astype(F32)
            face = jnp.where(ahead, mine, other)
            moved[slots[0], rows, columns(t)] = (rate_plus * face).astype(BF16)
            moved[slots[1], rows, columns(t)] = (rate_minus * face).astype(BF16)


def second_step_kernel(
    core_ref, alone_ref, edge_ref, mine_ref, other_ref, first_ref, second_ref, beyond_ref, v_ref, m_ref,
    out_ref, next_ref, sent_ref, held, moved,
):
    planes, orient, _ = alone_ref.shape
    matrix = m_ref[...]
    first, second = boltzmann(first_ref[...]), boltzmann(second_ref[...])
    beyond = boltzmann(beyond_ref[...])
    face_drifts(v_ref, mine_ref, other_ref, moved, (0, 1))

    @each_row_block(orient)
    def _(index):
        rows = rows_of(index)
        _, rate_plus, rate_minus = face_parts(v_ref, rows)
        for t in range(edge_ref.shape[1] // LANES):
            edge = edge_ref[rows, columns(t)].astype(F32)
            moved[2, rows, columns(t)] = (rate_minus * edge).astype(BF16)
            moved[3, rows, columns(t)] = (rate_plus * edge).astype(BF16)

    squared = first * first
    for p in range(planes):
        kept = alone_ref[p]
        if p in (0, planes - 1):
            arrived = squared[p : p + 1] * mix(matrix, moved[min(p, 1)])
            kept = (kept.astype(F32) + arrived).astype(BF16)
        held[p + 1] = kept
        out_ref[p] = kept
    held[0] = (beyond[0:1] * beyond[0:1] * mix(matrix, moved[2])).astype(BF16)
    held[planes + 1] = (beyond[2:3] * beyond[2:3] * mix(matrix, moved[3])).astype(BF16)
    count = planes + 2

    @each_row_block(orient)
    def _(index):
        rows = rows_of(index)
        geo = geometry(v_ref, rows)
        _, rate_plus, rate_minus = face_parts(v_ref, rows)
        loaded = [load_plane(held, p, rows) for p in range(count)]
        for p in range(count):
            before = loaded[p - 1] if p > 0 else None
            after = loaded[p + 1] if p < count - 1 else None
            store_plane(moved, p + 1, rows, drift(loaded[p], before, after, geo))
        store_plane(moved, 0, rows, [rate_minus * tile.astype(F32) for tile in loaded[0]])
        store_plane(moved, count + 1, rows, [rate_plus * tile.astype(F32) for tile in loaded[-1]])

    cross = first * second
    factors = [beyond[1:2] * beyond[5:6], beyond[0:1] * beyond[4:5]]
    factors += [cross[p : p + 1] for p in range(planes)]
    factors += [beyond[2:3] * beyond[6:7], beyond[3:4] * beyond[7:8]]
    for p, factor in enumerate(factors):
        next_ref[p] = (factor * mix(matrix, moved[p])).astype(BF16)
    core = core_ref[0]
    for p in range(planes // 2):
        sent_ref[p] = next_ref[2 + (planes - 1) * (1 - core) + (2 * core - 1) * p]


def middle_kernel(
    core_ref, own_ref, partner_ref, message_ref, first_ref, second_ref, v_ref, m_ref, out_ref, total_ref, moved
):
    orient, cells = message_ref.shape
    cross = boltzmann(first_ref[...]) * boltzmann(second_ref[...])
    core = core_ref[0]

    @each_row_block(orient)
    def _(index):
        rows = rows_of(index)
        ahead, rate_plus, rate_minus = face_parts(v_ref, rows)
        rate = rate_plus + rate_minus
        for t in range(cells // LANES):
            gained = rate * message_ref[rows, columns(t)].astype(F32)
            moved[0, rows, columns(t)] = jnp.where(ahead, gained, 0.0).astype(BF16)
            moved[1, rows, columns(t)] = jnp.where(ahead, 0.0, gained).astype(BF16)

    planes = own_ref.shape[0] - 4
    face_plane = 2 + (planes - 1) * core
    own_face = own_ref[face_plane].astype(F32) + cross[0:1] * mix(m_ref[...], moved[0])
    partner_face = partner_ref[0].astype(F32) + cross[0:1] * mix(m_ref[...], moved[1])
    face = jnp.sum(own_face * partner_face, axis=0, keepdims=True)
    total = jnp.zeros((1, 1), F32)
    for p in range(planes // 2):
        if p > 0:
            own = own_ref[face_plane + p - 2 * p * core].astype(F32)
            face = jnp.sum(own * partner_ref[p].astype(F32), axis=0, keepdims=True)
        met = face / (orient * cross[p : p + 1])
        out_ref[p : p + 1] = met
        total = total + jnp.sum(met, axis=1, keepdims=True)
    total_ref[...] = jnp.broadcast_to(total, total_ref.shape)


def third_step_kernel(
    held_ref, mine_ref, other_ref, first_ref, second_ref, beyond_ref, v_ref, m_ref, next_ref, held, moved
):
    planes, orient, _ = held.shape
    matrix = m_ref[...]
    first, second = boltzmann(first_ref[...]), boltzmann(second_ref[...])
    beyond = boltzmann(beyond_ref[...])
    face_drifts(v_ref, mine_ref, other_ref, moved, (0, 1))
    cross = first * second
    for p in range(planes):
        kept = held_ref[p + 2]
        if p in (0, planes - 1):
            arrived = cross[p : p + 1] * mix(matrix, moved[min(p, 1)])
            kept = (kept.astype(F32) + arrived).astype(BF16)
        held[p] = kept

    @each_row_block(orient)
    def _(index):
        rows = rows_of(index)
        geo = geometry(v_ref, rows)
        loaded = [load_plane(held_ref, p, rows) for p in (0, 1)]
        loaded += [load_plane(held, p, rows) for p in range(planes)]
        loaded += [load_plane(held_ref, p, rows) for p in (planes + 2, planes + 3)]
        for p in range(planes + 2):
            store_plane(moved, p, rows, drift(loaded[p + 1], loaded[p], loaded[p + 2], geo))

    squared = second * second
    factors = [beyond[4:5] * beyond[4:5]] + [squared[p : p + 1] for p in range(planes)] + [beyond[6:7] * beyond[6:7]]
    for p, factor in enumerate(factors):
        next_ref[p] = (factor * mix(matrix, moved[p])).astype(BF16)


def weight_kernel(core_ref, partner_ref, start_ref, turned_ref, v_ref, weight_ref, last_ref):
    planes, orient, _ = partner_ref.shape
    face = core_ref[0] * (planes - 1)
    turned = turned_ref[...]
    for p in range(planes):
        weight_ref[p] = mix(turned, partner_ref[p]).astype(BF16)
    last_ref[...] = mix(turned, start_ref[face]).astype(BF16)

    @each_row_block(orient)
    def _(index):
        rows = rows_of(index)
        ahead = v_ref[3, rows, :] > 0
        rate = courant * jnp.abs(v_ref[3, rows, :])
        for t in range(last_ref.shape[1] // LANES):
            chosen = jnp.where(
                ahead, weight_ref[face, rows, columns(t)].astype(F32), last_ref[rows, columns(t)].astype(F32)
            )
            last_ref[rows, columns(t)] = (rate * chosen).astype(BF16)


def last_kernel(core_ref, weight_ref, message_ref, shared_ref, met_ref, own_ref, partner_ref, v_ref, sent_ref, kept_ref):
    planes, cells = shared_ref.shape
    orient = message_ref.shape[0]
    core = core_ref[0]
    half = planes // 2
    tiles = cells // LANES

    def fold(value):
        return jnp.sum(value.reshape(ROWS // 8, 8, LANES), axis=0)

    def body(index, sums):
        rows = rows_of(index)
        ahead = v_ref[3, rows, :] > 0
        new = []
        for t in range(tiles):
            product = weight_ref[rows, columns(t)].astype(F32) * message_ref[rows, columns(t)].astype(F32)
            new.append(sums[2 * t] + fold(jnp.where(ahead, product, 0.0)))
            new.append(sums[2 * t + 1] + fold(jnp.where(ahead, 0.0, product)))
        return tuple(new)

    zero = jnp.zeros((8, LANES), F32)
    sums = lax.fori_loop(0, orient // ROWS, body, (zero,) * (2 * tiles), unroll=UNROLL)
    for t in range(tiles):
        gains = [0.5 / orient * jnp.sum(total, axis=0, keepdims=True) for total in sums[2 * t : 2 * t + 2]]
        for p in range(planes):
            at = slice(p, p + 1), columns(t)
            mine = core == (0 if p < half else 1)
            far = min(p, planes - 1 - p)
            met = jnp.where(mine, 0.5 * met_ref[far : far + 1, columns(t)], 0.0)
            sent, kept = shared_ref[at] + met, met
            if far == 0:
                sent = sent + jnp.where(mine, boltzmann(partner_ref[at]) * gains[0], 0.0)
                kept = kept + jnp.where(mine, boltzmann(own_ref[at]) * gains[1], 0.0)
            sent_ref[at] = sent
            kept_ref[at] = kept


def pairing_kernel(
    held_ref, mine_ref, other_ref, second_ref, v_ref, m_ref, weight_ref, partner_ref, out_ref, held, moved
):
    planes, orient, cells = partner_ref.shape
    second = boltzmann(second_ref[...])
    squared = second * second
    face_drifts(v_ref, mine_ref, other_ref, moved, (0, 1))
    for p in range(planes):
        kept = held_ref[p + 1]
        if p in (0, planes - 1):
            arrived = squared[p : p + 1] * mix(m_ref[...], moved[min(p, 1)])
            kept = (kept.astype(F32) + arrived).astype(BF16)
        held[p] = kept

    tiles = cells // LANES

    def fold(value):
        return jnp.sum(value.reshape(ROWS // 8, 8, LANES), axis=0)

    def body(index, sums):
        rows = rows_of(index)
        geo = geometry(v_ref, rows)
        loaded = [load_plane(held_ref, 0, rows)]
        loaded += [load_plane(held, p, rows) for p in range(planes)]
        loaded += [load_plane(held_ref, planes + 1, rows)]
        new = []
        for p in range(planes):
            moved_tiles = drift(loaded[p + 1], loaded[p], loaded[p + 2], geo)
            weights = load_plane(weight_ref, p, rows)
            partner = load_plane(partner_ref, p, rows)
            for t in range(tiles):
                last, third = sums[2 * (p * tiles + t)], sums[2 * (p * tiles + t) + 1]
                new.append(last + fold(moved_tiles[t] * weights[t].astype(F32)))
                new.append(third + fold(loaded[p + 1][t].astype(F32) * partner[t].astype(F32)))
        return tuple(new)

    zero = jnp.zeros((8, LANES), F32)
    sums = lax.fori_loop(0, orient // ROWS, body, (zero,) * (2 * planes * tiles))
    for p in range(planes):
        for t in range(tiles):
            last = jnp.sum(sums[2 * (p * tiles + t)], axis=0, keepdims=True)
            third = jnp.sum(sums[2 * (p * tiles + t) + 1], axis=0, keepdims=True)
            factor = second[p : p + 1, columns(t)]
            out_ref[p : p + 1, columns(t)] = (0.5 * factor * last + third / (factor * factor)) / orient


def kernel_call(kernel, outs, scratch, args):
    vmem = pl.BlockSpec(memory_space=pltpu.VMEM)
    smem = pl.BlockSpec(memory_space=pltpu.SMEM)
    return pl.pallas_call(
        kernel,
        out_shape=outs,
        in_specs=[smem if arg.dtype == jnp.int32 else vmem for arg in args],
        out_specs=jax.tree.map(lambda _: vmem, outs),
        scratch_shapes=[pltpu.VMEM(shape, BF16) for shape in scratch],
        compiler_params=pltpu.CompilerParams(vmem_limit_bytes=12 << 20),
        cost_estimate=pl.CostEstimate(flops=0, bytes_accessed=0, transcendentals=0),
    )(*args)


def shards(fields, end_weights, directions, analysis, synthesis, decay_rates):
    device = lax.axis_index("space")
    core = device % 2
    is_first = core == 0
    planes, cells = fields.shape
    orient = end_weights.shape[0]
    plane_index = device // 2 * planes + lax.broadcasted_iota(jnp.int32, (planes, 1), 0)
    ramp = slope * plane_index.astype(F32) / (planes * lax.axis_size("space") // 2)
    own = fields + ramp
    partner = swap_species(fields) + ramp

    signs = jnp.concatenate([jnp.where(is_first, 1.0, -1.0) * jnp.ones((3, 1), F32), jnp.ones((1, 1), F32)])
    spread = signs[:, :, None] * jnp.concatenate([directions, directions[:1]])[:, :, None]
    spread = lax.optimization_barrier(jnp.broadcast_to(spread, (4, orient, LANES)))
    ahead = spread[3, :, :1] > 0
    plus_x = spread[0, :, :1] > 0

    def message(mine, other):
        return jnp.where(ahead, mine, other)

    faces = jnp.where(plus_x, boltzmann(own[-1]) * end_weights[:, -1].astype(F32), boltzmann(own[0]) * end_weights[:, 0].astype(F32))
    edge0 = faces.astype(BF16)
    near = jnp.where(is_first, jnp.stack([own[-1], own[-2]]), own[:2])
    near_other = jnp.where(is_first, jnp.stack([partner[-1], partner[-2]]), partner[:2])
    field_rows = jnp.concatenate([near, near_other])
    high = lax.reduce_precision(field_rows, 8, 7)
    coded = jnp.concatenate([high, field_rows - high, jnp.zeros((8, cells), F32)]).astype(BF16)
    message0 = jnp.concatenate([message(edge0, swap_species(edge0)), coded])

    scaled = synthesis.astype(F32) * decay_rates[None]
    mixing = jnp.dot(scaled, analysis.astype(F32), precision=lax.Precision.HIGHEST) + 1.0 / orient
    matrix = mixing.astype(BF16)

    raw, _ = lax.optimization_barrier((end_weights, edge0))
    start, _ = lax.optimization_barrier((jnp.transpose(raw, (1, 0, 2)), message0))
    arrived0 = to_next_slab(message0)
    slab = jax.ShapeDtypeStruct((planes, orient, cells), BF16)
    wide = lambda extra: jax.ShapeDtypeStruct((planes + extra, orient, cells), BF16)
    alone, edges = kernel_call(
        alone_kernel,
        (slab, jax.ShapeDtypeStruct((STEPS - 1, orient, cells), BF16)),
        (slab.shape, slab.shape),
        (start, own, partner, spread, matrix),
    )
    edges, arrived0 = lax.optimization_barrier((edges, arrived0))
    swapped_edges = swap_species(edges)
    messages = [message(edges[s], swapped_edges[s]) for s in range(STEPS - 1)]
    arrived = [to_next_slab(block) for block in messages]
    crossed0 = swap_species(arrived0)

    def near_fields(block):
        rows = block[orient : orient + 4].astype(F32) + block[orient + 4 : orient + 8].astype(F32)
        return rows[:2], rows[2:]

    mine_first, mine_second = near_fields(arrived0)
    other_second, other_first = near_fields(crossed0)
    low_first = jnp.where(is_first, mine_first, other_first)
    high_first = jnp.where(is_first, other_first, mine_first)
    low_second = jnp.where(is_first, mine_second, other_second)
    high_second = jnp.where(is_first, other_second, mine_second)
    beyond = jnp.concatenate([low_first, high_first, low_second, high_second])

    alone, *_ = lax.optimization_barrier((alone, *messages))
    half = planes // 2
    half_slab = jax.ShapeDtypeStruct((half, orient, cells), BF16)
    core_word = jnp.reshape(core, (1,)).astype(jnp.int32)
    first_state, second_state, sent_half = kernel_call(
        second_step_kernel,
        (slab, wide(4), half_slab),
        (wide(2).shape, wide(4).shape),
        (core_word, alone, edge0, arrived0[:orient], crossed0[:orient], own, partner, beyond, spread, matrix),
    )
    arrived1, second_state = lax.optimization_barrier((arrived[0], second_state))
    sent_half, start, first_state, _ = lax.optimization_barrier((sent_half, start, first_state, arrived1))
    own_half_field = jnp.where(is_first, own[:half], own[half:][::-1])
    partner_half_field = jnp.where(is_first, partner[:half], partner[half:][::-1])
    met, partition = kernel_call(
        middle_kernel,
        (jax.ShapeDtypeStruct((half, cells), F32), jax.ShapeDtypeStruct((8, LANES), F32)),
        ((2, orient, cells),),
        (core_word, second_state, swap_species(sent_half), arrived1, own_half_field, partner_half_field, spread, matrix),
    )
    count = lax.axis_size("space")
    distance = 1
    while distance < count:
        partition = partition + lax.ppermute(partition, "space", [(i, i ^ distance) for i in range(count)])
        distance *= 2
    partition = partition[0, 0] / (count // 2 * planes * cells)

    crossed1 = swap_species(arrived1)
    third_state = kernel_call(
        third_step_kernel,
        wide(2),
        (slab.shape, wide(2).shape),
        (second_state, arrived1, crossed1, own, partner, beyond, spread, matrix),
    )
    arrived2, third_state = lax.optimization_barrier((arrived[1], third_state))
    crossed2 = swap_species(arrived2)
    weights, last_weight = kernel_call(
        weight_kernel,
        (slab, jax.ShapeDtypeStruct((orient, cells), BF16)),
        (),
        (core_word, swap_species(start), start, matrix.T, spread),
    )
    shared = kernel_call(
        pairing_kernel,
        jax.ShapeDtypeStruct((planes, cells), F32),
        (slab.shape, (2, orient, cells)),
        (third_state, arrived2, crossed2, partner, spread, matrix, weights, swap_species(first_state)),
    )
    arrived3, shared = lax.optimization_barrier((arrived[2], shared))
    density = jax.ShapeDtypeStruct((planes, cells), F32)
    sent, kept = kernel_call(
        last_kernel,
        (density, density),
        (),
        (core_word, last_weight, arrived3, shared, met, own, partner, spread),
    )
    return (kept + swap_species(sent)) / partition


def solution(mesh):
    return jax.shard_map(
        shards,
        mesh=mesh,
        in_specs=(P(("runs", "space"), None), P(None, ("runs", "space"), None), P(), P(), P(), P()),
        out_specs=P(("runs", "space"), None),
        check_vma=False,
    )
```

```python
import functools

import jax
import jax.numpy as jnp
from jax import lax
from jax.experimental import pallas as pl
from jax.experimental.pallas import tpu as pltpu
from jax.sharding import PartitionSpec as P

NZ = 16
STEPS = 4
LANES = 128
ROWS = 16
UNROLL = 4

courant = 0.3
slope = 0.6

BF16 = jnp.bfloat16
F32 = jnp.float32


def swap_species(block):
    count = lax.axis_size("space")
    return lax.ppermute(block, "space", [(i ^ 1, i) for i in range(count)])


def to_next_slab(block):
    count = lax.axis_size("space")
    return lax.ppermute(block, "space", [(i, (i + (2 if i % 2 == 0 else -2)) % count) for i in range(count)])


def rows_of(index):
    return pl.ds(pl.multiple_of(index * ROWS, ROWS), ROWS)


def each_row_block(orient):
    def run(body):
        def step(index, carry):
            body(index)
            return carry

        lax.fori_loop(0, orient // ROWS, step, 0, unroll=UNROLL)

    return run


def columns(tile):
    return slice(LANES * tile, LANES * (tile + 1))


def geometry(v_ref, rows, sign=1.0):
    lane = lax.broadcasted_iota(jnp.int32, (ROWS, LANES), 1)
    vx, vy, vz = (sign * v_ref[c, rows, :] for c in range(3))
    narrow = vx.astype(BF16)
    plus_x, narrow_plus, plus_y, plus_z = vx > 0, narrow > jnp.zeros_like(narrow), vy > 0, vz > 0
    rate_x, rate_y, rate_z = (courant * jnp.abs(t) for t in (vx, vy, vz))
    stay = 1.0 - (rate_x + rate_y + rate_z)
    z_from = (lane & (LANES - NZ)) | (jnp.where(plus_z, lane - 1, lane + 1) & (NZ - 1))
    y_from = jnp.where(plus_y, lane - NZ, lane + NZ) & (LANES - 1)
    y_edge = jnp.where(plus_y, lane, LANES - 1 - lane) < NZ
    return plus_x, narrow_plus, plus_y, stay, rate_x, rate_y, rate_z, z_from, y_from, y_edge


def pick(tile, index):
    return jnp.take_along_axis(tile, index, axis=1, mode="promise_in_bounds")


def load_plane(ref, plane, rows):
    return [ref[plane, rows, columns(t)] for t in range(ref.shape[2] // LANES)]


def drift(center, before, after, geo):
    plus_x, narrow_plus, plus_y, stay, rate_x, rate_y, rate_z, z_from, y_from, y_edge = geo
    tiles = len(center)
    center = [tile.astype(F32) for tile in center]
    turned = [pick(tile, y_from) for tile in center]
    moved = []
    for t in range(tiles):
        total = stay * center[t]
        if before is not None and after is not None:
            total = total + rate_x * jnp.where(narrow_plus, before[t], after[t]).astype(F32)
        elif before is not None:
            total = total + jnp.where(plus_x, rate_x, 0.0) * before[t].astype(F32)
        elif after is not None:
            total = total + jnp.where(plus_x, 0.0, rate_x) * after[t].astype(F32)
        over = jnp.where(plus_y, turned[t - 1], turned[(t + 1) % tiles])
        total = total + rate_y * jnp.where(y_edge, over, turned[t])
        total = total + rate_z * pick(center[t], z_from)
        moved.append(total)
    return moved


def store_plane(ref, plane, rows, tiles):
    for t, tile in enumerate(tiles):
        ref[plane, rows, columns(t)] = tile.astype(ref.dtype)


def mix(matrix, moved):
    return jnp.dot(matrix, moved, preferred_element_type=F32)


def boltzmann(field):
    return jnp.exp(-0.5 * field)


def prologue_kernel(core_ref, directions_ref, low_ref, high_ref, fields_ref, spread_ref, edge_ref):
    sign = 1.0 - 2.0 * core_ref[0].astype(F32)
    orient, cells = edge_ref.shape
    low = boltzmann(fields_ref[0:1])
    high = boltzmann(fields_ref[fields_ref.shape[0] - 1 :])
    for c in range(4):
        row = directions_ref[c % 3 : c % 3 + 1]
        column = jnp.broadcast_to(row, (LANES, orient)).T
        spread_ref[c] = column if c == 3 else sign * column

    @each_row_block(orient)
    def _(index):
        rows = rows_of(index)
        plus_x = spread_ref[0, rows, :] > 0
        for t in range(cells // LANES):
            at = rows, columns(t)
            chosen = jnp.where(
                plus_x, high[:, columns(t)] * high_ref[at].astype(F32), low[:, columns(t)] * low_ref[at].astype(F32)
            )
            edge_ref[at] = chosen.astype(BF16)


def write_edge(edges_ref, step, faces, rows, v_ref):
    narrow = v_ref[0, rows, :].astype(BF16)
    plus_x = narrow > jnp.zeros_like(narrow)
    for t in range(len(faces[0])):
        edges_ref[step, rows, columns(t)] = jnp.where(plus_x, faces[-1][t], faces[0][t])


def alone_step(source_ref, moved, targets, v_ref, edges_ref, step):
    planes, orient, _ = source_ref.shape

    @each_row_block(orient)
    def _(index):
        rows = rows_of(index)
        geo = geometry(v_ref, rows)
        loaded = [load_plane(source_ref, p, rows) for p in range(planes)]
        if edges_ref is not None:
            write_edge(edges_ref, step, loaded, rows, v_ref)
        for p in targets:
            before = loaded[p - 1] if p > 0 else None
            after = loaded[p + 1] if p < planes - 1 else None
            store_plane(moved, p, rows, drift(loaded[p], before, after, geo))


def first_alone_kernel(start_ref, first_ref, v_ref, m_ref, out_ref, edges_ref, held, moved):
    planes, orient, _ = start_ref.shape
    first = boltzmann(first_ref[...])
    for p in range(planes):
        held[p] = (first[p : p + 1] * start_ref[p].astype(F32)).astype(BF16)
    alone_step(held, moved, range(planes), v_ref, None, 0)
    for p in (0, planes - 1, *range(1, planes - 1)):
        out_ref[p] = (first[p : p + 1] * first[p : p + 1] * mix(m_ref[...], moved[p])).astype(BF16)

    @each_row_block(orient)
    def _(index):
        rows = rows_of(index)
        write_edge(edges_ref, 0, [load_plane(out_ref, p, rows) for p in (0, planes - 1)], rows, v_ref)


def next_alone_kernel(state_ref, first_ref, second_ref, v_ref, m_ref, edges_ref, held, moved):
    planes, orient, _ = state_ref.shape
    first = boltzmann(first_ref[...])
    second = boltzmann(second_ref[...])
    alone_step(state_ref, moved, range(planes), v_ref, None, 0)
    for p in range(planes):
        held[p] = (first[p : p + 1] * second[p : p + 1] * mix(m_ref[...], moved[p])).astype(BF16)
    alone_step(held, moved, (0, planes - 1), v_ref, edges_ref, 0)
    for p in (0, planes - 1):
        held[p] = (second[p : p + 1] * second[p : p + 1] * mix(m_ref[...], moved[p])).astype(BF16)

    @each_row_block(orient)
    def _(index):
        rows = rows_of(index)
        write_edge(edges_ref, 1, [load_plane(held, p, rows) for p in (0, planes - 1)], rows, v_ref)


def face_parts(v_ref, rows):
    vx = v_ref[0, rows, :]
    rate = courant * jnp.abs(vx)
    return v_ref[3, rows, :] > 0, jnp.where(vx > 0, rate, 0.0), jnp.where(vx > 0, 0.0, rate)


def face_drifts(v_ref, mine_ref, other_ref, moved, slots):
    @each_row_block(v_ref.shape[1])
    def _(index):
        rows = rows_of(index)
        ahead, rate_plus, rate_minus = face_parts(v_ref, rows)
        for t in range(mine_ref.shape[1] // LANES):
            mine = mine_ref[rows, columns(t)].astype(F32)
            other = other_ref[rows, columns(t)].astype(F32)
            face = jnp.where(ahead, mine, other)
            moved[slots[0], rows, columns(t)] = (rate_plus * face).astype(BF16)
            moved[slots[1], rows, columns(t)] = (rate_minus * face).astype(BF16)


def second_step_kernel(
    core_ref, alone_ref, edge_ref, mine_ref, other_ref, first_ref, second_ref, beyond_ref, v_ref, m_ref,
    out_ref, next_ref, sent_ref, held, moved,
):
    planes, orient, _ = alone_ref.shape
    matrix = m_ref[...]
    first, second = boltzmann(first_ref[...]), boltzmann(second_ref[...])
    beyond = boltzmann(beyond_ref[...])
    face_drifts(v_ref, mine_ref, other_ref, moved, (0, 1))

    @each_row_block(orient)
    def _(index):
        rows = rows_of(index)
        _, rate_plus, rate_minus = face_parts(v_ref, rows)
        for t in range(edge_ref.shape[1] // LANES):
            edge = edge_ref[rows, columns(t)].astype(F32)
            moved[2, rows, columns(t)] = (rate_minus * edge).astype(BF16)
            moved[3, rows, columns(t)] = (rate_plus * edge).astype(BF16)

    squared = first * first
    for p in range(planes):
        kept = alone_ref[p]
        if p in (0, planes - 1):
            arrived = squared[p : p + 1] * mix(matrix, moved[min(p, 1)])
            kept = (kept.astype(F32) + arrived).astype(BF16)
        held[p + 1] = kept
        out_ref[p] = kept
    held[0] = (beyond[0:1] * beyond[0:1] * mix(matrix, moved[2])).astype(BF16)
    held[planes + 1] = (beyond[2:3] * beyond[2:3] * mix(matrix, moved[3])).astype(BF16)
    count = planes + 2

    @each_row_block(orient)
    def _(index):
        rows = rows_of(index)
        geo = geometry(v_ref, rows)
        _, rate_plus, rate_minus = face_parts(v_ref, rows)
        loaded = [load_plane(held, p, rows) for p in range(count)]
        for p in range(count):
            before = loaded[p - 1] if p > 0 else None
            after = loaded[p + 1] if p < count - 1 else None
            store_plane(moved, p + 1, rows, drift(loaded[p], before, after, geo))
        store_plane(moved, 0, rows, [rate_minus * tile.astype(F32) for tile in loaded[0]])
        store_plane(moved, count + 1, rows, [rate_plus * tile.astype(F32) for tile in loaded[-1]])

    cross = first * second
    factors = [beyond[1:2] * beyond[5:6], beyond[0:1] * beyond[4:5]]
    factors += [cross[p : p + 1] for p in range(planes)]
    factors += [beyond[2:3] * beyond[6:7], beyond[3:4] * beyond[7:8]]
    for p, factor in enumerate(factors):
        next_ref[p] = (factor * mix(matrix, moved[p])).astype(BF16)
    core = core_ref[0]
    for p in range(planes // 2):
        sent_ref[p] = next_ref[2 + (planes - 1) * (1 - core) + (2 * core - 1) * p]


def middle_kernel(
    core_ref, own_ref, partner_ref, message_ref, first_ref, second_ref, v_ref, m_ref, out_ref, total_ref, moved
):
    orient, cells = message_ref.shape
    cross = boltzmann(first_ref[...]) * boltzmann(second_ref[...])
    core = core_ref[0]

    @each_row_block(orient)
    def _(index):
        rows = rows_of(index)
        ahead, rate_plus, rate_minus = face_parts(v_ref, rows)
        rate = rate_plus + rate_minus
        for t in range(cells // LANES):
            gained = rate * message_ref[rows, columns(t)].astype(F32)
            moved[0, rows, columns(t)] = jnp.where(ahead, gained, 0.0).astype(BF16)
            moved[1, rows, columns(t)] = jnp.where(ahead, 0.0, gained).astype(BF16)

    planes = own_ref.shape[0] - 4
    face_plane = 2 + (planes - 1) * core
    own_face = own_ref[face_plane].astype(F32) + cross[0:1] * mix(m_ref[...], moved[0])
    partner_face = partner_ref[0].astype(F32) + cross[0:1] * mix(m_ref[...], moved[1])
    face = jnp.sum(own_face * partner_face, axis=0, keepdims=True)
    total = jnp.zeros((1, 1), F32)
    for p in range(planes // 2):
        if p > 0:
            own = own_ref[face_plane + p - 2 * p * core].astype(F32)
            face = jnp.sum(own * partner_ref[p].astype(F32), axis=0, keepdims=True)
        met = face / (orient * cross[p : p + 1])
        out_ref[p : p + 1] = met
        total = total + jnp.sum(met, axis=1, keepdims=True)
    total_ref[...] = jnp.broadcast_to(total, total_ref.shape)


def third_step_kernel(
    held_ref, mine_ref, other_ref, first_ref, second_ref, beyond_ref, v_ref, m_ref, next_ref, held, moved
):
    planes, orient, _ = held.shape
    matrix = m_ref[...]
    first, second = boltzmann(first_ref[...]), boltzmann(second_ref[...])
    beyond = boltzmann(beyond_ref[...])
    face_drifts(v_ref, mine_ref, other_ref, moved, (0, 1))
    cross = first * second
    for p in range(planes):
        kept = held_ref[p + 2]
        if p in (0, planes - 1):
            arrived = cross[p : p + 1] * mix(matrix, moved[min(p, 1)])
            kept = (kept.astype(F32) + arrived).astype(BF16)
        held[p] = kept

    @each_row_block(orient)
    def _(index):
        rows = rows_of(index)
        geo = geometry(v_ref, rows)
        loaded = [load_plane(held_ref, p, rows) for p in (0, 1)]
        loaded += [load_plane(held, p, rows) for p in range(planes)]
        loaded += [load_plane(held_ref, p, rows) for p in (planes + 2, planes + 3)]
        for p in range(planes + 2):
            store_plane(moved, p, rows, drift(loaded[p + 1], loaded[p], loaded[p + 2], geo))

    squared = second * second
    factors = [beyond[4:5] * beyond[4:5]] + [squared[p : p + 1] for p in range(planes)] + [beyond[6:7] * beyond[6:7]]
    for p, factor in enumerate(factors):
        next_ref[p] = (factor * mix(matrix, moved[p])).astype(BF16)


def weight_kernel(core_ref, partner_ref, start_ref, turned_ref, weight_ref, own_ref):
    planes = partner_ref.shape[0]
    core = core_ref[0]
    for p in range(planes):
        weight_ref[p] = mix(turned_ref[...], partner_ref[p]).astype(BF16)
    for p in range(2):
        own_ref[p] = mix(turned_ref[...], start_ref[core * (planes - 1) + p - 2 * p * core]).astype(BF16)


def fold(value):
    return jnp.sum(value.reshape(ROWS // 8, 8, LANES), axis=0)


def pairing_kernel(held_ref, second_ref, v_ref, weight_ref, partner_ref, out_ref):
    planes, orient, cells = partner_ref.shape
    second = boltzmann(second_ref[...])
    tiles = cells // LANES

    def body(index, sums):
        rows = rows_of(index)
        geo = geometry(v_ref, rows)
        loaded = [load_plane(held_ref, p, rows) for p in range(planes + 2)]
        new = []
        for p in range(planes):
            moved_tiles = drift(loaded[p + 1], loaded[p], loaded[p + 2], geo)
            weights = load_plane(weight_ref, p, rows)
            partner = load_plane(partner_ref, p, rows)
            for t in range(tiles):
                last, third = sums[2 * (p * tiles + t)], sums[2 * (p * tiles + t) + 1]
                new.append(last + fold(moved_tiles[t] * weights[t].astype(F32)))
                new.append(third + fold(loaded[p + 1][t].astype(F32) * partner[t].astype(F32)))
        return tuple(new)

    zero = jnp.zeros((8, LANES), F32)
    sums = lax.fori_loop(0, orient // ROWS, body, (zero,) * (2 * planes * tiles))
    for p in range(planes):
        for t in range(tiles):
            last = jnp.sum(sums[2 * (p * tiles + t)], axis=0, keepdims=True)
            third = jnp.sum(sums[2 * (p * tiles + t) + 1], axis=0, keepdims=True)
            factor = second[p : p + 1, columns(t)]
            out_ref[p : p + 1, columns(t)] = (0.5 * factor * last + third / (factor * factor)) / orient


def last_kernel(
    core_ref, message_ref, weight_ref, own_weight_ref, own_state_ref, partner_state_ref, shared_ref, met_ref,
    own_ref, partner_ref, v_ref, m_ref, sent_ref, kept_ref, moved, gained,
):
    planes, cells = shared_ref.shape
    orient = m_ref.shape[0]
    tiles = cells // LANES
    core = core_ref[0]
    half = planes // 2
    face = core * (planes - 1)
    inner = face + 1 - 2 * core

    def at_face(ref, depth):
        return jnp.where(core == 0, boltzmann(ref[depth : depth + 1]), boltzmann(ref[planes - 1 - depth : planes - depth]))

    factors = [[at_face(ref, depth) for depth in range(2)] for ref in (partner_ref, own_ref)]

    @each_row_block(orient)
    def _(index):
        rows = rows_of(index)
        ahead, rate_plus, rate_minus = face_parts(v_ref, rows)
        rate = rate_plus + rate_minus
        for t in range(tiles):
            got = rate * message_ref[0, rows, columns(t)].astype(F32)
            moved[0, rows, columns(t)] = jnp.where(ahead, got, 0.0).astype(BF16)
            moved[1, rows, columns(t)] = jnp.where(ahead, 0.0, got).astype(BF16)

    for s in range(2):
        gained[s] = (factors[s][0] * factors[s][0] * mix(m_ref[...], moved[s])).astype(BF16)

    def body(index, sums):
        rows = rows_of(index)
        ahead, rate_plus, rate_minus = face_parts(v_ref, rows)
        rate = rate_plus + rate_minus
        sides = (jnp.where(ahead, rate, 0.0), jnp.where(ahead, 0.0, rate))
        message = load_plane(message_ref, 1, rows)
        new = []
        for s in range(2):
            change = load_plane(gained, s, rows)
            moved_tiles = drift(change, None, None, geometry(v_ref, rows, 1.0 - 2.0 * s))
            if s == 0:
                weights = [load_plane(weight_ref, p, rows) for p in (face, inner)]
            else:
                weights = [load_plane(own_weight_ref, p, rows) for p in (0, 1)]
            third = load_plane((partner_state_ref, own_state_ref)[s], face, rows)
            for t in range(tiles):
                on_face = moved_tiles[t] + sides[s] * message[t].astype(F32)
                wide = change[t].astype(F32)
                terms = (
                    on_face * weights[0][t].astype(F32),
                    sides[s] * wide * weights[1][t].astype(F32),
                    wide * third[t].astype(F32),
                )
                base = 3 * (s * tiles + t)
                new += [sums[base + k] + fold(term) for k, term in enumerate(terms)]
        return tuple(new)

    zero = jnp.zeros((8, LANES), F32)
    sums = lax.fori_loop(0, orient // ROWS, body, (zero,) * (6 * tiles))
    for t in range(tiles):
        shares = []
        for s in range(2):
            base = 3 * (s * tiles + t)
            last, onward, third = (jnp.sum(sums[base + k], axis=0, keepdims=True) / orient for k in range(3))
            near, far = (factors[s][depth][:, columns(t)] for depth in range(2))
            shares.append((0.5 * near * last + third / (near * near), 0.5 * far * onward))
        for p in range(planes):
            at = slice(p, p + 1), columns(t)
            mine = core == (0 if p < half else 1)
            depth = min(p, planes - 1 - p)
            met = jnp.where(mine, 0.5 * met_ref[depth : depth + 1, columns(t)], 0.0)
            sent, kept = shared_ref[at] + met, met
            if depth < 2:
                sent = sent + jnp.where(mine, shares[0][depth], 0.0)
                kept = kept + jnp.where(mine, shares[1][depth], 0.0)
            sent_ref[at] = sent
            kept_ref[at] = kept


def kernel_call(kernel, outs, scratch, args):
    vmem = pl.BlockSpec(memory_space=pltpu.VMEM)
    smem = pl.BlockSpec(memory_space=pltpu.SMEM)
    return pl.pallas_call(
        kernel,
        out_shape=outs,
        in_specs=[smem if arg.dtype == jnp.int32 else vmem for arg in args],
        out_specs=jax.tree.map(lambda _: vmem, outs),
        scratch_shapes=[pltpu.VMEM(shape, BF16) for shape in scratch],
        compiler_params=pltpu.CompilerParams(vmem_limit_bytes=12 << 20),
        cost_estimate=pl.CostEstimate(flops=0, bytes_accessed=0, transcendentals=0),
    )(*args)


def shards(fields, end_weights, directions, analysis, synthesis, decay_rates):
    device = lax.axis_index("space")
    core = device % 2
    is_first = core == 0
    planes, cells = fields.shape
    orient = end_weights.shape[0]
    plane_index = device // 2 * planes + lax.broadcasted_iota(jnp.int32, (planes, 1), 0)
    ramp = slope * plane_index.astype(F32) / (planes * lax.axis_size("space") // 2)
    own = fields + ramp
    partner = swap_species(fields) + ramp

    slab = jax.ShapeDtypeStruct((planes, orient, cells), BF16)
    plane = jax.ShapeDtypeStruct((orient, cells), BF16)
    wide = lambda extra: jax.ShapeDtypeStruct((planes + extra, orient, cells), BF16)
    core_word = jnp.reshape(core, (1,)).astype(jnp.int32)
    spread, edge0 = kernel_call(
        prologue_kernel,
        (jax.ShapeDtypeStruct((4, orient, LANES), F32), plane),
        (),
        (core_word, directions, end_weights[:, 0], end_weights[:, -1], own),
    )
    ahead = spread[3, :, :1] > 0

    def message(mine, other):
        return jnp.where(ahead, mine, other)

    near = jnp.where(is_first, jnp.stack([own[-1], own[-2]]), own[:2])
    near_other = jnp.where(is_first, jnp.stack([partner[-1], partner[-2]]), partner[:2])
    field_rows = jnp.concatenate([near, near_other])
    high = lax.reduce_precision(field_rows, 8, 7)
    coded = jnp.concatenate([high, field_rows - high, jnp.zeros((8, cells), F32)]).astype(BF16)
    message0 = jnp.concatenate([message(edge0, swap_species(edge0)), coded])

    scaled = synthesis.astype(F32) * decay_rates[None]
    mixing = jnp.dot(scaled, analysis.astype(F32), precision=lax.Precision.HIGHEST) + 1.0 / orient
    matrix = mixing.astype(BF16)

    raw, _ = lax.optimization_barrier((end_weights, edge0))
    start, _ = lax.optimization_barrier((jnp.transpose(raw, (1, 0, 2)), message0))
    arrived0 = to_next_slab(message0)
    alone, edges1 = kernel_call(
        first_alone_kernel,
        (slab, jax.ShapeDtypeStruct((1, orient, cells), BF16)),
        (slab.shape, slab.shape),
        (start, own, spread, matrix),
    )
    message1 = message(edges1, swap_species(edges1))
    edges = kernel_call(
        next_alone_kernel,
        jax.ShapeDtypeStruct((2, orient, cells), BF16),
        (slab.shape, slab.shape),
        (alone, own, partner, spread, matrix),
    )
    edges, arrived0 = lax.optimization_barrier((edges, arrived0))
    message2 = message(edges, swap_species(edges))
    arrived = [to_next_slab(message1)[0], to_next_slab(message2)]
    crossed0 = swap_species(arrived0)

    def near_fields(block):
        rows = block[orient : orient + 4].astype(F32) + block[orient + 4 : orient + 8].astype(F32)
        return rows[:2], rows[2:]

    mine_first, mine_second = near_fields(arrived0)
    other_second, other_first = near_fields(crossed0)
    low_first = jnp.where(is_first, mine_first, other_first)
    high_first = jnp.where(is_first, other_first, mine_first)
    low_second = jnp.where(is_first, mine_second, other_second)
    high_second = jnp.where(is_first, other_second, mine_second)
    beyond = jnp.concatenate([low_first, high_first, low_second, high_second])

    alone, *_ = lax.optimization_barrier((alone, message1, message2))
    half = planes // 2
    half_slab = jax.ShapeDtypeStruct((half, orient, cells), BF16)
    first_state, second_state, sent_half = kernel_call(
        second_step_kernel,
        (slab, wide(4), half_slab),
        (wide(2).shape, wide(4).shape),
        (core_word, alone, edge0, arrived0[:orient], crossed0[:orient], own, partner, beyond, spread, matrix),
    )
    arrived1, second_state = lax.optimization_barrier((arrived[0], second_state))
    sent_half, start, first_state, _ = lax.optimization_barrier((sent_half, start, first_state, arrived1))
    own_half_field = jnp.where(is_first, own[:half], own[half:][::-1])
    partner_half_field = jnp.where(is_first, partner[:half], partner[half:][::-1])
    met, partition = kernel_call(
        middle_kernel,
        (jax.ShapeDtypeStruct((half, cells), F32), jax.ShapeDtypeStruct((8, LANES), F32)),
        ((2, orient, cells),),
        (core_word, second_state, swap_species(sent_half), arrived1, own_half_field, partner_half_field, spread, matrix),
    )
    count = lax.axis_size("space")
    distance = 1
    while distance < count:
        partition = partition + lax.ppermute(partition, "space", [(i, i ^ distance) for i in range(count)])
        distance *= 2
    partition = partition[0, 0] / (count // 2 * planes * cells)

    crossed1 = swap_species(arrived1)
    third_state = kernel_call(
        third_step_kernel,
        wide(2),
        (slab.shape, wide(2).shape),
        (second_state, arrived1, crossed1, own, partner, beyond, spread, matrix),
    )
    weights, own_weights = kernel_call(
        weight_kernel,
        (slab, jax.ShapeDtypeStruct((2, orient, cells), BF16)),
        (),
        (core_word, swap_species(start), start, matrix.T),
    )
    partner_state = swap_species(first_state)
    density = jax.ShapeDtypeStruct((planes, cells), F32)
    shared = kernel_call(pairing_kernel, density, (), (third_state, partner, spread, weights, partner_state))
    arrived2, shared = lax.optimization_barrier((arrived[1], shared))
    sent, kept = kernel_call(
        last_kernel,
        (density, density),
        ((2, orient, cells), (2, orient, cells)),
        (
            core_word, arrived2, weights, own_weights, first_state, partner_state, shared, met,
            own, partner, spread, matrix,
        ),
    )
    return (kept + swap_species(sent)) / partition


def solution(mesh):
    return jax.shard_map(
        shards,
        mesh=mesh,
        in_specs=(P(("runs", "space"), None), P(None, ("runs", "space"), None), P(), P(), P(), P()),
        out_specs=P(("runs", "space"), None),
        check_vma=False,
    )
```

```python
import functools

import jax
import jax.numpy as jnp
from jax import lax
from jax.experimental import pallas as pl
from jax.experimental.pallas import tpu as pltpu
from jax.sharding import PartitionSpec as P

NZ = 16
STEPS = 4
LANES = 128
ROWS = 16
UNROLL = 4

courant = 0.3
slope = 0.6

BF16 = jnp.bfloat16
F32 = jnp.float32


def swap_species(block):
    count = lax.axis_size("space")
    return lax.ppermute(block, "space", [(i ^ 1, i) for i in range(count)])


def to_next_slab(block):
    count = lax.axis_size("space")
    return lax.ppermute(block, "space", [(i, (i + (2 if i % 2 == 0 else -2)) % count) for i in range(count)])


def rows_of(index):
    return pl.ds(pl.multiple_of(index * ROWS, ROWS), ROWS)


def each_row_block(orient):
    def run(body):
        def step(index, carry):
            body(index)
            return carry

        lax.fori_loop(0, orient // ROWS, step, 0, unroll=UNROLL)

    return run


def columns(tile):
    return slice(LANES * tile, LANES * (tile + 1))


def geometry(v_ref, rows, sign=1.0):
    lane = lax.broadcasted_iota(jnp.int32, (ROWS, LANES), 1)
    vx, vy, vz = (sign * v_ref[c, rows, :] for c in range(3))
    narrow = vx.astype(BF16)
    plus_x, narrow_plus, plus_y, plus_z = vx > 0, narrow > jnp.zeros_like(narrow), vy > 0, vz > 0
    rate_x, rate_y, rate_z = (courant * jnp.abs(t) for t in (vx, vy, vz))
    stay = 1.0 - (rate_x + rate_y + rate_z)
    z_from = (lane & (LANES - NZ)) | (jnp.where(plus_z, lane - 1, lane + 1) & (NZ - 1))
    y_from = jnp.where(plus_y, lane - NZ, lane + NZ) & (LANES - 1)
    y_edge = jnp.where(plus_y, lane, LANES - 1 - lane) < NZ
    return plus_x, narrow_plus, plus_y, stay, rate_x, rate_y, rate_z, z_from, y_from, y_edge


def pick(tile, index):
    return jnp.take_along_axis(tile, index, axis=1, mode="promise_in_bounds")


def load_plane(ref, plane, rows):
    return [ref[plane, rows, columns(t)] for t in range(ref.shape[2] // LANES)]


def drift(center, before, after, geo):
    plus_x, narrow_plus, plus_y, stay, rate_x, rate_y, rate_z, z_from, y_from, y_edge = geo
    tiles = len(center)
    center = [tile.astype(F32) for tile in center]
    turned = [pick(tile, y_from) for tile in center]
    moved = []
    for t in range(tiles):
        total = stay * center[t]
        if before is not None and after is not None:
            total = total + rate_x * jnp.where(narrow_plus, before[t], after[t]).astype(F32)
        elif before is not None:
            total = total + jnp.where(plus_x, rate_x, 0.0) * before[t].astype(F32)
        elif after is not None:
            total = total + jnp.where(plus_x, 0.0, rate_x) * after[t].astype(F32)
        over = jnp.where(plus_y, turned[t - 1], turned[(t + 1) % tiles])
        total = total + rate_y * jnp.where(y_edge, over, turned[t])
        total = total + rate_z * pick(center[t], z_from)
        moved.append(total)
    return moved


def store_plane(ref, plane, rows, tiles):
    for t, tile in enumerate(tiles):
        ref[plane, rows, columns(t)] = tile.astype(ref.dtype)


def mix(matrix, moved):
    return jnp.dot(matrix, moved, preferred_element_type=F32)


def boltzmann(field):
    return jnp.exp(-0.5 * field)


def prologue_kernel(core_ref, directions_ref, start_ref, fields_ref, spread_ref, edge_ref):
    sign = 1.0 - 2.0 * core_ref[0].astype(F32)
    planes, orient, cells = start_ref.shape
    low = boltzmann(fields_ref[0:1])
    high = boltzmann(fields_ref[fields_ref.shape[0] - 1 :])
    for c in range(4):
        row = directions_ref[c % 3 : c % 3 + 1]
        column = jnp.broadcast_to(row, (LANES, orient)).T
        spread_ref[c] = column if c == 3 else sign * column

    @each_row_block(orient)
    def _(index):
        rows = rows_of(index)
        plus_x = spread_ref[0, rows, :] > 0
        for t in range(cells // LANES):
            at = rows, columns(t)
            chosen = jnp.where(
                plus_x,
                high[:, columns(t)] * start_ref[planes - 1, *at].astype(F32),
                low[:, columns(t)] * start_ref[0, *at].astype(F32),
            )
            edge_ref[at] = chosen.astype(BF16)


def write_edge(edges_ref, step, faces, rows, v_ref):
    narrow = v_ref[0, rows, :].astype(BF16)
    plus_x = narrow > jnp.zeros_like(narrow)
    for t in range(len(faces[0])):
        edges_ref[step, rows, columns(t)] = jnp.where(plus_x, faces[-1][t], faces[0][t])


def alone_step(source_ref, moved, targets, v_ref, edges_ref, step):
    planes, orient, _ = source_ref.shape

    @each_row_block(orient)
    def _(index):
        rows = rows_of(index)
        geo = geometry(v_ref, rows)
        loaded = [load_plane(source_ref, p, rows) for p in range(planes)]
        if edges_ref is not None:
            write_edge(edges_ref, step, loaded, rows, v_ref)
        for p in targets:
            before = loaded[p - 1] if p > 0 else None
            after = loaded[p + 1] if p < planes - 1 else None
            store_plane(moved, p, rows, drift(loaded[p], before, after, geo))


def first_alone_kernel(start_ref, first_ref, v_ref, m_ref, out_ref, inner_ref, edges_ref, held, moved):
    planes, orient, _ = start_ref.shape
    first = boltzmann(first_ref[...])
    for p in range(planes):
        held[p] = (first[p : p + 1] * start_ref[p].astype(F32)).astype(BF16)
    alone_step(held, moved, range(planes), v_ref, None, 0)
    for p in (0, planes - 1, *range(1, planes - 1)):
        state = (first[p : p + 1] * first[p : p + 1] * mix(m_ref[...], moved[p])).astype(BF16)
        out_ref[p] = state
        if 0 < p < planes - 1:
            inner_ref[p - 1] = state

    @each_row_block(orient)
    def _(index):
        rows = rows_of(index)
        write_edge(edges_ref, 0, [load_plane(out_ref, p, rows) for p in (0, planes - 1)], rows, v_ref)


def next_alone_kernel(state_ref, first_ref, second_ref, v_ref, m_ref, edges_ref, held, moved):
    planes, orient, _ = state_ref.shape
    first = boltzmann(first_ref[...])
    second = boltzmann(second_ref[...])
    alone_step(state_ref, moved, range(planes), v_ref, None, 0)
    for p in range(planes):
        held[p] = (first[p : p + 1] * second[p : p + 1] * mix(m_ref[...], moved[p])).astype(BF16)
    alone_step(held, moved, (0, planes - 1), v_ref, edges_ref, 0)
    for p in (0, planes - 1):
        held[p] = (second[p : p + 1] * second[p : p + 1] * mix(m_ref[...], moved[p])).astype(BF16)

    @each_row_block(orient)
    def _(index):
        rows = rows_of(index)
        write_edge(edges_ref, 1, [load_plane(held, p, rows) for p in (0, planes - 1)], rows, v_ref)


def face_parts(v_ref, rows):
    vx = v_ref[0, rows, :]
    rate = courant * jnp.abs(vx)
    return v_ref[3, rows, :] > 0, jnp.where(vx > 0, rate, 0.0), jnp.where(vx > 0, 0.0, rate)


def face_drifts(v_ref, mine_ref, other_ref, moved, slots):
    @each_row_block(v_ref.shape[1])
    def _(index):
        rows = rows_of(index)
        ahead, rate_plus, rate_minus = face_parts(v_ref, rows)
        for t in range(mine_ref.shape[1] // LANES):
            mine = mine_ref[rows, columns(t)].astype(F32)
            other = other_ref[rows, columns(t)].astype(F32)
            face = jnp.where(ahead, mine, other)
            moved[slots[0], rows, columns(t)] = (rate_plus * face).astype(BF16)
            moved[slots[1], rows, columns(t)] = (rate_minus * face).astype(BF16)


def second_step_kernel(
    core_ref, alone_ref, edge_ref, mine_ref, other_ref, first_ref, second_ref, beyond_ref, v_ref, m_ref,
    out_ref, next_ref, sent_ref, kept_ref, outer_ref, held, moved,
):
    planes, orient, _ = alone_ref.shape
    matrix = m_ref[...]
    first, second = boltzmann(first_ref[...]), boltzmann(second_ref[...])
    beyond = boltzmann(beyond_ref[...])
    face_drifts(v_ref, mine_ref, other_ref, moved, (0, 1))

    @each_row_block(orient)
    def _(index):
        rows = rows_of(index)
        _, rate_plus, rate_minus = face_parts(v_ref, rows)
        for t in range(edge_ref.shape[1] // LANES):
            edge = edge_ref[rows, columns(t)].astype(F32)
            moved[2, rows, columns(t)] = (rate_minus * edge).astype(BF16)
            moved[3, rows, columns(t)] = (rate_plus * edge).astype(BF16)

    squared = first * first
    for p in range(planes):
        kept = alone_ref[p]
        if p in (0, planes - 1):
            arrived = squared[p : p + 1] * mix(matrix, moved[min(p, 1)])
            kept = (kept.astype(F32) + arrived).astype(BF16)
            out_ref[min(p, 1)] = kept
        held[p + 1] = kept
    held[0] = (beyond[0:1] * beyond[0:1] * mix(matrix, moved[2])).astype(BF16)
    held[planes + 1] = (beyond[2:3] * beyond[2:3] * mix(matrix, moved[3])).astype(BF16)
    count = planes + 2

    @each_row_block(orient)
    def _(index):
        rows = rows_of(index)
        geo = geometry(v_ref, rows)
        _, rate_plus, rate_minus = face_parts(v_ref, rows)
        loaded = [load_plane(held, p, rows) for p in range(count)]
        for p in range(count):
            before = loaded[p - 1] if p > 0 else None
            after = loaded[p + 1] if p < count - 1 else None
            store_plane(moved, p + 1, rows, drift(loaded[p], before, after, geo))
        store_plane(moved, 0, rows, [rate_minus * tile.astype(F32) for tile in loaded[0]])
        store_plane(moved, count + 1, rows, [rate_plus * tile.astype(F32) for tile in loaded[-1]])

    cross = first * second
    factors = [beyond[1:2] * beyond[5:6], beyond[0:1] * beyond[4:5]]
    factors += [cross[p : p + 1] for p in range(planes)]
    factors += [beyond[2:3] * beyond[6:7], beyond[3:4] * beyond[7:8]]
    for p, factor in enumerate(factors):
        next_ref[p] = (factor * mix(matrix, moved[p])).astype(BF16)
    core = core_ref[0]
    for p in range(planes // 2):
        sent_ref[p] = next_ref[2 + (planes - 1) * (1 - core) + (2 * core - 1) * p]
        kept_ref[p] = next_ref[2 + (planes - 1) * core + (1 - 2 * core) * p]
    outer_ref[0:1] = beyond[4:5] * beyond[4:5]
    outer_ref[1:2] = beyond[6:7] * beyond[6:7]


def middle_kernel(
    own_ref, partner_ref, message_ref, first_ref, second_ref, v_ref, m_ref, out_ref, total_ref, moved
):
    orient, cells = message_ref.shape
    cross = boltzmann(first_ref[...]) * boltzmann(second_ref[...])

    @each_row_block(orient)
    def _(index):
        rows = rows_of(index)
        ahead, rate_plus, rate_minus = face_parts(v_ref, rows)
        rate = rate_plus + rate_minus
        for t in range(cells // LANES):
            gained = rate * message_ref[rows, columns(t)].astype(F32)
            moved[0, rows, columns(t)] = jnp.where(ahead, gained, 0.0).astype(BF16)
            moved[1, rows, columns(t)] = jnp.where(ahead, 0.0, gained).astype(BF16)

    own_face = own_ref[0].astype(F32) + cross[0:1] * mix(m_ref[...], moved[0])
    partner_face = partner_ref[0].astype(F32) + cross[0:1] * mix(m_ref[...], moved[1])
    face = jnp.sum(own_face * partner_face, axis=0, keepdims=True)
    total = jnp.zeros((1, 1), F32)
    for p in range(own_ref.shape[0]):
        if p > 0:
            face = jnp.sum(own_ref[p].astype(F32) * partner_ref[p].astype(F32), axis=0, keepdims=True)
        met = face / (orient * cross[p : p + 1])
        out_ref[p : p + 1] = met
        total = total + jnp.sum(met, axis=1, keepdims=True)
    total_ref[...] = jnp.broadcast_to(total, total_ref.shape)


def third_step_kernel(
    held_ref, mine_ref, other_ref, first_ref, second_ref, outer_ref, v_ref, m_ref, next_ref, held, moved
):
    planes, orient, _ = held.shape
    matrix = m_ref[...]
    first, second = boltzmann(first_ref[...]), boltzmann(second_ref[...])
    face_drifts(v_ref, mine_ref, other_ref, moved, (0, 1))
    cross = first * second
    for p in range(planes):
        kept = held_ref[p + 2]
        if p in (0, planes - 1):
            arrived = cross[p : p + 1] * mix(matrix, moved[min(p, 1)])
            kept = (kept.astype(F32) + arrived).astype(BF16)
        held[p] = kept

    @each_row_block(orient)
    def _(index):
        rows = rows_of(index)
        geo = geometry(v_ref, rows)
        loaded = [load_plane(held_ref, p, rows) for p in (0, 1)]
        loaded += [load_plane(held, p, rows) for p in range(planes)]
        loaded += [load_plane(held_ref, p, rows) for p in (planes + 2, planes + 3)]
        for p in range(planes + 2):
            store_plane(moved, p, rows, drift(loaded[p + 1], loaded[p], loaded[p + 2], geo))

    squared = second * second
    factors = [outer_ref[0:1]] + [squared[p : p + 1] for p in range(planes)] + [outer_ref[1:2]]
    for p, factor in enumerate(factors):
        next_ref[p] = (factor * mix(matrix, moved[p])).astype(BF16)


def weight_kernel(core_ref, partner_ref, start_ref, turned_ref, weight_ref, own_ref):
    planes = partner_ref.shape[0]
    core = core_ref[0]
    for p in range(planes):
        weight_ref[p] = mix(turned_ref[...], partner_ref[p]).astype(BF16)
    for p in range(2):
        own_ref[p] = mix(turned_ref[...], start_ref[core * (planes - 1) + p - 2 * p * core]).astype(BF16)


def fold(value):
    return jnp.sum(value.reshape(ROWS // 8, 8, LANES), axis=0)


def pairing_kernel(held_ref, second_ref, v_ref, weight_ref, faces_ref, inner_ref, out_ref):
    planes, orient, cells = weight_ref.shape
    second = boltzmann(second_ref[...])
    tiles = cells // LANES

    def body(index, sums):
        rows = rows_of(index)
        geo = geometry(v_ref, rows)
        loaded = [load_plane(held_ref, p, rows) for p in range(planes + 2)]
        new = []
        for p in range(planes):
            moved_tiles = drift(loaded[p + 1], loaded[p], loaded[p + 2], geo)
            weights = load_plane(weight_ref, p, rows)
            on_face = p in (0, planes - 1)
            partner = load_plane(faces_ref, min(p, 1), rows) if on_face else load_plane(inner_ref, p - 1, rows)
            for t in range(tiles):
                last, third = sums[2 * (p * tiles + t)], sums[2 * (p * tiles + t) + 1]
                new.append(last + fold(moved_tiles[t] * weights[t].astype(F32)))
                new.append(third + fold(loaded[p + 1][t].astype(F32) * partner[t].astype(F32)))
        return tuple(new)

    zero = jnp.zeros((8, LANES), F32)
    sums = lax.fori_loop(0, orient // ROWS, body, (zero,) * (2 * planes * tiles), unroll=UNROLL)
    for p in range(planes):
        for t in range(tiles):
            last = jnp.sum(sums[2 * (p * tiles + t)], axis=0, keepdims=True)
            third = jnp.sum(sums[2 * (p * tiles + t) + 1], axis=0, keepdims=True)
            factor = second[p : p + 1, columns(t)]
            out_ref[p : p + 1, columns(t)] = (0.5 * factor * last + third / (factor * factor)) / orient


def last_kernel(
    core_ref, message_ref, weight_ref, own_weight_ref, own_faces_ref, partner_faces_ref, shared_ref, met_ref,
    own_ref, partner_ref, v_ref, m_ref, sent_ref, kept_ref, moved, gained,
):
    planes, cells = shared_ref.shape
    orient = m_ref.shape[0]
    tiles = cells // LANES
    core = core_ref[0]
    half = planes // 2
    face = core * (planes - 1)
    inner = face + 1 - 2 * core

    def at_face(ref, depth):
        return jnp.where(core == 0, boltzmann(ref[depth : depth + 1]), boltzmann(ref[planes - 1 - depth : planes - depth]))

    factors = [[at_face(ref, depth) for depth in range(2)] for ref in (partner_ref, own_ref)]

    @each_row_block(orient)
    def _(index):
        rows = rows_of(index)
        ahead, rate_plus, rate_minus = face_parts(v_ref, rows)
        rate = rate_plus + rate_minus
        for t in range(tiles):
            got = rate * message_ref[0, rows, columns(t)].astype(F32)
            moved[0, rows, columns(t)] = jnp.where(ahead, got, 0.0).astype(BF16)
            moved[1, rows, columns(t)] = jnp.where(ahead, 0.0, got).astype(BF16)

    for s in range(2):
        gained[s] = (factors[s][0] * factors[s][0] * mix(m_ref[...], moved[s])).astype(BF16)

    def body(index, sums):
        rows = rows_of(index)
        ahead, rate_plus, rate_minus = face_parts(v_ref, rows)
        rate = rate_plus + rate_minus
        sides = (jnp.where(ahead, rate, 0.0), jnp.where(ahead, 0.0, rate))
        message = load_plane(message_ref, 1, rows)
        new = []
        for s in range(2):
            change = load_plane(gained, s, rows)
            moved_tiles = drift(change, None, None, geometry(v_ref, rows, 1.0 - 2.0 * s))
            if s == 0:
                weights = [load_plane(weight_ref, p, rows) for p in (face, inner)]
            else:
                weights = [load_plane(own_weight_ref, p, rows) for p in (0, 1)]
            third = load_plane((partner_faces_ref, own_faces_ref)[s], core, rows)
            for t in range(tiles):
                on_face = moved_tiles[t] + sides[s] * message[t].astype(F32)
                wide = change[t].astype(F32)
                terms = (
                    on_face * weights[0][t].astype(F32),
                    sides[s] * wide * weights[1][t].astype(F32),
                    wide * third[t].astype(F32),
                )
                base = 3 * (s * tiles + t)
                new += [sums[base + k] + fold(term) for k, term in enumerate(terms)]
        return tuple(new)

    zero = jnp.zeros((8, LANES), F32)
    sums = lax.fori_loop(0, orient // ROWS, body, (zero,) * (6 * tiles), unroll=UNROLL)
    for t in range(tiles):
        shares = []
        for s in range(2):
            base = 3 * (s * tiles + t)
            last, onward, third = (jnp.sum(sums[base + k], axis=0, keepdims=True) / orient for k in range(3))
            near, far = (factors[s][depth][:, columns(t)] for depth in range(2))
            shares.append((0.5 * near * last + third / (near * near), 0.5 * far * onward))
        for p in range(planes):
            at = slice(p, p + 1), columns(t)
            mine = core == (0 if p < half else 1)
            depth = min(p, planes - 1 - p)
            met = jnp.where(mine, 0.5 * met_ref[depth : depth + 1, columns(t)], 0.0)
            sent, kept = shared_ref[at] + met, met
            if depth < 2:
                sent = sent + jnp.where(mine, shares[0][depth], 0.0)
                kept = kept + jnp.where(mine, shares[1][depth], 0.0)
            sent_ref[at] = sent
            kept_ref[at] = kept


def kernel_call(kernel, outs, scratch, args):
    vmem = pl.BlockSpec(memory_space=pltpu.VMEM)
    smem = pl.BlockSpec(memory_space=pltpu.SMEM)
    return pl.pallas_call(
        kernel,
        out_shape=outs,
        in_specs=[smem if arg.dtype == jnp.int32 else vmem for arg in args],
        out_specs=jax.tree.map(lambda _: vmem, outs),
        scratch_shapes=[pltpu.VMEM(shape, BF16) for shape in scratch],
        compiler_params=pltpu.CompilerParams(vmem_limit_bytes=8 << 20),
        cost_estimate=pl.CostEstimate(flops=0, bytes_accessed=0, transcendentals=0),
    )(*args)


def shards(fields, end_weights, directions, analysis, synthesis, decay_rates):
    device = lax.axis_index("space")
    core = device % 2
    is_first = core == 0
    planes, cells = fields.shape
    orient = end_weights.shape[0]
    plane_index = device // 2 * planes + lax.broadcasted_iota(jnp.int32, (planes, 1), 0)
    ramp = slope * plane_index.astype(F32) / (planes * lax.axis_size("space") // 2)
    own = fields + ramp
    partner = swap_species(fields) + ramp

    slab = jax.ShapeDtypeStruct((planes, orient, cells), BF16)
    plane = jax.ShapeDtypeStruct((orient, cells), BF16)
    wide = lambda extra: jax.ShapeDtypeStruct((planes + extra, orient, cells), BF16)
    core_word = jnp.reshape(core, (1,)).astype(jnp.int32)
    start = jnp.transpose(end_weights, (1, 0, 2))
    spread, edge0 = kernel_call(
        prologue_kernel,
        (jax.ShapeDtypeStruct((4, orient, LANES), F32), plane),
        (),
        (core_word, directions, start, own),
    )
    ahead = spread[3, :, :1] > 0

    def message(mine, other):
        return jnp.where(ahead, mine, other)

    near = jnp.where(is_first, jnp.stack([own[-1], own[-2]]), own[:2])
    near_other = jnp.where(is_first, jnp.stack([partner[-1], partner[-2]]), partner[:2])
    field_rows = jnp.concatenate([near, near_other])
    high = lax.reduce_precision(field_rows, 8, 7)
    coded = jnp.concatenate([high, field_rows - high, jnp.zeros((8, cells), F32)]).astype(BF16)
    message0 = jnp.concatenate([message(edge0, swap_species(edge0)), coded])

    scaled = synthesis.astype(F32) * decay_rates[None]
    mixing = jnp.dot(scaled, analysis.astype(F32), precision=lax.Precision.HIGHEST) + 1.0 / orient
    matrix = mixing.astype(BF16)

    start, _ = lax.optimization_barrier((start, message0))
    arrived0 = to_next_slab(message0)
    alone, inner, edges1 = kernel_call(
        first_alone_kernel,
        (slab, wide(-2), jax.ShapeDtypeStruct((1, orient, cells), BF16)),
        (slab.shape, slab.shape),
        (start, own, spread, matrix),
    )
    message1 = message(edges1, swap_species(edges1))
    edges = kernel_call(
        next_alone_kernel,
        jax.ShapeDtypeStruct((2, orient, cells), BF16),
        (slab.shape, slab.shape),
        (alone, own, partner, spread, matrix),
    )
    weights, own_weights = kernel_call(
        weight_kernel,
        (slab, jax.ShapeDtypeStruct((2, orient, cells), BF16)),
        (),
        (core_word, swap_species(start), start, matrix.T),
    )
    edges, arrived0, weights, inner = lax.optimization_barrier((edges, arrived0, weights, inner))
    partner_inner = swap_species(inner)
    message2 = message(edges, swap_species(edges))
    arrived = [to_next_slab(message1)[0], to_next_slab(message2)]
    crossed0 = swap_species(arrived0)

    def near_fields(block):
        rows = block[orient : orient + 4].astype(F32) + block[orient + 4 : orient + 8].astype(F32)
        return rows[:2], rows[2:]

    mine_first, mine_second = near_fields(arrived0)
    other_second, other_first = near_fields(crossed0)
    low_first = jnp.where(is_first, mine_first, other_first)
    high_first = jnp.where(is_first, other_first, mine_first)
    low_second = jnp.where(is_first, mine_second, other_second)
    high_second = jnp.where(is_first, other_second, mine_second)
    beyond = jnp.concatenate([low_first, high_first, low_second, high_second])

    alone, *_ = lax.optimization_barrier((alone, message1, message2, partner_inner))
    half = planes // 2
    half_slab = jax.ShapeDtypeStruct((half, orient, cells), BF16)
    first_faces, second_state, sent_half, kept_half, outer = kernel_call(
        second_step_kernel,
        (wide(2 - planes), wide(4), half_slab, half_slab, jax.ShapeDtypeStruct((2, cells), F32)),
        (wide(2).shape, wide(4).shape),
        (core_word, alone, edge0, arrived0[:orient], crossed0[:orient], own, partner, beyond, spread, matrix),
    )
    arrived1, second_state = lax.optimization_barrier((arrived[0], second_state))
    sent_half, first_faces, _ = lax.optimization_barrier((sent_half, first_faces, arrived1))
    partner_faces = swap_species(first_faces)
    partner_half, crossed1 = lax.optimization_barrier((swap_species(sent_half), swap_species(arrived1)))
    own_half_field = jnp.where(is_first, own[:half], own[half:][::-1])
    partner_half_field = jnp.where(is_first, partner[:half], partner[half:][::-1])
    density = jax.ShapeDtypeStruct((planes, cells), F32)
    met, partition = kernel_call(
        middle_kernel,
        (jax.ShapeDtypeStruct((half, cells), F32), density),
        ((2, orient, cells),),
        (kept_half, partner_half, arrived1, own_half_field, partner_half_field, spread, matrix),
    )
    count = lax.axis_size("space")

    def gathered(value, distance, after):
        received = lax.ppermute(value, "space", [(i, i ^ distance) for i in range(count)])
        received, after = lax.optimization_barrier((received, after))
        return value + received, after

    partition, second_state = gathered(partition, 1, second_state)
    second_state, _ = lax.optimization_barrier((second_state, partition))
    third_state = kernel_call(
        third_step_kernel,
        wide(2),
        (slab.shape, wide(2).shape),
        (second_state, arrived1, crossed1, own, partner, outer, spread, matrix),
    )
    partition, third_state = gathered(partition, 2, third_state)
    third_state, _ = lax.optimization_barrier((third_state, partition))
    shared = kernel_call(pairing_kernel, density, (), (third_state, partner, spread, weights, partner_faces, partner_inner))
    distance = 4
    while distance < count:
        partition, shared = gathered(partition, distance, shared)
        distance *= 2
    partition = partition / (count // 2 * planes * cells)
    arrived2, shared = lax.optimization_barrier((arrived[1], shared))
    sent, kept = kernel_call(
        last_kernel,
        (density, density),
        ((2, orient, cells), (2, orient, cells)),
        (
            core_word, arrived2, weights, own_weights, first_faces, partner_faces, shared, met,
            own, partner, spread, matrix,
        ),
    )
    return (kept + swap_species(sent)) / partition


def solution(mesh):
    return jax.shard_map(
        shards,
        mesh=mesh,
        in_specs=(P(("runs", "space"), None), P(None, ("runs", "space"), None), P(), P(), P(), P()),
        out_specs=P(("runs", "space"), None),
        check_vma=False,
    )
```

```python
import functools

import jax
import jax.numpy as jnp
from jax import lax
from jax.experimental import pallas as pl
from jax.experimental.pallas import tpu as pltpu
from jax.sharding import PartitionSpec as P

NZ = 16
STEPS = 4
LANES = 128
ROWS = 16
UNROLL = 4

courant = 0.3
slope = 0.6

BF16 = jnp.bfloat16
F32 = jnp.float32


def swap_species(block):
    count = lax.axis_size("space")
    return lax.ppermute(block, "space", [(i ^ 1, i) for i in range(count)])


def swap_each(blocks):
    return jnp.concatenate([swap_species(blocks[k : k + 1]) for k in range(blocks.shape[0])])


def to_next_slab(block):
    count = lax.axis_size("space")
    return lax.ppermute(block, "space", [(i, (i + (2 if i % 2 == 0 else -2)) % count) for i in range(count)])


def rows_of(index):
    return pl.ds(pl.multiple_of(index * ROWS, ROWS), ROWS)


def each_row_block(orient):
    def run(body):
        def step(index, carry):
            body(index)
            return carry

        lax.fori_loop(0, orient // ROWS, step, 0, unroll=UNROLL)

    return run


def columns(tile):
    return slice(LANES * tile, LANES * (tile + 1))


def geometry(v_ref, rows, sign=1.0):
    lane = lax.broadcasted_iota(jnp.int32, (ROWS, LANES), 1)
    vx, vy, vz = (sign * v_ref[c, rows, :] for c in range(3))
    narrow = vx.astype(BF16)
    plus_x, narrow_plus, plus_y, plus_z = vx > 0, narrow > jnp.zeros_like(narrow), vy > 0, vz > 0
    rate_x, rate_y, rate_z = (courant * jnp.abs(t) for t in (vx, vy, vz))
    stay = 1.0 - (rate_x + rate_y + rate_z)
    z_from = (lane & (LANES - NZ)) | (jnp.where(plus_z, lane - 1, lane + 1) & (NZ - 1))
    y_from = jnp.where(plus_y, lane - NZ, lane + NZ) & (LANES - 1)
    y_edge = jnp.where(plus_y, lane, LANES - 1 - lane) < NZ
    return plus_x, narrow_plus, plus_y, stay, rate_x, rate_y, rate_z, z_from, y_from, y_edge


def pick(tile, index):
    return jnp.take_along_axis(tile, index, axis=1, mode="promise_in_bounds")


def load_plane(ref, plane, rows):
    return [ref[plane, rows, columns(t)] for t in range(ref.shape[2] // LANES)]


def drift(center, before, after, geo):
    plus_x, narrow_plus, plus_y, stay, rate_x, rate_y, rate_z, z_from, y_from, y_edge = geo
    tiles = len(center)
    center = [tile.astype(F32) for tile in center]
    turned = [pick(tile, y_from) for tile in center]
    moved = []
    for t in range(tiles):
        total = stay * center[t]
        if before is not None and after is not None:
            total = total + rate_x * jnp.where(narrow_plus, before[t], after[t]).astype(F32)
        elif before is not None:
            total = total + jnp.where(plus_x, rate_x, 0.0) * before[t].astype(F32)
        elif after is not None:
            total = total + jnp.where(plus_x, 0.0, rate_x) * after[t].astype(F32)
        over = jnp.where(plus_y, turned[t - 1], turned[(t + 1) % tiles])
        total = total + rate_y * jnp.where(y_edge, over, turned[t])
        total = total + rate_z * pick(center[t], z_from)
        moved.append(total)
    return moved


def store_plane(ref, plane, rows, tiles):
    for t, tile in enumerate(tiles):
        ref[plane, rows, columns(t)] = tile.astype(ref.dtype)


def mix(matrix, moved):
    return jnp.dot(matrix, moved, preferred_element_type=F32)


def boltzmann(field):
    return jnp.exp(-0.5 * field)


def prologue_kernel(
    core_ref, directions_ref, start_ref, fields_ref, partner_ref, spread_ref, edge_ref, coded_ref, near
):
    sign = 1.0 - 2.0 * core_ref[0].astype(F32)
    planes, orient, cells = start_ref.shape
    low = boltzmann(fields_ref[0:1])
    high = boltzmann(fields_ref[fields_ref.shape[0] - 1 :])
    for c in range(4):
        row = directions_ref[c % 3 : c % 3 + 1]
        column = jnp.broadcast_to(row, (LANES, orient)).T
        spread_ref[c] = column if c == 3 else sign * column

    @each_row_block(orient)
    def _(index):
        rows = rows_of(index)
        plus_x = spread_ref[0, rows, :] > 0
        for t in range(cells // LANES):
            at = rows, columns(t)
            chosen = jnp.where(
                plus_x,
                high[:, columns(t)] * start_ref[planes - 1, *at].astype(F32),
                low[:, columns(t)] * start_ref[0, *at].astype(F32),
            )
            edge_ref[0, *at] = chosen.astype(BF16)

    near[...] = jnp.zeros_like(near)
    for s, ref in enumerate((fields_ref, partner_ref)):
        for depth in range(2):
            high_row, low_row = (ref[p : p + 1] for p in (planes - 1 - depth, depth))
            row = jnp.where(core_ref[0] == 0, high_row, low_row)
            coarse = row.astype(BF16).astype(F32)
            at = 2 * s + depth
            near[at : at + 1] = coarse
            near[at + 4 : at + 5] = row - coarse
    coded_ref[...] = near[...].astype(BF16)


def message_kernel(mine_ref, other_ref, v_ref, out_ref):
    orient, cells = mine_ref.shape[1:]

    @each_row_block(orient)
    def _(index):
        rows = rows_of(index)
        narrow = v_ref[3, rows, :].astype(BF16)
        ahead = narrow > jnp.zeros_like(narrow)
        for p in range(mine_ref.shape[0]):
            for t in range(cells // LANES):
                at = p, rows, columns(t)
                out_ref[at] = jnp.where(ahead, mine_ref[at], other_ref[at])


def first_message_kernel(mine_ref, other_ref, coded_ref, v_ref, out_ref):
    message_kernel(mine_ref, other_ref, v_ref, out_ref)
    orient = mine_ref.shape[1]
    out_ref[0, orient:] = coded_ref[...]


def write_edge(edges_ref, step, faces, rows, v_ref):
    narrow = v_ref[0, rows, :].astype(BF16)
    plus_x = narrow > jnp.zeros_like(narrow)
    for t in range(len(faces[0])):
        edges_ref[step, rows, columns(t)] = jnp.where(plus_x, faces[-1][t], faces[0][t])


def alone_step(source_ref, moved, targets, v_ref, edges_ref, step):
    planes, orient, _ = source_ref.shape

    @each_row_block(orient)
    def _(index):
        rows = rows_of(index)
        geo = geometry(v_ref, rows)
        loaded = [load_plane(source_ref, p, rows) for p in range(planes)]
        if edges_ref is not None:
            write_edge(edges_ref, step, loaded, rows, v_ref)
        for p in targets:
            before = loaded[p - 1] if p > 0 else None
            after = loaded[p + 1] if p < planes - 1 else None
            store_plane(moved, p, rows, drift(loaded[p], before, after, geo))


def first_alone_kernel(start_ref, first_ref, v_ref, m_ref, out_ref, inner_ref, edges_ref, held, moved):
    planes, orient, _ = start_ref.shape
    first = boltzmann(first_ref[...])
    for p in range(planes):
        held[p] = (first[p : p + 1] * start_ref[p].astype(F32)).astype(BF16)
    alone_step(held, moved, range(planes), v_ref, None, 0)
    for p in (0, planes - 1, *range(1, planes - 1)):
        state = (first[p : p + 1] * first[p : p + 1] * mix(m_ref[...], moved[p])).astype(BF16)
        out_ref[p] = state
        if 0 < p < planes - 1:
            inner_ref[p - 1] = state

    @each_row_block(orient)
    def _(index):
        rows = rows_of(index)
        write_edge(edges_ref, 0, [load_plane(out_ref, p, rows) for p in (0, planes - 1)], rows, v_ref)


def next_alone_kernel(state_ref, first_ref, second_ref, v_ref, m_ref, edges_ref, held, moved):
    planes, orient, _ = state_ref.shape
    first = boltzmann(first_ref[...])
    second = boltzmann(second_ref[...])
    alone_step(state_ref, moved, range(planes), v_ref, None, 0)
    for p in range(planes):
        held[p] = (first[p : p + 1] * second[p : p + 1] * mix(m_ref[...], moved[p])).astype(BF16)
    alone_step(held, moved, (0, planes - 1), v_ref, edges_ref, 0)
    for p in (0, planes - 1):
        held[p] = (second[p : p + 1] * second[p : p + 1] * mix(m_ref[...], moved[p])).astype(BF16)

    @each_row_block(orient)
    def _(index):
        rows = rows_of(index)
        write_edge(edges_ref, 1, [load_plane(held, p, rows) for p in (0, planes - 1)], rows, v_ref)


def face_parts(v_ref, rows):
    vx = v_ref[0, rows, :]
    rate = courant * jnp.abs(vx)
    return v_ref[3, rows, :] > 0, jnp.where(vx > 0, rate, 0.0), jnp.where(vx > 0, 0.0, rate)


def face_drifts(v_ref, mine_ref, other_ref, moved, slots):
    @each_row_block(v_ref.shape[1])
    def _(index):
        rows = rows_of(index)
        ahead, rate_plus, rate_minus = face_parts(v_ref, rows)
        for t in range(mine_ref.shape[2] // LANES):
            mine = mine_ref[0, rows, columns(t)].astype(F32)
            other = other_ref[0, rows, columns(t)].astype(F32)
            face = jnp.where(ahead, mine, other)
            moved[slots[0], rows, columns(t)] = (rate_plus * face).astype(BF16)
            moved[slots[1], rows, columns(t)] = (rate_minus * face).astype(BF16)


def second_step_kernel(
    core_ref, alone_ref, edge_ref, mine_ref, other_ref, first_ref, second_ref, v_ref, m_ref,
    out_ref, next_ref, sent_ref, kept_ref, outer_ref, held, moved,
):
    planes, orient, _ = alone_ref.shape
    matrix = m_ref[...]
    first, second = boltzmann(first_ref[...]), boltzmann(second_ref[...])
    core = core_ref[0]
    mine, other = (block[:4] + block[4:8] for block in (ref[0, orient:].astype(F32) for ref in (mine_ref, other_ref)))
    other = (other[2:4], other[0:2])
    mine = (mine[0:2], mine[2:4])
    low = [jnp.where(core == 0, mine[k], other[k]) for k in range(2)]
    high = [jnp.where(core == 0, other[k], mine[k]) for k in range(2)]
    beyond = [boltzmann(block[k : k + 1]) for block in (low[0], high[0], low[1], high[1]) for k in range(2)]
    face_drifts(v_ref, mine_ref, other_ref, moved, (0, 1))

    @each_row_block(orient)
    def _(index):
        rows = rows_of(index)
        _, rate_plus, rate_minus = face_parts(v_ref, rows)
        for t in range(edge_ref.shape[2] // LANES):
            edge = edge_ref[0, rows, columns(t)].astype(F32)
            moved[2, rows, columns(t)] = (rate_minus * edge).astype(BF16)
            moved[3, rows, columns(t)] = (rate_plus * edge).astype(BF16)

    squared = first * first
    for p in range(planes):
        kept = alone_ref[p]
        if p in (0, planes - 1):
            arrived = squared[p : p + 1] * mix(matrix, moved[min(p, 1)])
            kept = (kept.astype(F32) + arrived).astype(BF16)
            out_ref[min(p, 1)] = kept
        held[p + 1] = kept
    held[0] = (beyond[0] * beyond[0] * mix(matrix, moved[2])).astype(BF16)
    held[planes + 1] = (beyond[2] * beyond[2] * mix(matrix, moved[3])).astype(BF16)
    count = planes + 2

    @each_row_block(orient)
    def _(index):
        rows = rows_of(index)
        geo = geometry(v_ref, rows)
        _, rate_plus, rate_minus = face_parts(v_ref, rows)
        loaded = [load_plane(held, p, rows) for p in range(count)]
        for p in range(count):
            before = loaded[p - 1] if p > 0 else None
            after = loaded[p + 1] if p < count - 1 else None
            store_plane(moved, p + 1, rows, drift(loaded[p], before, after, geo))
        store_plane(moved, 0, rows, [rate_minus * tile.astype(F32) for tile in loaded[0]])
        store_plane(moved, count + 1, rows, [rate_plus * tile.astype(F32) for tile in loaded[-1]])

    cross = first * second
    factors = [beyond[1] * beyond[5], beyond[0] * beyond[4]]
    factors += [cross[p : p + 1] for p in range(planes)]
    factors += [beyond[2] * beyond[6], beyond[3] * beyond[7]]
    for p, factor in enumerate(factors):
        next_ref[p] = (factor * mix(matrix, moved[p])).astype(BF16)
    for p in range(planes // 2):
        sent_ref[p] = next_ref[2 + (planes - 1) * (1 - core) + (2 * core - 1) * p]
        kept_ref[p] = next_ref[2 + (planes - 1) * core + (1 - 2 * core) * p]
    outer_ref[0:1] = beyond[4] * beyond[4]
    outer_ref[1:2] = beyond[6] * beyond[6]


def middle_kernel(
    own_ref, partner_ref, message_ref, first_ref, second_ref, v_ref, m_ref, out_ref, total_ref, moved
):
    _, orient, cells = own_ref.shape
    cross = boltzmann(first_ref[...]) * boltzmann(second_ref[...])

    @each_row_block(orient)
    def _(index):
        rows = rows_of(index)
        ahead, rate_plus, rate_minus = face_parts(v_ref, rows)
        rate = rate_plus + rate_minus
        for t in range(cells // LANES):
            gained = rate * message_ref[0, rows, columns(t)].astype(F32)
            moved[0, rows, columns(t)] = jnp.where(ahead, gained, 0.0).astype(BF16)
            moved[1, rows, columns(t)] = jnp.where(ahead, 0.0, gained).astype(BF16)

    own_face = own_ref[0].astype(F32) + cross[0:1] * mix(m_ref[...], moved[0])
    partner_face = partner_ref[0].astype(F32) + cross[0:1] * mix(m_ref[...], moved[1])
    face = jnp.sum(own_face * partner_face, axis=0, keepdims=True)
    total = jnp.zeros((1, 1), F32)
    for p in range(own_ref.shape[0]):
        if p > 0:
            face = jnp.sum(own_ref[p].astype(F32) * partner_ref[p].astype(F32), axis=0, keepdims=True)
        met = face / (orient * cross[p : p + 1])
        out_ref[p : p + 1] = met
        total = total + jnp.sum(met, axis=1, keepdims=True)
    total_ref[...] = jnp.broadcast_to(total, total_ref.shape)


def third_step_kernel(
    held_ref, mine_ref, other_ref, first_ref, second_ref, outer_ref, v_ref, m_ref, next_ref, held, moved
):
    planes, orient, _ = held.shape
    matrix = m_ref[...]
    first, second = boltzmann(first_ref[...]), boltzmann(second_ref[...])
    face_drifts(v_ref, mine_ref, other_ref, moved, (0, 1))
    cross = first * second
    for p in range(planes):
        kept = held_ref[p + 2]
        if p in (0, planes - 1):
            arrived = cross[p : p + 1] * mix(matrix, moved[min(p, 1)])
            kept = (kept.astype(F32) + arrived).astype(BF16)
        held[p] = kept

    @each_row_block(orient)
    def _(index):
        rows = rows_of(index)
        geo = geometry(v_ref, rows)
        loaded = [load_plane(held_ref, p, rows) for p in (0, 1)]
        loaded += [load_plane(held, p, rows) for p in range(planes)]
        loaded += [load_plane(held_ref, p, rows) for p in (planes + 2, planes + 3)]
        for p in range(planes + 2):
            store_plane(moved, p, rows, drift(loaded[p + 1], loaded[p], loaded[p + 2], geo))

    squared = second * second
    factors = [outer_ref[0:1]] + [squared[p : p + 1] for p in range(planes)] + [outer_ref[1:2]]
    for p, factor in enumerate(factors):
        next_ref[p] = (factor * mix(matrix, moved[p])).astype(BF16)


def weight_kernel(core_ref, partner_ref, start_ref, turned_ref, weight_ref, own_ref):
    planes = partner_ref.shape[0]
    core = core_ref[0]
    for p in range(planes):
        weight_ref[p] = mix(turned_ref[...], partner_ref[p]).astype(BF16)
    for p in range(2):
        own_ref[p] = mix(turned_ref[...], start_ref[core * (planes - 1) + p - 2 * p * core]).astype(BF16)


def fold(value):
    return jnp.sum(value.reshape(ROWS // 8, 8, LANES), axis=0)


def pairing_kernel(held_ref, second_ref, v_ref, weight_ref, faces_ref, inner_ref, out_ref):
    planes, orient, cells = weight_ref.shape
    second = boltzmann(second_ref[...])
    tiles = cells // LANES

    def body(index, sums):
        rows = rows_of(index)
        geo = geometry(v_ref, rows)
        loaded = [load_plane(held_ref, p, rows) for p in range(planes + 2)]
        new = []
        for p in range(planes):
            moved_tiles = drift(loaded[p + 1], loaded[p], loaded[p + 2], geo)
            weights = load_plane(weight_ref, p, rows)
            on_face = p in (0, planes - 1)
            partner = load_plane(faces_ref, min(p, 1), rows) if on_face else load_plane(inner_ref, p - 1, rows)
            for t in range(tiles):
                last, third = sums[2 * (p * tiles + t)], sums[2 * (p * tiles + t) + 1]
                new.append(last + fold(moved_tiles[t] * weights[t].astype(F32)))
                new.append(third + fold(loaded[p + 1][t].astype(F32) * partner[t].astype(F32)))
        return tuple(new)

    zero = jnp.zeros((8, LANES), F32)
    sums = lax.fori_loop(0, orient // ROWS, body, (zero,) * (2 * planes * tiles), unroll=UNROLL)
    for p in range(planes):
        for t in range(tiles):
            last = jnp.sum(sums[2 * (p * tiles + t)], axis=0, keepdims=True)
            third = jnp.sum(sums[2 * (p * tiles + t) + 1], axis=0, keepdims=True)
            factor = second[p : p + 1, columns(t)]
            out_ref[p : p + 1, columns(t)] = (0.5 * factor * last + third / (factor * factor)) / orient


def last_kernel(
    core_ref, message_ref, weight_ref, own_weight_ref, own_faces_ref, partner_faces_ref, shared_ref, met_ref,
    own_ref, partner_ref, v_ref, m_ref, sent_ref, kept_ref, moved, gained,
):
    planes, cells = shared_ref.shape
    orient = m_ref.shape[0]
    tiles = cells // LANES
    core = core_ref[0]
    half = planes // 2
    face = core * (planes - 1)
    inner = face + 1 - 2 * core

    def at_face(ref, depth):
        return jnp.where(core == 0, boltzmann(ref[depth : depth + 1]), boltzmann(ref[planes - 1 - depth : planes - depth]))

    factors = [[at_face(ref, depth) for depth in range(2)] for ref in (partner_ref, own_ref)]

    @each_row_block(orient)
    def _(index):
        rows = rows_of(index)
        ahead, rate_plus, rate_minus = face_parts(v_ref, rows)
        rate = rate_plus + rate_minus
        for t in range(tiles):
            got = rate * message_ref[0, rows, columns(t)].astype(F32)
            moved[0, rows, columns(t)] = jnp.where(ahead, got, 0.0).astype(BF16)
            moved[1, rows, columns(t)] = jnp.where(ahead, 0.0, got).astype(BF16)

    for s in range(2):
        gained[s] = (factors[s][0] * factors[s][0] * mix(m_ref[...], moved[s])).astype(BF16)

    def body(index, sums):
        rows = rows_of(index)
        ahead, rate_plus, rate_minus = face_parts(v_ref, rows)
        rate = rate_plus + rate_minus
        sides = (jnp.where(ahead, rate, 0.0), jnp.where(ahead, 0.0, rate))
        message = load_plane(message_ref, 1, rows)
        new = []
        for s in range(2):
            change = load_plane(gained, s, rows)
            moved_tiles = drift(change, None, None, geometry(v_ref, rows, 1.0 - 2.0 * s))
            if s == 0:
                weights = [load_plane(weight_ref, p, rows) for p in (face, inner)]
            else:
                weights = [load_plane(own_weight_ref, p, rows) for p in (0, 1)]
            third = load_plane((partner_faces_ref, own_faces_ref)[s], core, rows)
            for t in range(tiles):
                on_face = moved_tiles[t] + sides[s] * message[t].astype(F32)
                wide = change[t].astype(F32)
                terms = (
                    on_face * weights[0][t].astype(F32),
                    sides[s] * wide * weights[1][t].astype(F32),
                    wide * third[t].astype(F32),
                )
                base = 3 * (s * tiles + t)
                new += [sums[base + k] + fold(term) for k, term in enumerate(terms)]
        return tuple(new)

    zero = jnp.zeros((8, LANES), F32)
    sums = lax.fori_loop(0, orient // ROWS, body, (zero,) * (6 * tiles), unroll=UNROLL)
    for t in range(tiles):
        shares = []
        for s in range(2):
            base = 3 * (s * tiles + t)
            last, onward, third = (jnp.sum(sums[base + k], axis=0, keepdims=True) / orient for k in range(3))
            near, far = (factors[s][depth][:, columns(t)] for depth in range(2))
            shares.append((0.5 * near * last + third / (near * near), 0.5 * far * onward))
        for p in range(planes):
            at = slice(p, p + 1), columns(t)
            mine = core == (0 if p < half else 1)
            depth = min(p, planes - 1 - p)
            met = jnp.where(mine, 0.5 * met_ref[depth : depth + 1, columns(t)], 0.0)
            sent, kept = shared_ref[at] + met, met
            if depth < 2:
                sent = sent + jnp.where(mine, shares[0][depth], 0.0)
                kept = kept + jnp.where(mine, shares[1][depth], 0.0)
            sent_ref[at] = sent
            kept_ref[at] = kept


def kernel_call(kernel, outs, scratch, args):
    vmem = pl.BlockSpec(memory_space=pltpu.VMEM)
    smem = pl.BlockSpec(memory_space=pltpu.SMEM)
    return pl.pallas_call(
        kernel,
        out_shape=outs,
        in_specs=[smem if arg.dtype == jnp.int32 else vmem for arg in args],
        out_specs=jax.tree.map(lambda _: vmem, outs),
        scratch_shapes=[pltpu.VMEM(*s) if len(s) == 2 else pltpu.VMEM(s, BF16) for s in scratch],
        compiler_params=pltpu.CompilerParams(vmem_limit_bytes=8 << 20),
        cost_estimate=pl.CostEstimate(flops=0, bytes_accessed=0, transcendentals=0),
    )(*args)


def shards(fields, end_weights, directions, analysis, synthesis, decay_rates):
    device = lax.axis_index("space")
    core = device % 2
    is_first = core == 0
    planes, cells = fields.shape
    orient = end_weights.shape[0]
    plane_index = device // 2 * planes + lax.broadcasted_iota(jnp.int32, (planes, 1), 0)
    ramp = slope * plane_index.astype(F32) / (planes * lax.axis_size("space") // 2)
    own = fields + ramp
    partner = swap_species(fields) + ramp

    wide = lambda extra: jax.ShapeDtypeStruct((planes + extra, orient, cells), BF16)
    slab, plane = wide(0), wide(1 - planes)
    core_word = jnp.reshape(core, (1,)).astype(jnp.int32)
    start = jnp.transpose(end_weights, (1, 0, 2))
    spread, edge0, coded = kernel_call(
        prologue_kernel,
        (jax.ShapeDtypeStruct((4, orient, LANES), F32), plane, jax.ShapeDtypeStruct((16, cells), BF16)),
        (((16, cells), F32),),
        (core_word, directions, start, own, partner),
    )
    message0 = kernel_call(
        first_message_kernel,
        jax.ShapeDtypeStruct((1, orient + 16, cells), BF16),
        (),
        (edge0, swap_species(edge0), coded, spread),
    )

    def message(mine):
        shape = jax.ShapeDtypeStruct(mine.shape, BF16)
        return kernel_call(message_kernel, shape, (), (mine, swap_each(mine), spread))

    scaled = synthesis.astype(F32) * decay_rates[None]
    mixing = jnp.dot(scaled, analysis.astype(F32), precision=lax.Precision.HIGHEST) + 1.0 / orient
    matrix = mixing.astype(BF16)

    start, _ = lax.optimization_barrier((start, message0))
    arrived0 = to_next_slab(message0)
    alone, inner, edges1 = kernel_call(
        first_alone_kernel,
        (slab, wide(-2), jax.ShapeDtypeStruct((1, orient, cells), BF16)),
        (slab.shape, slab.shape),
        (start, own, spread, matrix),
    )
    weights, own_weights = kernel_call(
        weight_kernel,
        (slab, wide(2 - planes)),
        (),
        (core_word, swap_species(start), start, matrix.T),
    )
    edges1, _ = lax.optimization_barrier((edges1, alone))
    message1 = message(edges1)
    state, *_ = lax.optimization_barrier((alone, message1, weights))
    edges = kernel_call(
        next_alone_kernel,
        jax.ShapeDtypeStruct((2, orient, cells), BF16),
        (slab.shape, slab.shape),
        (state, own, partner, spread, matrix),
    )
    edges, arrived0 = lax.optimization_barrier((edges, arrived0))
    message2 = message(edges)
    arrived = [to_next_slab(message1), to_next_slab(message2)]
    crossed0 = swap_species(arrived0)
    inner, _ = lax.optimization_barrier((inner, arrived0))
    partner_inner = swap_species(inner)
    alone, *_ = lax.optimization_barrier((alone, message1, message2))
    half = planes // 2
    half_slab = jax.ShapeDtypeStruct((half, orient, cells), BF16)
    first_faces, second_state, sent_half, kept_half, outer = kernel_call(
        second_step_kernel,
        (wide(2 - planes), wide(4), half_slab, half_slab, jax.ShapeDtypeStruct((2, cells), F32)),
        (wide(2).shape, wide(4).shape),
        (core_word, alone, edge0, arrived0, crossed0, own, partner, spread, matrix),
    )
    arrived1, second_state, partner_inner = lax.optimization_barrier((arrived[0], second_state, partner_inner))
    sent_half, first_faces, _ = lax.optimization_barrier((sent_half, first_faces, arrived1))
    partner_faces = swap_each(first_faces)
    partner_half, crossed1 = lax.optimization_barrier((swap_each(sent_half), swap_species(arrived1)))
    own_half_field = jnp.where(is_first, own[:half], own[half:][::-1])
    partner_half_field = jnp.where(is_first, partner[:half], partner[half:][::-1])
    density = jax.ShapeDtypeStruct((planes, cells), F32)
    met, partition = kernel_call(
        middle_kernel,
        (jax.ShapeDtypeStruct((half, cells), F32), density),
        ((2, orient, cells),),
        (kept_half, partner_half, arrived1, own_half_field, partner_half_field, spread, matrix),
    )
    count = lax.axis_size("space")

    def gathered(value, distance, after):
        received = lax.ppermute(value, "space", [(i, i ^ distance) for i in range(count)])
        received, after = lax.optimization_barrier((received, after))
        return value + received, after

    partition, second_state = gathered(partition, 1, second_state)
    second_state, _ = lax.optimization_barrier((second_state, partition))
    third_state = kernel_call(
        third_step_kernel,
        wide(2),
        (slab.shape, wide(2).shape),
        (second_state, arrived1, crossed1, own, partner, outer, spread, matrix),
    )
    partition, third_state = gathered(partition, 4, third_state)
    third_state, _ = lax.optimization_barrier((third_state, partition))
    shared = kernel_call(pairing_kernel, density, (), (third_state, partner, spread, weights, partner_faces, partner_inner))
    arrived2, shared = lax.optimization_barrier((arrived[1], shared))
    distance = 8
    while distance < count:
        partition, shared = gathered(partition, distance, shared)
        distance *= 2
    partition, shared = gathered(partition, 2, shared)
    partition = partition / (count // 2 * planes * cells)
    sent, kept = kernel_call(
        last_kernel,
        (density, density),
        ((2, orient, cells), (2, orient, cells)),
        (
            core_word, arrived2, weights, own_weights, first_faces, partner_faces, shared, met,
            own, partner, spread, matrix,
        ),
    )
    return (kept + swap_species(sent)) / partition


def solution(mesh):
    return jax.shard_map(
        shards,
        mesh=mesh,
        in_specs=(P(("runs", "space"), None), P(None, ("runs", "space"), None), P(), P(), P(), P()),
        out_specs=P(("runs", "space"), None),
        check_vma=False,
    )
```

```python
import functools

import jax
import jax.numpy as jnp
from jax import lax
from jax.experimental import pallas as pl
from jax.experimental.pallas import tpu as pltpu
from jax.sharding import PartitionSpec as P

NZ = 16
STEPS = 4
LANES = 128
ROWS = 16
UNROLL = 4

courant = 0.3
slope = 0.6

BF16 = jnp.bfloat16
F32 = jnp.float32


def swap_species(block):
    count = lax.axis_size("space")
    return lax.ppermute(block, "space", [(i ^ 1, i) for i in range(count)])


def to_next_slab(block):
    count = lax.axis_size("space")
    return lax.ppermute(block, "space", [(i, (i + (2 if i % 2 == 0 else -2)) % count) for i in range(count)])


def rows_of(index):
    return pl.ds(pl.multiple_of(index * ROWS, ROWS), ROWS)


def each_row_block(orient):
    def run(body):
        def step(index, carry):
            body(index)
            return carry

        lax.fori_loop(0, orient // ROWS, step, 0, unroll=UNROLL)

    return run


def columns(tile):
    return slice(LANES * tile, LANES * (tile + 1))


def geometry(v_ref, rows, sign=1.0):
    lane = lax.broadcasted_iota(jnp.int32, (ROWS, LANES), 1)
    vx, vy, vz = (sign * v_ref[c, rows, :] for c in range(3))
    narrow = vx.astype(BF16)
    plus_x, narrow_plus, plus_y, plus_z = vx > 0, narrow > jnp.zeros_like(narrow), vy > 0, vz > 0
    rate_x, rate_y, rate_z = (courant * jnp.abs(t) for t in (vx, vy, vz))
    stay = 1.0 - (rate_x + rate_y + rate_z)
    z_from = (lane & (LANES - NZ)) | (jnp.where(plus_z, lane - 1, lane + 1) & (NZ - 1))
    y_from = jnp.where(plus_y, lane - NZ, lane + NZ) & (LANES - 1)
    y_edge = jnp.where(plus_y, lane, LANES - 1 - lane) < NZ
    return plus_x, narrow_plus, plus_y, stay, rate_x, rate_y, rate_z, z_from, y_from, y_edge


def pick(tile, index):
    return jnp.take_along_axis(tile, index, axis=1, mode="promise_in_bounds")


def load_plane(ref, plane, rows):
    return [ref[plane, rows, columns(t)] for t in range(ref.shape[2] // LANES)]


def drift(center, before, after, geo):
    plus_x, narrow_plus, plus_y, stay, rate_x, rate_y, rate_z, z_from, y_from, y_edge = geo
    tiles = len(center)
    center = [tile.astype(F32) for tile in center]
    turned = [pick(tile, y_from) for tile in center]
    moved = []
    for t in range(tiles):
        total = stay * center[t]
        if before is not None and after is not None:
            total = total + rate_x * jnp.where(narrow_plus, before[t], after[t]).astype(F32)
        elif before is not None:
            total = total + jnp.where(plus_x, rate_x, 0.0) * before[t].astype(F32)
        elif after is not None:
            total = total + jnp.where(plus_x, 0.0, rate_x) * after[t].astype(F32)
        over = jnp.where(plus_y, turned[t - 1], turned[(t + 1) % tiles])
        total = total + rate_y * jnp.where(y_edge, over, turned[t])
        total = total + rate_z * pick(center[t], z_from)
        moved.append(total)
    return moved


def store_plane(ref, plane, rows, tiles):
    for t, tile in enumerate(tiles):
        ref[plane, rows, columns(t)] = tile.astype(ref.dtype)


def mix(matrix, moved):
    return jnp.dot(matrix, moved, preferred_element_type=F32)


def boltzmann(field):
    return jnp.exp(-0.5 * field)


def prologue_kernel(
    core_ref, directions_ref, start_ref, fields_ref, partner_ref, spread_ref, edge_ref, coded_ref, near
):
    sign = 1.0 - 2.0 * core_ref[0].astype(F32)
    planes, orient, cells = start_ref.shape
    low = boltzmann(fields_ref[0:1])
    high = boltzmann(fields_ref[fields_ref.shape[0] - 1 :])
    for c in range(4):
        row = directions_ref[c % 3 : c % 3 + 1]
        column = jnp.broadcast_to(row, (LANES, orient)).T
        spread_ref[c] = column if c == 3 else sign * column

    @each_row_block(orient)
    def _(index):
        rows = rows_of(index)
        plus_x = spread_ref[0, rows, :] > 0
        for t in range(cells // LANES):
            at = rows, columns(t)
            chosen = jnp.where(
                plus_x,
                high[:, columns(t)] * start_ref[planes - 1, *at].astype(F32),
                low[:, columns(t)] * start_ref[0, *at].astype(F32),
            )
            edge_ref[0, *at] = chosen.astype(BF16)

    near[...] = jnp.zeros_like(near)
    for s, ref in enumerate((fields_ref, partner_ref)):
        for depth in range(2):
            high_row, low_row = (ref[p : p + 1] for p in (planes - 1 - depth, depth))
            row = jnp.where(core_ref[0] == 0, high_row, low_row)
            coarse = row.astype(BF16).astype(F32)
            at = 2 * s + depth
            near[at : at + 1] = coarse
            near[at + 4 : at + 5] = row - coarse
    coded_ref[...] = near[...].astype(BF16)


def matrix_kernel(synthesis_ref, decay_ref, analysis_ref, out_ref, turned_ref):
    rest = synthesis_ref[...].astype(F32) * decay_ref[...]
    total = jnp.full(out_ref.shape, 1.0 / out_ref.shape[1], F32)
    for _ in range(3):
        part = rest.astype(BF16)
        rest = rest - part.astype(F32)
        total = total + jnp.dot(part, analysis_ref[...], preferred_element_type=F32)
    out_ref[...] = total.astype(BF16)
    turned_ref[...] = total.T.astype(BF16)


def add_kernel(one_ref, two_ref, out_ref):
    out_ref[...] = one_ref[...] + two_ref[...]


def divide_kernel(cells, kept_ref, arrived_ref, one_ref, two_ref, out_ref):
    out_ref[...] = (kept_ref[...] + arrived_ref[...]) * (cells / (one_ref[...] + two_ref[...]))


def message_kernel(*refs):
    count = (len(refs) - 2) // 2
    v_ref, out_ref = refs[-2:]
    orient, cells = refs[0].shape[1:]

    @each_row_block(orient)
    def _(index):
        rows = rows_of(index)
        narrow = v_ref[3, rows, :].astype(BF16)
        ahead = narrow > jnp.zeros_like(narrow)
        for p in range(count):
            for t in range(cells // LANES):
                at = 0, rows, columns(t)
                out_ref[p, rows, columns(t)] = jnp.where(ahead, refs[p][at], refs[count + p][at])


def first_message_kernel(mine_ref, other_ref, coded_ref, v_ref, out_ref):
    message_kernel(mine_ref, other_ref, v_ref, out_ref)
    orient = mine_ref.shape[1]
    out_ref[0, orient:] = coded_ref[...]


def write_edge(edges_ref, step, faces, rows, v_ref):
    narrow = v_ref[0, rows, :].astype(BF16)
    plus_x = narrow > jnp.zeros_like(narrow)
    for t in range(len(faces[0])):
        edges_ref[step, rows, columns(t)] = jnp.where(plus_x, faces[-1][t], faces[0][t])


def alone_step(source_ref, moved, targets, v_ref, edges_ref, step):
    planes, orient, _ = source_ref.shape

    @each_row_block(orient)
    def _(index):
        rows = rows_of(index)
        geo = geometry(v_ref, rows)
        loaded = [load_plane(source_ref, p, rows) for p in range(planes)]
        if edges_ref is not None:
            write_edge(edges_ref, step, loaded, rows, v_ref)
        for p in targets:
            before = loaded[p - 1] if p > 0 else None
            after = loaded[p + 1] if p < planes - 1 else None
            store_plane(moved, p, rows, drift(loaded[p], before, after, geo))


def first_alone_kernel(start_ref, first_ref, v_ref, m_ref, out_ref, inner_ref, edges_ref, held, moved):
    planes, orient, _ = start_ref.shape
    first = boltzmann(first_ref[...])
    for p in range(planes):
        held[p] = (first[p : p + 1] * start_ref[p].astype(F32)).astype(BF16)
    alone_step(held, moved, range(planes), v_ref, None, 0)
    for p in (0, planes - 1, *range(1, planes - 1)):
        state = (first[p : p + 1] * first[p : p + 1] * mix(m_ref[...], moved[p])).astype(BF16)
        out_ref[p] = state
        if 0 < p < planes - 1:
            inner_ref[p - 1] = state

    @each_row_block(orient)
    def _(index):
        rows = rows_of(index)
        write_edge(edges_ref, 0, [load_plane(out_ref, p, rows) for p in (0, planes - 1)], rows, v_ref)


def next_alone_kernel(state_ref, first_ref, second_ref, v_ref, m_ref, edges2_ref, edges3_ref, held, moved):
    planes, orient, _ = state_ref.shape
    first = boltzmann(first_ref[...])
    second = boltzmann(second_ref[...])
    alone_step(state_ref, moved, range(planes), v_ref, None, 0)
    for p in range(planes):
        held[p] = (first[p : p + 1] * second[p : p + 1] * mix(m_ref[...], moved[p])).astype(BF16)
    alone_step(held, moved, (0, planes - 1), v_ref, edges2_ref, 0)
    for p in (0, planes - 1):
        held[p] = (second[p : p + 1] * second[p : p + 1] * mix(m_ref[...], moved[p])).astype(BF16)

    @each_row_block(orient)
    def _(index):
        rows = rows_of(index)
        write_edge(edges3_ref, 0, [load_plane(held, p, rows) for p in (0, planes - 1)], rows, v_ref)


def face_parts(v_ref, rows):
    vx = v_ref[0, rows, :]
    rate = courant * jnp.abs(vx)
    return v_ref[3, rows, :] > 0, jnp.where(vx > 0, rate, 0.0), jnp.where(vx > 0, 0.0, rate)


def face_drifts(v_ref, mine_ref, other_ref, moved, slots):
    @each_row_block(v_ref.shape[1])
    def _(index):
        rows = rows_of(index)
        ahead, rate_plus, rate_minus = face_parts(v_ref, rows)
        for t in range(mine_ref.shape[2] // LANES):
            mine = mine_ref[0, rows, columns(t)].astype(F32)
            other = other_ref[0, rows, columns(t)].astype(F32)
            face = jnp.where(ahead, mine, other)
            moved[slots[0], rows, columns(t)] = (rate_plus * face).astype(BF16)
            moved[slots[1], rows, columns(t)] = (rate_minus * face).astype(BF16)


def second_step_kernel(
    core_ref, alone_ref, edge_ref, mine_ref, other_ref, first_ref, second_ref, v_ref, m_ref,
    face_low_ref, face_high_ref, next_ref, sent_near_ref, sent_far_ref, kept_ref, outer_ref, held, moved,
):
    planes, orient, _ = alone_ref.shape
    matrix = m_ref[...]
    first, second = boltzmann(first_ref[...]), boltzmann(second_ref[...])
    core = core_ref[0]
    mine, other = (block[:4] + block[4:8] for block in (ref[0, orient:].astype(F32) for ref in (mine_ref, other_ref)))
    other = (other[2:4], other[0:2])
    mine = (mine[0:2], mine[2:4])
    low = [jnp.where(core == 0, mine[k], other[k]) for k in range(2)]
    high = [jnp.where(core == 0, other[k], mine[k]) for k in range(2)]
    beyond = [boltzmann(block[k : k + 1]) for block in (low[0], high[0], low[1], high[1]) for k in range(2)]
    face_drifts(v_ref, mine_ref, other_ref, moved, (0, 1))

    @each_row_block(orient)
    def _(index):
        rows = rows_of(index)
        _, rate_plus, rate_minus = face_parts(v_ref, rows)
        for t in range(edge_ref.shape[2] // LANES):
            edge = edge_ref[0, rows, columns(t)].astype(F32)
            moved[2, rows, columns(t)] = (rate_minus * edge).astype(BF16)
            moved[3, rows, columns(t)] = (rate_plus * edge).astype(BF16)

    squared = first * first
    for p in range(planes):
        kept = alone_ref[p]
        if p in (0, planes - 1):
            arrived = squared[p : p + 1] * mix(matrix, moved[min(p, 1)])
            kept = (kept.astype(F32) + arrived).astype(BF16)
            (face_high_ref if p else face_low_ref)[0] = kept
        held[p + 1] = kept
    held[0] = (beyond[0] * beyond[0] * mix(matrix, moved[2])).astype(BF16)
    held[planes + 1] = (beyond[2] * beyond[2] * mix(matrix, moved[3])).astype(BF16)
    count = planes + 2

    @each_row_block(orient)
    def _(index):
        rows = rows_of(index)
        geo = geometry(v_ref, rows)
        _, rate_plus, rate_minus = face_parts(v_ref, rows)
        loaded = [load_plane(held, p, rows) for p in range(count)]
        for p in range(count):
            before = loaded[p - 1] if p > 0 else None
            after = loaded[p + 1] if p < count - 1 else None
            store_plane(moved, p + 1, rows, drift(loaded[p], before, after, geo))
        store_plane(moved, 0, rows, [rate_minus * tile.astype(F32) for tile in loaded[0]])
        store_plane(moved, count + 1, rows, [rate_plus * tile.astype(F32) for tile in loaded[-1]])

    cross = first * second
    factors = [beyond[1] * beyond[5], beyond[0] * beyond[4]]
    factors += [cross[p : p + 1] for p in range(planes)]
    factors += [beyond[2] * beyond[6], beyond[3] * beyond[7]]
    for p, factor in enumerate(factors):
        next_ref[p] = (factor * mix(matrix, moved[p])).astype(BF16)
    for p in range(planes // 2):
        sent_ref = (sent_near_ref, sent_far_ref)[p]
        sent_ref[0] = next_ref[2 + (planes - 1) * (1 - core) + (2 * core - 1) * p]
        kept_ref[p] = next_ref[2 + (planes - 1) * core + (1 - 2 * core) * p]
    outer_ref[0:1] = beyond[4] * beyond[4]
    outer_ref[1:2] = beyond[6] * beyond[6]


def middle_kernel(
    core_ref, own_ref, near_ref, far_ref, message_ref, first_ref, second_ref, v_ref, m_ref, out_ref, total_ref, moved
):
    _, orient, cells = own_ref.shape
    planes = first_ref.shape[0]

    def cross_of(depth):
        low, high = (
            boltzmann(first_ref[p : p + 1]) * boltzmann(second_ref[p : p + 1]) for p in (depth, planes - 1 - depth)
        )
        return jnp.where(core_ref[0] == 0, low, high)

    cross = [cross_of(depth) for depth in range(2)]

    @each_row_block(orient)
    def _(index):
        rows = rows_of(index)
        ahead, rate_plus, rate_minus = face_parts(v_ref, rows)
        rate = rate_plus + rate_minus
        for t in range(cells // LANES):
            gained = rate * message_ref[0, rows, columns(t)].astype(F32)
            moved[0, rows, columns(t)] = jnp.where(ahead, gained, 0.0).astype(BF16)
            moved[1, rows, columns(t)] = jnp.where(ahead, 0.0, gained).astype(BF16)

    own_face = own_ref[0].astype(F32) + cross[0] * mix(m_ref[...], moved[0])
    partner_face = near_ref[0].astype(F32) + cross[0] * mix(m_ref[...], moved[1])
    face = jnp.sum(own_face * partner_face, axis=0, keepdims=True)
    total = jnp.zeros((1, 1), F32)
    for p in range(own_ref.shape[0]):
        if p > 0:
            face = jnp.sum(own_ref[p].astype(F32) * far_ref[0].astype(F32), axis=0, keepdims=True)
        met = face / (orient * cross[p])
        out_ref[p : p + 1] = met
        total = total + jnp.sum(met, axis=1, keepdims=True)
    total_ref[...] = jnp.broadcast_to(total, total_ref.shape)


def third_step_kernel(
    held_ref, mine_ref, other_ref, first_ref, second_ref, outer_ref, v_ref, m_ref, next_ref, held, moved
):
    planes, orient, _ = held.shape
    matrix = m_ref[...]
    first, second = boltzmann(first_ref[...]), boltzmann(second_ref[...])
    face_drifts(v_ref, mine_ref, other_ref, moved, (0, 1))
    cross = first * second
    for p in range(planes):
        kept = held_ref[p + 2]
        if p in (0, planes - 1):
            arrived = cross[p : p + 1] * mix(matrix, moved[min(p, 1)])
            kept = (kept.astype(F32) + arrived).astype(BF16)
        held[p] = kept

    @each_row_block(orient)
    def _(index):
        rows = rows_of(index)
        geo = geometry(v_ref, rows)
        loaded = [load_plane(held_ref, p, rows) for p in (0, 1)]
        loaded += [load_plane(held, p, rows) for p in range(planes)]
        loaded += [load_plane(held_ref, p, rows) for p in (planes + 2, planes + 3)]
        for p in range(planes + 2):
            store_plane(moved, p, rows, drift(loaded[p + 1], loaded[p], loaded[p + 2], geo))

    squared = second * second
    factors = [outer_ref[0:1]] + [squared[p : p + 1] for p in range(planes)] + [outer_ref[1:2]]
    for p, factor in enumerate(factors):
        next_ref[p] = (factor * mix(matrix, moved[p])).astype(BF16)


def weight_kernel(core_ref, partner_ref, start_ref, turned_ref, weight_ref, own_ref):
    planes = partner_ref.shape[0]
    core = core_ref[0]
    for p in range(planes):
        weight_ref[p] = mix(turned_ref[...], partner_ref[p]).astype(BF16)
    for p in range(2):
        own_ref[p] = mix(turned_ref[...], start_ref[core * (planes - 1) + p - 2 * p * core]).astype(BF16)


def fold(value):
    return jnp.sum(value.reshape(ROWS // 8, 8, LANES), axis=0)


def pairing_kernel(held_ref, second_ref, v_ref, weight_ref, low_ref, inner_ref, high_ref, out_ref):
    planes, orient, cells = weight_ref.shape
    second = boltzmann(second_ref[...])
    tiles = cells // LANES

    def body(index, sums):
        rows = rows_of(index)
        geo = geometry(v_ref, rows)
        loaded = [load_plane(held_ref, p, rows) for p in range(planes + 2)]
        new = []
        for p in range(planes):
            moved_tiles = drift(loaded[p + 1], loaded[p], loaded[p + 2], geo)
            weights = load_plane(weight_ref, p, rows)
            partner_refs = [(low_ref, 0)] + [(inner_ref, k) for k in range(planes - 2)] + [(high_ref, 0)]
            partner = load_plane(*partner_refs[p], rows)
            for t in range(tiles):
                last, third = sums[2 * (p * tiles + t)], sums[2 * (p * tiles + t) + 1]
                new.append(last + fold(moved_tiles[t] * weights[t].astype(F32)))
                new.append(third + fold(loaded[p + 1][t].astype(F32) * partner[t].astype(F32)))
        return tuple(new)

    zero = jnp.zeros((8, LANES), F32)
    sums = lax.fori_loop(0, orient // ROWS, body, (zero,) * (2 * planes * tiles), unroll=UNROLL)
    for p in range(planes):
        for t in range(tiles):
            last = jnp.sum(sums[2 * (p * tiles + t)], axis=0, keepdims=True)
            third = jnp.sum(sums[2 * (p * tiles + t) + 1], axis=0, keepdims=True)
            factor = second[p : p + 1, columns(t)]
            out_ref[p : p + 1, columns(t)] = (0.5 * factor * last + third / (factor * factor)) / orient


def last_kernel(
    core_ref, message_ref, weight_ref, own_weight_ref, own_low_ref, own_high_ref, partner_low_ref, partner_high_ref,
    shared_ref, met_ref,    own_ref, partner_ref, v_ref, m_ref, sent_ref, kept_ref, moved, gained,
):
    planes, cells = shared_ref.shape
    orient = m_ref.shape[0]
    tiles = cells // LANES
    core = core_ref[0]
    half = planes // 2
    face = core * (planes - 1)
    inner = face + 1 - 2 * core

    def at_face(ref, depth):
        return jnp.where(core == 0, boltzmann(ref[depth : depth + 1]), boltzmann(ref[planes - 1 - depth : planes - depth]))

    factors = [[at_face(ref, depth) for depth in range(2)] for ref in (partner_ref, own_ref)]

    @each_row_block(orient)
    def _(index):
        rows = rows_of(index)
        ahead, rate_plus, rate_minus = face_parts(v_ref, rows)
        rate = rate_plus + rate_minus
        for t in range(tiles):
            got = rate * message_ref[0, rows, columns(t)].astype(F32)
            moved[0, rows, columns(t)] = jnp.where(ahead, got, 0.0).astype(BF16)
            moved[1, rows, columns(t)] = jnp.where(ahead, 0.0, got).astype(BF16)

    for s in range(2):
        gained[s] = (factors[s][0] * factors[s][0] * mix(m_ref[...], moved[s])).astype(BF16)

    def body(index, sums):
        rows = rows_of(index)
        ahead, rate_plus, rate_minus = face_parts(v_ref, rows)
        rate = rate_plus + rate_minus
        sides = (jnp.where(ahead, rate, 0.0), jnp.where(ahead, 0.0, rate))
        message = load_plane(message_ref, 1, rows)
        new = []
        for s in range(2):
            change = load_plane(gained, s, rows)
            moved_tiles = drift(change, None, None, geometry(v_ref, rows, 1.0 - 2.0 * s))
            if s == 0:
                weights = [load_plane(weight_ref, p, rows) for p in (face, inner)]
            else:
                weights = [load_plane(own_weight_ref, p, rows) for p in (0, 1)]
            pair = ((partner_low_ref, partner_high_ref), (own_low_ref, own_high_ref))[s]
            third = [jnp.where(core == 0, low, high) for low, high in zip(*(load_plane(ref, 0, rows) for ref in pair))]
            for t in range(tiles):
                on_face = moved_tiles[t] + sides[s] * message[t].astype(F32)
                wide = change[t].astype(F32)
                terms = (
                    on_face * weights[0][t].astype(F32),
                    sides[s] * wide * weights[1][t].astype(F32),
                    wide * third[t].astype(F32),
                )
                base = 3 * (s * tiles + t)
                new += [sums[base + k] + fold(term) for k, term in enumerate(terms)]
        return tuple(new)

    zero = jnp.zeros((8, LANES), F32)
    sums = lax.fori_loop(0, orient // ROWS, body, (zero,) * (6 * tiles), unroll=UNROLL)
    for t in range(tiles):
        shares = []
        for s in range(2):
            base = 3 * (s * tiles + t)
            last, onward, third = (jnp.sum(sums[base + k], axis=0, keepdims=True) / orient for k in range(3))
            near, far = (factors[s][depth][:, columns(t)] for depth in range(2))
            shares.append((0.5 * near * last + third / (near * near), 0.5 * far * onward))
        for p in range(planes):
            at = slice(p, p + 1), columns(t)
            mine = core == (0 if p < half else 1)
            depth = min(p, planes - 1 - p)
            met = jnp.where(mine, 0.5 * met_ref[depth : depth + 1, columns(t)], 0.0)
            sent, kept = shared_ref[at] + met, met
            if depth < 2:
                sent = sent + jnp.where(mine, shares[0][depth], 0.0)
                kept = kept + jnp.where(mine, shares[1][depth], 0.0)
            sent_ref[at] = sent
            kept_ref[at] = kept


def split_outputs(outs):
    low, high, state, near, far, kept, outer = outs
    return (low, high), state, (near, far), kept, outer


def kernel_call(kernel, outs, scratch, args):
    vmem = pl.BlockSpec(memory_space=pltpu.VMEM)
    smem = pl.BlockSpec(memory_space=pltpu.SMEM)
    return pl.pallas_call(
        kernel,
        out_shape=outs,
        in_specs=[smem if arg.dtype == jnp.int32 else vmem for arg in args],
        out_specs=jax.tree.map(lambda _: vmem, outs),
        scratch_shapes=[pltpu.VMEM(*s) if len(s) == 2 else pltpu.VMEM(s, BF16) for s in scratch],
        compiler_params=pltpu.CompilerParams(vmem_limit_bytes=7 << 20),
        cost_estimate=pl.CostEstimate(flops=0, bytes_accessed=0, transcendentals=0),
    )(*args)


def shards(fields, end_weights, directions, analysis, synthesis, decay_rates):
    device = lax.axis_index("space")
    core = device % 2
    is_first = core == 0
    planes, cells = fields.shape
    orient = end_weights.shape[0]
    plane_index = device // 2 * planes + lax.broadcasted_iota(jnp.int32, (planes, 1), 0)
    ramp = slope * plane_index.astype(F32) / (planes * lax.axis_size("space") // 2)
    own = fields + ramp
    partner = swap_species(fields) + ramp

    wide = lambda extra: jax.ShapeDtypeStruct((planes + extra, orient, cells), BF16)
    slab, plane = wide(0), wide(1 - planes)
    core_word = jnp.reshape(core, (1,)).astype(jnp.int32)
    start = jnp.transpose(end_weights, (1, 0, 2))
    spread, edge0, coded = kernel_call(
        prologue_kernel,
        (jax.ShapeDtypeStruct((4, orient, LANES), F32), plane, jax.ShapeDtypeStruct((16, cells), BF16)),
        (((16, cells), F32),),
        (core_word, directions, start, own, partner),
    )
    matrix, turned = kernel_call(
        matrix_kernel,
        (jax.ShapeDtypeStruct((orient, orient), BF16),) * 2,
        (),
        (synthesis, decay_rates[None], analysis),
    )
    other0, matrix = lax.optimization_barrier((swap_species(edge0), matrix))
    message0 = kernel_call(
        first_message_kernel,
        jax.ShapeDtypeStruct((1, orient + 16, cells), BF16),
        (),
        (edge0, other0, coded, spread),
    )

    def message(blocks, others):
        shape = jax.ShapeDtypeStruct((len(blocks),) + blocks[0].shape[1:], BF16)
        return kernel_call(message_kernel, shape, (), (*blocks, *others, spread))

    start, _ = lax.optimization_barrier((start, message0))
    arrived0 = to_next_slab(message0)
    alone, inner, edges1 = kernel_call(
        first_alone_kernel, (slab, wide(-2), plane), (slab.shape, slab.shape), (start, own, spread, matrix)
    )
    weights, own_weights = kernel_call(
        weight_kernel, (slab, wide(2 - planes)), (), (core_word, swap_species(start), start, turned)
    )
    others1, weights = lax.optimization_barrier((swap_species(edges1), weights))
    message1 = message([edges1], [others1])
    state, *_ = lax.optimization_barrier((alone, message1, weights))
    edges2, edges3 = kernel_call(
        next_alone_kernel, (plane, plane), (slab.shape, slab.shape), (state, own, partner, spread, matrix)
    )
    edges2, edges3, arrived0 = lax.optimization_barrier((edges2, edges3, arrived0))
    message2 = message([edges2, edges3], [swap_species(edges2), swap_species(edges3)])
    arrived = [to_next_slab(message1), to_next_slab(message2)]
    crossed0 = swap_species(arrived0)
    inner, _ = lax.optimization_barrier((inner, arrived0))
    partner_inner = swap_species(inner)

    alone, *_ = lax.optimization_barrier((alone, message1, message2))
    half = planes // 2
    faces, second_state, sent_half, kept_half, outer = split_outputs(
        kernel_call(
            second_step_kernel,
            (plane, plane, wide(4), plane, plane, wide(half - planes), jax.ShapeDtypeStruct((2, cells), F32)),
            (wide(2).shape, wide(4).shape),
            (core_word, alone, edge0, arrived0, crossed0, own, partner, spread, matrix),
        )
    )
    arrived1, second_state, partner_inner = lax.optimization_barrier((arrived[0], second_state, partner_inner))
    *moving, _ = lax.optimization_barrier((*sent_half, *faces, arrived1))
    partner_faces = [swap_species(block) for block in moving[2:]]
    *partner_half, crossed1 = lax.optimization_barrier((*map(swap_species, moving[:2]), swap_species(arrived1)))
    density = jax.ShapeDtypeStruct((planes, cells), F32)
    met, partition = kernel_call(
        middle_kernel,
        (jax.ShapeDtypeStruct((half, cells), F32), density),
        ((2, orient, cells),),
        (core_word, kept_half, *partner_half, arrived1, own, partner, spread, matrix),
    )
    count = lax.axis_size("space")

    def received(value, distance, after):
        block = lax.ppermute(value, "space", [(i, i ^ distance) for i in range(count)])
        return lax.optimization_barrier((block, after))

    def gathered(value, distance, after):
        block, after = received(value, distance, after)
        return kernel_call(add_kernel, density, (), (value, block)), after

    partition, second_state = gathered(partition, 1, second_state)
    second_state, _ = lax.optimization_barrier((second_state, partition))
    third_state = kernel_call(
        third_step_kernel,
        wide(2),
        (slab.shape, wide(2).shape),
        (second_state, arrived1, crossed1, own, partner, outer, spread, matrix),
    )
    partition, third_state = gathered(partition, 4, third_state)
    third_state, _ = lax.optimization_barrier((third_state, partition))
    shared = kernel_call(
        pairing_kernel,
        density,
        (),
        (third_state, partner, spread, weights, partner_faces[0], partner_inner, partner_faces[1]),
    )
    arrived2, shared = lax.optimization_barrier((arrived[1], shared))
    distance = 8
    while distance < count:
        partition, shared = gathered(partition, distance, shared)
        distance *= 2
    beside, shared = received(partition, 2, shared)
    sent, kept = kernel_call(
        last_kernel,
        (density, density),
        ((2, orient, cells), (2, orient, cells)),
        (
            core_word, arrived2, weights, own_weights, *faces, *partner_faces, shared, met,
            own, partner, spread, matrix,
        ),
    )
    return kernel_call(
        functools.partial(divide_kernel, count // 2 * planes * cells),
        density,
        (),
        (kept, swap_species(sent), partition, beside),
    )


def solution(mesh):
    return jax.shard_map(
        shards,
        mesh=mesh,
        in_specs=(P(("runs", "space"), None), P(None, ("runs", "space"), None), P(), P(), P(), P()),
        out_specs=P(("runs", "space"), None),
        check_vma=False,
    )
```

```python
import functools

import jax
import jax.numpy as jnp
from jax import lax
from jax.experimental import pallas as pl
from jax.experimental.pallas import tpu as pltpu
from jax.sharding import PartitionSpec as P

NZ = 16
STEPS = 4
LANES = 128
ROWS = 16
UNROLL = 4

courant = 0.3
slope = 0.6

BF16 = jnp.bfloat16
F32 = jnp.float32


def swap_species(block):
    count = lax.axis_size("space")
    return lax.ppermute(block, "space", [(i ^ 1, i) for i in range(count)])


def exchange_faces(block):
    count = lax.axis_size("space")
    route = []
    for slab in range(count // 2):
        beside = ((slab + 1) ^ 1) - 1
        route += [(2 * slab, 2 * (slab ^ 1)), (2 * slab + 1, 2 * beside % count + 1)]
    return lax.ppermute(block, "space", route)


def rows_of(index):
    return pl.ds(pl.multiple_of(index * ROWS, ROWS), ROWS)


def each_row_block(orient):
    def run(body):
        def step(index, carry):
            body(index)
            return carry

        lax.fori_loop(0, orient // ROWS, step, 0, unroll=UNROLL)

    return run


def columns(tile):
    return slice(LANES * tile, LANES * (tile + 1))


def geometry(v_ref, rows, sign=1.0):
    lane = lax.broadcasted_iota(jnp.int32, (ROWS, LANES), 1)
    vx, vy, vz = (sign * v_ref[c, rows, :] for c in range(3))
    narrow = vx.astype(BF16)
    plus_x, narrow_plus, plus_y, plus_z = vx > 0, narrow > jnp.zeros_like(narrow), vy > 0, vz > 0
    rate_x, rate_y, rate_z = (courant * jnp.abs(t) for t in (vx, vy, vz))
    stay = 1.0 - (rate_x + rate_y + rate_z)
    z_from = (lane & (LANES - NZ)) | (jnp.where(plus_z, lane - 1, lane + 1) & (NZ - 1))
    y_from = jnp.where(plus_y, lane - NZ, lane + NZ) & (LANES - 1)
    y_edge = jnp.where(plus_y, lane, LANES - 1 - lane) < NZ
    return plus_x, narrow_plus, plus_y, stay, rate_x, rate_y, rate_z, z_from, y_from, y_edge


def pick(tile, index):
    return jnp.take_along_axis(tile, index, axis=1, mode="promise_in_bounds")


def load_plane(ref, plane, rows):
    return [ref[plane, rows, columns(t)] for t in range(ref.shape[2] // LANES)]


def drift(center, before, after, geo):
    plus_x, narrow_plus, plus_y, stay, rate_x, rate_y, rate_z, z_from, y_from, y_edge = geo
    tiles = len(center)
    center = [tile.astype(F32) for tile in center]
    turned = [pick(tile, y_from) for tile in center]
    moved = []
    for t in range(tiles):
        total = stay * center[t]
        if before is not None and after is not None:
            total = total + rate_x * jnp.where(narrow_plus, before[t], after[t]).astype(F32)
        elif before is not None:
            total = total + jnp.where(plus_x, rate_x, 0.0) * before[t].astype(F32)
        elif after is not None:
            total = total + jnp.where(plus_x, 0.0, rate_x) * after[t].astype(F32)
        over = jnp.where(plus_y, turned[t - 1], turned[(t + 1) % tiles])
        total = total + rate_y * jnp.where(y_edge, over, turned[t])
        total = total + rate_z * pick(center[t], z_from)
        moved.append(total)
    return moved


def store_plane(ref, plane, rows, tiles):
    for t, tile in enumerate(tiles):
        ref[plane, rows, columns(t)] = tile.astype(ref.dtype)


def mix(matrix, moved):
    return jnp.dot(matrix, moved, preferred_element_type=F32)


def boltzmann(field):
    return jnp.exp(-0.5 * field)


def prologue_kernel(
    core_ref, directions_ref, start_ref, fields_ref, partner_ref, spread_ref, edge_ref, coded_ref, near
):
    sign = 1.0 - 2.0 * core_ref[1].astype(F32)
    toward = sign * (1.0 - 2.0 * core_ref[0].astype(F32))
    planes, orient, cells = start_ref.shape
    low = boltzmann(fields_ref[0:1])
    high = boltzmann(fields_ref[fields_ref.shape[0] - 1 :])
    for c in range(4):
        row = directions_ref[c % 3 : c % 3 + 1]
        column = jnp.broadcast_to(row, (LANES, orient)).T
        spread_ref[c] = (toward if c == 3 else sign) * column

    @each_row_block(orient)
    def _(index):
        rows = rows_of(index)
        plus_x = spread_ref[0, rows, :] > 0
        for t in range(cells // LANES):
            at = rows, columns(t)
            chosen = jnp.where(
                plus_x,
                high[:, columns(t)] * start_ref[planes - 1, *at].astype(F32),
                low[:, columns(t)] * start_ref[0, *at].astype(F32),
            )
            edge_ref[0, *at] = chosen.astype(BF16)

    near[...] = jnp.zeros_like(near)
    for s, ref in enumerate((fields_ref, partner_ref)):
        for depth in range(2):
            high_row, low_row = (ref[p : p + 1] for p in (planes - 1 - depth, depth))
            row = jnp.where(core_ref[0] == 1, high_row, low_row)
            coarse = row.astype(BF16).astype(F32)
            at = 2 * s + depth
            near[at : at + 1] = coarse
            near[at + 4 : at + 5] = row - coarse
    coded_ref[...] = near[...].astype(BF16)


def matrix_kernel(synthesis_ref, decay_ref, analysis_ref, out_ref, turned_ref):
    rest = synthesis_ref[...].astype(F32) * decay_ref[...]
    total = jnp.full(out_ref.shape, 1.0 / out_ref.shape[1], F32)
    for _ in range(3):
        part = rest.astype(BF16)
        rest = rest - part.astype(F32)
        total = total + jnp.dot(part, analysis_ref[...], preferred_element_type=F32)
    out_ref[...] = total.astype(BF16)
    turned_ref[...] = total.T.astype(BF16)


def add_kernel(one_ref, two_ref, out_ref):
    out_ref[...] = one_ref[...] + two_ref[...]


def divide_kernel(cells, kept_ref, arrived_ref, one_ref, two_ref, out_ref):
    out_ref[...] = (kept_ref[...] + arrived_ref[...]) * (cells / (one_ref[...] + two_ref[...]))


def message_kernel(*refs):
    count = (len(refs) - 2) // 2
    v_ref, out_ref = refs[-2:]
    orient, cells = refs[0].shape[1:]

    @each_row_block(orient)
    def _(index):
        rows = rows_of(index)
        narrow = v_ref[3, rows, :].astype(BF16)
        leaves = narrow < jnp.zeros_like(narrow)
        for p in range(count):
            for t in range(cells // LANES):
                at = 0, rows, columns(t)
                out_ref[p, rows, columns(t)] = jnp.where(leaves, refs[p][at], refs[count + p][at])


def first_message_kernel(mine_ref, other_ref, coded_ref, v_ref, out_ref):
    message_kernel(mine_ref, other_ref, v_ref, out_ref)
    orient = mine_ref.shape[1]
    out_ref[0, orient:] = coded_ref[...]


def write_edge(edges_ref, step, faces, rows, v_ref):
    narrow = v_ref[0, rows, :].astype(BF16)
    plus_x = narrow > jnp.zeros_like(narrow)
    for t in range(len(faces[0])):
        edges_ref[step, rows, columns(t)] = jnp.where(plus_x, faces[-1][t], faces[0][t])


def alone_step(source_ref, moved, targets, v_ref, edges_ref, step):
    planes, orient, _ = source_ref.shape

    @each_row_block(orient)
    def _(index):
        rows = rows_of(index)
        geo = geometry(v_ref, rows)
        loaded = [load_plane(source_ref, p, rows) for p in range(planes)]
        if edges_ref is not None:
            write_edge(edges_ref, step, loaded, rows, v_ref)
        for p in targets:
            before = loaded[p - 1] if p > 0 else None
            after = loaded[p + 1] if p < planes - 1 else None
            store_plane(moved, p, rows, drift(loaded[p], before, after, geo))


def first_alone_kernel(start_ref, first_ref, v_ref, m_ref, out_ref, inner_ref, edges_ref, held, moved):
    planes, orient, _ = start_ref.shape
    first = boltzmann(first_ref[...])
    for p in range(planes):
        held[p] = (first[p : p + 1] * start_ref[p].astype(F32)).astype(BF16)
    alone_step(held, moved, range(planes), v_ref, None, 0)
    for p in (0, planes - 1, *range(1, planes - 1)):
        state = (first[p : p + 1] * first[p : p + 1] * mix(m_ref[...], moved[p])).astype(BF16)
        out_ref[p] = state
        if 0 < p < planes - 1:
            inner_ref[p - 1] = state

    @each_row_block(orient)
    def _(index):
        rows = rows_of(index)
        write_edge(edges_ref, 0, [load_plane(out_ref, p, rows) for p in (0, planes - 1)], rows, v_ref)


def next_alone_kernel(state_ref, first_ref, second_ref, v_ref, m_ref, edges2_ref, edges3_ref, held, moved):
    planes, orient, _ = state_ref.shape
    first = boltzmann(first_ref[...])
    second = boltzmann(second_ref[...])
    alone_step(state_ref, moved, range(planes), v_ref, None, 0)
    for p in range(planes):
        held[p] = (first[p : p + 1] * second[p : p + 1] * mix(m_ref[...], moved[p])).astype(BF16)
    alone_step(held, moved, (0, planes - 1), v_ref, edges2_ref, 0)
    for p in (0, planes - 1):
        held[p] = (second[p : p + 1] * second[p : p + 1] * mix(m_ref[...], moved[p])).astype(BF16)

    @each_row_block(orient)
    def _(index):
        rows = rows_of(index)
        write_edge(edges3_ref, 0, [load_plane(held, p, rows) for p in (0, planes - 1)], rows, v_ref)


def face_parts(v_ref, rows):
    vx = v_ref[0, rows, :]
    rate = courant * jnp.abs(vx)
    return v_ref[3, rows, :] > 0, jnp.where(vx > 0, rate, 0.0), jnp.where(vx > 0, 0.0, rate)


def face_drifts(v_ref, mine_ref, other_ref, moved, slots):
    @each_row_block(v_ref.shape[1])
    def _(index):
        rows = rows_of(index)
        ahead, rate_plus, rate_minus = face_parts(v_ref, rows)
        for t in range(mine_ref.shape[2] // LANES):
            mine = mine_ref[0, rows, columns(t)].astype(F32)
            other = other_ref[0, rows, columns(t)].astype(F32)
            face = jnp.where(ahead, mine, other)
            moved[slots[0], rows, columns(t)] = (rate_plus * face).astype(BF16)
            moved[slots[1], rows, columns(t)] = (rate_minus * face).astype(BF16)


def second_step_kernel(
    core_ref, alone_ref, edge_ref, mine_ref, other_ref, first_ref, second_ref, v_ref, m_ref,
    face_low_ref, face_high_ref, next_ref, sent_near_ref, sent_far_ref, kept_ref, outer_ref, held, moved,
):
    planes, orient, _ = alone_ref.shape
    matrix = m_ref[...]
    first, second = boltzmann(first_ref[...]), boltzmann(second_ref[...])
    core = core_ref[0]
    mine, other = (block[:4] + block[4:8] for block in (ref[0, orient:].astype(F32) for ref in (mine_ref, other_ref)))
    other = (other[2:4], other[0:2])
    mine = (mine[0:2], mine[2:4])
    low = [jnp.where(core == 0, mine[k], other[k]) for k in range(2)]
    high = [jnp.where(core == 0, other[k], mine[k]) for k in range(2)]
    beyond = [boltzmann(block[k : k + 1]) for block in (low[0], high[0], low[1], high[1]) for k in range(2)]
    face_drifts(v_ref, mine_ref, other_ref, moved, (0, 1))

    @each_row_block(orient)
    def _(index):
        rows = rows_of(index)
        _, rate_plus, rate_minus = face_parts(v_ref, rows)
        for t in range(edge_ref.shape[2] // LANES):
            edge = edge_ref[0, rows, columns(t)].astype(F32)
            moved[2, rows, columns(t)] = (rate_minus * edge).astype(BF16)
            moved[3, rows, columns(t)] = (rate_plus * edge).astype(BF16)

    squared = first * first
    for p in range(planes):
        kept = alone_ref[p]
        if p in (0, planes - 1):
            arrived = squared[p : p + 1] * mix(matrix, moved[min(p, 1)])
            kept = (kept.astype(F32) + arrived).astype(BF16)
            (face_high_ref if p else face_low_ref)[0] = kept
        held[p + 1] = kept
    held[0] = (beyond[0] * beyond[0] * mix(matrix, moved[2])).astype(BF16)
    held[planes + 1] = (beyond[2] * beyond[2] * mix(matrix, moved[3])).astype(BF16)
    count = planes + 2

    @each_row_block(orient)
    def _(index):
        rows = rows_of(index)
        geo = geometry(v_ref, rows)
        _, rate_plus, rate_minus = face_parts(v_ref, rows)
        loaded = [load_plane(held, p, rows) for p in range(count)]
        for p in range(count):
            before = loaded[p - 1] if p > 0 else None
            after = loaded[p + 1] if p < count - 1 else None
            store_plane(moved, p + 1, rows, drift(loaded[p], before, after, geo))
        store_plane(moved, 0, rows, [rate_minus * tile.astype(F32) for tile in loaded[0]])
        store_plane(moved, count + 1, rows, [rate_plus * tile.astype(F32) for tile in loaded[-1]])

    cross = first * second
    factors = [beyond[1] * beyond[5], beyond[0] * beyond[4]]
    factors += [cross[p : p + 1] for p in range(planes)]
    factors += [beyond[2] * beyond[6], beyond[3] * beyond[7]]
    for p, factor in enumerate(factors):
        next_ref[p] = (factor * mix(matrix, moved[p])).astype(BF16)
    for p in range(planes // 2):
        sent_ref = (sent_near_ref, sent_far_ref)[p]
        sent_ref[0] = next_ref[2 + (planes - 1) * (1 - core) + (2 * core - 1) * p]
        kept_ref[p] = next_ref[2 + (planes - 1) * core + (1 - 2 * core) * p]
    outer_ref[0:1] = beyond[4] * beyond[4]
    outer_ref[1:2] = beyond[6] * beyond[6]


def middle_kernel(
    core_ref, own_ref, near_ref, far_ref, message_ref, first_ref, second_ref, v_ref, m_ref, out_ref, total_ref, moved
):
    _, orient, cells = own_ref.shape
    planes = first_ref.shape[0]

    def cross_of(depth):
        low, high = (
            boltzmann(first_ref[p : p + 1]) * boltzmann(second_ref[p : p + 1]) for p in (depth, planes - 1 - depth)
        )
        return jnp.where(core_ref[0] == 0, low, high)

    cross = [cross_of(depth) for depth in range(2)]

    @each_row_block(orient)
    def _(index):
        rows = rows_of(index)
        ahead, rate_plus, rate_minus = face_parts(v_ref, rows)
        rate = rate_plus + rate_minus
        for t in range(cells // LANES):
            gained = rate * message_ref[0, rows, columns(t)].astype(F32)
            moved[0, rows, columns(t)] = jnp.where(ahead, gained, 0.0).astype(BF16)
            moved[1, rows, columns(t)] = jnp.where(ahead, 0.0, gained).astype(BF16)

    own_face = own_ref[0].astype(F32) + cross[0] * mix(m_ref[...], moved[0])
    partner_face = near_ref[0].astype(F32) + cross[0] * mix(m_ref[...], moved[1])
    face = jnp.sum(own_face * partner_face, axis=0, keepdims=True)
    total = jnp.zeros((1, 1), F32)
    for p in range(own_ref.shape[0]):
        if p > 0:
            face = jnp.sum(own_ref[p].astype(F32) * far_ref[0].astype(F32), axis=0, keepdims=True)
        met = face / (orient * cross[p])
        out_ref[p : p + 1] = met
        total = total + jnp.sum(met, axis=1, keepdims=True)
    total_ref[...] = jnp.broadcast_to(total, total_ref.shape)


def third_step_kernel(
    held_ref, mine_ref, other_ref, first_ref, second_ref, outer_ref, v_ref, m_ref, next_ref, held, moved
):
    planes, orient, _ = held.shape
    matrix = m_ref[...]
    first, second = boltzmann(first_ref[...]), boltzmann(second_ref[...])
    face_drifts(v_ref, mine_ref, other_ref, moved, (0, 1))
    cross = first * second
    for p in range(planes):
        kept = held_ref[p + 2]
        if p in (0, planes - 1):
            arrived = cross[p : p + 1] * mix(matrix, moved[min(p, 1)])
            kept = (kept.astype(F32) + arrived).astype(BF16)
        held[p] = kept

    @each_row_block(orient)
    def _(index):
        rows = rows_of(index)
        geo = geometry(v_ref, rows)
        loaded = [load_plane(held_ref, p, rows) for p in (0, 1)]
        loaded += [load_plane(held, p, rows) for p in range(planes)]
        loaded += [load_plane(held_ref, p, rows) for p in (planes + 2, planes + 3)]
        for p in range(planes + 2):
            store_plane(moved, p, rows, drift(loaded[p + 1], loaded[p], loaded[p + 2], geo))

    squared = second * second
    factors = [outer_ref[0:1]] + [squared[p : p + 1] for p in range(planes)] + [outer_ref[1:2]]
    for p, factor in enumerate(factors):
        next_ref[p] = (factor * mix(matrix, moved[p])).astype(BF16)


def weight_kernel(core_ref, partner_ref, start_ref, turned_ref, weight_ref, own_ref):
    planes = partner_ref.shape[0]
    core = core_ref[0]
    for p in range(planes):
        weight_ref[p] = mix(turned_ref[...], partner_ref[p]).astype(BF16)
    for p in range(2):
        own_ref[p] = mix(turned_ref[...], start_ref[core * (planes - 1) + p - 2 * p * core]).astype(BF16)


def fold(value):
    return jnp.sum(value.reshape(ROWS // 8, 8, LANES), axis=0)


def pairing_kernel(held_ref, second_ref, v_ref, weight_ref, low_ref, inner_ref, high_ref, out_ref):
    planes, orient, cells = weight_ref.shape
    second = boltzmann(second_ref[...])
    tiles = cells // LANES

    def body(index, sums):
        rows = rows_of(index)
        geo = geometry(v_ref, rows)
        loaded = [load_plane(held_ref, p, rows) for p in range(planes + 2)]
        new = []
        for p in range(planes):
            moved_tiles = drift(loaded[p + 1], loaded[p], loaded[p + 2], geo)
            weights = load_plane(weight_ref, p, rows)
            partner_refs = [(low_ref, 0)] + [(inner_ref, k) for k in range(planes - 2)] + [(high_ref, 0)]
            partner = load_plane(*partner_refs[p], rows)
            for t in range(tiles):
                last, third = sums[2 * (p * tiles + t)], sums[2 * (p * tiles + t) + 1]
                new.append(last + fold(moved_tiles[t] * weights[t].astype(F32)))
                new.append(third + fold(loaded[p + 1][t].astype(F32) * partner[t].astype(F32)))
        return tuple(new)

    zero = jnp.zeros((8, LANES), F32)
    sums = lax.fori_loop(0, orient // ROWS, body, (zero,) * (2 * planes * tiles), unroll=UNROLL)
    for p in range(planes):
        for t in range(tiles):
            last = jnp.sum(sums[2 * (p * tiles + t)], axis=0, keepdims=True)
            third = jnp.sum(sums[2 * (p * tiles + t) + 1], axis=0, keepdims=True)
            factor = second[p : p + 1, columns(t)]
            out_ref[p : p + 1, columns(t)] = (0.5 * factor * last + third / (factor * factor)) / orient


def last_kernel(
    core_ref, message_ref, weight_ref, own_weight_ref, own_low_ref, own_high_ref, partner_low_ref, partner_high_ref,
    shared_ref, met_ref,    own_ref, partner_ref, v_ref, m_ref, sent_ref, kept_ref, moved, gained,
):
    planes, cells = shared_ref.shape
    orient = m_ref.shape[0]
    tiles = cells // LANES
    core = core_ref[0]
    half = planes // 2
    face = core * (planes - 1)
    inner = face + 1 - 2 * core

    def at_face(ref, depth):
        return jnp.where(core == 0, boltzmann(ref[depth : depth + 1]), boltzmann(ref[planes - 1 - depth : planes - depth]))

    factors = [[at_face(ref, depth) for depth in range(2)] for ref in (partner_ref, own_ref)]

    @each_row_block(orient)
    def _(index):
        rows = rows_of(index)
        ahead, rate_plus, rate_minus = face_parts(v_ref, rows)
        rate = rate_plus + rate_minus
        for t in range(tiles):
            got = rate * message_ref[0, rows, columns(t)].astype(F32)
            moved[0, rows, columns(t)] = jnp.where(ahead, got, 0.0).astype(BF16)
            moved[1, rows, columns(t)] = jnp.where(ahead, 0.0, got).astype(BF16)

    for s in range(2):
        gained[s] = (factors[s][0] * factors[s][0] * mix(m_ref[...], moved[s])).astype(BF16)

    def body(index, sums):
        rows = rows_of(index)
        ahead, rate_plus, rate_minus = face_parts(v_ref, rows)
        rate = rate_plus + rate_minus
        sides = (jnp.where(ahead, rate, 0.0), jnp.where(ahead, 0.0, rate))
        message = load_plane(message_ref, 1, rows)
        new = []
        for s in range(2):
            change = load_plane(gained, s, rows)
            moved_tiles = drift(change, None, None, geometry(v_ref, rows, 1.0 - 2.0 * s))
            if s == 0:
                weights = [load_plane(weight_ref, p, rows) for p in (face, inner)]
            else:
                weights = [load_plane(own_weight_ref, p, rows) for p in (0, 1)]
            pair = ((partner_low_ref, partner_high_ref), (own_low_ref, own_high_ref))[s]
            third = [jnp.where(core == 0, low, high) for low, high in zip(*(load_plane(ref, 0, rows) for ref in pair))]
            for t in range(tiles):
                on_face = moved_tiles[t] + sides[s] * message[t].astype(F32)
                wide = change[t].astype(F32)
                terms = (
                    on_face * weights[0][t].astype(F32),
                    sides[s] * wide * weights[1][t].astype(F32),
                    wide * third[t].astype(F32),
                )
                base = 3 * (s * tiles + t)
                new += [sums[base + k] + fold(term) for k, term in enumerate(terms)]
        return tuple(new)

    zero = jnp.zeros((8, LANES), F32)
    sums = lax.fori_loop(0, orient // ROWS, body, (zero,) * (6 * tiles), unroll=UNROLL)
    for t in range(tiles):
        shares = []
        for s in range(2):
            base = 3 * (s * tiles + t)
            last, onward, third = (jnp.sum(sums[base + k], axis=0, keepdims=True) / orient for k in range(3))
            near, far = (factors[s][depth][:, columns(t)] for depth in range(2))
            shares.append((0.5 * near * last + third / (near * near), 0.5 * far * onward))
        for p in range(planes):
            at = slice(p, p + 1), columns(t)
            mine = core == (0 if p < half else 1)
            depth = min(p, planes - 1 - p)
            met = jnp.where(mine, 0.5 * met_ref[depth : depth + 1, columns(t)], 0.0)
            sent, kept = shared_ref[at] + met, met
            if depth < 2:
                sent = sent + jnp.where(mine, shares[0][depth], 0.0)
                kept = kept + jnp.where(mine, shares[1][depth], 0.0)
            sent_ref[at] = sent
            kept_ref[at] = kept


def split_outputs(outs):
    low, high, state, near, far, kept, outer = outs
    return (low, high), state, (near, far), kept, outer


def kernel_call(kernel, outs, scratch, args):
    vmem = pl.BlockSpec(memory_space=pltpu.VMEM)
    smem = pl.BlockSpec(memory_space=pltpu.SMEM)
    return pl.pallas_call(
        kernel,
        out_shape=outs,
        in_specs=[smem if arg.dtype == jnp.int32 else vmem for arg in args],
        out_specs=jax.tree.map(lambda _: vmem, outs),
        scratch_shapes=[pltpu.VMEM(*s) if len(s) == 2 else pltpu.VMEM(s, BF16) for s in scratch],
        compiler_params=pltpu.CompilerParams(vmem_limit_bytes=7 << 20),
        cost_estimate=pl.CostEstimate(flops=0, bytes_accessed=0, transcendentals=0),
    )(*args)


def shards(fields, end_weights, directions, analysis, synthesis, decay_rates):
    device = lax.axis_index("space")
    core = device % 2
    planes, cells = fields.shape
    orient = end_weights.shape[0]
    plane_index = device // 2 * planes + lax.broadcasted_iota(jnp.int32, (planes, 1), 0)
    ramp = slope * plane_index.astype(F32) / (planes * lax.axis_size("space") // 2)
    own = fields + ramp
    partner = swap_species(fields) + ramp

    wide = lambda extra: jax.ShapeDtypeStruct((planes + extra, orient, cells), BF16)
    slab, plane = wide(0), wide(1 - planes)
    face = core ^ (1 - device // 2 % 2)
    core_word = jnp.stack([face, core]).astype(jnp.int32)
    start = jnp.transpose(end_weights, (1, 0, 2))
    spread, edge0, coded = kernel_call(
        prologue_kernel,
        (jax.ShapeDtypeStruct((4, orient, LANES), F32), plane, jax.ShapeDtypeStruct((16, cells), BF16)),
        (((16, cells), F32),),
        (core_word, directions, start, own, partner),
    )
    matrix, turned = kernel_call(
        matrix_kernel,
        (jax.ShapeDtypeStruct((orient, orient), BF16),) * 2,
        (),
        (synthesis, decay_rates[None], analysis),
    )
    other0, matrix = lax.optimization_barrier((swap_species(edge0), matrix))
    message0 = kernel_call(
        first_message_kernel,
        jax.ShapeDtypeStruct((1, orient + 16, cells), BF16),
        (),
        (edge0, other0, coded, spread),
    )

    def message(blocks, others):
        shape = jax.ShapeDtypeStruct((len(blocks),) + blocks[0].shape[1:], BF16)
        return kernel_call(message_kernel, shape, (), (*blocks, *others, spread))

    start, _ = lax.optimization_barrier((start, message0))
    arrived0 = exchange_faces(message0)
    alone, inner, edges1 = kernel_call(
        first_alone_kernel, (slab, wide(-2), plane), (slab.shape, slab.shape), (start, own, spread, matrix)
    )
    weights, own_weights = kernel_call(
        weight_kernel, (slab, wide(2 - planes)), (), (core_word, swap_species(start), start, turned)
    )
    others1, weights = lax.optimization_barrier((swap_species(edges1), weights))
    message1 = message([edges1], [others1])
    state, *_ = lax.optimization_barrier((alone, message1, weights))
    edges2, edges3 = kernel_call(
        next_alone_kernel, (plane, plane), (slab.shape, slab.shape), (state, own, partner, spread, matrix)
    )
    edges2, edges3, arrived0 = lax.optimization_barrier((edges2, edges3, arrived0))
    message2 = message([edges2, edges3], [swap_species(edges2), swap_species(edges3)])
    arrived = [exchange_faces(message1), exchange_faces(message2)]
    crossed0 = swap_species(arrived0)
    inner, _ = lax.optimization_barrier((inner, arrived0))
    partner_inner = swap_species(inner)

    alone, *_ = lax.optimization_barrier((alone, message1, message2))
    half = planes // 2
    faces, second_state, sent_half, kept_half, outer = split_outputs(
        kernel_call(
            second_step_kernel,
            (plane, plane, wide(4), plane, plane, wide(half - planes), jax.ShapeDtypeStruct((2, cells), F32)),
            (wide(2).shape, wide(4).shape),
            (core_word, alone, edge0, arrived0, crossed0, own, partner, spread, matrix),
        )
    )
    arrived1, second_state, partner_inner = lax.optimization_barrier((arrived[0], second_state, partner_inner))
    *moving, _ = lax.optimization_barrier((*sent_half, *faces, arrived1))
    partner_faces = [swap_species(block) for block in moving[2:]]
    *partner_half, crossed1 = lax.optimization_barrier((*map(swap_species, moving[:2]), swap_species(arrived1)))
    density = jax.ShapeDtypeStruct((planes, cells), F32)
    met, partition = kernel_call(
        middle_kernel,
        (jax.ShapeDtypeStruct((half, cells), F32), density),
        ((2, orient, cells),),
        (core_word, kept_half, *partner_half, arrived1, own, partner, spread, matrix),
    )
    count = lax.axis_size("space")

    def received(value, distance, after):
        block = lax.ppermute(value, "space", [(i, i ^ distance) for i in range(count)])
        return lax.optimization_barrier((block, after))

    def gathered(value, distance, after):
        block, after = received(value, distance, after)
        return kernel_call(add_kernel, density, (), (value, block)), after

    partition, second_state = gathered(partition, 1, second_state)
    second_state, _ = lax.optimization_barrier((second_state, partition))
    third_state = kernel_call(
        third_step_kernel,
        wide(2),
        (slab.shape, wide(2).shape),
        (second_state, arrived1, crossed1, own, partner, outer, spread, matrix),
    )
    partition, third_state = gathered(partition, 4, third_state)
    third_state, _ = lax.optimization_barrier((third_state, partition))
    shared = kernel_call(
        pairing_kernel,
        density,
        (),
        (third_state, partner, spread, weights, partner_faces[0], partner_inner, partner_faces[1]),
    )
    arrived2, shared = lax.optimization_barrier((arrived[1], shared))
    distance = 8
    while distance < count:
        partition, shared = gathered(partition, distance, shared)
        distance *= 2
    beside, shared = received(partition, 2, shared)
    sent, kept = kernel_call(
        last_kernel,
        (density, density),
        ((2, orient, cells), (2, orient, cells)),
        (
            core_word, arrived2, weights, own_weights, *faces, *partner_faces, shared, met,
            own, partner, spread, matrix,
        ),
    )
    return kernel_call(
        functools.partial(divide_kernel, count // 2 * planes * cells),
        density,
        (),
        (kept, swap_species(sent), partition, beside),
    )


def solution(mesh):
    return jax.shard_map(
        shards,
        mesh=mesh,
        in_specs=(P(("runs", "space"), None), P(None, ("runs", "space"), None), P(), P(), P(), P()),
        out_specs=P(("runs", "space"), None),
        check_vma=False,
    )
```

```python
import functools

import jax
import jax.numpy as jnp
from jax import lax
from jax.experimental import pallas as pl
from jax.experimental.pallas import tpu as pltpu
from jax.sharding import PartitionSpec as P

NZ = 16
STEPS = 4
LANES = 128
ROWS = 16
UNROLL = 4

courant = 0.3
slope = 0.6

BF16 = jnp.bfloat16
F32 = jnp.float32


def swap_species(block):
    count = lax.axis_size("space")
    return lax.ppermute(block, "space", [(i ^ 1, i) for i in range(count)])


def exchange_faces(block):
    count = lax.axis_size("space")
    route = []
    for slab in range(count // 2):
        beside = ((slab + 1) ^ 1) - 1
        route += [(2 * slab, 2 * (slab ^ 1)), (2 * slab + 1, 2 * beside % count + 1)]
    return lax.ppermute(block, "space", route)


def rows_of(index):
    return pl.ds(pl.multiple_of(index * ROWS, ROWS), ROWS)


def each_row_block(orient):
    def run(body):
        def step(index, carry):
            body(index)
            return carry

        lax.fori_loop(0, orient // ROWS, step, 0, unroll=UNROLL)

    return run


def columns(tile):
    return slice(LANES * tile, LANES * (tile + 1))


def geometry(v_ref, rows, sign=1.0):
    lane = lax.broadcasted_iota(jnp.int32, (ROWS, LANES), 1)
    vx, vy, vz = (sign * v_ref[c, rows, :] for c in range(3))
    narrow = vx.astype(BF16)
    plus_x, narrow_plus, plus_y, plus_z = vx > 0, narrow > jnp.zeros_like(narrow), vy > 0, vz > 0
    rate_x, rate_y, rate_z = (courant * jnp.abs(t) for t in (vx, vy, vz))
    stay = 1.0 - (rate_x + rate_y + rate_z)
    z_from = (lane & (LANES - NZ)) | (jnp.where(plus_z, lane - 1, lane + 1) & (NZ - 1))
    y_from = jnp.where(plus_y, lane - NZ, lane + NZ) & (LANES - 1)
    y_edge = jnp.where(plus_y, lane, LANES - 1 - lane) < NZ
    return plus_x, narrow_plus, plus_y, stay, rate_x, rate_y, rate_z, z_from, y_from, y_edge


def pick(tile, index):
    return jnp.take_along_axis(tile, index, axis=1, mode="promise_in_bounds")


def load_plane(ref, plane, rows):
    return [ref[plane, rows, columns(t)] for t in range(ref.shape[2] // LANES)]


def drift(center, before, after, geo):
    plus_x, narrow_plus, plus_y, stay, rate_x, rate_y, rate_z, z_from, y_from, y_edge = geo
    tiles = len(center)
    center = [tile.astype(F32) for tile in center]
    turned = [pick(tile, y_from) for tile in center]
    moved = []
    for t in range(tiles):
        total = stay * center[t]
        if before is not None and after is not None:
            total = total + rate_x * jnp.where(narrow_plus, before[t], after[t]).astype(F32)
        elif before is not None:
            total = total + jnp.where(plus_x, rate_x, 0.0) * before[t].astype(F32)
        elif after is not None:
            total = total + jnp.where(plus_x, 0.0, rate_x) * after[t].astype(F32)
        over = jnp.where(plus_y, turned[t - 1], turned[(t + 1) % tiles])
        total = total + rate_y * jnp.where(y_edge, over, turned[t])
        total = total + rate_z * pick(center[t], z_from)
        moved.append(total)
    return moved


def store_plane(ref, plane, rows, tiles):
    for t, tile in enumerate(tiles):
        ref[plane, rows, columns(t)] = tile.astype(ref.dtype)


def mix(matrix, moved):
    return jnp.dot(matrix, moved, preferred_element_type=F32)


def boltzmann(field):
    return jnp.exp(-0.5 * field)


def prologue_kernel(
    core_ref, species_ref, directions_ref, start_ref, fields_ref, partner_ref, spread_ref, edge_ref, coded_ref, near
):
    sign = 1.0 - 2.0 * species_ref[0].astype(F32)
    toward = sign * (1.0 - 2.0 * core_ref[0].astype(F32))
    planes, orient, cells = start_ref.shape
    low = boltzmann(fields_ref[0:1])
    high = boltzmann(fields_ref[fields_ref.shape[0] - 1 :])
    for c in range(4):
        row = directions_ref[c % 3 : c % 3 + 1]
        column = jnp.broadcast_to(row, (LANES, orient)).T
        spread_ref[c] = (toward if c == 3 else sign) * column

    @each_row_block(orient)
    def _(index):
        rows = rows_of(index)
        plus_x = spread_ref[0, rows, :] > 0
        for t in range(cells // LANES):
            at = rows, columns(t)
            chosen = jnp.where(
                plus_x,
                high[:, columns(t)] * start_ref[planes - 1, *at].astype(F32),
                low[:, columns(t)] * start_ref[0, *at].astype(F32),
            )
            edge_ref[0, *at] = chosen.astype(BF16)

    near[...] = jnp.zeros_like(near)
    for s, ref in enumerate((fields_ref, partner_ref)):
        for depth in range(2):
            high_row, low_row = (ref[p : p + 1] for p in (planes - 1 - depth, depth))
            row = jnp.where(core_ref[0] == 1, high_row, low_row)
            coarse = row.astype(BF16).astype(F32)
            at = 2 * s + depth
            near[at : at + 1] = coarse
            near[at + 4 : at + 5] = row - coarse
    coded_ref[...] = near[...].astype(BF16)


def matrix_kernel(synthesis_ref, decay_ref, analysis_ref, out_ref, turned_ref):
    rest = synthesis_ref[...].astype(F32) * decay_ref[...]
    total = jnp.full(out_ref.shape, 1.0 / out_ref.shape[1], F32)
    for _ in range(3):
        part = rest.astype(BF16)
        rest = rest - part.astype(F32)
        total = total + jnp.dot(part, analysis_ref[...], preferred_element_type=F32)
    out_ref[...] = total.astype(BF16)
    turned_ref[...] = total.T.astype(BF16)


def add_kernel(one_ref, two_ref, out_ref):
    out_ref[...] = one_ref[...] + two_ref[...]


def divide_kernel(cells, kept_ref, arrived_ref, one_ref, two_ref, out_ref):
    out_ref[...] = (kept_ref[...] + arrived_ref[...]) * (cells / (one_ref[...] + two_ref[...]))


def message_kernel(*refs):
    count = (len(refs) - 2) // 2
    v_ref, out_ref = refs[-2:]
    orient, cells = refs[0].shape[1:]

    @each_row_block(orient)
    def _(index):
        rows = rows_of(index)
        narrow = v_ref[3, rows, :].astype(BF16)
        leaves = narrow < jnp.zeros_like(narrow)
        for p in range(count):
            for t in range(cells // LANES):
                at = 0, rows, columns(t)
                out_ref[p, rows, columns(t)] = jnp.where(leaves, refs[p][at], refs[count + p][at])


def first_message_kernel(mine_ref, other_ref, coded_ref, v_ref, out_ref):
    message_kernel(mine_ref, other_ref, v_ref, out_ref)
    orient = mine_ref.shape[1]
    out_ref[0, orient:] = coded_ref[...]


def write_edge(edges_ref, step, faces, rows, v_ref):
    narrow = v_ref[0, rows, :].astype(BF16)
    plus_x = narrow > jnp.zeros_like(narrow)
    for t in range(len(faces[0])):
        edges_ref[step, rows, columns(t)] = jnp.where(plus_x, faces[-1][t], faces[0][t])


def alone_step(source_ref, moved, targets, v_ref, edges_ref, step):
    planes, orient, _ = source_ref.shape

    @each_row_block(orient)
    def _(index):
        rows = rows_of(index)
        geo = geometry(v_ref, rows)
        loaded = [load_plane(source_ref, p, rows) for p in range(planes)]
        if edges_ref is not None:
            write_edge(edges_ref, step, loaded, rows, v_ref)
        for p in targets:
            before = loaded[p - 1] if p > 0 else None
            after = loaded[p + 1] if p < planes - 1 else None
            store_plane(moved, p, rows, drift(loaded[p], before, after, geo))


def first_alone_kernel(start_ref, first_ref, v_ref, m_ref, out_ref, inner_ref, edges_ref, held, moved):
    planes, orient, _ = start_ref.shape
    first = boltzmann(first_ref[...])
    for p in range(planes):
        held[p] = (first[p : p + 1] * start_ref[p].astype(F32)).astype(BF16)
    alone_step(held, moved, range(planes), v_ref, None, 0)
    for p in (0, planes - 1, *range(1, planes - 1)):
        state = (first[p : p + 1] * first[p : p + 1] * mix(m_ref[...], moved[p])).astype(BF16)
        out_ref[p] = state
        if 0 < p < planes - 1:
            inner_ref[p - 1] = state

    @each_row_block(orient)
    def _(index):
        rows = rows_of(index)
        write_edge(edges_ref, 0, [load_plane(out_ref, p, rows) for p in (0, planes - 1)], rows, v_ref)


def next_alone_kernel(state_ref, first_ref, second_ref, v_ref, m_ref, edges2_ref, edges3_ref, held, moved):
    planes, orient, _ = state_ref.shape
    first = boltzmann(first_ref[...])
    second = boltzmann(second_ref[...])
    alone_step(state_ref, moved, range(planes), v_ref, None, 0)
    for p in range(planes):
        held[p] = (first[p : p + 1] * second[p : p + 1] * mix(m_ref[...], moved[p])).astype(BF16)
    alone_step(held, moved, (0, planes - 1), v_ref, edges2_ref, 0)
    for p in (0, planes - 1):
        held[p] = (second[p : p + 1] * second[p : p + 1] * mix(m_ref[...], moved[p])).astype(BF16)

    @each_row_block(orient)
    def _(index):
        rows = rows_of(index)
        write_edge(edges3_ref, 0, [load_plane(held, p, rows) for p in (0, planes - 1)], rows, v_ref)


def face_parts(v_ref, rows):
    vx = v_ref[0, rows, :]
    rate = courant * jnp.abs(vx)
    return v_ref[3, rows, :] > 0, jnp.where(vx > 0, rate, 0.0), jnp.where(vx > 0, 0.0, rate)


def face_drifts(v_ref, mine_ref, other_ref, moved, slots):
    @each_row_block(v_ref.shape[1])
    def _(index):
        rows = rows_of(index)
        ahead, rate_plus, rate_minus = face_parts(v_ref, rows)
        for t in range(mine_ref.shape[2] // LANES):
            mine = mine_ref[0, rows, columns(t)].astype(F32)
            other = other_ref[0, rows, columns(t)].astype(F32)
            face = jnp.where(ahead, mine, other)
            moved[slots[0], rows, columns(t)] = (rate_plus * face).astype(BF16)
            moved[slots[1], rows, columns(t)] = (rate_minus * face).astype(BF16)


def second_step_kernel(
    core_ref, alone_ref, edge_ref, mine_ref, other_ref, first_ref, second_ref, v_ref, m_ref,
    face_low_ref, face_high_ref, next_ref, sent_near_ref, sent_far_ref, kept_ref, outer_ref, held, moved,
):
    planes, orient, _ = alone_ref.shape
    matrix = m_ref[...]
    first, second = boltzmann(first_ref[...]), boltzmann(second_ref[...])
    core = core_ref[0]
    mine, other = (block[:4] + block[4:8] for block in (ref[0, orient:].astype(F32) for ref in (mine_ref, other_ref)))
    other = (other[2:4], other[0:2])
    mine = (mine[0:2], mine[2:4])
    low = [jnp.where(core == 0, mine[k], other[k]) for k in range(2)]
    high = [jnp.where(core == 0, other[k], mine[k]) for k in range(2)]
    beyond = [boltzmann(block[k : k + 1]) for block in (low[0], high[0], low[1], high[1]) for k in range(2)]
    face_drifts(v_ref, mine_ref, other_ref, moved, (0, 1))

    @each_row_block(orient)
    def _(index):
        rows = rows_of(index)
        _, rate_plus, rate_minus = face_parts(v_ref, rows)
        for t in range(edge_ref.shape[2] // LANES):
            edge = edge_ref[0, rows, columns(t)].astype(F32)
            moved[2, rows, columns(t)] = (rate_minus * edge).astype(BF16)
            moved[3, rows, columns(t)] = (rate_plus * edge).astype(BF16)

    squared = first * first
    for p in range(planes):
        kept = alone_ref[p]
        if p in (0, planes - 1):
            arrived = squared[p : p + 1] * mix(matrix, moved[min(p, 1)])
            kept = (kept.astype(F32) + arrived).astype(BF16)
            (face_high_ref if p else face_low_ref)[0] = kept
        held[p + 1] = kept
    held[0] = (beyond[0] * beyond[0] * mix(matrix, moved[2])).astype(BF16)
    held[planes + 1] = (beyond[2] * beyond[2] * mix(matrix, moved[3])).astype(BF16)
    count = planes + 2

    @each_row_block(orient)
    def _(index):
        rows = rows_of(index)
        geo = geometry(v_ref, rows)
        _, rate_plus, rate_minus = face_parts(v_ref, rows)
        loaded = [load_plane(held, p, rows) for p in range(count)]
        for p in range(count):
            before = loaded[p - 1] if p > 0 else None
            after = loaded[p + 1] if p < count - 1 else None
            store_plane(moved, p + 1, rows, drift(loaded[p], before, after, geo))
        store_plane(moved, 0, rows, [rate_minus * tile.astype(F32) for tile in loaded[0]])
        store_plane(moved, count + 1, rows, [rate_plus * tile.astype(F32) for tile in loaded[-1]])

    cross = first * second
    factors = [beyond[1] * beyond[5], beyond[0] * beyond[4]]
    factors += [cross[p : p + 1] for p in range(planes)]
    factors += [beyond[2] * beyond[6], beyond[3] * beyond[7]]
    for p, factor in enumerate(factors):
        next_ref[p] = (factor * mix(matrix, moved[p])).astype(BF16)
    for p in range(planes // 2):
        sent_ref = (sent_near_ref, sent_far_ref)[p]
        sent_ref[0] = next_ref[2 + (planes - 1) * (1 - core) + (2 * core - 1) * p]
        kept_ref[p] = next_ref[2 + (planes - 1) * core + (1 - 2 * core) * p]
    outer_ref[0:1] = beyond[4] * beyond[4]
    outer_ref[1:2] = beyond[6] * beyond[6]


def middle_kernel(
    core_ref, own_ref, near_ref, far_ref, message_ref, first_ref, second_ref, v_ref, m_ref, out_ref, total_ref, moved
):
    _, orient, cells = own_ref.shape
    planes = first_ref.shape[0]

    def cross_of(depth):
        low, high = (
            boltzmann(first_ref[p : p + 1]) * boltzmann(second_ref[p : p + 1]) for p in (depth, planes - 1 - depth)
        )
        return jnp.where(core_ref[0] == 0, low, high)

    cross = [cross_of(depth) for depth in range(2)]

    @each_row_block(orient)
    def _(index):
        rows = rows_of(index)
        ahead, rate_plus, rate_minus = face_parts(v_ref, rows)
        rate = rate_plus + rate_minus
        for t in range(cells // LANES):
            gained = rate * message_ref[0, rows, columns(t)].astype(F32)
            moved[0, rows, columns(t)] = jnp.where(ahead, gained, 0.0).astype(BF16)
            moved[1, rows, columns(t)] = jnp.where(ahead, 0.0, gained).astype(BF16)

    own_face = own_ref[0].astype(F32) + cross[0] * mix(m_ref[...], moved[0])
    partner_face = near_ref[0].astype(F32) + cross[0] * mix(m_ref[...], moved[1])
    face = jnp.sum(own_face * partner_face, axis=0, keepdims=True)
    total = jnp.zeros((1, 1), F32)
    for p in range(own_ref.shape[0]):
        if p > 0:
            face = jnp.sum(own_ref[p].astype(F32) * far_ref[0].astype(F32), axis=0, keepdims=True)
        met = face / (orient * cross[p])
        out_ref[p : p + 1] = met
        total = total + jnp.sum(met, axis=1, keepdims=True)
    total_ref[...] = jnp.broadcast_to(total, total_ref.shape)


def third_step_kernel(
    held_ref, mine_ref, other_ref, first_ref, second_ref, outer_ref, v_ref, m_ref, next_ref, held, moved
):
    planes, orient, _ = held.shape
    matrix = m_ref[...]
    first, second = boltzmann(first_ref[...]), boltzmann(second_ref[...])
    face_drifts(v_ref, mine_ref, other_ref, moved, (0, 1))
    cross = first * second
    for p in range(planes):
        kept = held_ref[p + 2]
        if p in (0, planes - 1):
            arrived = cross[p : p + 1] * mix(matrix, moved[min(p, 1)])
            kept = (kept.astype(F32) + arrived).astype(BF16)
        held[p] = kept

    @each_row_block(orient)
    def _(index):
        rows = rows_of(index)
        geo = geometry(v_ref, rows)
        loaded = [load_plane(held_ref, p, rows) for p in (0, 1)]
        loaded += [load_plane(held, p, rows) for p in range(planes)]
        loaded += [load_plane(held_ref, p, rows) for p in (planes + 2, planes + 3)]
        for p in range(planes + 2):
            store_plane(moved, p, rows, drift(loaded[p + 1], loaded[p], loaded[p + 2], geo))

    squared = second * second
    factors = [outer_ref[0:1]] + [squared[p : p + 1] for p in range(planes)] + [outer_ref[1:2]]
    for p, factor in enumerate(factors):
        next_ref[p] = (factor * mix(matrix, moved[p])).astype(BF16)


def weight_kernel(core_ref, partner_ref, start_ref, turned_ref, weight_ref, own_ref):
    planes = partner_ref.shape[0]
    core = core_ref[0]
    for p in range(planes):
        weight_ref[p] = mix(turned_ref[...], partner_ref[p]).astype(BF16)
    for p in range(2):
        own_ref[p] = mix(turned_ref[...], start_ref[core * (planes - 1) + p - 2 * p * core]).astype(BF16)


def fold(value):
    return jnp.sum(value.reshape(ROWS // 8, 8, LANES), axis=0)


def pairing_kernel(held_ref, second_ref, v_ref, weight_ref, low_ref, inner_ref, high_ref, out_ref):
    planes, orient, cells = weight_ref.shape
    second = boltzmann(second_ref[...])
    tiles = cells // LANES

    def body(index, sums):
        rows = rows_of(index)
        geo = geometry(v_ref, rows)
        loaded = [load_plane(held_ref, p, rows) for p in range(planes + 2)]
        new = []
        for p in range(planes):
            moved_tiles = drift(loaded[p + 1], loaded[p], loaded[p + 2], geo)
            weights = load_plane(weight_ref, p, rows)
            partner_refs = [(low_ref, 0)] + [(inner_ref, k) for k in range(planes - 2)] + [(high_ref, 0)]
            partner = load_plane(*partner_refs[p], rows)
            for t in range(tiles):
                last, third = sums[2 * (p * tiles + t)], sums[2 * (p * tiles + t) + 1]
                new.append(last + fold(moved_tiles[t] * weights[t].astype(F32)))
                new.append(third + fold(loaded[p + 1][t].astype(F32) * partner[t].astype(F32)))
        return tuple(new)

    zero = jnp.zeros((8, LANES), F32)
    sums = lax.fori_loop(0, orient // ROWS, body, (zero,) * (2 * planes * tiles), unroll=UNROLL)
    for p in range(planes):
        for t in range(tiles):
            last = jnp.sum(sums[2 * (p * tiles + t)], axis=0, keepdims=True)
            third = jnp.sum(sums[2 * (p * tiles + t) + 1], axis=0, keepdims=True)
            factor = second[p : p + 1, columns(t)]
            out_ref[p : p + 1, columns(t)] = (0.5 * factor * last + third / (factor * factor)) / orient


def last_kernel(
    core_ref, message_ref, weight_ref, own_weight_ref, own_low_ref, own_high_ref, partner_low_ref, partner_high_ref,
    shared_ref, met_ref,    own_ref, partner_ref, v_ref, m_ref, sent_ref, kept_ref, moved, gained,
):
    planes, cells = shared_ref.shape
    orient = m_ref.shape[0]
    tiles = cells // LANES
    core = core_ref[0]
    half = planes // 2
    face = core * (planes - 1)
    inner = face + 1 - 2 * core

    def at_face(ref, depth):
        return jnp.where(core == 0, boltzmann(ref[depth : depth + 1]), boltzmann(ref[planes - 1 - depth : planes - depth]))

    factors = [[at_face(ref, depth) for depth in range(2)] for ref in (partner_ref, own_ref)]

    @each_row_block(orient)
    def _(index):
        rows = rows_of(index)
        ahead, rate_plus, rate_minus = face_parts(v_ref, rows)
        rate = rate_plus + rate_minus
        for t in range(tiles):
            got = rate * message_ref[0, rows, columns(t)].astype(F32)
            moved[0, rows, columns(t)] = jnp.where(ahead, got, 0.0).astype(BF16)
            moved[1, rows, columns(t)] = jnp.where(ahead, 0.0, got).astype(BF16)

    for s in range(2):
        gained[s] = (factors[s][0] * factors[s][0] * mix(m_ref[...], moved[s])).astype(BF16)

    def body(index, sums):
        rows = rows_of(index)
        ahead, rate_plus, rate_minus = face_parts(v_ref, rows)
        rate = rate_plus + rate_minus
        sides = (jnp.where(ahead, rate, 0.0), jnp.where(ahead, 0.0, rate))
        message = load_plane(message_ref, 1, rows)
        new = []
        for s in range(2):
            change = load_plane(gained, s, rows)
            moved_tiles = drift(change, None, None, geometry(v_ref, rows, 1.0 - 2.0 * s))
            if s == 0:
                weights = [load_plane(weight_ref, p, rows) for p in (face, inner)]
            else:
                weights = [load_plane(own_weight_ref, p, rows) for p in (0, 1)]
            pair = ((partner_low_ref, partner_high_ref), (own_low_ref, own_high_ref))[s]
            third = [jnp.where(core == 0, low, high) for low, high in zip(*(load_plane(ref, 0, rows) for ref in pair))]
            for t in range(tiles):
                on_face = moved_tiles[t] + sides[s] * message[t].astype(F32)
                wide = change[t].astype(F32)
                terms = (
                    on_face * weights[0][t].astype(F32),
                    sides[s] * wide * weights[1][t].astype(F32),
                    wide * third[t].astype(F32),
                )
                base = 3 * (s * tiles + t)
                new += [sums[base + k] + fold(term) for k, term in enumerate(terms)]
        return tuple(new)

    zero = jnp.zeros((8, LANES), F32)
    sums = lax.fori_loop(0, orient // ROWS, body, (zero,) * (6 * tiles), unroll=UNROLL)
    for t in range(tiles):
        shares = []
        for s in range(2):
            base = 3 * (s * tiles + t)
            last, onward, third = (jnp.sum(sums[base + k], axis=0, keepdims=True) / orient for k in range(3))
            near, far = (factors[s][depth][:, columns(t)] for depth in range(2))
            shares.append((0.5 * near * last + third / (near * near), 0.5 * far * onward))
        for p in range(planes):
            at = slice(p, p + 1), columns(t)
            mine = core == (0 if p < half else 1)
            depth = min(p, planes - 1 - p)
            met = jnp.where(mine, 0.5 * met_ref[depth : depth + 1, columns(t)], 0.0)
            sent, kept = shared_ref[at] + met, met
            if depth < 2:
                sent = sent + jnp.where(mine, shares[0][depth], 0.0)
                kept = kept + jnp.where(mine, shares[1][depth], 0.0)
            sent_ref[at] = sent
            kept_ref[at] = kept


def split_outputs(outs):
    low, high, state, near, far, kept, outer = outs
    return (low, high), state, (near, far), kept, outer


def kernel_call(kernel, outs, scratch, args):
    vmem = pl.BlockSpec(memory_space=pltpu.VMEM)
    smem = pl.BlockSpec(memory_space=pltpu.SMEM)
    return pl.pallas_call(
        kernel,
        out_shape=outs,
        in_specs=[smem if arg.dtype == jnp.int32 else vmem for arg in args],
        out_specs=jax.tree.map(lambda _: vmem, outs),
        scratch_shapes=[pltpu.VMEM(*s) if len(s) == 2 else pltpu.VMEM(s, BF16) for s in scratch],
        compiler_params=pltpu.CompilerParams(vmem_limit_bytes=7 << 20),
        cost_estimate=pl.CostEstimate(flops=0, bytes_accessed=0, transcendentals=0),
    )(*args)


def shards(fields, end_weights, directions, analysis, synthesis, decay_rates):
    device = lax.axis_index("space")
    core = device % 2
    planes, cells = fields.shape
    orient = end_weights.shape[0]
    plane_index = device // 2 * planes + lax.broadcasted_iota(jnp.int32, (planes, 1), 0)
    ramp = slope * plane_index.astype(F32) / (planes * lax.axis_size("space") // 2)
    own = fields + ramp
    partner = swap_species(fields) + ramp

    wide = lambda extra: jax.ShapeDtypeStruct((planes + extra, orient, cells), BF16)
    slab, plane = wide(0), wide(1 - planes)
    face = core ^ (1 - device // 2 % 2)
    core_word = jnp.reshape(face, (1,)).astype(jnp.int32)
    species_word = jnp.reshape(core, (1,)).astype(jnp.int32)
    start = jnp.transpose(end_weights, (1, 0, 2))
    spread, edge0, coded = kernel_call(
        prologue_kernel,
        (jax.ShapeDtypeStruct((4, orient, LANES), F32), plane, jax.ShapeDtypeStruct((16, cells), BF16)),
        (((16, cells), F32),),
        (core_word, species_word, directions, start, own, partner),
    )
    matrix, turned = kernel_call(
        matrix_kernel,
        (jax.ShapeDtypeStruct((orient, orient), BF16),) * 2,
        (),
        (synthesis, decay_rates[None], analysis),
    )
    other0, matrix = lax.optimization_barrier((swap_species(edge0), matrix))
    message0 = kernel_call(
        first_message_kernel,
        jax.ShapeDtypeStruct((1, orient + 16, cells), BF16),
        (),
        (edge0, other0, coded, spread),
    )

    def message(blocks, others):
        shape = jax.ShapeDtypeStruct((len(blocks),) + blocks[0].shape[1:], BF16)
        return kernel_call(message_kernel, shape, (), (*blocks, *others, spread))

    start, _ = lax.optimization_barrier((start, message0))
    arrived0 = exchange_faces(message0)
    alone, inner, edges1 = kernel_call(
        first_alone_kernel, (slab, wide(-2), plane), (slab.shape, slab.shape), (start, own, spread, matrix)
    )
    weights, own_weights = kernel_call(
        weight_kernel, (slab, wide(2 - planes)), (), (core_word, swap_species(start), start, turned)
    )
    others1, weights = lax.optimization_barrier((swap_species(edges1), weights))
    message1 = message([edges1], [others1])
    state, *_ = lax.optimization_barrier((alone, message1, weights))
    edges2, edges3 = kernel_call(
        next_alone_kernel, (plane, plane), (slab.shape, slab.shape), (state, own, partner, spread, matrix)
    )
    edges2, edges3, arrived0 = lax.optimization_barrier((edges2, edges3, arrived0))
    message2 = message([edges2, edges3], [swap_species(edges2), swap_species(edges3)])
    arrived = [exchange_faces(message1), exchange_faces(message2)]
    crossed0 = swap_species(arrived0)
    inner, _ = lax.optimization_barrier((inner, arrived0))
    partner_inner = swap_species(inner)

    alone, *_ = lax.optimization_barrier((alone, message1, message2))
    half = planes // 2
    faces, second_state, sent_half, kept_half, outer = split_outputs(
        kernel_call(
            second_step_kernel,
            (plane, plane, wide(4), plane, plane, wide(half - planes), jax.ShapeDtypeStruct((2, cells), F32)),
            (wide(2).shape, wide(4).shape),
            (core_word, alone, edge0, arrived0, crossed0, own, partner, spread, matrix),
        )
    )
    arrived1, second_state, partner_inner = lax.optimization_barrier((arrived[0], second_state, partner_inner))
    *moving, _ = lax.optimization_barrier((*sent_half, *faces, arrived1))
    partner_faces = [swap_species(block) for block in moving[2:]]
    *partner_half, crossed1 = lax.optimization_barrier((*map(swap_species, moving[:2]), swap_species(arrived1)))
    density = jax.ShapeDtypeStruct((planes, cells), F32)
    met, partition = kernel_call(
        middle_kernel,
        (jax.ShapeDtypeStruct((half, cells), F32), density),
        ((2, orient, cells),),
        (core_word, kept_half, *partner_half, arrived1, own, partner, spread, matrix),
    )
    count = lax.axis_size("space")

    def received(value, distance, after):
        block = lax.ppermute(value, "space", [(i, i ^ distance) for i in range(count)])
        return lax.optimization_barrier((block, after))

    def gathered(value, distance, after):
        block, after = received(value, distance, after)
        return kernel_call(add_kernel, density, (), (value, block)), after

    partition, second_state = gathered(partition, 1, second_state)
    second_state, _ = lax.optimization_barrier((second_state, partition))
    third_state = kernel_call(
        third_step_kernel,
        wide(2),
        (slab.shape, wide(2).shape),
        (second_state, arrived1, crossed1, own, partner, outer, spread, matrix),
    )
    partition, third_state = gathered(partition, 4, third_state)
    third_state, _ = lax.optimization_barrier((third_state, partition))
    shared = kernel_call(
        pairing_kernel,
        density,
        (),
        (third_state, partner, spread, weights, partner_faces[0], partner_inner, partner_faces[1]),
    )
    arrived2, shared = lax.optimization_barrier((arrived[1], shared))
    distance = 8
    while distance < count:
        partition, shared = gathered(partition, distance, shared)
        distance *= 2
    beside, shared = received(partition, 2, shared)
    sent, kept = kernel_call(
        last_kernel,
        (density, density),
        ((2, orient, cells), (2, orient, cells)),
        (
            core_word, arrived2, weights, own_weights, *faces, *partner_faces, shared, met,
            own, partner, spread, matrix,
        ),
    )
    return kernel_call(
        functools.partial(divide_kernel, count // 2 * planes * cells),
        density,
        (),
        (kept, swap_species(sent), partition, beside),
    )


def solution(mesh):
    return jax.shard_map(
        shards,
        mesh=mesh,
        in_specs=(P(("runs", "space"), None), P(None, ("runs", "space"), None), P(), P(), P(), P()),
        out_specs=P(("runs", "space"), None),
        check_vma=False,
    )
```

```python
import functools

import jax
import jax.numpy as jnp
from jax import lax
from jax.experimental import pallas as pl
from jax.experimental.pallas import tpu as pltpu
from jax.sharding import PartitionSpec as P

NZ = 16
STEPS = 4
LANES = 128
ROWS = 16
UNROLL = 4

courant = 0.3
slope = 0.6

BF16 = jnp.bfloat16
F32 = jnp.float32


def swap_species(block):
    count = lax.axis_size("space")
    return lax.ppermute(block, "space", [(i ^ 1, i) for i in range(count)])


def exchange_faces(block):
    count = lax.axis_size("space")
    route = []
    for slab in range(count // 2):
        beside = ((slab + 1) ^ 1) - 1
        route += [(2 * slab, 2 * (slab ^ 1)), (2 * slab + 1, 2 * beside % count + 1)]
    return lax.ppermute(block, "space", route)


def rows_of(index):
    return pl.ds(pl.multiple_of(index * ROWS, ROWS), ROWS)


def each_row_block(orient):
    def run(body):
        def step(index, carry):
            body(index)
            return carry

        lax.fori_loop(0, orient // ROWS, step, 0, unroll=UNROLL)

    return run


def columns(tile):
    return slice(LANES * tile, LANES * (tile + 1))


def geometry(v_ref, rows, sign=1.0):
    lane = lax.broadcasted_iota(jnp.int32, (ROWS, LANES), 1)
    vx, vy, vz = (sign * v_ref[c, rows, :] for c in range(3))
    narrow = vx.astype(BF16)
    plus_x, narrow_plus, plus_y, plus_z = vx > 0, narrow > jnp.zeros_like(narrow), vy > 0, vz > 0
    rate_x, rate_y, rate_z = (courant * jnp.abs(t) for t in (vx, vy, vz))
    stay = 1.0 - (rate_x + rate_y + rate_z)
    z_from = (lane & (LANES - NZ)) | (jnp.where(plus_z, lane - 1, lane + 1) & (NZ - 1))
    y_from = jnp.where(plus_y, lane - NZ, lane + NZ) & (LANES - 1)
    y_edge = jnp.where(plus_y, lane, LANES - 1 - lane) < NZ
    return plus_x, narrow_plus, plus_y, stay, rate_x, rate_y, rate_z, z_from, y_from, y_edge


def pick(tile, index):
    return jnp.take_along_axis(tile, index, axis=1, mode="promise_in_bounds")


def load_plane(ref, plane, rows):
    return [ref[plane, rows, columns(t)] for t in range(ref.shape[2] // LANES)]


def drift(center, before, after, geo):
    plus_x, narrow_plus, plus_y, stay, rate_x, rate_y, rate_z, z_from, y_from, y_edge = geo
    tiles = len(center)
    center = [tile.astype(F32) for tile in center]
    turned = [pick(tile, y_from) for tile in center]
    moved = []
    for t in range(tiles):
        total = stay * center[t]
        if before is not None and after is not None:
            total = total + rate_x * jnp.where(narrow_plus, before[t], after[t]).astype(F32)
        elif before is not None:
            total = total + jnp.where(plus_x, rate_x, 0.0) * before[t].astype(F32)
        elif after is not None:
            total = total + jnp.where(plus_x, 0.0, rate_x) * after[t].astype(F32)
        over = jnp.where(plus_y, turned[t - 1], turned[(t + 1) % tiles])
        total = total + rate_y * jnp.where(y_edge, over, turned[t])
        total = total + rate_z * pick(center[t], z_from)
        moved.append(total)
    return moved


def store_plane(ref, plane, rows, tiles):
    for t, tile in enumerate(tiles):
        ref[plane, rows, columns(t)] = tile.astype(ref.dtype)


def mix(matrix, moved):
    return jnp.dot(matrix, moved, preferred_element_type=F32)


def boltzmann(field):
    return jnp.exp(-0.5 * field)


def prologue_kernel(
    core_ref, species_ref, directions_ref, start_ref, fields_ref, partner_ref, spread_ref, edge_ref, coded_ref, near
):
    sign = 1.0 - 2.0 * species_ref[0].astype(F32)
    toward = sign * (1.0 - 2.0 * core_ref[0].astype(F32))
    planes, orient, cells = start_ref.shape
    low = boltzmann(fields_ref[0:1])
    high = boltzmann(fields_ref[fields_ref.shape[0] - 1 :])
    for c in range(4):
        row = directions_ref[c % 3 : c % 3 + 1]
        column = jnp.broadcast_to(row, (LANES, orient)).T
        spread_ref[c] = (toward if c == 3 else sign) * column

    @each_row_block(orient)
    def _(index):
        rows = rows_of(index)
        plus_x = spread_ref[0, rows, :] > 0
        for t in range(cells // LANES):
            at = rows, columns(t)
            chosen = jnp.where(
                plus_x,
                high[:, columns(t)] * start_ref[planes - 1, *at].astype(F32),
                low[:, columns(t)] * start_ref[0, *at].astype(F32),
            )
            edge_ref[0, *at] = chosen.astype(BF16)

    near[...] = jnp.zeros_like(near)
    for s, ref in enumerate((fields_ref, partner_ref)):
        for depth in range(2):
            high_row, low_row = (ref[p : p + 1] for p in (planes - 1 - depth, depth))
            row = jnp.where(core_ref[0] == 1, high_row, low_row)
            coarse = row.astype(BF16).astype(F32)
            at = 2 * s + depth
            near[at : at + 1] = coarse
            near[at + 4 : at + 5] = row - coarse
    coded_ref[...] = near[...].astype(BF16)


def matrix_kernel(synthesis_ref, decay_ref, analysis_ref, out_ref, turned_ref):
    rest = synthesis_ref[...].astype(F32) * decay_ref[...]
    total = jnp.full(out_ref.shape, 1.0 / out_ref.shape[1], F32)
    for _ in range(3):
        part = rest.astype(BF16)
        rest = rest - part.astype(F32)
        total = total + jnp.dot(part, analysis_ref[...], preferred_element_type=F32)
    out_ref[...] = total.astype(BF16)
    turned_ref[...] = total.T.astype(BF16)


def add_kernel(one_ref, two_ref, out_ref):
    out_ref[...] = one_ref[...] + two_ref[...]


def join_kernel(sent_ref, one_ref, two_ref, out_ref):
    planes = sent_ref.shape[0]
    out_ref[:planes] = sent_ref[...]
    out_ref[planes:] = one_ref[...] + two_ref[...]


def divide_kernel(cells, kept_ref, mine_ref, arrived_ref, out_ref):
    planes = kept_ref.shape[0]
    total = mine_ref[planes:] + arrived_ref[planes:]
    out_ref[...] = (kept_ref[...] + arrived_ref[:planes]) * (cells / total)


def message_kernel(*refs):
    count = (len(refs) - 2) // 2
    v_ref, out_ref = refs[-2:]
    orient, cells = refs[0].shape[1:]

    @each_row_block(orient)
    def _(index):
        rows = rows_of(index)
        narrow = v_ref[3, rows, :].astype(BF16)
        leaves = narrow < jnp.zeros_like(narrow)
        for p in range(count):
            for t in range(cells // LANES):
                at = 0, rows, columns(t)
                out_ref[p, rows, columns(t)] = jnp.where(leaves, refs[p][at], refs[count + p][at])


def first_message_kernel(mine_ref, other_ref, coded_ref, v_ref, out_ref):
    message_kernel(mine_ref, other_ref, v_ref, out_ref)
    orient = mine_ref.shape[1]
    out_ref[0, orient:] = coded_ref[...]


def write_edge(edges_ref, step, faces, rows, v_ref):
    narrow = v_ref[0, rows, :].astype(BF16)
    plus_x = narrow > jnp.zeros_like(narrow)
    for t in range(len(faces[0])):
        edges_ref[step, rows, columns(t)] = jnp.where(plus_x, faces[-1][t], faces[0][t])


def alone_step(source_ref, moved, targets, v_ref, edges_ref, step):
    planes, orient, _ = source_ref.shape

    @each_row_block(orient)
    def _(index):
        rows = rows_of(index)
        geo = geometry(v_ref, rows)
        loaded = [load_plane(source_ref, p, rows) for p in range(planes)]
        if edges_ref is not None:
            write_edge(edges_ref, step, loaded, rows, v_ref)
        for p in targets:
            before = loaded[p - 1] if p > 0 else None
            after = loaded[p + 1] if p < planes - 1 else None
            store_plane(moved, p, rows, drift(loaded[p], before, after, geo))


def first_alone_kernel(start_ref, first_ref, v_ref, m_ref, out_ref, inner_ref, edges_ref, held, moved):
    planes, orient, _ = start_ref.shape
    first = boltzmann(first_ref[...])
    for p in range(planes):
        held[p] = (first[p : p + 1] * start_ref[p].astype(F32)).astype(BF16)
    alone_step(held, moved, range(planes), v_ref, None, 0)
    for p in (0, planes - 1, *range(1, planes - 1)):
        state = (first[p : p + 1] * first[p : p + 1] * mix(m_ref[...], moved[p])).astype(BF16)
        out_ref[p] = state
        if 0 < p < planes - 1:
            inner_ref[p - 1] = state

    @each_row_block(orient)
    def _(index):
        rows = rows_of(index)
        write_edge(edges_ref, 0, [load_plane(out_ref, p, rows) for p in (0, planes - 1)], rows, v_ref)


def next_alone_kernel(state_ref, first_ref, second_ref, v_ref, m_ref, edges2_ref, edges3_ref, held, moved):
    planes, orient, _ = state_ref.shape
    first = boltzmann(first_ref[...])
    second = boltzmann(second_ref[...])
    alone_step(state_ref, moved, range(planes), v_ref, None, 0)
    for p in range(planes):
        held[p] = (first[p : p + 1] * second[p : p + 1] * mix(m_ref[...], moved[p])).astype(BF16)
    alone_step(held, moved, (0, planes - 1), v_ref, edges2_ref, 0)
    for p in (0, planes - 1):
        held[p] = (second[p : p + 1] * second[p : p + 1] * mix(m_ref[...], moved[p])).astype(BF16)

    @each_row_block(orient)
    def _(index):
        rows = rows_of(index)
        write_edge(edges3_ref, 0, [load_plane(held, p, rows) for p in (0, planes - 1)], rows, v_ref)


def face_parts(v_ref, rows):
    vx = v_ref[0, rows, :]
    rate = courant * jnp.abs(vx)
    return v_ref[3, rows, :] > 0, jnp.where(vx > 0, rate, 0.0), jnp.where(vx > 0, 0.0, rate)


def face_drifts(v_ref, mine_ref, other_ref, moved, slots):
    @each_row_block(v_ref.shape[1])
    def _(index):
        rows = rows_of(index)
        ahead, rate_plus, rate_minus = face_parts(v_ref, rows)
        for t in range(mine_ref.shape[2] // LANES):
            mine = mine_ref[0, rows, columns(t)].astype(F32)
            other = other_ref[0, rows, columns(t)].astype(F32)
            face = jnp.where(ahead, mine, other)
            moved[slots[0], rows, columns(t)] = (rate_plus * face).astype(BF16)
            moved[slots[1], rows, columns(t)] = (rate_minus * face).astype(BF16)


def second_step_kernel(
    core_ref, alone_ref, edge_ref, mine_ref, other_ref, first_ref, second_ref, v_ref, m_ref,
    face_low_ref, face_high_ref, next_ref, sent_near_ref, sent_far_ref, kept_ref, outer_ref, held, moved,
):
    planes, orient, _ = alone_ref.shape
    matrix = m_ref[...]
    first, second = boltzmann(first_ref[...]), boltzmann(second_ref[...])
    core = core_ref[0]
    mine, other = (block[:4] + block[4:8] for block in (ref[0, orient:].astype(F32) for ref in (mine_ref, other_ref)))
    other = (other[2:4], other[0:2])
    mine = (mine[0:2], mine[2:4])
    low = [jnp.where(core == 0, mine[k], other[k]) for k in range(2)]
    high = [jnp.where(core == 0, other[k], mine[k]) for k in range(2)]
    beyond = [boltzmann(block[k : k + 1]) for block in (low[0], high[0], low[1], high[1]) for k in range(2)]
    face_drifts(v_ref, mine_ref, other_ref, moved, (0, 1))

    @each_row_block(orient)
    def _(index):
        rows = rows_of(index)
        _, rate_plus, rate_minus = face_parts(v_ref, rows)
        for t in range(edge_ref.shape[2] // LANES):
            edge = edge_ref[0, rows, columns(t)].astype(F32)
            moved[2, rows, columns(t)] = (rate_minus * edge).astype(BF16)
            moved[3, rows, columns(t)] = (rate_plus * edge).astype(BF16)

    squared = first * first
    for p in range(planes):
        kept = alone_ref[p]
        if p in (0, planes - 1):
            arrived = squared[p : p + 1] * mix(matrix, moved[min(p, 1)])
            kept = (kept.astype(F32) + arrived).astype(BF16)
            (face_high_ref if p else face_low_ref)[0] = kept
        held[p + 1] = kept
    held[0] = (beyond[0] * beyond[0] * mix(matrix, moved[2])).astype(BF16)
    held[planes + 1] = (beyond[2] * beyond[2] * mix(matrix, moved[3])).astype(BF16)
    count = planes + 2

    @each_row_block(orient)
    def _(index):
        rows = rows_of(index)
        geo = geometry(v_ref, rows)
        _, rate_plus, rate_minus = face_parts(v_ref, rows)
        loaded = [load_plane(held, p, rows) for p in range(count)]
        for p in range(count):
            before = loaded[p - 1] if p > 0 else None
            after = loaded[p + 1] if p < count - 1 else None
            store_plane(moved, p + 1, rows, drift(loaded[p], before, after, geo))
        store_plane(moved, 0, rows, [rate_minus * tile.astype(F32) for tile in loaded[0]])
        store_plane(moved, count + 1, rows, [rate_plus * tile.astype(F32) for tile in loaded[-1]])

    cross = first * second
    factors = [beyond[1] * beyond[5], beyond[0] * beyond[4]]
    factors += [cross[p : p + 1] for p in range(planes)]
    factors += [beyond[2] * beyond[6], beyond[3] * beyond[7]]
    for p, factor in enumerate(factors):
        next_ref[p] = (factor * mix(matrix, moved[p])).astype(BF16)
    for p in range(planes // 2):
        sent_ref = (sent_near_ref, sent_far_ref)[p]
        sent_ref[0] = next_ref[2 + (planes - 1) * (1 - core) + (2 * core - 1) * p]
        kept_ref[p] = next_ref[2 + (planes - 1) * core + (1 - 2 * core) * p]
    outer_ref[0:1] = beyond[4] * beyond[4]
    outer_ref[1:2] = beyond[6] * beyond[6]


def middle_kernel(
    core_ref, own_ref, near_ref, far_ref, message_ref, first_ref, second_ref, v_ref, m_ref, out_ref, total_ref, moved
):
    _, orient, cells = own_ref.shape
    planes = first_ref.shape[0]

    def cross_of(depth):
        low, high = (
            boltzmann(first_ref[p : p + 1]) * boltzmann(second_ref[p : p + 1]) for p in (depth, planes - 1 - depth)
        )
        return jnp.where(core_ref[0] == 0, low, high)

    cross = [cross_of(depth) for depth in range(2)]

    @each_row_block(orient)
    def _(index):
        rows = rows_of(index)
        ahead, rate_plus, rate_minus = face_parts(v_ref, rows)
        rate = rate_plus + rate_minus
        for t in range(cells // LANES):
            gained = rate * message_ref[0, rows, columns(t)].astype(F32)
            moved[0, rows, columns(t)] = jnp.where(ahead, gained, 0.0).astype(BF16)
            moved[1, rows, columns(t)] = jnp.where(ahead, 0.0, gained).astype(BF16)

    own_face = own_ref[0].astype(F32) + cross[0] * mix(m_ref[...], moved[0])
    partner_face = near_ref[0].astype(F32) + cross[0] * mix(m_ref[...], moved[1])
    face = jnp.sum(own_face * partner_face, axis=0, keepdims=True)
    total = jnp.zeros((1, 1), F32)
    for p in range(own_ref.shape[0]):
        if p > 0:
            face = jnp.sum(own_ref[p].astype(F32) * far_ref[0].astype(F32), axis=0, keepdims=True)
        met = face / (orient * cross[p])
        out_ref[p : p + 1] = met
        total = total + jnp.sum(met, axis=1, keepdims=True)
    total_ref[...] = jnp.broadcast_to(total, total_ref.shape)


def third_step_kernel(
    held_ref, mine_ref, other_ref, first_ref, second_ref, outer_ref, v_ref, m_ref, next_ref, held, moved
):
    planes, orient, _ = held.shape
    matrix = m_ref[...]
    first, second = boltzmann(first_ref[...]), boltzmann(second_ref[...])
    face_drifts(v_ref, mine_ref, other_ref, moved, (0, 1))
    cross = first * second
    for p in range(planes):
        kept = held_ref[p + 2]
        if p in (0, planes - 1):
            arrived = cross[p : p + 1] * mix(matrix, moved[min(p, 1)])
            kept = (kept.astype(F32) + arrived).astype(BF16)
        held[p] = kept

    @each_row_block(orient)
    def _(index):
        rows = rows_of(index)
        geo = geometry(v_ref, rows)
        loaded = [load_plane(held_ref, p, rows) for p in (0, 1)]
        loaded += [load_plane(held, p, rows) for p in range(planes)]
        loaded += [load_plane(held_ref, p, rows) for p in (planes + 2, planes + 3)]
        for p in range(planes + 2):
            store_plane(moved, p, rows, drift(loaded[p + 1], loaded[p], loaded[p + 2], geo))

    squared = second * second
    factors = [outer_ref[0:1]] + [squared[p : p + 1] for p in range(planes)] + [outer_ref[1:2]]
    for p, factor in enumerate(factors):
        next_ref[p] = (factor * mix(matrix, moved[p])).astype(BF16)


def weight_kernel(core_ref, partner_ref, start_ref, turned_ref, weight_ref, own_ref):
    planes = partner_ref.shape[0]
    core = core_ref[0]
    for p in range(planes):
        weight_ref[p] = mix(turned_ref[...], partner_ref[p]).astype(BF16)
    for p in range(2):
        own_ref[p] = mix(turned_ref[...], start_ref[core * (planes - 1) + p - 2 * p * core]).astype(BF16)


def fold(value):
    return jnp.sum(value.reshape(ROWS // 8, 8, LANES), axis=0)


def pairing_kernel(held_ref, second_ref, v_ref, weight_ref, low_ref, inner_ref, high_ref, out_ref):
    planes, orient, cells = weight_ref.shape
    second = boltzmann(second_ref[...])
    tiles = cells // LANES

    def body(index, sums):
        rows = rows_of(index)
        geo = geometry(v_ref, rows)
        loaded = [load_plane(held_ref, p, rows) for p in range(planes + 2)]
        new = []
        for p in range(planes):
            moved_tiles = drift(loaded[p + 1], loaded[p], loaded[p + 2], geo)
            weights = load_plane(weight_ref, p, rows)
            partner_refs = [(low_ref, 0)] + [(inner_ref, k) for k in range(planes - 2)] + [(high_ref, 0)]
            partner = load_plane(*partner_refs[p], rows)
            for t in range(tiles):
                last, third = sums[2 * (p * tiles + t)], sums[2 * (p * tiles + t) + 1]
                new.append(last + fold(moved_tiles[t] * weights[t].astype(F32)))
                new.append(third + fold(loaded[p + 1][t].astype(F32) * partner[t].astype(F32)))
        return tuple(new)

    zero = jnp.zeros((8, LANES), F32)
    sums = lax.fori_loop(0, orient // ROWS, body, (zero,) * (2 * planes * tiles), unroll=UNROLL)
    for p in range(planes):
        for t in range(tiles):
            last = jnp.sum(sums[2 * (p * tiles + t)], axis=0, keepdims=True)
            third = jnp.sum(sums[2 * (p * tiles + t) + 1], axis=0, keepdims=True)
            factor = second[p : p + 1, columns(t)]
            out_ref[p : p + 1, columns(t)] = (0.5 * factor * last + third / (factor * factor)) / orient


def last_kernel(
    core_ref, message_ref, weight_ref, own_weight_ref, own_low_ref, own_high_ref, partner_low_ref, partner_high_ref,
    shared_ref, met_ref,    own_ref, partner_ref, v_ref, m_ref, sent_ref, kept_ref, moved, gained,
):
    planes, cells = shared_ref.shape
    orient = m_ref.shape[0]
    tiles = cells // LANES
    core = core_ref[0]
    half = planes // 2
    face = core * (planes - 1)
    inner = face + 1 - 2 * core

    def at_face(ref, depth):
        return jnp.where(core == 0, boltzmann(ref[depth : depth + 1]), boltzmann(ref[planes - 1 - depth : planes - depth]))

    factors = [[at_face(ref, depth) for depth in range(2)] for ref in (partner_ref, own_ref)]

    @each_row_block(orient)
    def _(index):
        rows = rows_of(index)
        ahead, rate_plus, rate_minus = face_parts(v_ref, rows)
        rate = rate_plus + rate_minus
        for t in range(tiles):
            got = rate * message_ref[0, rows, columns(t)].astype(F32)
            moved[0, rows, columns(t)] = jnp.where(ahead, got, 0.0).astype(BF16)
            moved[1, rows, columns(t)] = jnp.where(ahead, 0.0, got).astype(BF16)

    for s in range(2):
        gained[s] = (factors[s][0] * factors[s][0] * mix(m_ref[...], moved[s])).astype(BF16)

    def body(index, sums):
        rows = rows_of(index)
        ahead, rate_plus, rate_minus = face_parts(v_ref, rows)
        rate = rate_plus + rate_minus
        sides = (jnp.where(ahead, rate, 0.0), jnp.where(ahead, 0.0, rate))
        message = load_plane(message_ref, 1, rows)
        new = []
        for s in range(2):
            change = load_plane(gained, s, rows)
            moved_tiles = drift(change, None, None, geometry(v_ref, rows, 1.0 - 2.0 * s))
            if s == 0:
                weights = [load_plane(weight_ref, p, rows) for p in (face, inner)]
            else:
                weights = [load_plane(own_weight_ref, p, rows) for p in (0, 1)]
            pair = ((partner_low_ref, partner_high_ref), (own_low_ref, own_high_ref))[s]
            third = [jnp.where(core == 0, low, high) for low, high in zip(*(load_plane(ref, 0, rows) for ref in pair))]
            for t in range(tiles):
                on_face = moved_tiles[t] + sides[s] * message[t].astype(F32)
                wide = change[t].astype(F32)
                terms = (
                    on_face * weights[0][t].astype(F32),
                    sides[s] * wide * weights[1][t].astype(F32),
                    wide * third[t].astype(F32),
                )
                base = 3 * (s * tiles + t)
                new += [sums[base + k] + fold(term) for k, term in enumerate(terms)]
        return tuple(new)

    zero = jnp.zeros((8, LANES), F32)
    sums = lax.fori_loop(0, orient // ROWS, body, (zero,) * (6 * tiles), unroll=UNROLL)
    for t in range(tiles):
        shares = []
        for s in range(2):
            base = 3 * (s * tiles + t)
            last, onward, third = (jnp.sum(sums[base + k], axis=0, keepdims=True) / orient for k in range(3))
            near, far = (factors[s][depth][:, columns(t)] for depth in range(2))
            shares.append((0.5 * near * last + third / (near * near), 0.5 * far * onward))
        for p in range(planes):
            at = slice(p, p + 1), columns(t)
            mine = core == (0 if p < half else 1)
            depth = min(p, planes - 1 - p)
            met = jnp.where(mine, 0.5 * met_ref[depth : depth + 1, columns(t)], 0.0)
            sent, kept = shared_ref[at] + met, met
            if depth < 2:
                sent = sent + jnp.where(mine, shares[0][depth], 0.0)
                kept = kept + jnp.where(mine, shares[1][depth], 0.0)
            sent_ref[at] = sent
            kept_ref[at] = kept


def split_outputs(outs):
    low, high, state, near, far, kept, outer = outs
    return (low, high), state, (near, far), kept, outer


def kernel_call(kernel, outs, scratch, args):
    vmem = pl.BlockSpec(memory_space=pltpu.VMEM)
    smem = pl.BlockSpec(memory_space=pltpu.SMEM)
    return pl.pallas_call(
        kernel,
        out_shape=outs,
        in_specs=[smem if arg.dtype == jnp.int32 else vmem for arg in args],
        out_specs=jax.tree.map(lambda _: vmem, outs),
        scratch_shapes=[pltpu.VMEM(*s) if len(s) == 2 else pltpu.VMEM(s, BF16) for s in scratch],
        compiler_params=pltpu.CompilerParams(vmem_limit_bytes=7 << 20),
        cost_estimate=pl.CostEstimate(flops=0, bytes_accessed=0, transcendentals=0),
    )(*args)


def shards(fields, end_weights, directions, analysis, synthesis, decay_rates):
    device = lax.axis_index("space")
    core = device % 2
    planes, cells = fields.shape
    orient = end_weights.shape[0]
    plane_index = device // 2 * planes + lax.broadcasted_iota(jnp.int32, (planes, 1), 0)
    ramp = slope * plane_index.astype(F32) / (planes * lax.axis_size("space") // 2)
    own = fields + ramp
    partner = swap_species(fields) + ramp

    wide = lambda extra: jax.ShapeDtypeStruct((planes + extra, orient, cells), BF16)
    slab, plane = wide(0), wide(1 - planes)
    face = core ^ (1 - device // 2 % 2)
    core_word = jnp.reshape(face, (1,)).astype(jnp.int32)
    species_word = jnp.reshape(core, (1,)).astype(jnp.int32)
    start = jnp.transpose(end_weights, (1, 0, 2))
    spread, edge0, coded = kernel_call(
        prologue_kernel,
        (jax.ShapeDtypeStruct((4, orient, LANES), F32), plane, jax.ShapeDtypeStruct((16, cells), BF16)),
        (((16, cells), F32),),
        (core_word, species_word, directions, start, own, partner),
    )
    matrix, turned = kernel_call(
        matrix_kernel,
        (jax.ShapeDtypeStruct((orient, orient), BF16),) * 2,
        (),
        (synthesis, decay_rates[None], analysis),
    )
    other0, matrix = lax.optimization_barrier((swap_species(edge0), matrix))
    message0 = kernel_call(
        first_message_kernel,
        jax.ShapeDtypeStruct((1, orient + 16, cells), BF16),
        (),
        (edge0, other0, coded, spread),
    )

    def message(blocks, others):
        shape = jax.ShapeDtypeStruct((len(blocks),) + blocks[0].shape[1:], BF16)
        return kernel_call(message_kernel, shape, (), (*blocks, *others, spread))

    start, _ = lax.optimization_barrier((start, message0))
    arrived0 = exchange_faces(message0)
    alone, inner, edges1 = kernel_call(
        first_alone_kernel, (slab, wide(-2), plane), (slab.shape, slab.shape), (start, own, spread, matrix)
    )
    weights, own_weights = kernel_call(
        weight_kernel, (slab, wide(2 - planes)), (), (core_word, swap_species(start), start, turned)
    )
    others1, weights = lax.optimization_barrier((swap_species(edges1), weights))
    message1 = message([edges1], [others1])
    state, *_ = lax.optimization_barrier((alone, message1, weights))
    edges2, edges3 = kernel_call(
        next_alone_kernel, (plane, plane), (slab.shape, slab.shape), (state, own, partner, spread, matrix)
    )
    edges2, edges3, arrived0 = lax.optimization_barrier((edges2, edges3, arrived0))
    message2 = message([edges2, edges3], [swap_species(edges2), swap_species(edges3)])
    arrived = [exchange_faces(message1), exchange_faces(message2)]
    crossed0 = swap_species(arrived0)
    inner, _ = lax.optimization_barrier((inner, arrived0))
    partner_inner = swap_species(inner)

    alone, *_ = lax.optimization_barrier((alone, message1, message2))
    half = planes // 2
    faces, second_state, sent_half, kept_half, outer = split_outputs(
        kernel_call(
            second_step_kernel,
            (plane, plane, wide(4), plane, plane, wide(half - planes), jax.ShapeDtypeStruct((2, cells), F32)),
            (wide(2).shape, wide(4).shape),
            (core_word, alone, edge0, arrived0, crossed0, own, partner, spread, matrix),
        )
    )
    arrived1, second_state, partner_inner = lax.optimization_barrier((arrived[0], second_state, partner_inner))
    *moving, _ = lax.optimization_barrier((*sent_half, arrived1))
    *partner_half, crossed1 = lax.optimization_barrier((*map(swap_species, moving), swap_species(arrived1)))
    density = jax.ShapeDtypeStruct((planes, cells), F32)
    met, partition = kernel_call(
        middle_kernel,
        (jax.ShapeDtypeStruct((half, cells), F32), density),
        ((2, orient, cells),),
        (core_word, kept_half, *partner_half, arrived1, own, partner, spread, matrix),
    )
    count = lax.axis_size("space")

    def received(value, distance, after):
        block = lax.ppermute(value, "space", [(i, i ^ distance) for i in range(count)])
        return lax.optimization_barrier((block, after))

    def gathered(value, distance, after):
        block, after = received(value, distance, after)
        return kernel_call(add_kernel, density, (), (value, block)), after

    *faces, second_state, _ = lax.optimization_barrier((*faces, second_state, met))
    partner_faces = [swap_species(block) for block in faces]
    third_state = kernel_call(
        third_step_kernel,
        wide(2),
        (slab.shape, wide(2).shape),
        (second_state, arrived1, crossed1, own, partner, outer, spread, matrix),
    )
    partition, third_state = gathered(partition, 4, third_state)
    third_state, _ = lax.optimization_barrier((third_state, partition))
    shared = kernel_call(
        pairing_kernel,
        density,
        (),
        (third_state, partner, spread, weights, partner_faces[0], partner_inner, partner_faces[1]),
    )
    distance = 8
    while distance < count:
        partition, shared = gathered(partition, distance, shared)
        distance *= 2
    arrived2, shared, _ = lax.optimization_barrier((arrived[1], shared, partition))
    sent, kept = kernel_call(
        last_kernel,
        (density, density),
        ((2, orient, cells), (2, orient, cells)),
        (
            core_word, arrived2, weights, own_weights, *faces, *partner_faces, shared, met,
            own, partner, spread, matrix,
        ),
    )
    beside, sent = received(partition, 2, sent)
    joined = kernel_call(
        join_kernel, jax.ShapeDtypeStruct((2 * planes, cells), F32), (), (sent, partition, beside)
    )
    return kernel_call(
        functools.partial(divide_kernel, count // 2 * planes * cells),
        density,
        (),
        (kept, joined, swap_species(joined)),
    )


def solution(mesh):
    return jax.shard_map(
        shards,
        mesh=mesh,
        in_specs=(P(("runs", "space"), None), P(None, ("runs", "space"), None), P(), P(), P(), P()),
        out_specs=P(("runs", "space"), None),
        check_vma=False,
    )
```

```python
import functools

import jax
import jax.numpy as jnp
from jax import lax
from jax.experimental import pallas as pl
from jax.experimental.pallas import tpu as pltpu
from jax.sharding import PartitionSpec as P

NZ = 16
STEPS = 4
LANES = 128
ROWS = 16
UNROLL = 4
PAD = 2

courant = 0.3
slope = 0.6

BF16 = jnp.bfloat16
F32 = jnp.float32


def swap_species(block):
    count = lax.axis_size("space")
    return lax.ppermute(block, "space", [(i ^ 1, i) for i in range(count)])


def exchange_faces(block):
    count = lax.axis_size("space")
    route = []
    for slab in range(count // 2):
        beside = ((slab + 1) ^ 1) - 1
        route += [(2 * slab, 2 * (slab ^ 1)), (2 * slab + 1, 2 * beside % count + 1)]
    return lax.ppermute(block, "space", route)


def rows_of(index):
    return pl.ds(pl.multiple_of(index * ROWS, ROWS), ROWS)


def each_row_block(orient):
    def run(body):
        def step(index, carry):
            body(index)
            return carry

        lax.fori_loop(0, orient // ROWS, step, 0, unroll=UNROLL)

    return run


def columns(tile):
    return slice(LANES * tile, LANES * (tile + 1))


def geometry(v_ref, rows, sign=1.0):
    lane = lax.broadcasted_iota(jnp.int32, (ROWS, LANES), 1)
    vx, vy, vz = (sign * v_ref[c, rows, :] for c in range(3))
    narrow = vx.astype(BF16)
    plus_x, narrow_plus, plus_y, plus_z = vx > 0, narrow > jnp.zeros_like(narrow), vy > 0, vz > 0
    rate_x, rate_y, rate_z = (courant * jnp.abs(t) for t in (vx, vy, vz))
    stay = 1.0 - (rate_x + rate_y + rate_z)
    z_from = (lane & (LANES - NZ)) | (jnp.where(plus_z, lane - 1, lane + 1) & (NZ - 1))
    y_from = jnp.where(plus_y, lane - NZ, lane + NZ) & (LANES - 1)
    y_edge = jnp.where(plus_y, lane, LANES - 1 - lane) < NZ
    return plus_x, narrow_plus, plus_y, stay, rate_x, rate_y, rate_z, z_from, y_from, y_edge


def pick(tile, index):
    return jnp.take_along_axis(tile, index, axis=1, mode="promise_in_bounds")


def load_plane(ref, plane, rows):
    return [ref[plane, rows, columns(t)] for t in range(ref.shape[2] // LANES)]


def drift(center, before, after, geo):
    plus_x, narrow_plus, plus_y, stay, rate_x, rate_y, rate_z, z_from, y_from, y_edge = geo
    tiles = len(center)
    center = [tile.astype(F32) for tile in center]
    turned = [pick(tile, y_from) for tile in center]
    moved = []
    for t in range(tiles):
        total = stay * center[t]
        if before is not None and after is not None:
            total = total + rate_x * jnp.where(narrow_plus, before[t], after[t]).astype(F32)
        elif before is not None:
            total = total + jnp.where(plus_x, rate_x, 0.0) * before[t].astype(F32)
        elif after is not None:
            total = total + jnp.where(plus_x, 0.0, rate_x) * after[t].astype(F32)
        over = jnp.where(plus_y, turned[t - 1], turned[(t + 1) % tiles])
        total = total + rate_y * jnp.where(y_edge, over, turned[t])
        total = total + rate_z * pick(center[t], z_from)
        moved.append(total)
    return moved


def store_plane(ref, plane, rows, tiles):
    for t, tile in enumerate(tiles):
        ref[plane, rows, columns(t)] = tile.astype(ref.dtype)


def mix(matrix, moved):
    return jnp.dot(matrix, moved, preferred_element_type=F32)


def boltzmann(field):
    return jnp.exp(-0.5 * field)


def prologue_kernel(
    core_ref, species_ref, directions_ref, start_ref, fields_ref, partner_ref, spread_ref, edge_ref, coded_ref, near
):
    sign = 1.0 - 2.0 * species_ref[0].astype(F32)
    toward = sign * (1.0 - 2.0 * core_ref[0].astype(F32))
    planes, orient, cells = start_ref.shape
    low = boltzmann(fields_ref[0:1])
    high = boltzmann(fields_ref[fields_ref.shape[0] - 1 :])
    for c in range(4):
        row = directions_ref[c % 3 : c % 3 + 1]
        column = jnp.broadcast_to(row, (LANES, orient)).T
        spread_ref[c] = (toward if c == 3 else sign) * column

    @each_row_block(orient)
    def _(index):
        rows = rows_of(index)
        plus_x = spread_ref[0, rows, :] > 0
        for t in range(cells // LANES):
            at = rows, columns(t)
            chosen = jnp.where(
                plus_x,
                high[:, columns(t)] * start_ref[planes - 1, *at].astype(F32),
                low[:, columns(t)] * start_ref[0, *at].astype(F32),
            )
            edge_ref[0, *at] = chosen.astype(BF16)

    near[...] = jnp.zeros_like(near)
    for s, ref in enumerate((fields_ref, partner_ref)):
        for depth in range(2):
            high_row, low_row = (ref[p : p + 1] for p in (planes - 1 - depth, depth))
            row = jnp.where(core_ref[0] == 1, high_row, low_row)
            coarse = row.astype(BF16).astype(F32)
            at = 2 * s + depth
            near[at : at + 1] = coarse
            near[at + 4 : at + 5] = row - coarse
    coded_ref[...] = near[...].astype(BF16)


def matrix_kernel(synthesis_ref, decay_ref, analysis_ref, out_ref, turned_ref):
    rest = synthesis_ref[...].astype(F32) * decay_ref[...]
    total = jnp.full(out_ref.shape, 1.0 / out_ref.shape[1], F32)
    for _ in range(3):
        part = rest.astype(BF16)
        rest = rest - part.astype(F32)
        total = total + jnp.dot(part, analysis_ref[...], preferred_element_type=F32)
    out_ref[...] = total.astype(BF16)
    turned_ref[...] = total.T.astype(BF16)


def add_kernel(one_ref, two_ref, out_ref):
    out_ref[...] = one_ref[...] + two_ref[...]


def join_kernel(sent_ref, one_ref, two_ref, out_ref):
    planes = sent_ref.shape[0]
    out_ref[:planes] = sent_ref[...]
    out_ref[planes:] = one_ref[...] + two_ref[...]


def divide_kernel(cells, kept_ref, mine_ref, arrived_ref, out_ref):
    planes = kept_ref.shape[0]
    total = mine_ref[planes:] + arrived_ref[planes:]
    out_ref[...] = (kept_ref[...] + arrived_ref[:planes]) * (cells / total)


def message_kernel(*refs):
    count = (len(refs) - 2) // 2
    v_ref, out_ref = refs[-2:]
    orient, cells = refs[0].shape[1:]

    @each_row_block(orient)
    def _(index):
        rows = rows_of(index)
        narrow = v_ref[3, rows, :].astype(BF16)
        leaves = narrow < jnp.zeros_like(narrow)
        for p in range(count):
            for t in range(cells // LANES):
                at = 0, rows, columns(t)
                out_ref[p, rows, columns(t)] = jnp.where(leaves, refs[p][at], refs[count + p][at])


def first_message_kernel(mine_ref, other_ref, *refs):
    *coded_refs, v_ref, out_ref = refs
    message_kernel(mine_ref, other_ref, v_ref, out_ref)
    orient = mine_ref.shape[1]
    for k, ref in enumerate(coded_refs):
        out_ref[0, orient + 16 * k : orient + 16 * (k + 1)] = ref[...]


def write_edge(edges_ref, step, faces, rows, v_ref):
    narrow = v_ref[0, rows, :].astype(BF16)
    plus_x = narrow > jnp.zeros_like(narrow)
    for t in range(len(faces[0])):
        edges_ref[step, rows, columns(t)] = jnp.where(plus_x, faces[-1][t], faces[0][t])


def alone_step(source_ref, moved, targets, v_ref, edges_ref, step):
    planes, orient, _ = source_ref.shape

    @each_row_block(orient)
    def _(index):
        rows = rows_of(index)
        geo = geometry(v_ref, rows)
        loaded = [load_plane(source_ref, p, rows) for p in range(planes)]
        if edges_ref is not None:
            write_edge(edges_ref, step, loaded, rows, v_ref)
        for p in targets:
            before = loaded[p - 1] if p > 0 else None
            after = loaded[p + 1] if p < planes - 1 else None
            store_plane(moved, p, rows, drift(loaded[p], before, after, geo))


def first_alone_kernel(start_ref, first_ref, v_ref, m_ref, out_ref, edges_ref, *refs):
    *inner_refs, held, moved = refs
    planes, orient, _ = start_ref.shape
    first = boltzmann(first_ref[...])
    for p in range(planes):
        held[p] = (first[p : p + 1] * start_ref[p].astype(F32)).astype(BF16)
    alone_step(held, moved, range(planes), v_ref, None, 0)
    for p in (0, planes - 1, *range(1, planes - 1)):
        state = (first[p : p + 1] * first[p : p + 1] * mix(m_ref[...], moved[p])).astype(BF16)
        out_ref[p] = state
        if 0 < p < planes - 1:
            inner_refs[p - 1][0] = state

    @each_row_block(orient)
    def _(index):
        rows = rows_of(index)
        write_edge(edges_ref, 0, [load_plane(out_ref, p, rows) for p in (0, planes - 1)], rows, v_ref)


def next_alone_kernel(state_ref, first_ref, second_ref, v_ref, m_ref, edges2_ref, edges3_ref, held, moved):
    planes, orient, _ = state_ref.shape
    first = boltzmann(first_ref[...])
    second = boltzmann(second_ref[...])
    alone_step(state_ref, moved, range(planes), v_ref, None, 0)
    for p in range(planes):
        held[p] = (first[p : p + 1] * second[p : p + 1] * mix(m_ref[...], moved[p])).astype(BF16)
    alone_step(held, moved, (0, planes - 1), v_ref, edges2_ref, 0)
    for p in (0, planes - 1):
        held[p] = (second[p : p + 1] * second[p : p + 1] * mix(m_ref[...], moved[p])).astype(BF16)

    @each_row_block(orient)
    def _(index):
        rows = rows_of(index)
        write_edge(edges3_ref, 0, [load_plane(held, p, rows) for p in (0, planes - 1)], rows, v_ref)


def face_parts(v_ref, rows):
    vx = v_ref[0, rows, :]
    rate = courant * jnp.abs(vx)
    return v_ref[3, rows, :] > 0, jnp.where(vx > 0, rate, 0.0), jnp.where(vx > 0, 0.0, rate)


def face_drifts(v_ref, mine_ref, other_ref, moved, slots):
    @each_row_block(v_ref.shape[1])
    def _(index):
        rows = rows_of(index)
        ahead, rate_plus, rate_minus = face_parts(v_ref, rows)
        for t in range(mine_ref.shape[2] // LANES):
            mine = mine_ref[0, rows, columns(t)].astype(F32)
            other = other_ref[0, rows, columns(t)].astype(F32)
            face = jnp.where(ahead, mine, other)
            moved[slots[0], rows, columns(t)] = (rate_plus * face).astype(BF16)
            moved[slots[1], rows, columns(t)] = (rate_minus * face).astype(BF16)


def second_step_kernel(
    core_ref, alone_ref, edge_ref, mine_ref, other_ref, first_ref, second_ref, v_ref, m_ref,
    face_low_ref, face_high_ref, next_ref, sent_near_ref, sent_far_ref, kept_ref, outer_ref, held, moved,
):
    planes, orient, _ = alone_ref.shape
    matrix = m_ref[...]
    first, second = boltzmann(first_ref[...]), boltzmann(second_ref[...])
    core = core_ref[0]
    mine, other = (block[:4] + block[4:8] for block in (ref[0, orient:].astype(F32) for ref in (mine_ref, other_ref)))
    other = (other[2:4], other[0:2])
    mine = (mine[0:2], mine[2:4])
    low = [jnp.where(core == 0, mine[k], other[k]) for k in range(2)]
    high = [jnp.where(core == 0, other[k], mine[k]) for k in range(2)]
    beyond = [boltzmann(block[k : k + 1]) for block in (low[0], high[0], low[1], high[1]) for k in range(2)]
    face_drifts(v_ref, mine_ref, other_ref, moved, (0, 1))

    @each_row_block(orient)
    def _(index):
        rows = rows_of(index)
        _, rate_plus, rate_minus = face_parts(v_ref, rows)
        for t in range(edge_ref.shape[2] // LANES):
            edge = edge_ref[0, rows, columns(t)].astype(F32)
            moved[2, rows, columns(t)] = (rate_minus * edge).astype(BF16)
            moved[3, rows, columns(t)] = (rate_plus * edge).astype(BF16)

    squared = first * first
    for p in range(planes):
        kept = alone_ref[p]
        if p in (0, planes - 1):
            arrived = squared[p : p + 1] * mix(matrix, moved[min(p, 1)])
            kept = (kept.astype(F32) + arrived).astype(BF16)
            (face_high_ref if p else face_low_ref)[0] = kept
        held[p + 1] = kept
    held[0] = (beyond[0] * beyond[0] * mix(matrix, moved[2])).astype(BF16)
    held[planes + 1] = (beyond[2] * beyond[2] * mix(matrix, moved[3])).astype(BF16)
    count = planes + 2

    @each_row_block(orient)
    def _(index):
        rows = rows_of(index)
        geo = geometry(v_ref, rows)
        _, rate_plus, rate_minus = face_parts(v_ref, rows)
        loaded = [load_plane(held, p, rows) for p in range(count)]
        for p in range(count):
            before = loaded[p - 1] if p > 0 else None
            after = loaded[p + 1] if p < count - 1 else None
            store_plane(moved, p + 1, rows, drift(loaded[p], before, after, geo))
        store_plane(moved, 0, rows, [rate_minus * tile.astype(F32) for tile in loaded[0]])
        store_plane(moved, count + 1, rows, [rate_plus * tile.astype(F32) for tile in loaded[-1]])

    cross = first * second
    factors = [beyond[1] * beyond[5], beyond[0] * beyond[4]]
    factors += [cross[p : p + 1] for p in range(planes)]
    factors += [beyond[2] * beyond[6], beyond[3] * beyond[7]]
    for p, factor in enumerate(factors):
        next_ref[p] = (factor * mix(matrix, moved[p])).astype(BF16)
    for p in range(planes // 2):
        sent_ref = (sent_near_ref, sent_far_ref)[p]
        sent_ref[0] = next_ref[2 + (planes - 1) * (1 - core) + (2 * core - 1) * p]
        kept_ref[p] = next_ref[2 + (planes - 1) * core + (1 - 2 * core) * p]
    outer_ref[0:1] = beyond[4] * beyond[4]
    outer_ref[1:2] = beyond[6] * beyond[6]


def middle_kernel(
    core_ref, own_ref, near_ref, far_ref, message_ref, first_ref, second_ref, v_ref, m_ref, out_ref, total_ref, moved
):
    _, orient, cells = own_ref.shape
    planes = first_ref.shape[0]

    def cross_of(depth):
        low, high = (
            boltzmann(first_ref[p : p + 1]) * boltzmann(second_ref[p : p + 1]) for p in (depth, planes - 1 - depth)
        )
        return jnp.where(core_ref[0] == 0, low, high)

    cross = [cross_of(depth) for depth in range(2)]

    @each_row_block(orient)
    def _(index):
        rows = rows_of(index)
        ahead, rate_plus, rate_minus = face_parts(v_ref, rows)
        rate = rate_plus + rate_minus
        for t in range(cells // LANES):
            gained = rate * message_ref[0, rows, columns(t)].astype(F32)
            moved[0, rows, columns(t)] = jnp.where(ahead, gained, 0.0).astype(BF16)
            moved[1, rows, columns(t)] = jnp.where(ahead, 0.0, gained).astype(BF16)

    own_face = own_ref[0].astype(F32) + cross[0] * mix(m_ref[...], moved[0])
    partner_face = near_ref[0].astype(F32) + cross[0] * mix(m_ref[...], moved[1])
    face = jnp.sum(own_face * partner_face, axis=0, keepdims=True)
    total = jnp.zeros((1, 1), F32)
    for p in range(own_ref.shape[0]):
        if p > 0:
            face = jnp.sum(own_ref[p].astype(F32) * far_ref[0].astype(F32), axis=0, keepdims=True)
        met = face / (orient * cross[p])
        out_ref[p : p + 1] = met
        total = total + jnp.sum(met, axis=1, keepdims=True)
    total_ref[...] = jnp.broadcast_to(total, total_ref.shape)


def third_step_kernel(
    held_ref, mine_ref, other_ref, first_ref, second_ref, outer_ref, v_ref, m_ref, next_ref, held, moved
):
    planes, orient, _ = held.shape
    matrix = m_ref[...]
    first, second = boltzmann(first_ref[...]), boltzmann(second_ref[...])
    face_drifts(v_ref, mine_ref, other_ref, moved, (0, 1))
    cross = first * second
    for p in range(planes):
        kept = held_ref[p + 2]
        if p in (0, planes - 1):
            arrived = cross[p : p + 1] * mix(matrix, moved[min(p, 1)])
            kept = (kept.astype(F32) + arrived).astype(BF16)
        held[p] = kept

    @each_row_block(orient)
    def _(index):
        rows = rows_of(index)
        geo = geometry(v_ref, rows)
        loaded = [load_plane(held_ref, p, rows) for p in (0, 1)]
        loaded += [load_plane(held, p, rows) for p in range(planes)]
        loaded += [load_plane(held_ref, p, rows) for p in (planes + 2, planes + 3)]
        for p in range(planes + 2):
            store_plane(moved, p, rows, drift(loaded[p + 1], loaded[p], loaded[p + 2], geo))

    squared = second * second
    factors = [outer_ref[0:1]] + [squared[p : p + 1] for p in range(planes)] + [outer_ref[1:2]]
    for p, factor in enumerate(factors):
        next_ref[p] = (factor * mix(matrix, moved[p])).astype(BF16)


def weight_kernel(core_ref, partner_ref, start_ref, turned_ref, weight_ref, own_ref):
    planes = partner_ref.shape[0]
    core = core_ref[0]
    for p in range(planes):
        weight_ref[p] = mix(turned_ref[...], partner_ref[p]).astype(BF16)
    for p in range(2):
        own_ref[p] = mix(turned_ref[...], start_ref[core * (planes - 1) + p - 2 * p * core]).astype(BF16)


def fold(value):
    return jnp.sum(value.reshape(ROWS // 8, 8, LANES), axis=0)


def pairing_kernel(held_ref, second_ref, v_ref, weight_ref, *refs):
    *partner_refs, out_ref = refs
    planes, orient, cells = weight_ref.shape
    second = boltzmann(second_ref[...])
    tiles = cells // LANES

    def body(index, sums):
        rows = rows_of(index)
        geo = geometry(v_ref, rows)
        loaded = [load_plane(held_ref, p, rows) for p in range(planes + 2)]
        new = []
        for p in range(planes):
            moved_tiles = drift(loaded[p + 1], loaded[p], loaded[p + 2], geo)
            weights = load_plane(weight_ref, p, rows)
            partner = load_plane(partner_refs[p], 0, rows)
            for t in range(tiles):
                last, third = sums[2 * (p * tiles + t)], sums[2 * (p * tiles + t) + 1]
                new.append(last + fold(moved_tiles[t] * weights[t].astype(F32)))
                new.append(third + fold(loaded[p + 1][t].astype(F32) * partner[t].astype(F32)))
        return tuple(new)

    zero = jnp.zeros((8, LANES), F32)
    sums = lax.fori_loop(0, orient // ROWS, body, (zero,) * (2 * planes * tiles), unroll=UNROLL)
    for p in range(planes):
        for t in range(tiles):
            last = jnp.sum(sums[2 * (p * tiles + t)], axis=0, keepdims=True)
            third = jnp.sum(sums[2 * (p * tiles + t) + 1], axis=0, keepdims=True)
            factor = second[p : p + 1, columns(t)]
            out_ref[p : p + 1, columns(t)] = (0.5 * factor * last + third / (factor * factor)) / orient


def last_kernel(
    core_ref, message_ref, weight_ref, own_weight_ref, own_low_ref, own_high_ref, partner_low_ref, partner_high_ref,
    shared_ref, met_ref,    own_ref, partner_ref, v_ref, m_ref, sent_ref, kept_ref, moved, gained,
):
    planes, cells = shared_ref.shape
    orient = m_ref.shape[0]
    tiles = cells // LANES
    core = core_ref[0]
    half = planes // 2
    face = core * (planes - 1)
    inner = face + 1 - 2 * core

    def at_face(ref, depth):
        return jnp.where(core == 0, boltzmann(ref[depth : depth + 1]), boltzmann(ref[planes - 1 - depth : planes - depth]))

    factors = [[at_face(ref, depth) for depth in range(2)] for ref in (partner_ref, own_ref)]

    @each_row_block(orient)
    def _(index):
        rows = rows_of(index)
        ahead, rate_plus, rate_minus = face_parts(v_ref, rows)
        rate = rate_plus + rate_minus
        for t in range(tiles):
            got = rate * message_ref[0, rows, columns(t)].astype(F32)
            moved[0, rows, columns(t)] = jnp.where(ahead, got, 0.0).astype(BF16)
            moved[1, rows, columns(t)] = jnp.where(ahead, 0.0, got).astype(BF16)

    for s in range(2):
        gained[s] = (factors[s][0] * factors[s][0] * mix(m_ref[...], moved[s])).astype(BF16)

    def body(index, sums):
        rows = rows_of(index)
        ahead, rate_plus, rate_minus = face_parts(v_ref, rows)
        rate = rate_plus + rate_minus
        sides = (jnp.where(ahead, rate, 0.0), jnp.where(ahead, 0.0, rate))
        message = load_plane(message_ref, 1, rows)
        new = []
        for s in range(2):
            change = load_plane(gained, s, rows)
            moved_tiles = drift(change, None, None, geometry(v_ref, rows, 1.0 - 2.0 * s))
            if s == 0:
                weights = [load_plane(weight_ref, p, rows) for p in (face, inner)]
            else:
                weights = [load_plane(own_weight_ref, p, rows) for p in (0, 1)]
            pair = ((partner_low_ref, partner_high_ref), (own_low_ref, own_high_ref))[s]
            third = [jnp.where(core == 0, low, high) for low, high in zip(*(load_plane(ref, 0, rows) for ref in pair))]
            for t in range(tiles):
                on_face = moved_tiles[t] + sides[s] * message[t].astype(F32)
                wide = change[t].astype(F32)
                terms = (
                    on_face * weights[0][t].astype(F32),
                    sides[s] * wide * weights[1][t].astype(F32),
                    wide * third[t].astype(F32),
                )
                base = 3 * (s * tiles + t)
                new += [sums[base + k] + fold(term) for k, term in enumerate(terms)]
        return tuple(new)

    zero = jnp.zeros((8, LANES), F32)
    sums = lax.fori_loop(0, orient // ROWS, body, (zero,) * (6 * tiles), unroll=UNROLL)
    for t in range(tiles):
        shares = []
        for s in range(2):
            base = 3 * (s * tiles + t)
            last, onward, third = (jnp.sum(sums[base + k], axis=0, keepdims=True) / orient for k in range(3))
            near, far = (factors[s][depth][:, columns(t)] for depth in range(2))
            shares.append((0.5 * near * last + third / (near * near), 0.5 * far * onward))
        for p in range(planes):
            at = slice(p, p + 1), columns(t)
            mine = core == (0 if p < half else 1)
            depth = min(p, planes - 1 - p)
            met = jnp.where(mine, 0.5 * met_ref[depth : depth + 1, columns(t)], 0.0)
            sent, kept = shared_ref[at] + met, met
            if depth < 2:
                sent = sent + jnp.where(mine, shares[0][depth], 0.0)
                kept = kept + jnp.where(mine, shares[1][depth], 0.0)
            sent_ref[at] = sent
            kept_ref[at] = kept


def split_outputs(outs):
    low, high, state, near, far, kept, outer = outs
    return (low, high), state, (near, far), kept, outer


def kernel_call(kernel, outs, scratch, args):
    vmem = pl.BlockSpec(memory_space=pltpu.VMEM)
    smem = pl.BlockSpec(memory_space=pltpu.SMEM)
    return pl.pallas_call(
        kernel,
        out_shape=outs,
        in_specs=[smem if arg.dtype == jnp.int32 else vmem for arg in args],
        out_specs=jax.tree.map(lambda _: vmem, outs),
        scratch_shapes=[pltpu.VMEM(*s) if len(s) == 2 else pltpu.VMEM(s, BF16) for s in scratch],
        compiler_params=pltpu.CompilerParams(vmem_limit_bytes=7 << 20),
        cost_estimate=pl.CostEstimate(flops=0, bytes_accessed=0, transcendentals=0),
    )(*args)


def shards(fields, end_weights, directions, analysis, synthesis, decay_rates):
    device = lax.axis_index("space")
    core = device % 2
    planes, cells = fields.shape
    orient = end_weights.shape[0]
    plane_index = device // 2 * planes + lax.broadcasted_iota(jnp.int32, (planes, 1), 0)
    ramp = slope * plane_index.astype(F32) / (planes * lax.axis_size("space") // 2)
    own = fields + ramp
    partner = swap_species(fields) + ramp

    wide = lambda extra: jax.ShapeDtypeStruct((planes + extra, orient, cells), BF16)
    slab, plane = wide(0), wide(1 - planes)
    face = core ^ (1 - device // 2 % 2)
    core_word = jnp.reshape(face, (1,)).astype(jnp.int32)
    species_word = jnp.reshape(core, (1,)).astype(jnp.int32)
    start = jnp.transpose(end_weights, (1, 0, 2))
    spread, edge0, coded = kernel_call(
        prologue_kernel,
        (jax.ShapeDtypeStruct((4, orient, LANES), F32), plane, jax.ShapeDtypeStruct((16, cells), BF16)),
        (((16, cells), F32),),
        (core_word, species_word, directions, start, own, partner),
    )
    matrix, turned = kernel_call(
        matrix_kernel,
        (jax.ShapeDtypeStruct((orient, orient), BF16),) * 2,
        (),
        (synthesis, decay_rates[None], analysis),
    )
    other0, matrix = lax.optimization_barrier((swap_species(edge0), matrix))
    message0 = kernel_call(
        first_message_kernel,
        jax.ShapeDtypeStruct((1, orient + 16, cells), BF16),
        (),
        (edge0, other0, coded, spread),
    )

    def message(blocks, others):
        shape = jax.ShapeDtypeStruct((len(blocks),) + blocks[0].shape[1:], BF16)
        return kernel_call(message_kernel, shape, (), (*blocks, *others, spread))

    start, _ = lax.optimization_barrier((start, message0))
    arrived0 = exchange_faces(message0)
    alone, edges1, *inner = kernel_call(
        first_alone_kernel,
        (slab, plane) + (plane,) * (planes - 2),
        (slab.shape, slab.shape),
        (start, own, spread, matrix),
    )
    weights, own_weights = kernel_call(
        weight_kernel, (slab, wide(2 - planes)), (), (core_word, swap_species(start), start, turned)
    )
    others1, weights, *partner_inner = lax.optimization_barrier(
        (swap_species(edges1), weights, *map(swap_species, inner))
    )
    message1 = kernel_call(
        first_message_kernel,
        jax.ShapeDtypeStruct((1, orient + 16 * PAD, cells), BF16),
        (),
        (edges1, others1, *[coded] * PAD, spread),
    )
    state, *_ = lax.optimization_barrier((alone, message1, weights))
    edges2, edges3 = kernel_call(
        next_alone_kernel, (plane, plane), (slab.shape, slab.shape), (state, own, partner, spread, matrix)
    )
    edges2, edges3, arrived0 = lax.optimization_barrier((edges2, edges3, arrived0))
    message2 = message([edges2, edges3], [swap_species(edges2), swap_species(edges3)])
    arrived = [exchange_faces(message1), exchange_faces(message2)]
    crossed0 = swap_species(arrived0)

    alone, *_ = lax.optimization_barrier((alone, message1, message2))
    half = planes // 2
    faces, second_state, sent_half, kept_half, outer = split_outputs(
        kernel_call(
            second_step_kernel,
            (plane, plane, wide(4), plane, plane, wide(half - planes), jax.ShapeDtypeStruct((2, cells), F32)),
            (wide(2).shape, wide(4).shape),
            (core_word, alone, edge0, arrived0, crossed0, own, partner, spread, matrix),
        )
    )
    arrived1, second_state = lax.optimization_barrier((arrived[0], second_state))
    *moving, _ = lax.optimization_barrier((*sent_half, arrived1))
    *partner_half, crossed1 = lax.optimization_barrier((*map(swap_species, moving), swap_species(arrived1)))
    density = jax.ShapeDtypeStruct((planes, cells), F32)
    met, partition = kernel_call(
        middle_kernel,
        (jax.ShapeDtypeStruct((half, cells), F32), density),
        ((2, orient, cells),),
        (core_word, kept_half, *partner_half, arrived1, own, partner, spread, matrix),
    )
    count = lax.axis_size("space")

    def received(value, distance, after):
        block = lax.ppermute(value, "space", [(i, i ^ distance) for i in range(count)])
        return lax.optimization_barrier((block, after))

    def gathered(value, distance, after):
        block, after = received(value, distance, after)
        return kernel_call(add_kernel, density, (), (value, block)), after

    *faces, second_state, _ = lax.optimization_barrier((*faces, second_state, met))
    partner_faces = [swap_species(block) for block in faces]
    third_state = kernel_call(
        third_step_kernel,
        wide(2),
        (slab.shape, wide(2).shape),
        (second_state, arrived1, crossed1, own, partner, outer, spread, matrix),
    )
    partition, third_state = gathered(partition, 4, third_state)
    third_state, _ = lax.optimization_barrier((third_state, partition))
    shared = kernel_call(
        pairing_kernel,
        density,
        (),
        (third_state, partner, spread, weights, partner_faces[0], *partner_inner, partner_faces[1]),
    )
    distance = 8
    while distance < count:
        partition, shared = gathered(partition, distance, shared)
        distance *= 2
    arrived2, shared, _ = lax.optimization_barrier((arrived[1], shared, partition))
    sent, kept = kernel_call(
        last_kernel,
        (density, density),
        ((2, orient, cells), (2, orient, cells)),
        (
            core_word, arrived2, weights, own_weights, *faces, *partner_faces, shared, met,
            own, partner, spread, matrix,
        ),
    )
    beside, sent = received(partition, 2, sent)
    joined = kernel_call(
        join_kernel, jax.ShapeDtypeStruct((2 * planes, cells), F32), (), (sent, partition, beside)
    )
    return kernel_call(
        functools.partial(divide_kernel, count // 2 * planes * cells),
        density,
        (),
        (kept, joined, swap_species(joined)),
    )


def solution(mesh):
    return jax.shard_map(
        shards,
        mesh=mesh,
        in_specs=(P(("runs", "space"), None), P(None, ("runs", "space"), None), P(), P(), P(), P()),
        out_specs=P(("runs", "space"), None),
        check_vma=False,
    )
```

```python
import functools

import jax
import jax.numpy as jnp
from jax import lax
from jax.experimental import pallas as pl
from jax.experimental.pallas import tpu as pltpu
from jax.sharding import PartitionSpec as P

NZ = 16
STEPS = 4
LANES = 128
ROWS = 16
UNROLL = 16
PAD = 2

courant = 0.3
slope = 0.6

BF16 = jnp.bfloat16
F32 = jnp.float32


def swap_species(block):
    count = lax.axis_size("space")
    return lax.ppermute(block, "space", [(i ^ 1, i) for i in range(count)])


def exchange_faces(block):
    count = lax.axis_size("space")
    route = []
    for slab in range(count // 2):
        beside = ((slab + 1) ^ 1) - 1
        route += [(2 * slab, 2 * (slab ^ 1)), (2 * slab + 1, 2 * beside % count + 1)]
    return lax.ppermute(block, "space", route)


def rows_of(index):
    return pl.ds(pl.multiple_of(index * ROWS, ROWS), ROWS)


def each_row_block(orient):
    def run(body):
        def step(index, carry):
            body(index)
            return carry

        lax.fori_loop(0, orient // ROWS, step, 0, unroll=UNROLL)

    return run


def columns(tile):
    return slice(LANES * tile, LANES * (tile + 1))


def geometry(v_ref, rows, sign=1.0):
    lane = lax.broadcasted_iota(jnp.int32, (ROWS, LANES), 1)
    vx, vy, vz = (sign * v_ref[c, rows, :] for c in range(3))
    narrow = vx.astype(BF16)
    plus_x, narrow_plus, plus_y, plus_z = vx > 0, narrow > jnp.zeros_like(narrow), vy > 0, vz > 0
    rate_x, rate_y, rate_z = (courant * jnp.abs(t) for t in (vx, vy, vz))
    stay = 1.0 - (rate_x + rate_y + rate_z)
    z_from = (lane & (LANES - NZ)) | (jnp.where(plus_z, lane - 1, lane + 1) & (NZ - 1))
    y_from = jnp.where(plus_y, lane - NZ, lane + NZ) & (LANES - 1)
    y_edge = jnp.where(plus_y, lane, LANES - 1 - lane) < NZ
    return plus_x, narrow_plus, plus_y, stay, rate_x, rate_y, rate_z, z_from, y_from, y_edge


def pick(tile, index):
    return jnp.take_along_axis(tile, index, axis=1, mode="promise_in_bounds")


def load_plane(ref, plane, rows):
    return [ref[plane, rows, columns(t)] for t in range(ref.shape[2] // LANES)]


def drift(center, before, after, geo):
    plus_x, narrow_plus, plus_y, stay, rate_x, rate_y, rate_z, z_from, y_from, y_edge = geo
    tiles = len(center)
    center = [tile.astype(F32) for tile in center]
    turned = [pick(tile, y_from) for tile in center]
    moved = []
    for t in range(tiles):
        total = stay * center[t]
        if before is not None and after is not None:
            total = total + rate_x * jnp.where(narrow_plus, before[t], after[t]).astype(F32)
        elif before is not None:
            total = total + jnp.where(plus_x, rate_x, 0.0) * before[t].astype(F32)
        elif after is not None:
            total = total + jnp.where(plus_x, 0.0, rate_x) * after[t].astype(F32)
        over = jnp.where(plus_y, turned[t - 1], turned[(t + 1) % tiles])
        total = total + rate_y * jnp.where(y_edge, over, turned[t])
        total = total + rate_z * pick(center[t], z_from)
        moved.append(total)
    return moved


def store_plane(ref, plane, rows, tiles):
    for t, tile in enumerate(tiles):
        ref[plane, rows, columns(t)] = tile.astype(ref.dtype)


def mix(matrix, moved):
    return jnp.dot(matrix, moved, preferred_element_type=F32)


def boltzmann(field):
    return jnp.exp(-0.5 * field)


def prologue_kernel(
    core_ref, species_ref, directions_ref, start_ref, fields_ref, partner_ref, spread_ref, edge_ref, coded_ref, near
):
    sign = 1.0 - 2.0 * species_ref[0].astype(F32)
    toward = sign * (1.0 - 2.0 * core_ref[0].astype(F32))
    planes, orient, cells = start_ref.shape
    low = boltzmann(fields_ref[0:1])
    high = boltzmann(fields_ref[fields_ref.shape[0] - 1 :])
    for c in range(4):
        row = directions_ref[c % 3 : c % 3 + 1]
        column = jnp.broadcast_to(row, (LANES, orient)).T
        spread_ref[c] = (toward if c == 3 else sign) * column

    @each_row_block(orient)
    def _(index):
        rows = rows_of(index)
        plus_x = spread_ref[0, rows, :] > 0
        for t in range(cells // LANES):
            at = rows, columns(t)
            chosen = jnp.where(
                plus_x,
                high[:, columns(t)] * start_ref[planes - 1, *at].astype(F32),
                low[:, columns(t)] * start_ref[0, *at].astype(F32),
            )
            edge_ref[0, *at] = chosen.astype(BF16)

    near[...] = jnp.zeros_like(near)
    for s, ref in enumerate((fields_ref, partner_ref)):
        for depth in range(2):
            high_row, low_row = (ref[p : p + 1] for p in (planes - 1 - depth, depth))
            row = jnp.where(core_ref[0] == 1, high_row, low_row)
            coarse = row.astype(BF16).astype(F32)
            at = 2 * s + depth
            near[at : at + 1] = coarse
            near[at + 4 : at + 5] = row - coarse
    coded_ref[...] = near[...].astype(BF16)


def matrix_kernel(synthesis_ref, decay_ref, analysis_ref, out_ref, turned_ref):
    rest = synthesis_ref[...].astype(F32) * decay_ref[...]
    total = jnp.full(out_ref.shape, 1.0 / out_ref.shape[1], F32)
    for _ in range(3):
        part = rest.astype(BF16)
        rest = rest - part.astype(F32)
        total = total + jnp.dot(part, analysis_ref[...], preferred_element_type=F32)
    out_ref[...] = total.astype(BF16)
    turned_ref[...] = total.T.astype(BF16)


def add_kernel(one_ref, two_ref, out_ref):
    out_ref[...] = one_ref[...] + two_ref[...]


def join_kernel(sent_ref, one_ref, two_ref, out_ref):
    planes = sent_ref.shape[0]
    out_ref[:planes] = sent_ref[...]
    out_ref[planes:] = one_ref[...] + two_ref[...]


def divide_kernel(cells, kept_ref, mine_ref, arrived_ref, out_ref):
    planes = kept_ref.shape[0]
    total = mine_ref[planes:] + arrived_ref[planes:]
    out_ref[...] = (kept_ref[...] + arrived_ref[:planes]) * (cells / total)


def message_kernel(*refs):
    count = (len(refs) - 2) // 2
    v_ref, out_ref = refs[-2:]
    orient, cells = refs[0].shape[1:]

    @each_row_block(orient)
    def _(index):
        rows = rows_of(index)
        narrow = v_ref[3, rows, :].astype(BF16)
        leaves = narrow < jnp.zeros_like(narrow)
        for p in range(count):
            for t in range(cells // LANES):
                at = 0, rows, columns(t)
                out_ref[p, rows, columns(t)] = jnp.where(leaves, refs[p][at], refs[count + p][at])


def first_message_kernel(mine_ref, other_ref, *refs):
    *coded_refs, v_ref, out_ref = refs
    message_kernel(mine_ref, other_ref, v_ref, out_ref)
    orient = mine_ref.shape[1]
    for k, ref in enumerate(coded_refs):
        out_ref[0, orient + 16 * k : orient + 16 * (k + 1)] = ref[...]


def write_edge(edges_ref, step, faces, rows, v_ref):
    narrow = v_ref[0, rows, :].astype(BF16)
    plus_x = narrow > jnp.zeros_like(narrow)
    for t in range(len(faces[0])):
        edges_ref[step, rows, columns(t)] = jnp.where(plus_x, faces[-1][t], faces[0][t])


def alone_step(source_ref, moved, targets, v_ref, edges_ref, step):
    planes, orient, _ = source_ref.shape

    @each_row_block(orient)
    def _(index):
        rows = rows_of(index)
        geo = geometry(v_ref, rows)
        loaded = [load_plane(source_ref, p, rows) for p in range(planes)]
        if edges_ref is not None:
            write_edge(edges_ref, step, loaded, rows, v_ref)
        for p in targets:
            before = loaded[p - 1] if p > 0 else None
            after = loaded[p + 1] if p < planes - 1 else None
            store_plane(moved, p, rows, drift(loaded[p], before, after, geo))


def first_alone_kernel(start_ref, first_ref, v_ref, m_ref, out_ref, edges_ref, *refs):
    *inner_refs, held, moved = refs
    planes, orient, _ = start_ref.shape
    first = boltzmann(first_ref[...])
    for p in range(planes):
        held[p] = (first[p : p + 1] * start_ref[p].astype(F32)).astype(BF16)
    alone_step(held, moved, range(planes), v_ref, None, 0)
    for p in (0, planes - 1, *range(1, planes - 1)):
        state = (first[p : p + 1] * first[p : p + 1] * mix(m_ref[...], moved[p])).astype(BF16)
        out_ref[p] = state
        if 0 < p < planes - 1:
            inner_refs[p - 1][0] = state

    @each_row_block(orient)
    def _(index):
        rows = rows_of(index)
        write_edge(edges_ref, 0, [load_plane(out_ref, p, rows) for p in (0, planes - 1)], rows, v_ref)


def next_alone_kernel(state_ref, first_ref, second_ref, v_ref, m_ref, edges2_ref, edges3_ref, held, moved):
    planes, orient, _ = state_ref.shape
    first = boltzmann(first_ref[...])
    second = boltzmann(second_ref[...])
    alone_step(state_ref, moved, range(planes), v_ref, None, 0)
    for p in range(planes):
        held[p] = (first[p : p + 1] * second[p : p + 1] * mix(m_ref[...], moved[p])).astype(BF16)
    alone_step(held, moved, (0, planes - 1), v_ref, edges2_ref, 0)
    for p in (0, planes - 1):
        held[p] = (second[p : p + 1] * second[p : p + 1] * mix(m_ref[...], moved[p])).astype(BF16)

    @each_row_block(orient)
    def _(index):
        rows = rows_of(index)
        write_edge(edges3_ref, 0, [load_plane(held, p, rows) for p in (0, planes - 1)], rows, v_ref)


def face_parts(v_ref, rows):
    vx = v_ref[0, rows, :]
    rate = courant * jnp.abs(vx)
    return v_ref[3, rows, :] > 0, jnp.where(vx > 0, rate, 0.0), jnp.where(vx > 0, 0.0, rate)


def face_drifts(v_ref, mine_ref, other_ref, moved, slots):
    @each_row_block(v_ref.shape[1])
    def _(index):
        rows = rows_of(index)
        ahead, rate_plus, rate_minus = face_parts(v_ref, rows)
        for t in range(mine_ref.shape[2] // LANES):
            mine = mine_ref[0, rows, columns(t)].astype(F32)
            other = other_ref[0, rows, columns(t)].astype(F32)
            face = jnp.where(ahead, mine, other)
            moved[slots[0], rows, columns(t)] = (rate_plus * face).astype(BF16)
            moved[slots[1], rows, columns(t)] = (rate_minus * face).astype(BF16)


def second_step_kernel(
    core_ref, alone_ref, edge_ref, mine_ref, other_ref, first_ref, second_ref, v_ref, m_ref,
    face_low_ref, face_high_ref, next_ref, sent_near_ref, sent_far_ref, kept_ref, outer_ref, held, moved,
):
    planes, orient, _ = alone_ref.shape
    matrix = m_ref[...]
    first, second = boltzmann(first_ref[...]), boltzmann(second_ref[...])
    core = core_ref[0]
    mine, other = (block[:4] + block[4:8] for block in (ref[0, orient:].astype(F32) for ref in (mine_ref, other_ref)))
    other = (other[2:4], other[0:2])
    mine = (mine[0:2], mine[2:4])
    low = [jnp.where(core == 0, mine[k], other[k]) for k in range(2)]
    high = [jnp.where(core == 0, other[k], mine[k]) for k in range(2)]
    beyond = [boltzmann(block[k : k + 1]) for block in (low[0], high[0], low[1], high[1]) for k in range(2)]
    face_drifts(v_ref, mine_ref, other_ref, moved, (0, 1))

    @each_row_block(orient)
    def _(index):
        rows = rows_of(index)
        _, rate_plus, rate_minus = face_parts(v_ref, rows)
        for t in range(edge_ref.shape[2] // LANES):
            edge = edge_ref[0, rows, columns(t)].astype(F32)
            moved[2, rows, columns(t)] = (rate_minus * edge).astype(BF16)
            moved[3, rows, columns(t)] = (rate_plus * edge).astype(BF16)

    squared = first * first
    for p in range(planes):
        kept = alone_ref[p]
        if p in (0, planes - 1):
            arrived = squared[p : p + 1] * mix(matrix, moved[min(p, 1)])
            kept = (kept.astype(F32) + arrived).astype(BF16)
            (face_high_ref if p else face_low_ref)[0] = kept
        held[p + 1] = kept
    held[0] = (beyond[0] * beyond[0] * mix(matrix, moved[2])).astype(BF16)
    held[planes + 1] = (beyond[2] * beyond[2] * mix(matrix, moved[3])).astype(BF16)
    count = planes + 2

    @each_row_block(orient)
    def _(index):
        rows = rows_of(index)
        geo = geometry(v_ref, rows)
        _, rate_plus, rate_minus = face_parts(v_ref, rows)
        loaded = [load_plane(held, p, rows) for p in range(count)]
        for p in range(count):
            before = loaded[p - 1] if p > 0 else None
            after = loaded[p + 1] if p < count - 1 else None
            store_plane(moved, p + 1, rows, drift(loaded[p], before, after, geo))
        store_plane(moved, 0, rows, [rate_minus * tile.astype(F32) for tile in loaded[0]])
        store_plane(moved, count + 1, rows, [rate_plus * tile.astype(F32) for tile in loaded[-1]])

    cross = first * second
    factors = [beyond[1] * beyond[5], beyond[0] * beyond[4]]
    factors += [cross[p : p + 1] for p in range(planes)]
    factors += [beyond[2] * beyond[6], beyond[3] * beyond[7]]
    for p, factor in enumerate(factors):
        next_ref[p] = (factor * mix(matrix, moved[p])).astype(BF16)
    for p in range(planes // 2):
        sent_ref = (sent_near_ref, sent_far_ref)[p]
        sent_ref[0] = next_ref[2 + (planes - 1) * (1 - core) + (2 * core - 1) * p]
        kept_ref[p] = next_ref[2 + (planes - 1) * core + (1 - 2 * core) * p]
    outer_ref[0:1] = beyond[4] * beyond[4]
    outer_ref[1:2] = beyond[6] * beyond[6]


def middle_kernel(
    core_ref, own_ref, near_ref, far_ref, message_ref, first_ref, second_ref, v_ref, m_ref, out_ref, total_ref, moved
):
    _, orient, cells = own_ref.shape
    planes = first_ref.shape[0]

    def cross_of(depth):
        low, high = (
            boltzmann(first_ref[p : p + 1]) * boltzmann(second_ref[p : p + 1]) for p in (depth, planes - 1 - depth)
        )
        return jnp.where(core_ref[0] == 0, low, high)

    cross = [cross_of(depth) for depth in range(2)]

    @each_row_block(orient)
    def _(index):
        rows = rows_of(index)
        ahead, rate_plus, rate_minus = face_parts(v_ref, rows)
        rate = rate_plus + rate_minus
        for t in range(cells // LANES):
            gained = rate * message_ref[0, rows, columns(t)].astype(F32)
            moved[0, rows, columns(t)] = jnp.where(ahead, gained, 0.0).astype(BF16)
            moved[1, rows, columns(t)] = jnp.where(ahead, 0.0, gained).astype(BF16)

    own_face = own_ref[0].astype(F32) + cross[0] * mix(m_ref[...], moved[0])
    partner_face = near_ref[0].astype(F32) + cross[0] * mix(m_ref[...], moved[1])
    face = jnp.sum(own_face * partner_face, axis=0, keepdims=True)
    total = jnp.zeros((1, 1), F32)
    for p in range(own_ref.shape[0]):
        if p > 0:
            face = jnp.sum(own_ref[p].astype(F32) * far_ref[0].astype(F32), axis=0, keepdims=True)
        met = face / (orient * cross[p])
        out_ref[p : p + 1] = met
        total = total + jnp.sum(met, axis=1, keepdims=True)
    total_ref[...] = jnp.broadcast_to(total, total_ref.shape)


def third_step_kernel(
    held_ref, mine_ref, other_ref, first_ref, second_ref, outer_ref, v_ref, m_ref, next_ref, held, moved
):
    planes, orient, _ = held.shape
    matrix = m_ref[...]
    first, second = boltzmann(first_ref[...]), boltzmann(second_ref[...])
    face_drifts(v_ref, mine_ref, other_ref, moved, (0, 1))
    cross = first * second
    for p in range(planes):
        kept = held_ref[p + 2]
        if p in (0, planes - 1):
            arrived = cross[p : p + 1] * mix(matrix, moved[min(p, 1)])
            kept = (kept.astype(F32) + arrived).astype(BF16)
        held[p] = kept

    @each_row_block(orient)
    def _(index):
        rows = rows_of(index)
        geo = geometry(v_ref, rows)
        loaded = [load_plane(held_ref, p, rows) for p in (0, 1)]
        loaded += [load_plane(held, p, rows) for p in range(planes)]
        loaded += [load_plane(held_ref, p, rows) for p in (planes + 2, planes + 3)]
        for p in range(planes + 2):
            store_plane(moved, p, rows, drift(loaded[p + 1], loaded[p], loaded[p + 2], geo))

    squared = second * second
    factors = [outer_ref[0:1]] + [squared[p : p + 1] for p in range(planes)] + [outer_ref[1:2]]
    for p, factor in enumerate(factors):
        next_ref[p] = (factor * mix(matrix, moved[p])).astype(BF16)


def weight_kernel(core_ref, partner_ref, start_ref, turned_ref, weight_ref, own_ref):
    planes = partner_ref.shape[0]
    core = core_ref[0]
    for p in range(planes):
        weight_ref[p] = mix(turned_ref[...], partner_ref[p]).astype(BF16)
    for p in range(2):
        own_ref[p] = mix(turned_ref[...], start_ref[core * (planes - 1) + p - 2 * p * core]).astype(BF16)


def fold(value):
    return jnp.sum(value.reshape(ROWS // 8, 8, LANES), axis=0)


def pairing_kernel(held_ref, second_ref, v_ref, weight_ref, *refs):
    *partner_refs, out_ref = refs
    planes, orient, cells = weight_ref.shape
    second = boltzmann(second_ref[...])
    tiles = cells // LANES

    def body(index, sums):
        rows = rows_of(index)
        geo = geometry(v_ref, rows)
        loaded = [load_plane(held_ref, p, rows) for p in range(planes + 2)]
        new = []
        for p in range(planes):
            moved_tiles = drift(loaded[p + 1], loaded[p], loaded[p + 2], geo)
            weights = load_plane(weight_ref, p, rows)
            partner = load_plane(partner_refs[p], 0, rows)
            for t in range(tiles):
                last, third = sums[2 * (p * tiles + t)], sums[2 * (p * tiles + t) + 1]
                new.append(last + fold(moved_tiles[t] * weights[t].astype(F32)))
                new.append(third + fold(loaded[p + 1][t].astype(F32) * partner[t].astype(F32)))
        return tuple(new)

    zero = jnp.zeros((8, LANES), F32)
    sums = lax.fori_loop(0, orient // ROWS, body, (zero,) * (2 * planes * tiles), unroll=UNROLL)
    for p in range(planes):
        for t in range(tiles):
            last = jnp.sum(sums[2 * (p * tiles + t)], axis=0, keepdims=True)
            third = jnp.sum(sums[2 * (p * tiles + t) + 1], axis=0, keepdims=True)
            factor = second[p : p + 1, columns(t)]
            out_ref[p : p + 1, columns(t)] = (0.5 * factor * last + third / (factor * factor)) / orient


def last_kernel(
    core_ref, message_ref, weight_ref, own_weight_ref, own_low_ref, own_high_ref, partner_low_ref, partner_high_ref,
    shared_ref, met_ref,    own_ref, partner_ref, v_ref, m_ref, sent_ref, kept_ref, moved, gained,
):
    planes, cells = shared_ref.shape
    orient = m_ref.shape[0]
    tiles = cells // LANES
    core = core_ref[0]
    half = planes // 2
    face = core * (planes - 1)
    inner = face + 1 - 2 * core

    def at_face(ref, depth):
        return jnp.where(core == 0, boltzmann(ref[depth : depth + 1]), boltzmann(ref[planes - 1 - depth : planes - depth]))

    factors = [[at_face(ref, depth) for depth in range(2)] for ref in (partner_ref, own_ref)]

    @each_row_block(orient)
    def _(index):
        rows = rows_of(index)
        ahead, rate_plus, rate_minus = face_parts(v_ref, rows)
        rate = rate_plus + rate_minus
        for t in range(tiles):
            got = rate * message_ref[0, rows, columns(t)].astype(F32)
            moved[0, rows, columns(t)] = jnp.where(ahead, got, 0.0).astype(BF16)
            moved[1, rows, columns(t)] = jnp.where(ahead, 0.0, got).astype(BF16)

    for s in range(2):
        gained[s] = (factors[s][0] * factors[s][0] * mix(m_ref[...], moved[s])).astype(BF16)

    def body(index, sums):
        rows = rows_of(index)
        ahead, rate_plus, rate_minus = face_parts(v_ref, rows)
        rate = rate_plus + rate_minus
        sides = (jnp.where(ahead, rate, 0.0), jnp.where(ahead, 0.0, rate))
        message = load_plane(message_ref, 1, rows)
        new = []
        for s in range(2):
            change = load_plane(gained, s, rows)
            moved_tiles = drift(change, None, None, geometry(v_ref, rows, 1.0 - 2.0 * s))
            if s == 0:
                weights = [load_plane(weight_ref, p, rows) for p in (face, inner)]
            else:
                weights = [load_plane(own_weight_ref, p, rows) for p in (0, 1)]
            pair = ((partner_low_ref, partner_high_ref), (own_low_ref, own_high_ref))[s]
            third = [jnp.where(core == 0, low, high) for low, high in zip(*(load_plane(ref, 0, rows) for ref in pair))]
            for t in range(tiles):
                on_face = moved_tiles[t] + sides[s] * message[t].astype(F32)
                wide = change[t].astype(F32)
                terms = (
                    on_face * weights[0][t].astype(F32),
                    sides[s] * wide * weights[1][t].astype(F32),
                    wide * third[t].astype(F32),
                )
                base = 3 * (s * tiles + t)
                new += [sums[base + k] + fold(term) for k, term in enumerate(terms)]
        return tuple(new)

    zero = jnp.zeros((8, LANES), F32)
    sums = lax.fori_loop(0, orient // ROWS, body, (zero,) * (6 * tiles), unroll=UNROLL)
    for t in range(tiles):
        shares = []
        for s in range(2):
            base = 3 * (s * tiles + t)
            last, onward, third = (jnp.sum(sums[base + k], axis=0, keepdims=True) / orient for k in range(3))
            near, far = (factors[s][depth][:, columns(t)] for depth in range(2))
            shares.append((0.5 * near * last + third / (near * near), 0.5 * far * onward))
        for p in range(planes):
            at = slice(p, p + 1), columns(t)
            mine = core == (0 if p < half else 1)
            depth = min(p, planes - 1 - p)
            met = jnp.where(mine, 0.5 * met_ref[depth : depth + 1, columns(t)], 0.0)
            sent, kept = shared_ref[at] + met, met
            if depth < 2:
                sent = sent + jnp.where(mine, shares[0][depth], 0.0)
                kept = kept + jnp.where(mine, shares[1][depth], 0.0)
            sent_ref[at] = sent
            kept_ref[at] = kept


def split_outputs(outs):
    low, high, state, near, far, kept, outer = outs
    return (low, high), state, (near, far), kept, outer


def kernel_call(kernel, outs, scratch, args):
    vmem = pl.BlockSpec(memory_space=pltpu.VMEM)
    smem = pl.BlockSpec(memory_space=pltpu.SMEM)
    return pl.pallas_call(
        kernel,
        out_shape=outs,
        in_specs=[smem if arg.dtype == jnp.int32 else vmem for arg in args],
        out_specs=jax.tree.map(lambda _: vmem, outs),
        scratch_shapes=[pltpu.VMEM(*s) if len(s) == 2 else pltpu.VMEM(s, BF16) for s in scratch],
        compiler_params=pltpu.CompilerParams(vmem_limit_bytes=12 << 20),
        cost_estimate=pl.CostEstimate(flops=0, bytes_accessed=0, transcendentals=0),
    )(*args)


def shards(fields, end_weights, directions, analysis, synthesis, decay_rates):
    device = lax.axis_index("space")
    core = device % 2
    planes, cells = fields.shape
    orient = end_weights.shape[0]
    plane_index = device // 2 * planes + lax.broadcasted_iota(jnp.int32, (planes, 1), 0)
    ramp = slope * plane_index.astype(F32) / (planes * lax.axis_size("space") // 2)
    own = fields + ramp
    partner = swap_species(fields) + ramp

    wide = lambda extra: jax.ShapeDtypeStruct((planes + extra, orient, cells), BF16)
    slab, plane = wide(0), wide(1 - planes)
    face = core ^ (1 - device // 2 % 2)
    core_word = jnp.reshape(face, (1,)).astype(jnp.int32)
    species_word = jnp.reshape(core, (1,)).astype(jnp.int32)
    start = jnp.transpose(end_weights, (1, 0, 2))
    spread, edge0, coded = kernel_call(
        prologue_kernel,
        (jax.ShapeDtypeStruct((4, orient, LANES), F32), plane, jax.ShapeDtypeStruct((16, cells), BF16)),
        (((16, cells), F32),),
        (core_word, species_word, directions, start, own, partner),
    )
    matrix, turned = kernel_call(
        matrix_kernel,
        (jax.ShapeDtypeStruct((orient, orient), BF16),) * 2,
        (),
        (synthesis, decay_rates[None], analysis),
    )
    other0, matrix = lax.optimization_barrier((swap_species(edge0), matrix))
    message0 = kernel_call(
        first_message_kernel,
        jax.ShapeDtypeStruct((1, orient + 16, cells), BF16),
        (),
        (edge0, other0, coded, spread),
    )

    def message(blocks, others):
        shape = jax.ShapeDtypeStruct((len(blocks),) + blocks[0].shape[1:], BF16)
        return kernel_call(message_kernel, shape, (), (*blocks, *others, spread))

    start, _ = lax.optimization_barrier((start, message0))
    arrived0 = exchange_faces(message0)
    alone, edges1, *inner = kernel_call(
        first_alone_kernel,
        (slab, plane) + (plane,) * (planes - 2),
        (slab.shape, slab.shape),
        (start, own, spread, matrix),
    )
    weights, own_weights = kernel_call(
        weight_kernel, (slab, wide(2 - planes)), (), (core_word, swap_species(start), start, turned)
    )
    others1, weights, *partner_inner = lax.optimization_barrier(
        (swap_species(edges1), weights, *map(swap_species, inner))
    )
    message1 = kernel_call(
        first_message_kernel,
        jax.ShapeDtypeStruct((1, orient + 16 * PAD, cells), BF16),
        (),
        (edges1, others1, *[coded] * PAD, spread),
    )
    state, *_ = lax.optimization_barrier((alone, message1, weights))
    edges2, edges3 = kernel_call(
        next_alone_kernel, (plane, plane), (slab.shape, slab.shape), (state, own, partner, spread, matrix)
    )
    edges2, edges3, arrived0 = lax.optimization_barrier((edges2, edges3, arrived0))
    message2 = message([edges2, edges3], [swap_species(edges2), swap_species(edges3)])
    arrived = [exchange_faces(message1), exchange_faces(message2)]
    crossed0 = swap_species(arrived0)

    alone, *_ = lax.optimization_barrier((alone, message1, message2))
    half = planes // 2
    faces, second_state, sent_half, kept_half, outer = split_outputs(
        kernel_call(
            second_step_kernel,
            (plane, plane, wide(4), plane, plane, wide(half - planes), jax.ShapeDtypeStruct((2, cells), F32)),
            (wide(2).shape, wide(4).shape),
            (core_word, alone, edge0, arrived0, crossed0, own, partner, spread, matrix),
        )
    )
    arrived1, second_state = lax.optimization_barrier((arrived[0], second_state))
    *moving, _ = lax.optimization_barrier((*sent_half, arrived1))
    *partner_half, crossed1 = lax.optimization_barrier((*map(swap_species, moving), swap_species(arrived1)))
    density = jax.ShapeDtypeStruct((planes, cells), F32)
    met, partition = kernel_call(
        middle_kernel,
        (jax.ShapeDtypeStruct((half, cells), F32), density),
        ((2, orient, cells),),
        (core_word, kept_half, *partner_half, arrived1, own, partner, spread, matrix),
    )
    count = lax.axis_size("space")

    def received(value, distance, after):
        block = lax.ppermute(value, "space", [(i, i ^ distance) for i in range(count)])
        return lax.optimization_barrier((block, after))

    def gathered(value, distance, after):
        block, after = received(value, distance, after)
        return kernel_call(add_kernel, density, (), (value, block)), after

    *faces, second_state, _ = lax.optimization_barrier((*faces, second_state, met))
    partner_faces = [swap_species(block) for block in faces]
    third_state = kernel_call(
        third_step_kernel,
        wide(2),
        (slab.shape, wide(2).shape),
        (second_state, arrived1, crossed1, own, partner, outer, spread, matrix),
    )
    partition, third_state = gathered(partition, 4, third_state)
    third_state, _ = lax.optimization_barrier((third_state, partition))
    shared = kernel_call(
        pairing_kernel,
        density,
        (),
        (third_state, partner, spread, weights, partner_faces[0], *partner_inner, partner_faces[1]),
    )
    distance = 8
    while distance < count:
        partition, shared = gathered(partition, distance, shared)
        distance *= 2
    arrived2, shared, _ = lax.optimization_barrier((arrived[1], shared, partition))
    sent, kept = kernel_call(
        last_kernel,
        (density, density),
        ((2, orient, cells), (2, orient, cells)),
        (
            core_word, arrived2, weights, own_weights, *faces, *partner_faces, shared, met,
            own, partner, spread, matrix,
        ),
    )
    beside, sent = received(partition, 2, sent)
    joined = kernel_call(
        join_kernel, jax.ShapeDtypeStruct((2 * planes, cells), F32), (), (sent, partition, beside)
    )
    return kernel_call(
        functools.partial(divide_kernel, count // 2 * planes * cells),
        density,
        (),
        (kept, joined, swap_species(joined)),
    )


def solution(mesh):
    return jax.shard_map(
        shards,
        mesh=mesh,
        in_specs=(P(("runs", "space"), None), P(None, ("runs", "space"), None), P(), P(), P(), P()),
        out_specs=P(("runs", "space"), None),
        check_vma=False,
    )
```

```python
import functools

import jax
import jax.numpy as jnp
from jax import lax
from jax.experimental import pallas as pl
from jax.experimental.pallas import tpu as pltpu
from jax.sharding import PartitionSpec as P

NZ = 16
STEPS = 4
LANES = 128
ROWS = 16
UNROLL = 16
PAD = 2
PAD_ROWS = 32

courant = 0.3
slope = 0.6

BF16 = jnp.bfloat16
F32 = jnp.float32


def swap_species(block):
    count = lax.axis_size("space")
    return lax.ppermute(block, "space", [(i ^ 1, i) for i in range(count)])


def exchange_faces(block):
    count = lax.axis_size("space")
    route = []
    for slab in range(count // 2):
        beside = ((slab + 1) ^ 1) - 1
        route += [(2 * slab, 2 * (slab ^ 1)), (2 * slab + 1, 2 * beside % count + 1)]
    return lax.ppermute(block, "space", route)


def rows_of(index):
    return pl.ds(pl.multiple_of(index * ROWS, ROWS), ROWS)


def each_row_block(orient):
    def run(body):
        def step(index, carry):
            body(index)
            return carry

        lax.fori_loop(0, orient // ROWS, step, 0, unroll=UNROLL)

    return run


def columns(tile):
    return slice(LANES * tile, LANES * (tile + 1))


def geometry(v_ref, rows, sign=1.0):
    lane = lax.broadcasted_iota(jnp.int32, (ROWS, LANES), 1)
    vx, vy, vz = (sign * v_ref[c, rows, :] for c in range(3))
    narrow = vx.astype(BF16)
    plus_x, narrow_plus, plus_y, plus_z = vx > 0, narrow > jnp.zeros_like(narrow), vy > 0, vz > 0
    rate_x, rate_y, rate_z = (courant * jnp.abs(t) for t in (vx, vy, vz))
    stay = 1.0 - (rate_x + rate_y + rate_z)
    z_from = (lane & (LANES - NZ)) | (jnp.where(plus_z, lane - 1, lane + 1) & (NZ - 1))
    y_from = jnp.where(plus_y, lane - NZ, lane + NZ) & (LANES - 1)
    y_edge = jnp.where(plus_y, lane, LANES - 1 - lane) < NZ
    return plus_x, narrow_plus, plus_y, stay, rate_x, rate_y, rate_z, z_from, y_from, y_edge


def pick(tile, index):
    return jnp.take_along_axis(tile, index, axis=1, mode="promise_in_bounds")


def load_plane(ref, plane, rows):
    return [ref[plane, rows, columns(t)] for t in range(ref.shape[2] // LANES)]


def drift(center, before, after, geo):
    plus_x, narrow_plus, plus_y, stay, rate_x, rate_y, rate_z, z_from, y_from, y_edge = geo
    tiles = len(center)
    center = [tile.astype(F32) for tile in center]
    turned = [pick(tile, y_from) for tile in center]
    moved = []
    for t in range(tiles):
        total = stay * center[t]
        if before is not None and after is not None:
            total = total + rate_x * jnp.where(narrow_plus, before[t], after[t]).astype(F32)
        elif before is not None:
            total = total + jnp.where(plus_x, rate_x, 0.0) * before[t].astype(F32)
        elif after is not None:
            total = total + jnp.where(plus_x, 0.0, rate_x) * after[t].astype(F32)
        over = jnp.where(plus_y, turned[t - 1], turned[(t + 1) % tiles])
        total = total + rate_y * jnp.where(y_edge, over, turned[t])
        total = total + rate_z * pick(center[t], z_from)
        moved.append(total)
    return moved


def store_plane(ref, plane, rows, tiles):
    for t, tile in enumerate(tiles):
        ref[plane, rows, columns(t)] = tile.astype(ref.dtype)


def mix(matrix, moved):
    return jnp.dot(matrix, moved, preferred_element_type=F32)


def boltzmann(field):
    return jnp.exp(-0.5 * field)


def prologue_kernel(
    core_ref, species_ref, directions_ref, start_ref, fields_ref, partner_ref, spread_ref, edge_ref, coded_ref, near
):
    sign = 1.0 - 2.0 * species_ref[0].astype(F32)
    toward = sign * (1.0 - 2.0 * core_ref[0].astype(F32))
    planes, orient, cells = start_ref.shape
    low = boltzmann(fields_ref[0:1])
    high = boltzmann(fields_ref[fields_ref.shape[0] - 1 :])
    for c in range(4):
        row = directions_ref[c % 3 : c % 3 + 1]
        column = jnp.broadcast_to(row, (LANES, orient)).T
        spread_ref[c] = (toward if c == 3 else sign) * column

    @each_row_block(orient)
    def _(index):
        rows = rows_of(index)
        plus_x = spread_ref[0, rows, :] > 0
        for t in range(cells // LANES):
            at = rows, columns(t)
            chosen = jnp.where(
                plus_x,
                high[:, columns(t)] * start_ref[planes - 1, *at].astype(F32),
                low[:, columns(t)] * start_ref[0, *at].astype(F32),
            )
            edge_ref[0, *at] = chosen.astype(BF16)

    near[...] = jnp.zeros_like(near)
    for s, ref in enumerate((fields_ref, partner_ref)):
        for depth in range(2):
            high_row, low_row = (ref[p : p + 1] for p in (planes - 1 - depth, depth))
            row = jnp.where(core_ref[0] == 1, high_row, low_row)
            coarse = row.astype(BF16).astype(F32)
            at = 2 * s + depth
            near[at : at + 1] = coarse
            near[at + 4 : at + 5] = row - coarse
    coded_ref[...] = near[...].astype(BF16)


def matrix_kernel(synthesis_ref, decay_ref, analysis_ref, out_ref, turned_ref):
    rest = synthesis_ref[...].astype(F32) * decay_ref[...]
    total = jnp.full(out_ref.shape, 1.0 / out_ref.shape[1], F32)
    for _ in range(3):
        part = rest.astype(BF16)
        rest = rest - part.astype(F32)
        total = total + jnp.dot(part, analysis_ref[...], preferred_element_type=F32)
    out_ref[...] = total.astype(BF16)
    turned_ref[...] = total.T.astype(BF16)


def add_kernel(one_ref, two_ref, out_ref):
    out_ref[...] = one_ref[...] + two_ref[...]


def join_kernel(sent_ref, one_ref, two_ref, out_ref):
    planes = sent_ref.shape[0]
    out_ref[:planes] = sent_ref[...]
    out_ref[planes:] = one_ref[...] + two_ref[...]


def divide_kernel(cells, kept_ref, mine_ref, arrived_ref, out_ref):
    planes = kept_ref.shape[0]
    total = mine_ref[planes:] + arrived_ref[planes:]
    out_ref[...] = (kept_ref[...] + arrived_ref[:planes]) * (cells / total)


def message_kernel(*refs):
    count = (len(refs) - 2) // 2
    v_ref, out_ref = refs[-2:]
    orient, cells = refs[0].shape[1:]

    @each_row_block(orient)
    def _(index):
        rows = rows_of(index)
        narrow = v_ref[3, rows, :].astype(BF16)
        leaves = narrow < jnp.zeros_like(narrow)
        for p in range(count):
            for t in range(cells // LANES):
                at = 0, rows, columns(t)
                out_ref[p, rows, columns(t)] = jnp.where(leaves, refs[p][at], refs[count + p][at])

    if count > 1:
        out_ref[:, orient:] = jnp.zeros_like(out_ref[:, orient:])


def first_message_kernel(mine_ref, other_ref, *refs):
    *coded_refs, v_ref, out_ref = refs
    message_kernel(mine_ref, other_ref, v_ref, out_ref)
    orient = mine_ref.shape[1]
    for k, ref in enumerate(coded_refs):
        out_ref[0, orient + 16 * k : orient + 16 * (k + 1)] = ref[...]


def write_edge(edges_ref, step, faces, rows, v_ref):
    narrow = v_ref[0, rows, :].astype(BF16)
    plus_x = narrow > jnp.zeros_like(narrow)
    for t in range(len(faces[0])):
        edges_ref[step, rows, columns(t)] = jnp.where(plus_x, faces[-1][t], faces[0][t])


def alone_step(source_ref, moved, targets, v_ref, edges_ref, step):
    planes, orient, _ = source_ref.shape

    @each_row_block(orient)
    def _(index):
        rows = rows_of(index)
        geo = geometry(v_ref, rows)
        loaded = [load_plane(source_ref, p, rows) for p in range(planes)]
        if edges_ref is not None:
            write_edge(edges_ref, step, loaded, rows, v_ref)
        for p in targets:
            before = loaded[p - 1] if p > 0 else None
            after = loaded[p + 1] if p < planes - 1 else None
            store_plane(moved, p, rows, drift(loaded[p], before, after, geo))


def first_alone_kernel(start_ref, first_ref, v_ref, m_ref, out_ref, edges_ref, *refs):
    *inner_refs, held, moved = refs
    planes, orient, _ = start_ref.shape
    first = boltzmann(first_ref[...])
    for p in range(planes):
        held[p] = (first[p : p + 1] * start_ref[p].astype(F32)).astype(BF16)
    alone_step(held, moved, range(planes), v_ref, None, 0)
    for p in (0, planes - 1, *range(1, planes - 1)):
        state = (first[p : p + 1] * first[p : p + 1] * mix(m_ref[...], moved[p])).astype(BF16)
        out_ref[p] = state
        if 0 < p < planes - 1:
            inner_refs[p - 1][0] = state

    @each_row_block(orient)
    def _(index):
        rows = rows_of(index)
        write_edge(edges_ref, 0, [load_plane(out_ref, p, rows) for p in (0, planes - 1)], rows, v_ref)


def next_alone_kernel(state_ref, first_ref, second_ref, v_ref, m_ref, edges2_ref, edges3_ref, held, moved):
    planes, orient, _ = state_ref.shape
    first = boltzmann(first_ref[...])
    second = boltzmann(second_ref[...])
    alone_step(state_ref, moved, range(planes), v_ref, None, 0)
    for p in range(planes):
        held[p] = (first[p : p + 1] * second[p : p + 1] * mix(m_ref[...], moved[p])).astype(BF16)
    alone_step(held, moved, (0, planes - 1), v_ref, edges2_ref, 0)
    for p in (0, planes - 1):
        held[p] = (second[p : p + 1] * second[p : p + 1] * mix(m_ref[...], moved[p])).astype(BF16)

    @each_row_block(orient)
    def _(index):
        rows = rows_of(index)
        write_edge(edges3_ref, 0, [load_plane(held, p, rows) for p in (0, planes - 1)], rows, v_ref)


def face_parts(v_ref, rows):
    vx = v_ref[0, rows, :]
    rate = courant * jnp.abs(vx)
    return v_ref[3, rows, :] > 0, jnp.where(vx > 0, rate, 0.0), jnp.where(vx > 0, 0.0, rate)


def face_drifts(v_ref, mine_ref, other_ref, moved, slots):
    @each_row_block(v_ref.shape[1])
    def _(index):
        rows = rows_of(index)
        ahead, rate_plus, rate_minus = face_parts(v_ref, rows)
        for t in range(mine_ref.shape[2] // LANES):
            mine = mine_ref[0, rows, columns(t)].astype(F32)
            other = other_ref[0, rows, columns(t)].astype(F32)
            face = jnp.where(ahead, mine, other)
            moved[slots[0], rows, columns(t)] = (rate_plus * face).astype(BF16)
            moved[slots[1], rows, columns(t)] = (rate_minus * face).astype(BF16)


def second_step_kernel(
    core_ref, alone_ref, edge_ref, mine_ref, other_ref, first_ref, second_ref, v_ref, m_ref,
    face_low_ref, face_high_ref, next_ref, sent_near_ref, sent_far_ref, kept_ref, outer_ref, held, moved,
):
    planes, orient, _ = alone_ref.shape
    matrix = m_ref[...]
    first, second = boltzmann(first_ref[...]), boltzmann(second_ref[...])
    core = core_ref[0]
    mine, other = (block[:4] + block[4:8] for block in (ref[0, orient:].astype(F32) for ref in (mine_ref, other_ref)))
    other = (other[2:4], other[0:2])
    mine = (mine[0:2], mine[2:4])
    low = [jnp.where(core == 0, mine[k], other[k]) for k in range(2)]
    high = [jnp.where(core == 0, other[k], mine[k]) for k in range(2)]
    beyond = [boltzmann(block[k : k + 1]) for block in (low[0], high[0], low[1], high[1]) for k in range(2)]
    face_drifts(v_ref, mine_ref, other_ref, moved, (0, 1))

    @each_row_block(orient)
    def _(index):
        rows = rows_of(index)
        _, rate_plus, rate_minus = face_parts(v_ref, rows)
        for t in range(edge_ref.shape[2] // LANES):
            edge = edge_ref[0, rows, columns(t)].astype(F32)
            moved[2, rows, columns(t)] = (rate_minus * edge).astype(BF16)
            moved[3, rows, columns(t)] = (rate_plus * edge).astype(BF16)

    squared = first * first
    for p in range(planes):
        kept = alone_ref[p]
        if p in (0, planes - 1):
            arrived = squared[p : p + 1] * mix(matrix, moved[min(p, 1)])
            kept = (kept.astype(F32) + arrived).astype(BF16)
            (face_high_ref if p else face_low_ref)[0] = kept
        held[p + 1] = kept
    held[0] = (beyond[0] * beyond[0] * mix(matrix, moved[2])).astype(BF16)
    held[planes + 1] = (beyond[2] * beyond[2] * mix(matrix, moved[3])).astype(BF16)
    count = planes + 2

    @each_row_block(orient)
    def _(index):
        rows = rows_of(index)
        geo = geometry(v_ref, rows)
        _, rate_plus, rate_minus = face_parts(v_ref, rows)
        loaded = [load_plane(held, p, rows) for p in range(count)]
        for p in range(count):
            before = loaded[p - 1] if p > 0 else None
            after = loaded[p + 1] if p < count - 1 else None
            store_plane(moved, p + 1, rows, drift(loaded[p], before, after, geo))
        store_plane(moved, 0, rows, [rate_minus * tile.astype(F32) for tile in loaded[0]])
        store_plane(moved, count + 1, rows, [rate_plus * tile.astype(F32) for tile in loaded[-1]])

    cross = first * second
    factors = [beyond[1] * beyond[5], beyond[0] * beyond[4]]
    factors += [cross[p : p + 1] for p in range(planes)]
    factors += [beyond[2] * beyond[6], beyond[3] * beyond[7]]
    for p, factor in enumerate(factors):
        next_ref[p] = (factor * mix(matrix, moved[p])).astype(BF16)
    for p in range(planes // 2):
        sent_ref = (sent_near_ref, sent_far_ref)[p]
        sent_ref[0] = next_ref[2 + (planes - 1) * (1 - core) + (2 * core - 1) * p]
        kept_ref[p] = next_ref[2 + (planes - 1) * core + (1 - 2 * core) * p]
    outer_ref[0:1] = beyond[4] * beyond[4]
    outer_ref[1:2] = beyond[6] * beyond[6]


def middle_kernel(
    core_ref, own_ref, near_ref, far_ref, message_ref, first_ref, second_ref, v_ref, m_ref, out_ref, total_ref, moved
):
    _, orient, cells = own_ref.shape
    planes = first_ref.shape[0]

    def cross_of(depth):
        low, high = (
            boltzmann(first_ref[p : p + 1]) * boltzmann(second_ref[p : p + 1]) for p in (depth, planes - 1 - depth)
        )
        return jnp.where(core_ref[0] == 0, low, high)

    cross = [cross_of(depth) for depth in range(2)]

    @each_row_block(orient)
    def _(index):
        rows = rows_of(index)
        ahead, rate_plus, rate_minus = face_parts(v_ref, rows)
        rate = rate_plus + rate_minus
        for t in range(cells // LANES):
            gained = rate * message_ref[0, rows, columns(t)].astype(F32)
            moved[0, rows, columns(t)] = jnp.where(ahead, gained, 0.0).astype(BF16)
            moved[1, rows, columns(t)] = jnp.where(ahead, 0.0, gained).astype(BF16)

    own_face = own_ref[0].astype(F32) + cross[0] * mix(m_ref[...], moved[0])
    partner_face = near_ref[0].astype(F32) + cross[0] * mix(m_ref[...], moved[1])
    face = jnp.sum(own_face * partner_face, axis=0, keepdims=True)
    total = jnp.zeros((1, 1), F32)
    for p in range(own_ref.shape[0]):
        if p > 0:
            face = jnp.sum(own_ref[p].astype(F32) * far_ref[0].astype(F32), axis=0, keepdims=True)
        met = face / (orient * cross[p])
        out_ref[p : p + 1] = met
        total = total + jnp.sum(met, axis=1, keepdims=True)
    total_ref[...] = jnp.broadcast_to(total, total_ref.shape)


def third_step_kernel(
    held_ref, mine_ref, other_ref, first_ref, second_ref, outer_ref, v_ref, m_ref, next_ref, held, moved
):
    planes, orient, _ = held.shape
    matrix = m_ref[...]
    first, second = boltzmann(first_ref[...]), boltzmann(second_ref[...])
    face_drifts(v_ref, mine_ref, other_ref, moved, (0, 1))
    cross = first * second
    for p in range(planes):
        kept = held_ref[p + 2]
        if p in (0, planes - 1):
            arrived = cross[p : p + 1] * mix(matrix, moved[min(p, 1)])
            kept = (kept.astype(F32) + arrived).astype(BF16)
        held[p] = kept

    @each_row_block(orient)
    def _(index):
        rows = rows_of(index)
        geo = geometry(v_ref, rows)
        loaded = [load_plane(held_ref, p, rows) for p in (0, 1)]
        loaded += [load_plane(held, p, rows) for p in range(planes)]
        loaded += [load_plane(held_ref, p, rows) for p in (planes + 2, planes + 3)]
        for p in range(planes + 2):
            store_plane(moved, p, rows, drift(loaded[p + 1], loaded[p], loaded[p + 2], geo))

    squared = second * second
    factors = [outer_ref[0:1]] + [squared[p : p + 1] for p in range(planes)] + [outer_ref[1:2]]
    for p, factor in enumerate(factors):
        next_ref[p] = (factor * mix(matrix, moved[p])).astype(BF16)


def weight_kernel(core_ref, partner_ref, start_ref, turned_ref, weight_ref, own_ref):
    planes = partner_ref.shape[0]
    core = core_ref[0]
    for p in range(planes):
        weight_ref[p] = mix(turned_ref[...], partner_ref[p]).astype(BF16)
    for p in range(2):
        own_ref[p] = mix(turned_ref[...], start_ref[core * (planes - 1) + p - 2 * p * core]).astype(BF16)


def fold(value):
    return jnp.sum(value.reshape(ROWS // 8, 8, LANES), axis=0)


def pairing_kernel(held_ref, second_ref, v_ref, weight_ref, *refs):
    *partner_refs, out_ref = refs
    planes, orient, cells = weight_ref.shape
    second = boltzmann(second_ref[...])
    tiles = cells // LANES

    def body(index, sums):
        rows = rows_of(index)
        geo = geometry(v_ref, rows)
        loaded = [load_plane(held_ref, p, rows) for p in range(planes + 2)]
        new = []
        for p in range(planes):
            moved_tiles = drift(loaded[p + 1], loaded[p], loaded[p + 2], geo)
            weights = load_plane(weight_ref, p, rows)
            partner = load_plane(partner_refs[p], 0, rows)
            for t in range(tiles):
                last, third = sums[2 * (p * tiles + t)], sums[2 * (p * tiles + t) + 1]
                new.append(last + fold(moved_tiles[t] * weights[t].astype(F32)))
                new.append(third + fold(loaded[p + 1][t].astype(F32) * partner[t].astype(F32)))
        return tuple(new)

    zero = jnp.zeros((8, LANES), F32)
    sums = lax.fori_loop(0, orient // ROWS, body, (zero,) * (2 * planes * tiles), unroll=UNROLL)
    for p in range(planes):
        for t in range(tiles):
            last = jnp.sum(sums[2 * (p * tiles + t)], axis=0, keepdims=True)
            third = jnp.sum(sums[2 * (p * tiles + t) + 1], axis=0, keepdims=True)
            factor = second[p : p + 1, columns(t)]
            out_ref[p : p + 1, columns(t)] = (0.5 * factor * last + third / (factor * factor)) / orient


def last_kernel(
    core_ref, message_ref, weight_ref, own_weight_ref, own_low_ref, own_high_ref, partner_low_ref, partner_high_ref,
    shared_ref, met_ref,    own_ref, partner_ref, v_ref, m_ref, sent_ref, kept_ref, moved, gained,
):
    planes, cells = shared_ref.shape
    orient = m_ref.shape[0]
    tiles = cells // LANES
    core = core_ref[0]
    half = planes // 2
    face = core * (planes - 1)
    inner = face + 1 - 2 * core

    def at_face(ref, depth):
        return jnp.where(core == 0, boltzmann(ref[depth : depth + 1]), boltzmann(ref[planes - 1 - depth : planes - depth]))

    factors = [[at_face(ref, depth) for depth in range(2)] for ref in (partner_ref, own_ref)]

    @each_row_block(orient)
    def _(index):
        rows = rows_of(index)
        ahead, rate_plus, rate_minus = face_parts(v_ref, rows)
        rate = rate_plus + rate_minus
        for t in range(tiles):
            got = rate * message_ref[0, rows, columns(t)].astype(F32)
            moved[0, rows, columns(t)] = jnp.where(ahead, got, 0.0).astype(BF16)
            moved[1, rows, columns(t)] = jnp.where(ahead, 0.0, got).astype(BF16)

    for s in range(2):
        gained[s] = (factors[s][0] * factors[s][0] * mix(m_ref[...], moved[s])).astype(BF16)

    def body(index, sums):
        rows = rows_of(index)
        ahead, rate_plus, rate_minus = face_parts(v_ref, rows)
        rate = rate_plus + rate_minus
        sides = (jnp.where(ahead, rate, 0.0), jnp.where(ahead, 0.0, rate))
        message = load_plane(message_ref, 1, rows)
        new = []
        for s in range(2):
            change = load_plane(gained, s, rows)
            moved_tiles = drift(change, None, None, geometry(v_ref, rows, 1.0 - 2.0 * s))
            if s == 0:
                weights = [load_plane(weight_ref, p, rows) for p in (face, inner)]
            else:
                weights = [load_plane(own_weight_ref, p, rows) for p in (0, 1)]
            pair = ((partner_low_ref, partner_high_ref), (own_low_ref, own_high_ref))[s]
            third = [jnp.where(core == 0, low, high) for low, high in zip(*(load_plane(ref, 0, rows) for ref in pair))]
            for t in range(tiles):
                on_face = moved_tiles[t] + sides[s] * message[t].astype(F32)
                wide = change[t].astype(F32)
                terms = (
                    on_face * weights[0][t].astype(F32),
                    sides[s] * wide * weights[1][t].astype(F32),
                    wide * third[t].astype(F32),
                )
                base = 3 * (s * tiles + t)
                new += [sums[base + k] + fold(term) for k, term in enumerate(terms)]
        return tuple(new)

    zero = jnp.zeros((8, LANES), F32)
    sums = lax.fori_loop(0, orient // ROWS, body, (zero,) * (6 * tiles), unroll=UNROLL)
    for t in range(tiles):
        shares = []
        for s in range(2):
            base = 3 * (s * tiles + t)
            last, onward, third = (jnp.sum(sums[base + k], axis=0, keepdims=True) / orient for k in range(3))
            near, far = (factors[s][depth][:, columns(t)] for depth in range(2))
            shares.append((0.5 * near * last + third / (near * near), 0.5 * far * onward))
        for p in range(planes):
            at = slice(p, p + 1), columns(t)
            mine = core == (0 if p < half else 1)
            depth = min(p, planes - 1 - p)
            met = jnp.where(mine, 0.5 * met_ref[depth : depth + 1, columns(t)], 0.0)
            sent, kept = shared_ref[at] + met, met
            if depth < 2:
                sent = sent + jnp.where(mine, shares[0][depth], 0.0)
                kept = kept + jnp.where(mine, shares[1][depth], 0.0)
            sent_ref[at] = sent
            kept_ref[at] = kept


def split_outputs(outs):
    low, high, state, near, far, kept, outer = outs
    return (low, high), state, (near, far), kept, outer


def kernel_call(kernel, outs, scratch, args):
    vmem = pl.BlockSpec(memory_space=pltpu.VMEM)
    smem = pl.BlockSpec(memory_space=pltpu.SMEM)
    return pl.pallas_call(
        kernel,
        out_shape=outs,
        in_specs=[smem if arg.dtype == jnp.int32 else vmem for arg in args],
        out_specs=jax.tree.map(lambda _: vmem, outs),
        scratch_shapes=[pltpu.VMEM(*s) if len(s) == 2 else pltpu.VMEM(s, BF16) for s in scratch],
        compiler_params=pltpu.CompilerParams(vmem_limit_bytes=12 << 20),
        cost_estimate=pl.CostEstimate(flops=0, bytes_accessed=0, transcendentals=0),
    )(*args)


def shards(fields, end_weights, directions, analysis, synthesis, decay_rates):
    device = lax.axis_index("space")
    core = device % 2
    planes, cells = fields.shape
    orient = end_weights.shape[0]
    plane_index = device // 2 * planes + lax.broadcasted_iota(jnp.int32, (planes, 1), 0)
    ramp = slope * plane_index.astype(F32) / (planes * lax.axis_size("space") // 2)
    own = fields + ramp
    partner = swap_species(fields) + ramp

    wide = lambda extra: jax.ShapeDtypeStruct((planes + extra, orient, cells), BF16)
    slab, plane = wide(0), wide(1 - planes)
    face = core ^ (1 - device // 2 % 2)
    core_word = jnp.reshape(face, (1,)).astype(jnp.int32)
    species_word = jnp.reshape(core, (1,)).astype(jnp.int32)
    start = jnp.transpose(end_weights, (1, 0, 2))
    spread, edge0, coded = kernel_call(
        prologue_kernel,
        (jax.ShapeDtypeStruct((4, orient, LANES), F32), plane, jax.ShapeDtypeStruct((16, cells), BF16)),
        (((16, cells), F32),),
        (core_word, species_word, directions, start, own, partner),
    )
    matrix, turned = kernel_call(
        matrix_kernel,
        (jax.ShapeDtypeStruct((orient, orient), BF16),) * 2,
        (),
        (synthesis, decay_rates[None], analysis),
    )
    other0, matrix = lax.optimization_barrier((swap_species(edge0), matrix))
    message0 = kernel_call(
        first_message_kernel,
        jax.ShapeDtypeStruct((1, orient + 16, cells), BF16),
        (),
        (edge0, other0, coded, spread),
    )

    def message(blocks, others):
        shape = jax.ShapeDtypeStruct((len(blocks), orient + PAD_ROWS, cells), BF16)
        return kernel_call(message_kernel, shape, (), (*blocks, *others, spread))

    start, _ = lax.optimization_barrier((start, message0))
    arrived0 = exchange_faces(message0)
    alone, edges1, *inner = kernel_call(
        first_alone_kernel,
        (slab, plane) + (plane,) * (planes - 2),
        (slab.shape, slab.shape),
        (start, own, spread, matrix),
    )
    weights, own_weights = kernel_call(
        weight_kernel, (slab, wide(2 - planes)), (), (core_word, swap_species(start), start, turned)
    )
    others1, weights, *partner_inner = lax.optimization_barrier(
        (swap_species(edges1), weights, *map(swap_species, inner))
    )
    message1 = kernel_call(
        first_message_kernel,
        jax.ShapeDtypeStruct((1, orient + 16 * PAD, cells), BF16),
        (),
        (edges1, others1, *[coded] * PAD, spread),
    )
    state, *_ = lax.optimization_barrier((alone, message1, weights))
    edges2, edges3 = kernel_call(
        next_alone_kernel, (plane, plane), (slab.shape, slab.shape), (state, own, partner, spread, matrix)
    )
    edges2, edges3, arrived0 = lax.optimization_barrier((edges2, edges3, arrived0))
    message2 = message([edges2, edges3], [swap_species(edges2), swap_species(edges3)])
    arrived = [exchange_faces(message1), exchange_faces(message2)]
    crossed0 = swap_species(arrived0)

    alone, *_ = lax.optimization_barrier((alone, message1, message2))
    half = planes // 2
    faces, second_state, sent_half, kept_half, outer = split_outputs(
        kernel_call(
            second_step_kernel,
            (plane, plane, wide(4), plane, plane, wide(half - planes), jax.ShapeDtypeStruct((2, cells), F32)),
            (wide(2).shape, wide(4).shape),
            (core_word, alone, edge0, arrived0, crossed0, own, partner, spread, matrix),
        )
    )
    arrived1, second_state = lax.optimization_barrier((arrived[0], second_state))
    *moving, _ = lax.optimization_barrier((*sent_half, arrived1))
    *partner_half, crossed1 = lax.optimization_barrier((*map(swap_species, moving), swap_species(arrived1)))
    density = jax.ShapeDtypeStruct((planes, cells), F32)
    met, partition = kernel_call(
        middle_kernel,
        (jax.ShapeDtypeStruct((half, cells), F32), density),
        ((2, orient, cells),),
        (core_word, kept_half, *partner_half, arrived1, own, partner, spread, matrix),
    )
    count = lax.axis_size("space")

    def received(value, distance, after):
        block = lax.ppermute(value, "space", [(i, i ^ distance) for i in range(count)])
        return lax.optimization_barrier((block, after))

    def gathered(value, distance, after):
        block, after = received(value, distance, after)
        return kernel_call(add_kernel, density, (), (value, block)), after

    *faces, second_state, _ = lax.optimization_barrier((*faces, second_state, met))
    partner_faces = [swap_species(block) for block in faces]
    third_state = kernel_call(
        third_step_kernel,
        wide(2),
        (slab.shape, wide(2).shape),
        (second_state, arrived1, crossed1, own, partner, outer, spread, matrix),
    )
    partition, third_state = gathered(partition, 4, third_state)
    third_state, _ = lax.optimization_barrier((third_state, partition))
    shared = kernel_call(
        pairing_kernel,
        density,
        (),
        (third_state, partner, spread, weights, partner_faces[0], *partner_inner, partner_faces[1]),
    )
    distance = 8
    while distance < count:
        partition, shared = gathered(partition, distance, shared)
        distance *= 2
    arrived2, shared, _ = lax.optimization_barrier((arrived[1], shared, partition))
    sent, kept = kernel_call(
        last_kernel,
        (density, density),
        ((2, orient, cells), (2, orient, cells)),
        (
            core_word, arrived2, weights, own_weights, *faces, *partner_faces, shared, met,
            own, partner, spread, matrix,
        ),
    )
    beside, sent = received(partition, 2, sent)
    joined = kernel_call(
        join_kernel, jax.ShapeDtypeStruct((2 * planes, cells), F32), (), (sent, partition, beside)
    )
    return kernel_call(
        functools.partial(divide_kernel, count // 2 * planes * cells),
        density,
        (),
        (kept, joined, swap_species(joined)),
    )


def solution(mesh):
    return jax.shard_map(
        shards,
        mesh=mesh,
        in_specs=(P(("runs", "space"), None), P(None, ("runs", "space"), None), P(), P(), P(), P()),
        out_specs=P(("runs", "space"), None),
        check_vma=False,
    )
```

```python
import functools

import jax
import jax.numpy as jnp
from jax import lax
from jax.experimental import pallas as pl
from jax.experimental.pallas import tpu as pltpu
from jax.sharding import PartitionSpec as P

NZ = 16
STEPS = 4
LANES = 128
ROWS = 16
UNROLL = 16
PAD = 2
PAD_ROWS = 32

courant = 0.3
slope = 0.6

BF16 = jnp.bfloat16
F32 = jnp.float32


def swap_species(block):
    count = lax.axis_size("space")
    return lax.ppermute(block, "space", [(i ^ 1, i) for i in range(count)])


def exchange_faces(block):
    count = lax.axis_size("space")
    route = []
    for slab in range(count // 2):
        beside = ((slab + 1) ^ 1) - 1
        route += [(2 * slab, 2 * (slab ^ 1)), (2 * slab + 1, 2 * beside % count + 1)]
    return lax.ppermute(block, "space", route)


def rows_of(index):
    return pl.ds(pl.multiple_of(index * ROWS, ROWS), ROWS)


def each_row_block(orient):
    def run(body):
        def step(index, carry):
            body(index)
            return carry

        lax.fori_loop(0, orient // ROWS, step, 0, unroll=UNROLL)

    return run


def columns(tile):
    return slice(LANES * tile, LANES * (tile + 1))


def geometry(v_ref, rows, sign=1.0):
    lane = lax.broadcasted_iota(jnp.int32, (ROWS, LANES), 1)
    vx, vy, vz = (sign * v_ref[c, rows, :] for c in range(3))
    narrow = vx.astype(BF16)
    plus_x, narrow_plus, plus_y, plus_z = vx > 0, narrow > jnp.zeros_like(narrow), vy > 0, vz > 0
    rate_x, rate_y, rate_z = (courant * jnp.abs(t) for t in (vx, vy, vz))
    stay = 1.0 - (rate_x + rate_y + rate_z)
    z_from = (lane & (LANES - NZ)) | (jnp.where(plus_z, lane - 1, lane + 1) & (NZ - 1))
    y_from = jnp.where(plus_y, lane - NZ, lane + NZ) & (LANES - 1)
    y_edge = jnp.where(plus_y, lane, LANES - 1 - lane) < NZ
    return plus_x, narrow_plus, plus_y, stay, rate_x, rate_y, rate_z, z_from, y_from, y_edge


def pick(tile, index):
    return jnp.take_along_axis(tile, index, axis=1, mode="promise_in_bounds")


def load_plane(ref, plane, rows):
    return [ref[plane, rows, columns(t)] for t in range(ref.shape[2] // LANES)]


def drift(center, before, after, geo):
    plus_x, narrow_plus, plus_y, stay, rate_x, rate_y, rate_z, z_from, y_from, y_edge = geo
    tiles = len(center)
    center = [tile.astype(F32) for tile in center]
    turned = [pick(tile, y_from) for tile in center]
    moved = []
    for t in range(tiles):
        total = stay * center[t]
        if before is not None and after is not None:
            total = total + rate_x * jnp.where(narrow_plus, before[t], after[t]).astype(F32)
        elif before is not None:
            total = total + jnp.where(plus_x, rate_x, 0.0) * before[t].astype(F32)
        elif after is not None:
            total = total + jnp.where(plus_x, 0.0, rate_x) * after[t].astype(F32)
        over = jnp.where(plus_y, turned[t - 1], turned[(t + 1) % tiles])
        total = total + rate_y * jnp.where(y_edge, over, turned[t])
        total = total + rate_z * pick(center[t], z_from)
        moved.append(total)
    return moved


def store_plane(ref, plane, rows, tiles):
    for t, tile in enumerate(tiles):
        ref[plane, rows, columns(t)] = tile.astype(ref.dtype)


def mix(matrix, moved):
    return jnp.dot(matrix, moved, preferred_element_type=F32)


def boltzmann(field):
    return jnp.exp(-0.5 * field)


def prologue_kernel(
    core_ref, species_ref, directions_ref, start_ref, fields_ref, partner_ref, spread_ref, edge_ref, coded_ref, near
):
    sign = 1.0 - 2.0 * species_ref[0].astype(F32)
    toward = sign * (1.0 - 2.0 * core_ref[0].astype(F32))
    planes, orient, cells = start_ref.shape
    low = boltzmann(fields_ref[0:1])
    high = boltzmann(fields_ref[fields_ref.shape[0] - 1 :])
    for c in range(4):
        row = directions_ref[c % 3 : c % 3 + 1]
        column = jnp.broadcast_to(row, (LANES, orient)).T
        spread_ref[c] = (toward if c == 3 else sign) * column

    @each_row_block(orient)
    def _(index):
        rows = rows_of(index)
        plus_x = spread_ref[0, rows, :] > 0
        for t in range(cells // LANES):
            at = rows, columns(t)
            chosen = jnp.where(
                plus_x,
                high[:, columns(t)] * start_ref[planes - 1, *at].astype(F32),
                low[:, columns(t)] * start_ref[0, *at].astype(F32),
            )
            edge_ref[0, *at] = chosen.astype(BF16)

    near[...] = jnp.zeros_like(near)
    for s, ref in enumerate((fields_ref, partner_ref)):
        for depth in range(2):
            high_row, low_row = (ref[p : p + 1] for p in (planes - 1 - depth, depth))
            row = jnp.where(core_ref[0] == 1, high_row, low_row)
            coarse = row.astype(BF16).astype(F32)
            at = 2 * s + depth
            near[at : at + 1] = coarse
            near[at + 4 : at + 5] = row - coarse
    coded_ref[...] = near[...].astype(BF16)


def matrix_kernel(synthesis_ref, decay_ref, analysis_ref, out_ref, turned_ref):
    rest = synthesis_ref[...].astype(F32) * decay_ref[...]
    total = jnp.full(out_ref.shape, 1.0 / out_ref.shape[1], F32)
    for _ in range(3):
        part = rest.astype(BF16)
        rest = rest - part.astype(F32)
        total = total + jnp.dot(part, analysis_ref[...], preferred_element_type=F32)
    out_ref[...] = total.astype(BF16)
    turned_ref[...] = total.T.astype(BF16)


def add_kernel(one_ref, two_ref, out_ref):
    out_ref[...] = one_ref[...] + two_ref[...]


def join_kernel(sent_ref, one_ref, two_ref, out_ref):
    planes = sent_ref.shape[0]
    out_ref[:planes] = sent_ref[...]
    out_ref[planes:] = one_ref[...] + two_ref[...]


def divide_kernel(cells, kept_ref, mine_ref, arrived_ref, out_ref):
    planes = kept_ref.shape[0]
    total = mine_ref[planes:] + arrived_ref[planes:]
    out_ref[...] = (kept_ref[...] + arrived_ref[:planes]) * (cells / total)


def message_kernel(*refs):
    count = (len(refs) - 2) // 2
    v_ref, out_ref = refs[-2:]
    orient, cells = refs[0].shape[1:]

    @each_row_block(orient)
    def _(index):
        rows = rows_of(index)
        narrow = v_ref[3, rows, :].astype(BF16)
        leaves = narrow < jnp.zeros_like(narrow)
        for p in range(count):
            for t in range(cells // LANES):
                at = 0, rows, columns(t)
                out_ref[p, rows, columns(t)] = jnp.where(leaves, refs[p][at], refs[count + p][at])

    if count > 1:
        out_ref[:, orient:] = jnp.zeros_like(out_ref[:, orient:])


def first_message_kernel(mine_ref, other_ref, *refs):
    *coded_refs, v_ref, out_ref = refs
    message_kernel(mine_ref, other_ref, v_ref, out_ref)
    orient = mine_ref.shape[1]
    for k, ref in enumerate(coded_refs):
        out_ref[0, orient + 16 * k : orient + 16 * (k + 1)] = ref[...]


def write_edge(edges_ref, step, faces, rows, v_ref):
    narrow = v_ref[0, rows, :].astype(BF16)
    plus_x = narrow > jnp.zeros_like(narrow)
    for t in range(len(faces[0])):
        edges_ref[step, rows, columns(t)] = jnp.where(plus_x, faces[-1][t], faces[0][t])


def alone_step(source_ref, moved, targets, v_ref, edges_ref, step):
    planes, orient, _ = source_ref.shape

    @each_row_block(orient)
    def _(index):
        rows = rows_of(index)
        geo = geometry(v_ref, rows)
        loaded = [load_plane(source_ref, p, rows) for p in range(planes)]
        if edges_ref is not None:
            write_edge(edges_ref, step, loaded, rows, v_ref)
        for p in targets:
            before = loaded[p - 1] if p > 0 else None
            after = loaded[p + 1] if p < planes - 1 else None
            store_plane(moved, p, rows, drift(loaded[p], before, after, geo))


def first_alone_kernel(start_ref, first_ref, v_ref, m_ref, out_ref, edges_ref, *refs):
    *inner_refs, held, moved = refs
    planes, orient, _ = start_ref.shape
    first = boltzmann(first_ref[...])
    for p in range(planes):
        held[p] = (first[p : p + 1] * start_ref[p].astype(F32)).astype(BF16)
    alone_step(held, moved, range(planes), v_ref, None, 0)
    for p in (0, planes - 1, *range(1, planes - 1)):
        state = (first[p : p + 1] * first[p : p + 1] * mix(m_ref[...], moved[p])).astype(BF16)
        out_ref[p] = state
        if 0 < p < planes - 1:
            inner_refs[p - 1][0] = state

    @each_row_block(orient)
    def _(index):
        rows = rows_of(index)
        write_edge(edges_ref, 0, [load_plane(out_ref, p, rows) for p in (0, planes - 1)], rows, v_ref)


def next_alone_kernel(
    state_ref, first_ref, second_ref, v_ref, m_ref, out_ref, edges2_ref, edges3_ref, held, moved
):
    planes, orient, _ = state_ref.shape
    first = boltzmann(first_ref[...])
    second = boltzmann(second_ref[...])
    alone_step(state_ref, moved, range(planes), v_ref, None, 0)
    for p in range(planes):
        out_ref[p] = (first[p : p + 1] * second[p : p + 1] * mix(m_ref[...], moved[p])).astype(BF16)
    alone_step(out_ref, moved, (0, planes - 1), v_ref, edges2_ref, 0)
    for p in (0, planes - 1):
        held[p] = (second[p : p + 1] * second[p : p + 1] * mix(m_ref[...], moved[p])).astype(BF16)

    @each_row_block(orient)
    def _(index):
        rows = rows_of(index)
        write_edge(edges3_ref, 0, [load_plane(held, p, rows) for p in (0, planes - 1)], rows, v_ref)


def face_parts(v_ref, rows):
    vx = v_ref[0, rows, :]
    rate = courant * jnp.abs(vx)
    return v_ref[3, rows, :] > 0, jnp.where(vx > 0, rate, 0.0), jnp.where(vx > 0, 0.0, rate)


def face_drifts(v_ref, mine_ref, other_ref, moved, slots):
    @each_row_block(v_ref.shape[1])
    def _(index):
        rows = rows_of(index)
        ahead, rate_plus, rate_minus = face_parts(v_ref, rows)
        for t in range(mine_ref.shape[2] // LANES):
            mine = mine_ref[0, rows, columns(t)].astype(F32)
            other = other_ref[0, rows, columns(t)].astype(F32)
            face = jnp.where(ahead, mine, other)
            moved[slots[0], rows, columns(t)] = (rate_plus * face).astype(BF16)
            moved[slots[1], rows, columns(t)] = (rate_minus * face).astype(BF16)


def second_step_kernel(
    core_ref, alone_ref, later_ref, edge_ref, mine_ref, other_ref, first_ref, second_ref, v_ref, m_ref,
    face_low_ref, face_high_ref, next_ref, sent_near_ref, sent_far_ref, kept_ref, outer_ref, held, moved,
):
    planes, orient, _ = alone_ref.shape
    matrix = m_ref[...]
    first, second = boltzmann(first_ref[...]), boltzmann(second_ref[...])
    core = core_ref[0]
    mine, other = (block[:4] + block[4:8] for block in (ref[0, orient:].astype(F32) for ref in (mine_ref, other_ref)))
    other = (other[2:4], other[0:2])
    mine = (mine[0:2], mine[2:4])
    low = [jnp.where(core == 0, mine[k], other[k]) for k in range(2)]
    high = [jnp.where(core == 0, other[k], mine[k]) for k in range(2)]
    beyond = [boltzmann(block[k : k + 1]) for block in (low[0], high[0], low[1], high[1]) for k in range(2)]
    face_drifts(v_ref, mine_ref, other_ref, moved, (0, 1))

    @each_row_block(orient)
    def _(index):
        rows = rows_of(index)
        _, rate_plus, rate_minus = face_parts(v_ref, rows)
        for t in range(edge_ref.shape[2] // LANES):
            edge = edge_ref[0, rows, columns(t)].astype(F32)
            moved[2, rows, columns(t)] = (rate_minus * edge).astype(BF16)
            moved[3, rows, columns(t)] = (rate_plus * edge).astype(BF16)

    squared = first * first
    for p, slot, face_ref in ((0, 1, face_low_ref), (planes - 1, 2, face_high_ref)):
        arrived = squared[p : p + 1] * mix(matrix, moved[slot - 1])
        held[slot] = arrived.astype(BF16)
        face_ref[0] = (alone_ref[p].astype(F32) + arrived).astype(BF16)
    held[0] = (beyond[0] * beyond[0] * mix(matrix, moved[2])).astype(BF16)
    held[3] = (beyond[2] * beyond[2] * mix(matrix, moved[3])).astype(BF16)

    @each_row_block(orient)
    def _(index):
        rows = rows_of(index)
        geo = geometry(v_ref, rows)
        _, rate_plus, rate_minus = face_parts(v_ref, rows)
        below, low, high, above = (load_plane(held, p, rows) for p in range(4))
        face_low, face_high = (load_plane(ref, 0, rows) for ref in (face_low_ref, face_high_ref))

        def onward(rate, tiles):
            return [rate * tile.astype(F32) for tile in tiles]

        store_plane(moved, 0, rows, onward(rate_minus, below))
        store_plane(moved, 1, rows, drift(below, None, face_low, geo))
        store_plane(moved, 2, rows, drift(low, below, None, geo))
        store_plane(moved, 3, rows, onward(rate_plus, low))
        store_plane(moved, 4, rows, onward(rate_minus, high))
        store_plane(moved, 5, rows, drift(high, None, above, geo))
        store_plane(moved, 6, rows, drift(above, face_high, None, geo))
        store_plane(moved, 7, rows, onward(rate_plus, above))

    cross = first * second
    outer = ((0, 0, beyond[1] * beyond[5]), (1, 1, beyond[0] * beyond[4]))
    outer += ((planes + 2, 6, beyond[2] * beyond[6]), (planes + 3, 7, beyond[3] * beyond[7]))
    for p, slot, factor in outer:
        next_ref[p] = (factor * mix(matrix, moved[slot])).astype(BF16)
    slots = {0: 2, 1: 3, planes - 2: 4, planes - 1: 5}
    for p in range(planes):
        kept = later_ref[p]
        if p in slots:
            kept = (kept.astype(F32) + cross[p : p + 1] * mix(matrix, moved[slots[p]])).astype(BF16)
        next_ref[p + 2] = kept
    for p in range(planes // 2):
        sent_ref = (sent_near_ref, sent_far_ref)[p]
        sent_ref[0] = next_ref[2 + (planes - 1) * (1 - core) + (2 * core - 1) * p]
        kept_ref[p] = next_ref[2 + (planes - 1) * core + (1 - 2 * core) * p]
    outer_ref[0:1] = beyond[4] * beyond[4]
    outer_ref[1:2] = beyond[6] * beyond[6]


def middle_kernel(
    core_ref, own_ref, near_ref, far_ref, message_ref, first_ref, second_ref, v_ref, m_ref, out_ref, total_ref, moved
):
    _, orient, cells = own_ref.shape
    planes = first_ref.shape[0]

    def cross_of(depth):
        low, high = (
            boltzmann(first_ref[p : p + 1]) * boltzmann(second_ref[p : p + 1]) for p in (depth, planes - 1 - depth)
        )
        return jnp.where(core_ref[0] == 0, low, high)

    cross = [cross_of(depth) for depth in range(2)]

    @each_row_block(orient)
    def _(index):
        rows = rows_of(index)
        ahead, rate_plus, rate_minus = face_parts(v_ref, rows)
        rate = rate_plus + rate_minus
        for t in range(cells // LANES):
            gained = rate * message_ref[0, rows, columns(t)].astype(F32)
            moved[0, rows, columns(t)] = jnp.where(ahead, gained, 0.0).astype(BF16)
            moved[1, rows, columns(t)] = jnp.where(ahead, 0.0, gained).astype(BF16)

    own_face = own_ref[0].astype(F32) + cross[0] * mix(m_ref[...], moved[0])
    partner_face = near_ref[0].astype(F32) + cross[0] * mix(m_ref[...], moved[1])
    face = jnp.sum(own_face * partner_face, axis=0, keepdims=True)
    total = jnp.zeros((1, 1), F32)
    for p in range(own_ref.shape[0]):
        if p > 0:
            face = jnp.sum(own_ref[p].astype(F32) * far_ref[0].astype(F32), axis=0, keepdims=True)
        met = face / (orient * cross[p])
        out_ref[p : p + 1] = met
        total = total + jnp.sum(met, axis=1, keepdims=True)
    total_ref[...] = jnp.broadcast_to(total, total_ref.shape)


def third_step_kernel(
    held_ref, mine_ref, other_ref, first_ref, second_ref, outer_ref, v_ref, m_ref, next_ref, held, moved
):
    planes, orient, _ = held.shape
    matrix = m_ref[...]
    first, second = boltzmann(first_ref[...]), boltzmann(second_ref[...])
    face_drifts(v_ref, mine_ref, other_ref, moved, (0, 1))
    cross = first * second
    for p in range(planes):
        kept = held_ref[p + 2]
        if p in (0, planes - 1):
            arrived = cross[p : p + 1] * mix(matrix, moved[min(p, 1)])
            kept = (kept.astype(F32) + arrived).astype(BF16)
        held[p] = kept

    @each_row_block(orient)
    def _(index):
        rows = rows_of(index)
        geo = geometry(v_ref, rows)
        loaded = [load_plane(held_ref, p, rows) for p in (0, 1)]
        loaded += [load_plane(held, p, rows) for p in range(planes)]
        loaded += [load_plane(held_ref, p, rows) for p in (planes + 2, planes + 3)]
        for p in range(planes + 2):
            store_plane(moved, p, rows, drift(loaded[p + 1], loaded[p], loaded[p + 2], geo))

    squared = second * second
    factors = [outer_ref[0:1]] + [squared[p : p + 1] for p in range(planes)] + [outer_ref[1:2]]
    for p, factor in enumerate(factors):
        next_ref[p] = (factor * mix(matrix, moved[p])).astype(BF16)


def weight_kernel(core_ref, partner_ref, start_ref, turned_ref, weight_ref, own_ref):
    planes = partner_ref.shape[0]
    core = core_ref[0]
    for p in range(planes):
        weight_ref[p] = mix(turned_ref[...], partner_ref[p]).astype(BF16)
    for p in range(2):
        own_ref[p] = mix(turned_ref[...], start_ref[core * (planes - 1) + p - 2 * p * core]).astype(BF16)


def fold(value):
    return jnp.sum(value.reshape(ROWS // 8, 8, LANES), axis=0)


def pairing_kernel(held_ref, second_ref, v_ref, weight_ref, *refs):
    *partner_refs, out_ref = refs
    planes, orient, cells = weight_ref.shape
    second = boltzmann(second_ref[...])
    tiles = cells // LANES

    def body(index, sums):
        rows = rows_of(index)
        geo = geometry(v_ref, rows)
        loaded = [load_plane(held_ref, p, rows) for p in range(planes + 2)]
        new = []
        for p in range(planes):
            moved_tiles = drift(loaded[p + 1], loaded[p], loaded[p + 2], geo)
            weights = load_plane(weight_ref, p, rows)
            partner = load_plane(partner_refs[p], 0, rows)
            for t in range(tiles):
                last, third = sums[2 * (p * tiles + t)], sums[2 * (p * tiles + t) + 1]
                new.append(last + fold(moved_tiles[t] * weights[t].astype(F32)))
                new.append(third + fold(loaded[p + 1][t].astype(F32) * partner[t].astype(F32)))
        return tuple(new)

    zero = jnp.zeros((8, LANES), F32)
    sums = lax.fori_loop(0, orient // ROWS, body, (zero,) * (2 * planes * tiles), unroll=UNROLL)
    for p in range(planes):
        for t in range(tiles):
            last = jnp.sum(sums[2 * (p * tiles + t)], axis=0, keepdims=True)
            third = jnp.sum(sums[2 * (p * tiles + t) + 1], axis=0, keepdims=True)
            factor = second[p : p + 1, columns(t)]
            out_ref[p : p + 1, columns(t)] = (0.5 * factor * last + third / (factor * factor)) / orient


def last_kernel(
    core_ref, message_ref, weight_ref, own_weight_ref, own_low_ref, own_high_ref, partner_low_ref, partner_high_ref,
    shared_ref, met_ref,    own_ref, partner_ref, v_ref, m_ref, sent_ref, kept_ref, moved, gained,
):
    planes, cells = shared_ref.shape
    orient = m_ref.shape[0]
    tiles = cells // LANES
    core = core_ref[0]
    half = planes // 2
    face = core * (planes - 1)
    inner = face + 1 - 2 * core

    def at_face(ref, depth):
        return jnp.where(core == 0, boltzmann(ref[depth : depth + 1]), boltzmann(ref[planes - 1 - depth : planes - depth]))

    factors = [[at_face(ref, depth) for depth in range(2)] for ref in (partner_ref, own_ref)]

    @each_row_block(orient)
    def _(index):
        rows = rows_of(index)
        ahead, rate_plus, rate_minus = face_parts(v_ref, rows)
        rate = rate_plus + rate_minus
        for t in range(tiles):
            got = rate * message_ref[0, rows, columns(t)].astype(F32)
            moved[0, rows, columns(t)] = jnp.where(ahead, got, 0.0).astype(BF16)
            moved[1, rows, columns(t)] = jnp.where(ahead, 0.0, got).astype(BF16)

    for s in range(2):
        gained[s] = (factors[s][0] * factors[s][0] * mix(m_ref[...], moved[s])).astype(BF16)

    def body(index, sums):
        rows = rows_of(index)
        ahead, rate_plus, rate_minus = face_parts(v_ref, rows)
        rate = rate_plus + rate_minus
        sides = (jnp.where(ahead, rate, 0.0), jnp.where(ahead, 0.0, rate))
        message = load_plane(message_ref, 1, rows)
        new = []
        for s in range(2):
            change = load_plane(gained, s, rows)
            moved_tiles = drift(change, None, None, geometry(v_ref, rows, 1.0 - 2.0 * s))
            if s == 0:
                weights = [load_plane(weight_ref, p, rows) for p in (face, inner)]
            else:
                weights = [load_plane(own_weight_ref, p, rows) for p in (0, 1)]
            pair = ((partner_low_ref, partner_high_ref), (own_low_ref, own_high_ref))[s]
            third = [jnp.where(core == 0, low, high) for low, high in zip(*(load_plane(ref, 0, rows) for ref in pair))]
            for t in range(tiles):
                on_face = moved_tiles[t] + sides[s] * message[t].astype(F32)
                wide = change[t].astype(F32)
                terms = (
                    on_face * weights[0][t].astype(F32),
                    sides[s] * wide * weights[1][t].astype(F32),
                    wide * third[t].astype(F32),
                )
                base = 3 * (s * tiles + t)
                new += [sums[base + k] + fold(term) for k, term in enumerate(terms)]
        return tuple(new)

    zero = jnp.zeros((8, LANES), F32)
    sums = lax.fori_loop(0, orient // ROWS, body, (zero,) * (6 * tiles), unroll=UNROLL)
    for t in range(tiles):
        shares = []
        for s in range(2):
            base = 3 * (s * tiles + t)
            last, onward, third = (jnp.sum(sums[base + k], axis=0, keepdims=True) / orient for k in range(3))
            near, far = (factors[s][depth][:, columns(t)] for depth in range(2))
            shares.append((0.5 * near * last + third / (near * near), 0.5 * far * onward))
        for p in range(planes):
            at = slice(p, p + 1), columns(t)
            mine = core == (0 if p < half else 1)
            depth = min(p, planes - 1 - p)
            met = jnp.where(mine, 0.5 * met_ref[depth : depth + 1, columns(t)], 0.0)
            sent, kept = shared_ref[at] + met, met
            if depth < 2:
                sent = sent + jnp.where(mine, shares[0][depth], 0.0)
                kept = kept + jnp.where(mine, shares[1][depth], 0.0)
            sent_ref[at] = sent
            kept_ref[at] = kept


def split_outputs(outs):
    low, high, state, near, far, kept, outer = outs
    return (low, high), state, (near, far), kept, outer


def kernel_call(kernel, outs, scratch, args):
    vmem = pl.BlockSpec(memory_space=pltpu.VMEM)
    smem = pl.BlockSpec(memory_space=pltpu.SMEM)
    return pl.pallas_call(
        kernel,
        out_shape=outs,
        in_specs=[smem if arg.dtype == jnp.int32 else vmem for arg in args],
        out_specs=jax.tree.map(lambda _: vmem, outs),
        scratch_shapes=[pltpu.VMEM(*s) if len(s) == 2 else pltpu.VMEM(s, BF16) for s in scratch],
        compiler_params=pltpu.CompilerParams(vmem_limit_bytes=12 << 20),
        cost_estimate=pl.CostEstimate(flops=0, bytes_accessed=0, transcendentals=0),
    )(*args)


def shards(fields, end_weights, directions, analysis, synthesis, decay_rates):
    device = lax.axis_index("space")
    core = device % 2
    planes, cells = fields.shape
    orient = end_weights.shape[0]
    plane_index = device // 2 * planes + lax.broadcasted_iota(jnp.int32, (planes, 1), 0)
    ramp = slope * plane_index.astype(F32) / (planes * lax.axis_size("space") // 2)
    own = fields + ramp
    partner = swap_species(fields) + ramp

    wide = lambda extra: jax.ShapeDtypeStruct((planes + extra, orient, cells), BF16)
    slab, plane = wide(0), wide(1 - planes)
    face = core ^ (1 - device // 2 % 2)
    core_word = jnp.reshape(face, (1,)).astype(jnp.int32)
    species_word = jnp.reshape(core, (1,)).astype(jnp.int32)
    start = jnp.transpose(end_weights, (1, 0, 2))
    spread, edge0, coded = kernel_call(
        prologue_kernel,
        (jax.ShapeDtypeStruct((4, orient, LANES), F32), plane, jax.ShapeDtypeStruct((16, cells), BF16)),
        (((16, cells), F32),),
        (core_word, species_word, directions, start, own, partner),
    )
    matrix, turned = kernel_call(
        matrix_kernel,
        (jax.ShapeDtypeStruct((orient, orient), BF16),) * 2,
        (),
        (synthesis, decay_rates[None], analysis),
    )
    other0, matrix = lax.optimization_barrier((swap_species(edge0), matrix))
    message0 = kernel_call(
        first_message_kernel,
        jax.ShapeDtypeStruct((1, orient + 16, cells), BF16),
        (),
        (edge0, other0, coded, spread),
    )

    def message(blocks, others):
        shape = jax.ShapeDtypeStruct((len(blocks), orient + PAD_ROWS, cells), BF16)
        return kernel_call(message_kernel, shape, (), (*blocks, *others, spread))

    start, _ = lax.optimization_barrier((start, message0))
    arrived0 = exchange_faces(message0)
    alone, edges1, *inner = kernel_call(
        first_alone_kernel,
        (slab, plane) + (plane,) * (planes - 2),
        (slab.shape, slab.shape),
        (start, own, spread, matrix),
    )
    weights, own_weights = kernel_call(
        weight_kernel, (slab, wide(2 - planes)), (), (core_word, swap_species(start), start, turned)
    )
    others1, weights, *partner_inner = lax.optimization_barrier(
        (swap_species(edges1), weights, *map(swap_species, inner))
    )
    message1 = kernel_call(
        first_message_kernel,
        jax.ShapeDtypeStruct((1, orient + 16 * PAD, cells), BF16),
        (),
        (edges1, others1, *[coded] * PAD, spread),
    )
    state, *_ = lax.optimization_barrier((alone, message1, weights))
    later, edges2, edges3 = kernel_call(
        next_alone_kernel, (slab, plane, plane), (slab.shape, slab.shape), (state, own, partner, spread, matrix)
    )
    edges2, edges3, arrived0 = lax.optimization_barrier((edges2, edges3, arrived0))
    message2 = message([edges2, edges3], [swap_species(edges2), swap_species(edges3)])
    arrived = [exchange_faces(message1), exchange_faces(message2)]
    crossed0 = swap_species(arrived0)

    alone, *_ = lax.optimization_barrier((alone, message1, message2))
    half = planes // 2
    faces, second_state, sent_half, kept_half, outer = split_outputs(
        kernel_call(
            second_step_kernel,
            (plane, plane, wide(4), plane, plane, wide(half - planes), jax.ShapeDtypeStruct((2, cells), F32)),
            ((4, orient, cells), (8, orient, cells)),
            (core_word, alone, later, edge0, arrived0, crossed0, own, partner, spread, matrix),
        )
    )
    arrived1, second_state = lax.optimization_barrier((arrived[0], second_state))
    *moving, _ = lax.optimization_barrier((*sent_half, arrived1))
    *partner_half, crossed1 = lax.optimization_barrier((*map(swap_species, moving), swap_species(arrived1)))
    density = jax.ShapeDtypeStruct((planes, cells), F32)
    met, partition = kernel_call(
        middle_kernel,
        (jax.ShapeDtypeStruct((half, cells), F32), density),
        ((2, orient, cells),),
        (core_word, kept_half, *partner_half, arrived1, own, partner, spread, matrix),
    )
    count = lax.axis_size("space")

    def received(value, distance, after):
        block = lax.ppermute(value, "space", [(i, i ^ distance) for i in range(count)])
        return lax.optimization_barrier((block, after))

    def gathered(value, distance, after):
        block, after = received(value, distance, after)
        return kernel_call(add_kernel, density, (), (value, block)), after

    *faces, second_state, _ = lax.optimization_barrier((*faces, second_state, met))
    partner_faces = [swap_species(block) for block in faces]
    third_state = kernel_call(
        third_step_kernel,
        wide(2),
        (slab.shape, wide(2).shape),
        (second_state, arrived1, crossed1, own, partner, outer, spread, matrix),
    )
    partition, third_state = gathered(partition, 4, third_state)
    third_state, _ = lax.optimization_barrier((third_state, partition))
    shared = kernel_call(
        pairing_kernel,
        density,
        (),
        (third_state, partner, spread, weights, partner_faces[0], *partner_inner, partner_faces[1]),
    )
    distance = 8
    while distance < count:
        partition, shared = gathered(partition, distance, shared)
        distance *= 2
    arrived2, shared, _ = lax.optimization_barrier((arrived[1], shared, partition))
    sent, kept = kernel_call(
        last_kernel,
        (density, density),
        ((2, orient, cells), (2, orient, cells)),
        (
            core_word, arrived2, weights, own_weights, *faces, *partner_faces, shared, met,
            own, partner, spread, matrix,
        ),
    )
    beside, sent = received(partition, 2, sent)
    joined = kernel_call(
        join_kernel, jax.ShapeDtypeStruct((2 * planes, cells), F32), (), (sent, partition, beside)
    )
    return kernel_call(
        functools.partial(divide_kernel, count // 2 * planes * cells),
        density,
        (),
        (kept, joined, swap_species(joined)),
    )


def solution(mesh):
    return jax.shard_map(
        shards,
        mesh=mesh,
        in_specs=(P(("runs", "space"), None), P(None, ("runs", "space"), None), P(), P(), P(), P()),
        out_specs=P(("runs", "space"), None),
        check_vma=False,
    )
```

```python
import functools

import jax
import jax.numpy as jnp
from jax import lax
from jax.experimental import pallas as pl
from jax.experimental.pallas import tpu as pltpu
from jax.sharding import PartitionSpec as P

NZ = 16
STEPS = 4
LANES = 128
ROWS = 16
UNROLL = 16
PAD = 2
PAD_ROWS = 32

courant = 0.3
slope = 0.6

BF16 = jnp.bfloat16
F32 = jnp.float32


def swap_species(block):
    count = lax.axis_size("space")
    return lax.ppermute(block, "space", [(i ^ 1, i) for i in range(count)])


def exchange_faces(block):
    count = lax.axis_size("space")
    route = []
    for slab in range(count // 2):
        beside = ((slab + 1) ^ 1) - 1
        route += [(2 * slab, 2 * (slab ^ 1)), (2 * slab + 1, 2 * beside % count + 1)]
    return lax.ppermute(block, "space", route)


def rows_of(index):
    return pl.ds(pl.multiple_of(index * ROWS, ROWS), ROWS)


def each_row_block(orient):
    def run(body):
        def step(index, carry):
            body(index)
            return carry

        lax.fori_loop(0, orient // ROWS, step, 0, unroll=UNROLL)

    return run


def columns(tile):
    return slice(LANES * tile, LANES * (tile + 1))


def geometry(v_ref, rows, sign=1.0):
    lane = lax.broadcasted_iota(jnp.int32, (ROWS, LANES), 1)
    vx, vy, vz = (sign * v_ref[c, rows, :] for c in range(3))
    narrow = vx.astype(BF16)
    plus_x, narrow_plus, plus_y, plus_z = vx > 0, narrow > jnp.zeros_like(narrow), vy > 0, vz > 0
    rate_x, rate_y, rate_z = (courant * jnp.abs(t) for t in (vx, vy, vz))
    stay = 1.0 - (rate_x + rate_y + rate_z)
    z_from = (lane & (LANES - NZ)) | (jnp.where(plus_z, lane - 1, lane + 1) & (NZ - 1))
    y_from = jnp.where(plus_y, lane - NZ, lane + NZ) & (LANES - 1)
    y_edge = jnp.where(plus_y, lane, LANES - 1 - lane) < NZ
    return plus_x, narrow_plus, plus_y, stay, rate_x, rate_y, rate_z, z_from, y_from, y_edge


def pick(tile, index):
    return jnp.take_along_axis(tile, index, axis=1, mode="promise_in_bounds")


def load_plane(ref, plane, rows):
    return [ref[plane, rows, columns(t)] for t in range(ref.shape[2] // LANES)]


def drift(center, before, after, geo):
    plus_x, narrow_plus, plus_y, stay, rate_x, rate_y, rate_z, z_from, y_from, y_edge = geo
    tiles = len(center)
    center = [tile.astype(F32) for tile in center]
    turned = [pick(tile, y_from) for tile in center]
    moved = []
    for t in range(tiles):
        total = stay * center[t]
        if before is not None and after is not None:
            total = total + rate_x * jnp.where(narrow_plus, before[t], after[t]).astype(F32)
        elif before is not None:
            total = total + jnp.where(plus_x, rate_x, 0.0) * before[t].astype(F32)
        elif after is not None:
            total = total + jnp.where(plus_x, 0.0, rate_x) * after[t].astype(F32)
        over = jnp.where(plus_y, turned[t - 1], turned[(t + 1) % tiles])
        total = total + rate_y * jnp.where(y_edge, over, turned[t])
        total = total + rate_z * pick(center[t], z_from)
        moved.append(total)
    return moved


def store_plane(ref, plane, rows, tiles):
    for t, tile in enumerate(tiles):
        ref[plane, rows, columns(t)] = tile.astype(ref.dtype)


def mix(matrix, moved):
    return jnp.dot(matrix, moved, preferred_element_type=F32)


def boltzmann(field):
    return jnp.exp(-0.5 * field)


def prologue_kernel(
    core_ref, species_ref, directions_ref, start_ref, fields_ref, partner_ref, spread_ref, edge_ref, coded_ref, near
):
    sign = 1.0 - 2.0 * species_ref[0].astype(F32)
    toward = sign * (1.0 - 2.0 * core_ref[0].astype(F32))
    planes, orient, cells = start_ref.shape
    low = boltzmann(fields_ref[0:1])
    high = boltzmann(fields_ref[fields_ref.shape[0] - 1 :])
    for c in range(4):
        row = directions_ref[c % 3 : c % 3 + 1]
        column = jnp.broadcast_to(row, (LANES, orient)).T
        spread_ref[c] = (toward if c == 3 else sign) * column

    @each_row_block(orient)
    def _(index):
        rows = rows_of(index)
        plus_x = spread_ref[0, rows, :] > 0
        for t in range(cells // LANES):
            at = rows, columns(t)
            chosen = jnp.where(
                plus_x,
                high[:, columns(t)] * start_ref[planes - 1, *at].astype(F32),
                low[:, columns(t)] * start_ref[0, *at].astype(F32),
            )
            edge_ref[0, *at] = chosen.astype(BF16)

    near[...] = jnp.zeros_like(near)
    for s, ref in enumerate((fields_ref, partner_ref)):
        for depth in range(2):
            high_row, low_row = (ref[p : p + 1] for p in (planes - 1 - depth, depth))
            row = jnp.where(core_ref[0] == 1, high_row, low_row)
            coarse = row.astype(BF16).astype(F32)
            at = 2 * s + depth
            near[at : at + 1] = coarse
            near[at + 4 : at + 5] = row - coarse
    coded_ref[...] = near[...].astype(BF16)


def matrix_kernel(synthesis_ref, decay_ref, analysis_ref, out_ref, turned_ref):
    rest = synthesis_ref[...].astype(F32) * decay_ref[...]
    total = jnp.full(out_ref.shape, 1.0 / out_ref.shape[1], F32)
    for _ in range(3):
        part = rest.astype(BF16)
        rest = rest - part.astype(F32)
        total = total + jnp.dot(part, analysis_ref[...], preferred_element_type=F32)
    out_ref[...] = total.astype(BF16)
    turned_ref[...] = total.T.astype(BF16)


def add_kernel(one_ref, two_ref, out_ref):
    out_ref[...] = one_ref[...] + two_ref[...]


def join_kernel(sent_ref, one_ref, two_ref, out_ref):
    planes = sent_ref.shape[0]
    out_ref[:planes] = sent_ref[...]
    out_ref[planes:] = one_ref[...] + two_ref[...]


def divide_kernel(cells, kept_ref, mine_ref, arrived_ref, out_ref):
    planes = kept_ref.shape[0]
    total = mine_ref[planes:] + arrived_ref[planes:]
    out_ref[...] = (kept_ref[...] + arrived_ref[:planes]) * (cells / total)


def message_kernel(*refs):
    count = (len(refs) - 2) // 2
    v_ref, out_ref = refs[-2:]
    orient, cells = refs[0].shape[1:]

    @each_row_block(orient)
    def _(index):
        rows = rows_of(index)
        narrow = v_ref[3, rows, :].astype(BF16)
        leaves = narrow < jnp.zeros_like(narrow)
        for p in range(count):
            for t in range(cells // LANES):
                at = 0, rows, columns(t)
                out_ref[p, rows, columns(t)] = jnp.where(leaves, refs[p][at], refs[count + p][at])

    if count > 1:
        out_ref[:, orient:] = jnp.zeros_like(out_ref[:, orient:])


def first_message_kernel(mine_ref, other_ref, *refs):
    *coded_refs, v_ref, out_ref = refs
    message_kernel(mine_ref, other_ref, v_ref, out_ref)
    orient = mine_ref.shape[1]
    for k, ref in enumerate(coded_refs):
        out_ref[0, orient + 16 * k : orient + 16 * (k + 1)] = ref[...]


def write_edge(edges_ref, step, faces, rows, v_ref):
    narrow = v_ref[0, rows, :].astype(BF16)
    plus_x = narrow > jnp.zeros_like(narrow)
    for t in range(len(faces[0])):
        edges_ref[step, rows, columns(t)] = jnp.where(plus_x, faces[-1][t], faces[0][t])


def alone_step(source_ref, moved, targets, v_ref, edges_ref, step):
    planes, orient, _ = source_ref.shape

    @each_row_block(orient)
    def _(index):
        rows = rows_of(index)
        geo = geometry(v_ref, rows)
        loaded = [load_plane(source_ref, p, rows) for p in range(planes)]
        if edges_ref is not None:
            write_edge(edges_ref, step, loaded, rows, v_ref)
        for p in targets:
            before = loaded[p - 1] if p > 0 else None
            after = loaded[p + 1] if p < planes - 1 else None
            store_plane(moved, p, rows, drift(loaded[p], before, after, geo))


def first_alone_kernel(start_ref, first_ref, v_ref, m_ref, out_ref, edges_ref, *refs):
    *inner_refs, held, moved = refs
    planes, orient, _ = start_ref.shape
    first = boltzmann(first_ref[...])
    for p in range(planes):
        held[p] = (first[p : p + 1] * start_ref[p].astype(F32)).astype(BF16)
    alone_step(held, moved, range(planes), v_ref, None, 0)
    for p in (0, planes - 1, *range(1, planes - 1)):
        state = (first[p : p + 1] * first[p : p + 1] * mix(m_ref[...], moved[p])).astype(BF16)
        out_ref[p] = state
        if 0 < p < planes - 1:
            inner_refs[p - 1][0] = state

    @each_row_block(orient)
    def _(index):
        rows = rows_of(index)
        write_edge(edges_ref, 0, [load_plane(out_ref, p, rows) for p in (0, planes - 1)], rows, v_ref)


def next_alone_kernel(
    state_ref, first_ref, second_ref, v_ref, m_ref, out_ref, edges2_ref, edges3_ref, held, moved
):
    planes, orient, _ = state_ref.shape
    first = boltzmann(first_ref[...])
    second = boltzmann(second_ref[...])
    alone_step(state_ref, moved, range(planes), v_ref, None, 0)
    for p in range(planes):
        out_ref[p] = (first[p : p + 1] * second[p : p + 1] * mix(m_ref[...], moved[p])).astype(BF16)
    alone_step(out_ref, moved, (0, planes - 1), v_ref, edges2_ref, 0)
    for p in (0, planes - 1):
        held[p] = (second[p : p + 1] * second[p : p + 1] * mix(m_ref[...], moved[p])).astype(BF16)

    @each_row_block(orient)
    def _(index):
        rows = rows_of(index)
        write_edge(edges3_ref, 0, [load_plane(held, p, rows) for p in (0, planes - 1)], rows, v_ref)


def face_parts(v_ref, rows):
    vx = v_ref[0, rows, :]
    rate = courant * jnp.abs(vx)
    return v_ref[3, rows, :] > 0, jnp.where(vx > 0, rate, 0.0), jnp.where(vx > 0, 0.0, rate)


def face_drifts(v_ref, mine_ref, other_ref, moved, slots):
    @each_row_block(v_ref.shape[1])
    def _(index):
        rows = rows_of(index)
        ahead, rate_plus, rate_minus = face_parts(v_ref, rows)
        for t in range(mine_ref.shape[2] // LANES):
            mine = mine_ref[0, rows, columns(t)].astype(F32)
            other = other_ref[0, rows, columns(t)].astype(F32)
            face = jnp.where(ahead, mine, other)
            moved[slots[0], rows, columns(t)] = (rate_plus * face).astype(BF16)
            moved[slots[1], rows, columns(t)] = (rate_minus * face).astype(BF16)


def second_step_kernel(
    core_ref, alone_ref, later_ref, edge_ref, mine_ref, other_ref, first_ref, second_ref, v_ref, m_ref,
    face_low_ref, face_high_ref, next_ref, sent_near_ref, sent_far_ref, kept_ref, outer_ref, held, moved,
):
    planes, orient, _ = alone_ref.shape
    matrix = m_ref[...]
    first, second = boltzmann(first_ref[...]), boltzmann(second_ref[...])
    core = core_ref[0]
    mine, other = (block[:4] + block[4:8] for block in (ref[0, orient:].astype(F32) for ref in (mine_ref, other_ref)))
    other = (other[2:4], other[0:2])
    mine = (mine[0:2], mine[2:4])
    low = [jnp.where(core == 0, mine[k], other[k]) for k in range(2)]
    high = [jnp.where(core == 0, other[k], mine[k]) for k in range(2)]
    beyond = [boltzmann(block[k : k + 1]) for block in (low[0], high[0], low[1], high[1]) for k in range(2)]
    face_drifts(v_ref, mine_ref, other_ref, moved, (0, 1))

    @each_row_block(orient)
    def _(index):
        rows = rows_of(index)
        _, rate_plus, rate_minus = face_parts(v_ref, rows)
        for t in range(edge_ref.shape[2] // LANES):
            edge = edge_ref[0, rows, columns(t)].astype(F32)
            moved[2, rows, columns(t)] = (rate_minus * edge).astype(BF16)
            moved[3, rows, columns(t)] = (rate_plus * edge).astype(BF16)

    squared = first * first
    for p, slot, face_ref in ((0, 1, face_low_ref), (planes - 1, 2, face_high_ref)):
        arrived = squared[p : p + 1] * mix(matrix, moved[slot - 1])
        held[slot] = arrived.astype(BF16)
        face_ref[0] = (alone_ref[p].astype(F32) + arrived).astype(BF16)
    held[0] = (beyond[0] * beyond[0] * mix(matrix, moved[2])).astype(BF16)
    held[3] = (beyond[2] * beyond[2] * mix(matrix, moved[3])).astype(BF16)

    @each_row_block(orient)
    def _(index):
        rows = rows_of(index)
        geo = geometry(v_ref, rows)
        _, rate_plus, rate_minus = face_parts(v_ref, rows)
        below, low, high, above = (load_plane(held, p, rows) for p in range(4))
        face_low, face_high = (load_plane(ref, 0, rows) for ref in (face_low_ref, face_high_ref))

        def onward(rate, tiles):
            return [rate * tile.astype(F32) for tile in tiles]

        store_plane(moved, 0, rows, onward(rate_minus, below))
        store_plane(moved, 1, rows, drift(below, None, face_low, geo))
        store_plane(moved, 2, rows, drift(low, below, None, geo))
        store_plane(moved, 3, rows, onward(rate_plus, low))
        store_plane(moved, 4, rows, onward(rate_minus, high))
        store_plane(moved, 5, rows, drift(high, None, above, geo))
        store_plane(moved, 6, rows, drift(above, face_high, None, geo))
        store_plane(moved, 7, rows, onward(rate_plus, above))

    cross = first * second
    outer = ((0, 0, beyond[1] * beyond[5]), (1, 1, beyond[0] * beyond[4]))
    outer += ((planes + 2, 6, beyond[2] * beyond[6]), (planes + 3, 7, beyond[3] * beyond[7]))
    for p, slot, factor in outer:
        next_ref[p] = (factor * mix(matrix, moved[slot])).astype(BF16)
    slots = {0: 2, 1: 3, planes - 2: 4, planes - 1: 5}
    for p in range(planes):
        kept = later_ref[p]
        if p in slots:
            kept = (kept.astype(F32) + cross[p : p + 1] * mix(matrix, moved[slots[p]])).astype(BF16)
        next_ref[p + 2] = kept
    for p in range(planes // 2):
        sent_ref = (sent_near_ref, sent_far_ref)[p]
        sent_ref[0] = next_ref[2 + (planes - 1) * (1 - core) + (2 * core - 1) * p]
        kept_ref[p] = next_ref[2 + (planes - 1) * core + (1 - 2 * core) * p]
    outer_ref[0:1] = beyond[4] * beyond[4]
    outer_ref[1:2] = beyond[6] * beyond[6]


def middle_kernel(
    core_ref, own_ref, near_ref, far_ref, message_ref, first_ref, second_ref, v_ref, m_ref, out_ref, total_ref, moved
):
    _, orient, cells = own_ref.shape
    planes = first_ref.shape[0]

    def cross_of(depth):
        low, high = (
            boltzmann(first_ref[p : p + 1]) * boltzmann(second_ref[p : p + 1]) for p in (depth, planes - 1 - depth)
        )
        return jnp.where(core_ref[0] == 0, low, high)

    cross = [cross_of(depth) for depth in range(2)]

    @each_row_block(orient)
    def _(index):
        rows = rows_of(index)
        ahead, rate_plus, rate_minus = face_parts(v_ref, rows)
        rate = rate_plus + rate_minus
        for t in range(cells // LANES):
            gained = rate * message_ref[0, rows, columns(t)].astype(F32)
            moved[0, rows, columns(t)] = jnp.where(ahead, gained, 0.0).astype(BF16)
            moved[1, rows, columns(t)] = jnp.where(ahead, 0.0, gained).astype(BF16)

    own_face = own_ref[0].astype(F32) + cross[0] * mix(m_ref[...], moved[0])
    partner_face = near_ref[0].astype(F32) + cross[0] * mix(m_ref[...], moved[1])
    face = jnp.sum(own_face * partner_face, axis=0, keepdims=True)
    total = jnp.zeros((1, 1), F32)
    for p in range(own_ref.shape[0]):
        if p > 0:
            face = jnp.sum(own_ref[p].astype(F32) * far_ref[0].astype(F32), axis=0, keepdims=True)
        met = face / (orient * cross[p])
        out_ref[p : p + 1] = met
        total = total + jnp.sum(met, axis=1, keepdims=True)
    total_ref[...] = jnp.broadcast_to(total, total_ref.shape)


def third_step_kernel(
    held_ref, mine_ref, other_ref, first_ref, second_ref, outer_ref, v_ref, m_ref, next_ref, held, moved
):
    planes, orient, _ = held.shape
    matrix = m_ref[...]
    first, second = boltzmann(first_ref[...]), boltzmann(second_ref[...])
    face_drifts(v_ref, mine_ref, other_ref, moved, (0, 1))
    cross = first * second
    for p in range(planes):
        kept = held_ref[p + 2]
        if p in (0, planes - 1):
            arrived = cross[p : p + 1] * mix(matrix, moved[min(p, 1)])
            kept = (kept.astype(F32) + arrived).astype(BF16)
        held[p] = kept

    @each_row_block(orient)
    def _(index):
        rows = rows_of(index)
        geo = geometry(v_ref, rows)
        loaded = [load_plane(held_ref, p, rows) for p in (0, 1)]
        loaded += [load_plane(held, p, rows) for p in range(planes)]
        loaded += [load_plane(held_ref, p, rows) for p in (planes + 2, planes + 3)]
        for p in range(planes + 2):
            store_plane(moved, p, rows, drift(loaded[p + 1], loaded[p], loaded[p + 2], geo))

    squared = second * second
    factors = [outer_ref[0:1]] + [squared[p : p + 1] for p in range(planes)] + [outer_ref[1:2]]
    for p, factor in enumerate(factors):
        next_ref[p] = (factor * mix(matrix, moved[p])).astype(BF16)


def weight_kernel(core_ref, partner_ref, start_ref, turned_ref, weight_ref, own_ref):
    planes = partner_ref.shape[0]
    core = core_ref[0]
    for p in range(planes):
        weight_ref[p] = mix(turned_ref[...], partner_ref[p]).astype(BF16)
    for p in range(2):
        own_ref[p] = mix(turned_ref[...], start_ref[core * (planes - 1) + p - 2 * p * core]).astype(BF16)


def fold(value):
    return jnp.sum(value.reshape(ROWS // 8, 8, LANES), axis=0)


def pairing_kernel(held_ref, second_ref, v_ref, weight_ref, *refs):
    *partner_refs, out_ref = refs
    planes, orient, cells = weight_ref.shape
    second = boltzmann(second_ref[...])
    tiles = cells // LANES

    def body(index, sums):
        rows = rows_of(index)
        geo = geometry(v_ref, rows)
        loaded = [load_plane(held_ref, p, rows) for p in range(planes + 2)]
        new = []
        for p in range(planes):
            moved_tiles = drift(loaded[p + 1], loaded[p], loaded[p + 2], geo)
            weights = load_plane(weight_ref, p, rows)
            partner = load_plane(partner_refs[p], 0, rows)
            for t in range(tiles):
                last, third = sums[2 * (p * tiles + t)], sums[2 * (p * tiles + t) + 1]
                new.append(last + fold(moved_tiles[t] * weights[t].astype(F32)))
                new.append(third + fold(loaded[p + 1][t].astype(F32) * partner[t].astype(F32)))
        return tuple(new)

    zero = jnp.zeros((8, LANES), F32)
    sums = lax.fori_loop(0, orient // ROWS, body, (zero,) * (2 * planes * tiles), unroll=UNROLL)
    for p in range(planes):
        for t in range(tiles):
            last = jnp.sum(sums[2 * (p * tiles + t)], axis=0, keepdims=True)
            third = jnp.sum(sums[2 * (p * tiles + t) + 1], axis=0, keepdims=True)
            factor = second[p : p + 1, columns(t)]
            out_ref[p : p + 1, columns(t)] = (0.5 * factor * last + third / (factor * factor)) / orient


def last_kernel(
    core_ref, message_ref, weight_ref, own_weight_ref, own_low_ref, own_high_ref, partner_low_ref, partner_high_ref,
    shared_ref, met_ref,    own_ref, partner_ref, v_ref, m_ref, sent_ref, kept_ref, moved, gained,
):
    planes, cells = shared_ref.shape
    orient = m_ref.shape[0]
    tiles = cells // LANES
    core = core_ref[0]
    half = planes // 2
    face = core * (planes - 1)
    inner = face + 1 - 2 * core

    def at_face(ref, depth):
        return jnp.where(core == 0, boltzmann(ref[depth : depth + 1]), boltzmann(ref[planes - 1 - depth : planes - depth]))

    factors = [[at_face(ref, depth) for depth in range(2)] for ref in (partner_ref, own_ref)]

    @each_row_block(orient)
    def _(index):
        rows = rows_of(index)
        ahead, rate_plus, rate_minus = face_parts(v_ref, rows)
        rate = rate_plus + rate_minus
        for t in range(tiles):
            got = rate * message_ref[0, rows, columns(t)].astype(F32)
            moved[0, rows, columns(t)] = jnp.where(ahead, got, 0.0).astype(BF16)
            moved[1, rows, columns(t)] = jnp.where(ahead, 0.0, got).astype(BF16)

    for s in range(2):
        gained[s] = (factors[s][0] * factors[s][0] * mix(m_ref[...], moved[s])).astype(BF16)

    def body(index, sums):
        rows = rows_of(index)
        ahead, rate_plus, rate_minus = face_parts(v_ref, rows)
        rate = rate_plus + rate_minus
        sides = (jnp.where(ahead, rate, 0.0), jnp.where(ahead, 0.0, rate))
        message = load_plane(message_ref, 1, rows)
        new = []
        for s in range(2):
            change = load_plane(gained, s, rows)
            moved_tiles = drift(change, None, None, geometry(v_ref, rows, 1.0 - 2.0 * s))
            if s == 0:
                weights = [load_plane(weight_ref, p, rows) for p in (face, inner)]
            else:
                weights = [load_plane(own_weight_ref, p, rows) for p in (0, 1)]
            pair = ((partner_low_ref, partner_high_ref), (own_low_ref, own_high_ref))[s]
            third = [jnp.where(core == 0, low, high) for low, high in zip(*(load_plane(ref, 0, rows) for ref in pair))]
            for t in range(tiles):
                on_face = moved_tiles[t] + sides[s] * message[t].astype(F32)
                wide = change[t].astype(F32)
                terms = (
                    on_face * weights[0][t].astype(F32),
                    sides[s] * wide * weights[1][t].astype(F32),
                    wide * third[t].astype(F32),
                )
                base = 3 * (s * tiles + t)
                new += [sums[base + k] + fold(term) for k, term in enumerate(terms)]
        return tuple(new)

    zero = jnp.zeros((8, LANES), F32)
    sums = lax.fori_loop(0, orient // ROWS, body, (zero,) * (6 * tiles), unroll=UNROLL)
    for t in range(tiles):
        shares = []
        for s in range(2):
            base = 3 * (s * tiles + t)
            last, onward, third = (jnp.sum(sums[base + k], axis=0, keepdims=True) / orient for k in range(3))
            near, far = (factors[s][depth][:, columns(t)] for depth in range(2))
            shares.append((0.5 * near * last + third / (near * near), 0.5 * far * onward))
        for p in range(planes):
            at = slice(p, p + 1), columns(t)
            mine = core == (0 if p < half else 1)
            depth = min(p, planes - 1 - p)
            met = jnp.where(mine, 0.5 * met_ref[depth : depth + 1, columns(t)], 0.0)
            sent, kept = shared_ref[at] + met, met
            if depth < 2:
                sent = sent + jnp.where(mine, shares[0][depth], 0.0)
                kept = kept + jnp.where(mine, shares[1][depth], 0.0)
            sent_ref[at] = sent
            kept_ref[at] = kept


def split_outputs(outs):
    low, high, state, near, far, kept, outer = outs
    return (low, high), state, (near, far), kept, outer


def kernel_call(kernel, outs, scratch, args):
    vmem = pl.BlockSpec(memory_space=pltpu.VMEM)
    smem = pl.BlockSpec(memory_space=pltpu.SMEM)
    return pl.pallas_call(
        kernel,
        out_shape=outs,
        in_specs=[smem if arg.dtype == jnp.int32 else vmem for arg in args],
        out_specs=jax.tree.map(lambda _: vmem, outs),
        scratch_shapes=[pltpu.VMEM(*s) if len(s) == 2 else pltpu.VMEM(s, BF16) for s in scratch],
        compiler_params=pltpu.CompilerParams(vmem_limit_bytes=12 << 20),
        cost_estimate=pl.CostEstimate(flops=0, bytes_accessed=0, transcendentals=0),
    )(*args)


def shards(fields, end_weights, directions, analysis, synthesis, decay_rates):
    device = lax.axis_index("space")
    core = device % 2
    planes, cells = fields.shape
    orient = end_weights.shape[0]
    plane_index = device // 2 * planes + lax.broadcasted_iota(jnp.int32, (planes, 1), 0)
    ramp = slope * plane_index.astype(F32) / (planes * lax.axis_size("space") // 2)
    own = fields + ramp
    partner = swap_species(fields) + ramp

    wide = lambda extra: jax.ShapeDtypeStruct((planes + extra, orient, cells), BF16)
    slab, plane = wide(0), wide(1 - planes)
    face = core ^ (1 - device // 2 % 2)
    core_word = jnp.reshape(face, (1,)).astype(jnp.int32)
    species_word = jnp.reshape(core, (1,)).astype(jnp.int32)
    start = jnp.transpose(end_weights, (1, 0, 2))
    spread, edge0, coded = kernel_call(
        prologue_kernel,
        (jax.ShapeDtypeStruct((4, orient, LANES), F32), plane, jax.ShapeDtypeStruct((16, cells), BF16)),
        (((16, cells), F32),),
        (core_word, species_word, directions, start, own, partner),
    )
    matrix, turned = kernel_call(
        matrix_kernel,
        (jax.ShapeDtypeStruct((orient, orient), BF16),) * 2,
        (),
        (synthesis, decay_rates[None], analysis),
    )
    other0, matrix = lax.optimization_barrier((swap_species(edge0), matrix))
    message0 = kernel_call(
        first_message_kernel,
        jax.ShapeDtypeStruct((1, orient + 16, cells), BF16),
        (),
        (edge0, other0, coded, spread),
    )

    def message(blocks, others):
        shape = jax.ShapeDtypeStruct((len(blocks), orient + PAD_ROWS, cells), BF16)
        return kernel_call(message_kernel, shape, (), (*blocks, *others, spread))

    start, _ = lax.optimization_barrier((start, message0))
    arrived0 = exchange_faces(message0)
    alone, edges1, *inner = kernel_call(
        first_alone_kernel,
        (slab, plane) + (plane,) * (planes - 2),
        (slab.shape, slab.shape),
        (start, own, spread, matrix),
    )
    weights, own_weights = kernel_call(
        weight_kernel, (slab, wide(2 - planes)), (), (core_word, swap_species(start), start, turned)
    )
    later, edges2, edges3 = kernel_call(
        next_alone_kernel, (slab, plane, plane), (slab.shape, slab.shape), (alone, own, partner, spread, matrix)
    )
    edges1, edges2 = lax.optimization_barrier((edges1, edges2))
    others1, weights = lax.optimization_barrier((swap_species(edges1), weights))
    message1 = kernel_call(
        first_message_kernel,
        jax.ShapeDtypeStruct((1, orient + 16 * PAD, cells), BF16),
        (),
        (edges1, others1, *[coded] * PAD, spread),
    )
    message2 = message([edges2, edges3], [swap_species(edges2), swap_species(edges3)])
    arrived = [exchange_faces(message1), exchange_faces(message2)]
    arrived0, _ = lax.optimization_barrier((arrived0, message2))
    crossed0 = swap_species(arrived0)

    alone, *_ = lax.optimization_barrier((alone, message1, message2))
    half = planes // 2
    faces, second_state, sent_half, kept_half, outer = split_outputs(
        kernel_call(
            second_step_kernel,
            (plane, plane, wide(4), plane, plane, wide(half - planes), jax.ShapeDtypeStruct((2, cells), F32)),
            ((4, orient, cells), (8, orient, cells)),
            (core_word, alone, later, edge0, arrived0, crossed0, own, partner, spread, matrix),
        )
    )
    arrived1, second_state = lax.optimization_barrier((arrived[0], second_state))
    *moving, first_inner, _ = lax.optimization_barrier((*sent_half, inner[0], arrived1))
    *partner_half, partner_first, crossed1 = lax.optimization_barrier(
        (*map(swap_species, moving), swap_species(first_inner), swap_species(arrived1))
    )
    density = jax.ShapeDtypeStruct((planes, cells), F32)
    met, partition = kernel_call(
        middle_kernel,
        (jax.ShapeDtypeStruct((half, cells), F32), density),
        ((2, orient, cells),),
        (core_word, kept_half, *partner_half, arrived1, own, partner, spread, matrix),
    )
    count = lax.axis_size("space")

    def received(value, distance, after):
        block = lax.ppermute(value, "space", [(i, i ^ distance) for i in range(count)])
        return lax.optimization_barrier((block, after))

    def gathered(value, distance, after):
        block, after = received(value, distance, after)
        return kernel_call(add_kernel, density, (), (value, block)), after

    second_state, _, *moving = lax.optimization_barrier((second_state, met, *faces, *inner[1:]))
    faces, inner = moving[:2], moving[2:]
    partner_inner = [partner_first] + [swap_species(block) for block in inner]
    partner_faces = [swap_species(block) for block in faces]
    third_state = kernel_call(
        third_step_kernel,
        wide(2),
        (slab.shape, wide(2).shape),
        (second_state, arrived1, crossed1, own, partner, outer, spread, matrix),
    )
    partition, third_state = gathered(partition, 4, third_state)
    third_state, _ = lax.optimization_barrier((third_state, partition))
    shared = kernel_call(
        pairing_kernel,
        density,
        (),
        (third_state, partner, spread, weights, partner_faces[0], *partner_inner, partner_faces[1]),
    )
    distance = 8
    while distance < count:
        partition, shared = gathered(partition, distance, shared)
        distance *= 2
    arrived2, shared, _ = lax.optimization_barrier((arrived[1], shared, partition))
    sent, kept = kernel_call(
        last_kernel,
        (density, density),
        ((2, orient, cells), (2, orient, cells)),
        (
            core_word, arrived2, weights, own_weights, *faces, *partner_faces, shared, met,
            own, partner, spread, matrix,
        ),
    )
    beside, sent = received(partition, 2, sent)
    joined = kernel_call(
        join_kernel, jax.ShapeDtypeStruct((2 * planes, cells), F32), (), (sent, partition, beside)
    )
    return kernel_call(
        functools.partial(divide_kernel, count // 2 * planes * cells),
        density,
        (),
        (kept, joined, swap_species(joined)),
    )


def solution(mesh):
    return jax.shard_map(
        shards,
        mesh=mesh,
        in_specs=(P(("runs", "space"), None), P(None, ("runs", "space"), None), P(), P(), P(), P()),
        out_specs=P(("runs", "space"), None),
        check_vma=False,
    )
```

```python
import functools

import jax
import jax.numpy as jnp
from jax import lax
from jax.experimental import pallas as pl
from jax.experimental.pallas import tpu as pltpu
from jax.sharding import PartitionSpec as P

NZ = 16
STEPS = 4
LANES = 128
ROWS = 16
UNROLL = 16
PAD = 2
PAD_ROWS = 32

courant = 0.3
slope = 0.6

BF16 = jnp.bfloat16
F32 = jnp.float32


def swap_species(block):
    count = lax.axis_size("space")
    return lax.ppermute(block, "space", [(i ^ 1, i) for i in range(count)])


def exchange_faces(block):
    count = lax.axis_size("space")
    route = []
    for slab in range(count // 2):
        beside = ((slab + 1) ^ 1) - 1
        route += [(2 * slab, 2 * (slab ^ 1)), (2 * slab + 1, 2 * beside % count + 1)]
    return lax.ppermute(block, "space", route)


def rows_of(index):
    return pl.ds(pl.multiple_of(index * ROWS, ROWS), ROWS)


def each_row_block(orient):
    def run(body):
        def step(index, carry):
            body(index)
            return carry

        lax.fori_loop(0, orient // ROWS, step, 0, unroll=UNROLL)

    return run


def columns(tile):
    return slice(LANES * tile, LANES * (tile + 1))


def geometry(v_ref, rows, sign=1.0):
    lane = lax.broadcasted_iota(jnp.int32, (ROWS, LANES), 1)
    vx, vy, vz = (sign * v_ref[c, rows, :] for c in range(3))
    narrow = vx.astype(BF16)
    plus_x, narrow_plus, plus_y, plus_z = vx > 0, narrow > jnp.zeros_like(narrow), vy > 0, vz > 0
    rate_x, rate_y, rate_z = (courant * jnp.abs(t) for t in (vx, vy, vz))
    stay = 1.0 - (rate_x + rate_y + rate_z)
    z_from = (lane & (LANES - NZ)) | (jnp.where(plus_z, lane - 1, lane + 1) & (NZ - 1))
    y_from = jnp.where(plus_y, lane - NZ, lane + NZ) & (LANES - 1)
    y_edge = jnp.where(plus_y, lane, LANES - 1 - lane) < NZ
    return plus_x, narrow_plus, plus_y, stay, rate_x, rate_y, rate_z, z_from, y_from, y_edge


def pick(tile, index):
    return jnp.take_along_axis(tile, index, axis=1, mode="promise_in_bounds")


def load_plane(ref, plane, rows):
    return [ref[plane, rows, columns(t)] for t in range(ref.shape[2] // LANES)]


def drift(center, before, after, geo):
    plus_x, narrow_plus, plus_y, stay, rate_x, rate_y, rate_z, z_from, y_from, y_edge = geo
    tiles = len(center)
    center = [tile.astype(F32) for tile in center]
    turned = [pick(tile, y_from) for tile in center]
    moved = []
    for t in range(tiles):
        total = stay * center[t]
        if before is not None and after is not None:
            total = total + rate_x * jnp.where(narrow_plus, before[t], after[t]).astype(F32)
        elif before is not None:
            total = total + jnp.where(plus_x, rate_x, 0.0) * before[t].astype(F32)
        elif after is not None:
            total = total + jnp.where(plus_x, 0.0, rate_x) * after[t].astype(F32)
        over = jnp.where(plus_y, turned[t - 1], turned[(t + 1) % tiles])
        total = total + rate_y * jnp.where(y_edge, over, turned[t])
        total = total + rate_z * pick(center[t], z_from)
        moved.append(total)
    return moved


def store_plane(ref, plane, rows, tiles):
    for t, tile in enumerate(tiles):
        ref[plane, rows, columns(t)] = tile.astype(ref.dtype)


def mix(matrix, moved):
    return jnp.dot(matrix, moved, preferred_element_type=F32)


def boltzmann(field):
    return jnp.exp(-0.5 * field)


def prologue_kernel(
    core_ref, species_ref, directions_ref, start_ref, fields_ref, partner_ref, spread_ref, edge_ref, coded_ref, near
):
    sign = 1.0 - 2.0 * species_ref[0].astype(F32)
    toward = sign * (1.0 - 2.0 * core_ref[0].astype(F32))
    planes, orient, cells = start_ref.shape
    low = boltzmann(fields_ref[0:1])
    high = boltzmann(fields_ref[fields_ref.shape[0] - 1 :])
    for c in range(4):
        row = directions_ref[c % 3 : c % 3 + 1]
        column = jnp.broadcast_to(row, (LANES, orient)).T
        spread_ref[c] = (toward if c == 3 else sign) * column

    @each_row_block(orient)
    def _(index):
        rows = rows_of(index)
        plus_x = spread_ref[0, rows, :] > 0
        for t in range(cells // LANES):
            at = rows, columns(t)
            chosen = jnp.where(
                plus_x,
                high[:, columns(t)] * start_ref[planes - 1, *at].astype(F32),
                low[:, columns(t)] * start_ref[0, *at].astype(F32),
            )
            edge_ref[0, *at] = chosen.astype(BF16)

    near[...] = jnp.zeros_like(near)
    for s, ref in enumerate((fields_ref, partner_ref)):
        for depth in range(2):
            high_row, low_row = (ref[p : p + 1] for p in (planes - 1 - depth, depth))
            row = jnp.where(core_ref[0] == 1, high_row, low_row)
            coarse = row.astype(BF16).astype(F32)
            at = 2 * s + depth
            near[at : at + 1] = coarse
            near[at + 4 : at + 5] = row - coarse
    coded_ref[...] = near[...].astype(BF16)


def matrix_kernel(synthesis_ref, decay_ref, analysis_ref, out_ref, turned_ref):
    rest = synthesis_ref[...].astype(F32) * decay_ref[...]
    total = jnp.full(out_ref.shape, 1.0 / out_ref.shape[1], F32)
    for _ in range(3):
        part = rest.astype(BF16)
        rest = rest - part.astype(F32)
        total = total + jnp.dot(part, analysis_ref[...], preferred_element_type=F32)
    out_ref[...] = total.astype(BF16)
    turned_ref[...] = total.T.astype(BF16)


def add_kernel(*refs):
    *value_refs, out_ref = refs
    out_ref[...] = functools.reduce(jnp.add, [ref[...] for ref in value_refs])


def join_kernel(sent_ref, one_ref, two_ref, out_ref):
    planes = sent_ref.shape[0]
    out_ref[:planes] = sent_ref[...]
    out_ref[planes:] = one_ref[...] + two_ref[...]


def divide_kernel(cells, kept_ref, mine_ref, arrived_ref, out_ref):
    planes = kept_ref.shape[0]
    total = mine_ref[planes:] + arrived_ref[planes:]
    out_ref[...] = (kept_ref[...] + arrived_ref[:planes]) * (cells / total)


def message_kernel(*refs):
    count = (len(refs) - 2) // 2
    v_ref, out_ref = refs[-2:]
    orient, cells = refs[0].shape[1:]

    @each_row_block(orient)
    def _(index):
        rows = rows_of(index)
        narrow = v_ref[3, rows, :].astype(BF16)
        leaves = narrow < jnp.zeros_like(narrow)
        for p in range(count):
            for t in range(cells // LANES):
                at = 0, rows, columns(t)
                out_ref[p, rows, columns(t)] = jnp.where(leaves, refs[p][at], refs[count + p][at])

    if count > 1:
        out_ref[:, orient:] = jnp.zeros_like(out_ref[:, orient:])


def first_message_kernel(mine_ref, other_ref, *refs):
    *coded_refs, v_ref, out_ref = refs
    message_kernel(mine_ref, other_ref, v_ref, out_ref)
    orient = mine_ref.shape[1]
    for k, ref in enumerate(coded_refs):
        out_ref[0, orient + 16 * k : orient + 16 * (k + 1)] = ref[...]


def write_edge(edges_ref, step, faces, rows, v_ref):
    narrow = v_ref[0, rows, :].astype(BF16)
    plus_x = narrow > jnp.zeros_like(narrow)
    for t in range(len(faces[0])):
        edges_ref[step, rows, columns(t)] = jnp.where(plus_x, faces[-1][t], faces[0][t])


def alone_step(source_ref, moved, targets, v_ref, edges_ref, step):
    planes, orient, _ = source_ref.shape

    @each_row_block(orient)
    def _(index):
        rows = rows_of(index)
        geo = geometry(v_ref, rows)
        loaded = [load_plane(source_ref, p, rows) for p in range(planes)]
        if edges_ref is not None:
            write_edge(edges_ref, step, loaded, rows, v_ref)
        for p in targets:
            before = loaded[p - 1] if p > 0 else None
            after = loaded[p + 1] if p < planes - 1 else None
            store_plane(moved, p, rows, drift(loaded[p], before, after, geo))


def first_alone_kernel(start_ref, first_ref, v_ref, m_ref, out_ref, edges_ref, *refs):
    *inner_refs, held, moved = refs
    planes, orient, _ = start_ref.shape
    first = boltzmann(first_ref[...])
    for p in range(planes):
        held[p] = (first[p : p + 1] * start_ref[p].astype(F32)).astype(BF16)
    alone_step(held, moved, range(planes), v_ref, None, 0)
    for p in (0, planes - 1, *range(1, planes - 1)):
        state = (first[p : p + 1] * first[p : p + 1] * mix(m_ref[...], moved[p])).astype(BF16)
        out_ref[p] = state
        if 0 < p < planes - 1:
            inner_refs[p - 1][0] = state

    @each_row_block(orient)
    def _(index):
        rows = rows_of(index)
        write_edge(edges_ref, 0, [load_plane(out_ref, p, rows) for p in (0, planes - 1)], rows, v_ref)


def next_alone_kernel(
    state_ref, first_ref, second_ref, v_ref, m_ref, out_ref, edges2_ref, edges3_ref, held, moved
):
    planes, orient, _ = state_ref.shape
    first = boltzmann(first_ref[...])
    second = boltzmann(second_ref[...])
    alone_step(state_ref, moved, range(planes), v_ref, None, 0)
    for p in range(planes):
        out_ref[p] = (first[p : p + 1] * second[p : p + 1] * mix(m_ref[...], moved[p])).astype(BF16)
    alone_step(out_ref, moved, (0, planes - 1), v_ref, edges2_ref, 0)
    for p in (0, planes - 1):
        held[p] = (second[p : p + 1] * second[p : p + 1] * mix(m_ref[...], moved[p])).astype(BF16)

    @each_row_block(orient)
    def _(index):
        rows = rows_of(index)
        write_edge(edges3_ref, 0, [load_plane(held, p, rows) for p in (0, planes - 1)], rows, v_ref)


def face_parts(v_ref, rows):
    vx = v_ref[0, rows, :]
    rate = courant * jnp.abs(vx)
    return v_ref[3, rows, :] > 0, jnp.where(vx > 0, rate, 0.0), jnp.where(vx > 0, 0.0, rate)


def face_drifts(v_ref, mine_ref, other_ref, moved, slots):
    @each_row_block(v_ref.shape[1])
    def _(index):
        rows = rows_of(index)
        ahead, rate_plus, rate_minus = face_parts(v_ref, rows)
        for t in range(mine_ref.shape[2] // LANES):
            mine = mine_ref[0, rows, columns(t)].astype(F32)
            other = other_ref[0, rows, columns(t)].astype(F32)
            face = jnp.where(ahead, mine, other)
            moved[slots[0], rows, columns(t)] = (rate_plus * face).astype(BF16)
            moved[slots[1], rows, columns(t)] = (rate_minus * face).astype(BF16)


def second_step_kernel(
    core_ref, alone_ref, later_ref, edge_ref, mine_ref, other_ref, first_ref, second_ref, v_ref, m_ref,
    face_low_ref, face_high_ref, next_ref, sent_near_ref, sent_far_ref, kept_ref, outer_ref, held, moved,
):
    planes, orient, _ = alone_ref.shape
    matrix = m_ref[...]
    first, second = boltzmann(first_ref[...]), boltzmann(second_ref[...])
    core = core_ref[0]
    mine, other = (block[:4] + block[4:8] for block in (ref[0, orient:].astype(F32) for ref in (mine_ref, other_ref)))
    other = (other[2:4], other[0:2])
    mine = (mine[0:2], mine[2:4])
    low = [jnp.where(core == 0, mine[k], other[k]) for k in range(2)]
    high = [jnp.where(core == 0, other[k], mine[k]) for k in range(2)]
    beyond = [boltzmann(block[k : k + 1]) for block in (low[0], high[0], low[1], high[1]) for k in range(2)]
    face_drifts(v_ref, mine_ref, other_ref, moved, (0, 1))

    @each_row_block(orient)
    def _(index):
        rows = rows_of(index)
        _, rate_plus, rate_minus = face_parts(v_ref, rows)
        for t in range(edge_ref.shape[2] // LANES):
            edge = edge_ref[0, rows, columns(t)].astype(F32)
            moved[2, rows, columns(t)] = (rate_minus * edge).astype(BF16)
            moved[3, rows, columns(t)] = (rate_plus * edge).astype(BF16)

    squared = first * first
    for p, slot, face_ref in ((0, 1, face_low_ref), (planes - 1, 2, face_high_ref)):
        arrived = squared[p : p + 1] * mix(matrix, moved[slot - 1])
        held[slot] = arrived.astype(BF16)
        face_ref[0] = (alone_ref[p].astype(F32) + arrived).astype(BF16)
    held[0] = (beyond[0] * beyond[0] * mix(matrix, moved[2])).astype(BF16)
    held[3] = (beyond[2] * beyond[2] * mix(matrix, moved[3])).astype(BF16)

    @each_row_block(orient)
    def _(index):
        rows = rows_of(index)
        geo = geometry(v_ref, rows)
        _, rate_plus, rate_minus = face_parts(v_ref, rows)
        below, low, high, above = (load_plane(held, p, rows) for p in range(4))
        face_low, face_high = (load_plane(ref, 0, rows) for ref in (face_low_ref, face_high_ref))

        def onward(rate, tiles):
            return [rate * tile.astype(F32) for tile in tiles]

        store_plane(moved, 0, rows, onward(rate_minus, below))
        store_plane(moved, 1, rows, drift(below, None, face_low, geo))
        store_plane(moved, 2, rows, drift(low, below, None, geo))
        store_plane(moved, 3, rows, onward(rate_plus, low))
        store_plane(moved, 4, rows, onward(rate_minus, high))
        store_plane(moved, 5, rows, drift(high, None, above, geo))
        store_plane(moved, 6, rows, drift(above, face_high, None, geo))
        store_plane(moved, 7, rows, onward(rate_plus, above))

    cross = first * second
    outer = ((0, 0, beyond[1] * beyond[5]), (1, 1, beyond[0] * beyond[4]))
    outer += ((planes + 2, 6, beyond[2] * beyond[6]), (planes + 3, 7, beyond[3] * beyond[7]))
    for p, slot, factor in outer:
        next_ref[p] = (factor * mix(matrix, moved[slot])).astype(BF16)
    slots = {0: 2, 1: 3, planes - 2: 4, planes - 1: 5}
    for p in range(planes):
        kept = later_ref[p]
        if p in slots:
            kept = (kept.astype(F32) + cross[p : p + 1] * mix(matrix, moved[slots[p]])).astype(BF16)
        next_ref[p + 2] = kept
    for p in range(planes // 2):
        sent_ref = (sent_near_ref, sent_far_ref)[p]
        sent_ref[0] = next_ref[2 + (planes - 1) * (1 - core) + (2 * core - 1) * p]
        kept_ref[p] = next_ref[2 + (planes - 1) * core + (1 - 2 * core) * p]
    outer_ref[0:1] = beyond[4] * beyond[4]
    outer_ref[1:2] = beyond[6] * beyond[6]


def middle_kernel(
    core_ref, own_ref, near_ref, far_ref, message_ref, first_ref, second_ref, v_ref, m_ref, out_ref, total_ref, moved
):
    _, orient, cells = own_ref.shape
    planes = first_ref.shape[0]

    def cross_of(depth):
        low, high = (
            boltzmann(first_ref[p : p + 1]) * boltzmann(second_ref[p : p + 1]) for p in (depth, planes - 1 - depth)
        )
        return jnp.where(core_ref[0] == 0, low, high)

    cross = [cross_of(depth) for depth in range(2)]

    @each_row_block(orient)
    def _(index):
        rows = rows_of(index)
        ahead, rate_plus, rate_minus = face_parts(v_ref, rows)
        rate = rate_plus + rate_minus
        for t in range(cells // LANES):
            gained = rate * message_ref[0, rows, columns(t)].astype(F32)
            moved[0, rows, columns(t)] = jnp.where(ahead, gained, 0.0).astype(BF16)
            moved[1, rows, columns(t)] = jnp.where(ahead, 0.0, gained).astype(BF16)

    own_face = own_ref[0].astype(F32) + cross[0] * mix(m_ref[...], moved[0])
    partner_face = near_ref[0].astype(F32) + cross[0] * mix(m_ref[...], moved[1])
    face = jnp.sum(own_face * partner_face, axis=0, keepdims=True)
    total = jnp.zeros((1, 1), F32)
    for p in range(own_ref.shape[0]):
        if p > 0:
            face = jnp.sum(own_ref[p].astype(F32) * far_ref[0].astype(F32), axis=0, keepdims=True)
        met = face / (orient * cross[p])
        out_ref[p : p + 1] = met
        total = total + jnp.sum(met, axis=1, keepdims=True)
    total_ref[...] = jnp.broadcast_to(total, total_ref.shape)


def third_step_kernel(
    held_ref, mine_ref, other_ref, first_ref, second_ref, outer_ref, v_ref, m_ref, next_ref, held, moved
):
    planes, orient, _ = held.shape
    matrix = m_ref[...]
    first, second = boltzmann(first_ref[...]), boltzmann(second_ref[...])
    face_drifts(v_ref, mine_ref, other_ref, moved, (0, 1))
    cross = first * second
    for p in range(planes):
        kept = held_ref[p + 2]
        if p in (0, planes - 1):
            arrived = cross[p : p + 1] * mix(matrix, moved[min(p, 1)])
            kept = (kept.astype(F32) + arrived).astype(BF16)
        held[p] = kept

    @each_row_block(orient)
    def _(index):
        rows = rows_of(index)
        geo = geometry(v_ref, rows)
        loaded = [load_plane(held_ref, p, rows) for p in (0, 1)]
        loaded += [load_plane(held, p, rows) for p in range(planes)]
        loaded += [load_plane(held_ref, p, rows) for p in (planes + 2, planes + 3)]
        for p in range(planes + 2):
            store_plane(moved, p, rows, drift(loaded[p + 1], loaded[p], loaded[p + 2], geo))

    squared = second * second
    factors = [outer_ref[0:1]] + [squared[p : p + 1] for p in range(planes)] + [outer_ref[1:2]]
    for p, factor in enumerate(factors):
        next_ref[p] = (factor * mix(matrix, moved[p])).astype(BF16)


def weight_kernel(core_ref, partner_ref, start_ref, turned_ref, weight_ref, own_ref):
    planes = partner_ref.shape[0]
    core = core_ref[0]
    for p in range(planes):
        weight_ref[p] = mix(turned_ref[...], partner_ref[p]).astype(BF16)
    for p in range(2):
        own_ref[p] = mix(turned_ref[...], start_ref[core * (planes - 1) + p - 2 * p * core]).astype(BF16)


def fold(value):
    return jnp.sum(value.reshape(ROWS // 8, 8, LANES), axis=0)


def pairing_kernel(held_ref, second_ref, v_ref, weight_ref, *refs):
    *partner_refs, out_ref = refs
    planes, orient, cells = weight_ref.shape
    second = boltzmann(second_ref[...])
    tiles = cells // LANES

    def body(index, sums):
        rows = rows_of(index)
        geo = geometry(v_ref, rows)
        loaded = [load_plane(held_ref, p, rows) for p in range(planes + 2)]
        new = []
        for p in range(planes):
            moved_tiles = drift(loaded[p + 1], loaded[p], loaded[p + 2], geo)
            weights = load_plane(weight_ref, p, rows)
            partner = load_plane(partner_refs[p], 0, rows)
            for t in range(tiles):
                last, third = sums[2 * (p * tiles + t)], sums[2 * (p * tiles + t) + 1]
                new.append(last + fold(moved_tiles[t] * weights[t].astype(F32)))
                new.append(third + fold(loaded[p + 1][t].astype(F32) * partner[t].astype(F32)))
        return tuple(new)

    zero = jnp.zeros((8, LANES), F32)
    sums = lax.fori_loop(0, orient // ROWS, body, (zero,) * (2 * planes * tiles), unroll=UNROLL)
    for p in range(planes):
        for t in range(tiles):
            last = jnp.sum(sums[2 * (p * tiles + t)], axis=0, keepdims=True)
            third = jnp.sum(sums[2 * (p * tiles + t) + 1], axis=0, keepdims=True)
            factor = second[p : p + 1, columns(t)]
            out_ref[p : p + 1, columns(t)] = (0.5 * factor * last + third / (factor * factor)) / orient


def last_kernel(
    core_ref, message_ref, weight_ref, own_weight_ref, own_low_ref, own_high_ref, partner_low_ref, partner_high_ref,
    shared_ref, met_ref,    own_ref, partner_ref, v_ref, m_ref, sent_ref, kept_ref, moved, gained,
):
    planes, cells = shared_ref.shape
    orient = m_ref.shape[0]
    tiles = cells // LANES
    core = core_ref[0]
    half = planes // 2
    face = core * (planes - 1)
    inner = face + 1 - 2 * core

    def at_face(ref, depth):
        return jnp.where(core == 0, boltzmann(ref[depth : depth + 1]), boltzmann(ref[planes - 1 - depth : planes - depth]))

    factors = [[at_face(ref, depth) for depth in range(2)] for ref in (partner_ref, own_ref)]

    @each_row_block(orient)
    def _(index):
        rows = rows_of(index)
        ahead, rate_plus, rate_minus = face_parts(v_ref, rows)
        rate = rate_plus + rate_minus
        for t in range(tiles):
            got = rate * message_ref[0, rows, columns(t)].astype(F32)
            moved[0, rows, columns(t)] = jnp.where(ahead, got, 0.0).astype(BF16)
            moved[1, rows, columns(t)] = jnp.where(ahead, 0.0, got).astype(BF16)

    for s in range(2):
        gained[s] = (factors[s][0] * factors[s][0] * mix(m_ref[...], moved[s])).astype(BF16)

    def body(index, sums):
        rows = rows_of(index)
        ahead, rate_plus, rate_minus = face_parts(v_ref, rows)
        rate = rate_plus + rate_minus
        sides = (jnp.where(ahead, rate, 0.0), jnp.where(ahead, 0.0, rate))
        message = load_plane(message_ref, 1, rows)
        new = []
        for s in range(2):
            change = load_plane(gained, s, rows)
            moved_tiles = drift(change, None, None, geometry(v_ref, rows, 1.0 - 2.0 * s))
            if s == 0:
                weights = [load_plane(weight_ref, p, rows) for p in (face, inner)]
            else:
                weights = [load_plane(own_weight_ref, p, rows) for p in (0, 1)]
            pair = ((partner_low_ref, partner_high_ref), (own_low_ref, own_high_ref))[s]
            third = [jnp.where(core == 0, low, high) for low, high in zip(*(load_plane(ref, 0, rows) for ref in pair))]
            for t in range(tiles):
                on_face = moved_tiles[t] + sides[s] * message[t].astype(F32)
                wide = change[t].astype(F32)
                terms = (
                    on_face * weights[0][t].astype(F32),
                    sides[s] * wide * weights[1][t].astype(F32),
                    wide * third[t].astype(F32),
                )
                base = 3 * (s * tiles + t)
                new += [sums[base + k] + fold(term) for k, term in enumerate(terms)]
        return tuple(new)

    zero = jnp.zeros((8, LANES), F32)
    sums = lax.fori_loop(0, orient // ROWS, body, (zero,) * (6 * tiles), unroll=UNROLL)
    for t in range(tiles):
        shares = []
        for s in range(2):
            base = 3 * (s * tiles + t)
            last, onward, third = (jnp.sum(sums[base + k], axis=0, keepdims=True) / orient for k in range(3))
            near, far = (factors[s][depth][:, columns(t)] for depth in range(2))
            shares.append((0.5 * near * last + third / (near * near), 0.5 * far * onward))
        for p in range(planes):
            at = slice(p, p + 1), columns(t)
            mine = core == (0 if p < half else 1)
            depth = min(p, planes - 1 - p)
            met = jnp.where(mine, 0.5 * met_ref[depth : depth + 1, columns(t)], 0.0)
            sent, kept = shared_ref[at] + met, met
            if depth < 2:
                sent = sent + jnp.where(mine, shares[0][depth], 0.0)
                kept = kept + jnp.where(mine, shares[1][depth], 0.0)
            sent_ref[at] = sent
            kept_ref[at] = kept


def split_outputs(outs):
    low, high, state, near, far, kept, outer = outs
    return (low, high), state, (near, far), kept, outer


def kernel_call(kernel, outs, scratch, args):
    vmem = pl.BlockSpec(memory_space=pltpu.VMEM)
    smem = pl.BlockSpec(memory_space=pltpu.SMEM)
    return pl.pallas_call(
        kernel,
        out_shape=outs,
        in_specs=[smem if arg.dtype == jnp.int32 else vmem for arg in args],
        out_specs=jax.tree.map(lambda _: vmem, outs),
        scratch_shapes=[pltpu.VMEM(*s) if len(s) == 2 else pltpu.VMEM(s, BF16) for s in scratch],
        compiler_params=pltpu.CompilerParams(vmem_limit_bytes=12 << 20),
        cost_estimate=pl.CostEstimate(flops=0, bytes_accessed=0, transcendentals=0),
    )(*args)


def shards(fields, end_weights, directions, analysis, synthesis, decay_rates):
    device = lax.axis_index("space")
    core = device % 2
    planes, cells = fields.shape
    orient = end_weights.shape[0]
    plane_index = device // 2 * planes + lax.broadcasted_iota(jnp.int32, (planes, 1), 0)
    ramp = slope * plane_index.astype(F32) / (planes * lax.axis_size("space") // 2)
    own = fields + ramp
    partner = swap_species(fields) + ramp

    wide = lambda extra: jax.ShapeDtypeStruct((planes + extra, orient, cells), BF16)
    slab, plane = wide(0), wide(1 - planes)
    face = core ^ (1 - device // 2 % 2)
    core_word = jnp.reshape(face, (1,)).astype(jnp.int32)
    species_word = jnp.reshape(core, (1,)).astype(jnp.int32)
    start = jnp.transpose(end_weights, (1, 0, 2))
    spread, edge0, coded = kernel_call(
        prologue_kernel,
        (jax.ShapeDtypeStruct((4, orient, LANES), F32), plane, jax.ShapeDtypeStruct((16, cells), BF16)),
        (((16, cells), F32),),
        (core_word, species_word, directions, start, own, partner),
    )
    matrix, turned = kernel_call(
        matrix_kernel,
        (jax.ShapeDtypeStruct((orient, orient), BF16),) * 2,
        (),
        (synthesis, decay_rates[None], analysis),
    )
    other0, matrix = lax.optimization_barrier((swap_species(edge0), matrix))
    message0 = kernel_call(
        first_message_kernel,
        jax.ShapeDtypeStruct((1, orient + 16, cells), BF16),
        (),
        (edge0, other0, coded, spread),
    )

    def message(blocks, others):
        shape = jax.ShapeDtypeStruct((len(blocks), orient + PAD_ROWS, cells), BF16)
        return kernel_call(message_kernel, shape, (), (*blocks, *others, spread))

    start, _ = lax.optimization_barrier((start, message0))
    arrived0 = exchange_faces(message0)
    alone, edges1, *inner = kernel_call(
        first_alone_kernel,
        (slab, plane) + (plane,) * (planes - 2),
        (slab.shape, slab.shape),
        (start, own, spread, matrix),
    )
    weights, own_weights = kernel_call(
        weight_kernel, (slab, wide(2 - planes)), (), (core_word, swap_species(start), start, turned)
    )
    others1, weights, *partner_inner = lax.optimization_barrier(
        (swap_species(edges1), weights, *map(swap_species, inner))
    )
    message1 = kernel_call(
        first_message_kernel,
        jax.ShapeDtypeStruct((1, orient + 16 * PAD, cells), BF16),
        (),
        (edges1, others1, *[coded] * PAD, spread),
    )
    state, *_ = lax.optimization_barrier((alone, message1, weights))
    later, edges2, edges3 = kernel_call(
        next_alone_kernel, (slab, plane, plane), (slab.shape, slab.shape), (state, own, partner, spread, matrix)
    )
    edges2, edges3, arrived0 = lax.optimization_barrier((edges2, edges3, arrived0))
    message2 = message([edges2, edges3], [swap_species(edges2), swap_species(edges3)])
    arrived = [exchange_faces(message1), exchange_faces(message2)]
    crossed0 = swap_species(arrived0)

    alone, *_ = lax.optimization_barrier((alone, message1, message2))
    half = planes // 2
    faces, second_state, sent_half, kept_half, outer = split_outputs(
        kernel_call(
            second_step_kernel,
            (plane, plane, wide(4), plane, plane, wide(half - planes), jax.ShapeDtypeStruct((2, cells), F32)),
            ((4, orient, cells), (8, orient, cells)),
            (core_word, alone, later, edge0, arrived0, crossed0, own, partner, spread, matrix),
        )
    )
    arrived1, second_state = lax.optimization_barrier((arrived[0], second_state))
    *moving, low_face, _ = lax.optimization_barrier((*sent_half, faces[0], arrived1))
    *partner_half, partner_low, crossed1 = lax.optimization_barrier(
        (*map(swap_species, moving), swap_species(low_face), swap_species(arrived1))
    )
    density = jax.ShapeDtypeStruct((planes, cells), F32)
    met, partition = kernel_call(
        middle_kernel,
        (jax.ShapeDtypeStruct((half, cells), F32), density),
        ((2, orient, cells),),
        (core_word, kept_half, *partner_half, arrived1, own, partner, spread, matrix),
    )
    count = lax.axis_size("space")

    def received(value, distance, after):
        block = lax.ppermute(value, "space", [(i, i ^ distance) for i in range(count)])
        return lax.optimization_barrier((block, after))

    def gathered(value, distance, after):
        block, after = received(value, distance, after)
        return kernel_call(add_kernel, density, (), (value, block)), after

    high_face, second_state, _ = lax.optimization_barrier((faces[1], second_state, met))
    partner_faces = [partner_low, swap_species(high_face)]
    third_state = kernel_call(
        third_step_kernel,
        wide(2),
        (slab.shape, wide(2).shape),
        (second_state, arrived1, crossed1, own, partner, outer, spread, matrix),
    )
    shared = kernel_call(
        pairing_kernel,
        density,
        (),
        (third_state, partner, spread, weights, partner_faces[0], *partner_inner, partner_faces[1]),
    )
    blocks = [lax.ppermute(partition, "space", [(i, i ^ far) for i in range(count)]) for far in (4, 8, 12)]
    *blocks, shared = lax.optimization_barrier((*blocks, shared))
    partition = kernel_call(add_kernel, density, (), (partition, *blocks))
    distance = 16
    while distance < count:
        partition, shared = gathered(partition, distance, shared)
        distance *= 2
    arrived2, shared, _ = lax.optimization_barrier((arrived[1], shared, partition))
    sent, kept = kernel_call(
        last_kernel,
        (density, density),
        ((2, orient, cells), (2, orient, cells)),
        (
            core_word, arrived2, weights, own_weights, *faces, *partner_faces, shared, met,
            own, partner, spread, matrix,
        ),
    )
    beside, sent = received(partition, 2, sent)
    joined = kernel_call(
        join_kernel, jax.ShapeDtypeStruct((2 * planes, cells), F32), (), (sent, partition, beside)
    )
    return kernel_call(
        functools.partial(divide_kernel, count // 2 * planes * cells),
        density,
        (),
        (kept, joined, swap_species(joined)),
    )


def solution(mesh):
    return jax.shard_map(
        shards,
        mesh=mesh,
        in_specs=(P(("runs", "space"), None), P(None, ("runs", "space"), None), P(), P(), P(), P()),
        out_specs=P(("runs", "space"), None),
        check_vma=False,
    )
```

```python
import functools

import jax
import jax.numpy as jnp
from jax import lax
from jax.experimental import pallas as pl
from jax.experimental.pallas import tpu as pltpu
from jax.sharding import PartitionSpec as P

NZ = 16
STEPS = 4
LANES = 128
ROWS = 16
UNROLL = 16
PAD = 2
PAD_ROWS = 32

courant = 0.3
slope = 0.6

BF16 = jnp.bfloat16
F32 = jnp.float32


def swap_species(block):
    count = lax.axis_size("space")
    return lax.ppermute(block, "space", [(i ^ 1, i) for i in range(count)])


def exchange_faces(block):
    count = lax.axis_size("space")
    route = []
    for slab in range(count // 2):
        beside = ((slab + 1) ^ 1) - 1
        route += [(2 * slab, 2 * (slab ^ 1)), (2 * slab + 1, 2 * beside % count + 1)]
    return lax.ppermute(block, "space", route)


def rows_of(index):
    return pl.ds(pl.multiple_of(index * ROWS, ROWS), ROWS)


def each_row_block(orient):
    def run(body):
        def step(index, carry):
            body(index)
            return carry

        lax.fori_loop(0, orient // ROWS, step, 0, unroll=UNROLL)

    return run


def columns(tile):
    return slice(LANES * tile, LANES * (tile + 1))


def geometry(v_ref, rows, sign=1.0):
    lane = lax.broadcasted_iota(jnp.int32, (ROWS, LANES), 1)
    vx, vy, vz = (sign * v_ref[c, rows, :] for c in range(3))
    narrow = vx.astype(BF16)
    plus_x, narrow_plus, plus_y, plus_z = vx > 0, narrow > jnp.zeros_like(narrow), vy > 0, vz > 0
    rate_x, rate_y, rate_z = (courant * jnp.abs(t) for t in (vx, vy, vz))
    stay = 1.0 - (rate_x + rate_y + rate_z)
    z_from = (lane & (LANES - NZ)) | (jnp.where(plus_z, lane - 1, lane + 1) & (NZ - 1))
    y_from = jnp.where(plus_y, lane - NZ, lane + NZ) & (LANES - 1)
    y_edge = jnp.where(plus_y, lane, LANES - 1 - lane) < NZ
    return plus_x, narrow_plus, plus_y, stay, rate_x, rate_y, rate_z, z_from, y_from, y_edge


def pick(tile, index):
    return jnp.take_along_axis(tile, index, axis=1, mode="promise_in_bounds")


def load_plane(ref, plane, rows):
    return [ref[plane, rows, columns(t)] for t in range(ref.shape[2] // LANES)]


def drift(center, before, after, geo):
    plus_x, narrow_plus, plus_y, stay, rate_x, rate_y, rate_z, z_from, y_from, y_edge = geo
    tiles = len(center)
    center = [tile.astype(F32) for tile in center]
    turned = [pick(tile, y_from) for tile in center]
    moved = []
    for t in range(tiles):
        total = stay * center[t]
        if before is not None and after is not None:
            total = total + rate_x * jnp.where(narrow_plus, before[t], after[t]).astype(F32)
        elif before is not None:
            total = total + jnp.where(plus_x, rate_x, 0.0) * before[t].astype(F32)
        elif after is not None:
            total = total + jnp.where(plus_x, 0.0, rate_x) * after[t].astype(F32)
        over = jnp.where(plus_y, turned[t - 1], turned[(t + 1) % tiles])
        total = total + rate_y * jnp.where(y_edge, over, turned[t])
        total = total + rate_z * pick(center[t], z_from)
        moved.append(total)
    return moved


def store_plane(ref, plane, rows, tiles):
    for t, tile in enumerate(tiles):
        ref[plane, rows, columns(t)] = tile.astype(ref.dtype)


def mix(matrix, moved):
    return jnp.dot(matrix, moved, preferred_element_type=F32)


def boltzmann(field):
    return jnp.exp(-0.5 * field)


def prologue_kernel(
    core_ref, species_ref, directions_ref, start_ref, fields_ref, partner_ref, spread_ref, edge_ref, coded_ref, near
):
    sign = 1.0 - 2.0 * species_ref[0].astype(F32)
    toward = sign * (1.0 - 2.0 * core_ref[0].astype(F32))
    planes, orient, cells = start_ref.shape
    low = boltzmann(fields_ref[0:1])
    high = boltzmann(fields_ref[fields_ref.shape[0] - 1 :])
    for c in range(4):
        row = directions_ref[c % 3 : c % 3 + 1]
        column = jnp.broadcast_to(row, (LANES, orient)).T
        spread_ref[c] = (toward if c == 3 else sign) * column

    @each_row_block(orient)
    def _(index):
        rows = rows_of(index)
        plus_x = spread_ref[0, rows, :] > 0
        for t in range(cells // LANES):
            at = rows, columns(t)
            chosen = jnp.where(
                plus_x,
                high[:, columns(t)] * start_ref[planes - 1, *at].astype(F32),
                low[:, columns(t)] * start_ref[0, *at].astype(F32),
            )
            edge_ref[0, *at] = chosen.astype(BF16)

    near[...] = jnp.zeros_like(near)
    for s, ref in enumerate((fields_ref, partner_ref)):
        for depth in range(2):
            high_row, low_row = (ref[p : p + 1] for p in (planes - 1 - depth, depth))
            row = jnp.where(core_ref[0] == 1, high_row, low_row)
            coarse = row.astype(BF16).astype(F32)
            at = 2 * s + depth
            near[at : at + 1] = coarse
            near[at + 4 : at + 5] = row - coarse
    coded_ref[...] = near[...].astype(BF16)


def matrix_kernel(synthesis_ref, decay_ref, analysis_ref, out_ref, turned_ref):
    rest = synthesis_ref[...].astype(F32) * decay_ref[...]
    total = jnp.full(out_ref.shape, 1.0 / out_ref.shape[1], F32)
    for _ in range(3):
        part = rest.astype(BF16)
        rest = rest - part.astype(F32)
        total = total + jnp.dot(part, analysis_ref[...], preferred_element_type=F32)
    out_ref[...] = total.astype(BF16)
    turned_ref[...] = total.T.astype(BF16)


def add_kernel(one_ref, two_ref, out_ref):
    out_ref[...] = one_ref[...] + two_ref[...]


def add_wide_kernel(one_ref, two_ref, out_ref):
    planes = one_ref.shape[0]
    for k in range(out_ref.shape[0] // planes):
        out_ref[k * planes : (k + 1) * planes] = one_ref[...] + two_ref[...]


def divide_kernel(cells, kept_ref, arrived_ref, *refs):
    *total_refs, out_ref = refs
    planes = kept_ref.shape[0]
    total = functools.reduce(jnp.add, [ref[:planes] for ref in total_refs])
    out_ref[...] = (kept_ref[...] + arrived_ref[...]) * (cells / total)


def message_kernel(*refs):
    count = (len(refs) - 2) // 2
    v_ref, out_ref = refs[-2:]
    orient, cells = refs[0].shape[1:]

    @each_row_block(orient)
    def _(index):
        rows = rows_of(index)
        narrow = v_ref[3, rows, :].astype(BF16)
        leaves = narrow < jnp.zeros_like(narrow)
        for p in range(count):
            for t in range(cells // LANES):
                at = 0, rows, columns(t)
                out_ref[p, rows, columns(t)] = jnp.where(leaves, refs[p][at], refs[count + p][at])

    if count > 1:
        out_ref[:, orient:] = jnp.zeros_like(out_ref[:, orient:])


def first_message_kernel(mine_ref, other_ref, *refs):
    *coded_refs, v_ref, out_ref = refs
    message_kernel(mine_ref, other_ref, v_ref, out_ref)
    orient = mine_ref.shape[1]
    for k, ref in enumerate(coded_refs):
        out_ref[0, orient + 16 * k : orient + 16 * (k + 1)] = ref[...]


def write_edge(edges_ref, step, faces, rows, v_ref):
    narrow = v_ref[0, rows, :].astype(BF16)
    plus_x = narrow > jnp.zeros_like(narrow)
    for t in range(len(faces[0])):
        edges_ref[step, rows, columns(t)] = jnp.where(plus_x, faces[-1][t], faces[0][t])


def alone_step(source_ref, moved, targets, v_ref, edges_ref, step):
    planes, orient, _ = source_ref.shape

    @each_row_block(orient)
    def _(index):
        rows = rows_of(index)
        geo = geometry(v_ref, rows)
        loaded = [load_plane(source_ref, p, rows) for p in range(planes)]
        if edges_ref is not None:
            write_edge(edges_ref, step, loaded, rows, v_ref)
        for p in targets:
            before = loaded[p - 1] if p > 0 else None
            after = loaded[p + 1] if p < planes - 1 else None
            store_plane(moved, p, rows, drift(loaded[p], before, after, geo))


def first_alone_kernel(start_ref, first_ref, v_ref, m_ref, out_ref, edges_ref, *refs):
    *inner_refs, held, moved = refs
    planes, orient, _ = start_ref.shape
    first = boltzmann(first_ref[...])
    for p in range(planes):
        held[p] = (first[p : p + 1] * start_ref[p].astype(F32)).astype(BF16)
    alone_step(held, moved, range(planes), v_ref, None, 0)
    for p in (0, planes - 1, *range(1, planes - 1)):
        state = (first[p : p + 1] * first[p : p + 1] * mix(m_ref[...], moved[p])).astype(BF16)
        out_ref[p] = state
        if 0 < p < planes - 1:
            inner_refs[p - 1][0] = state

    @each_row_block(orient)
    def _(index):
        rows = rows_of(index)
        write_edge(edges_ref, 0, [load_plane(out_ref, p, rows) for p in (0, planes - 1)], rows, v_ref)


def next_alone_kernel(
    state_ref, first_ref, second_ref, v_ref, m_ref, out_ref, edges2_ref, edges3_ref, held, moved
):
    planes, orient, _ = state_ref.shape
    first = boltzmann(first_ref[...])
    second = boltzmann(second_ref[...])
    alone_step(state_ref, moved, range(planes), v_ref, None, 0)
    for p in range(planes):
        out_ref[p] = (first[p : p + 1] * second[p : p + 1] * mix(m_ref[...], moved[p])).astype(BF16)
    alone_step(out_ref, moved, (0, planes - 1), v_ref, edges2_ref, 0)
    for p in (0, planes - 1):
        held[p] = (second[p : p + 1] * second[p : p + 1] * mix(m_ref[...], moved[p])).astype(BF16)

    @each_row_block(orient)
    def _(index):
        rows = rows_of(index)
        write_edge(edges3_ref, 0, [load_plane(held, p, rows) for p in (0, planes - 1)], rows, v_ref)


def face_parts(v_ref, rows):
    vx = v_ref[0, rows, :]
    rate = courant * jnp.abs(vx)
    return v_ref[3, rows, :] > 0, jnp.where(vx > 0, rate, 0.0), jnp.where(vx > 0, 0.0, rate)


def face_drifts(v_ref, mine_ref, other_ref, moved, slots):
    @each_row_block(v_ref.shape[1])
    def _(index):
        rows = rows_of(index)
        ahead, rate_plus, rate_minus = face_parts(v_ref, rows)
        for t in range(mine_ref.shape[2] // LANES):
            mine = mine_ref[0, rows, columns(t)].astype(F32)
            other = other_ref[0, rows, columns(t)].astype(F32)
            face = jnp.where(ahead, mine, other)
            moved[slots[0], rows, columns(t)] = (rate_plus * face).astype(BF16)
            moved[slots[1], rows, columns(t)] = (rate_minus * face).astype(BF16)


def second_step_kernel(
    core_ref, alone_ref, later_ref, edge_ref, mine_ref, other_ref, first_ref, second_ref, v_ref, m_ref,
    face_low_ref, face_high_ref, next_ref, sent_near_ref, sent_far_ref, kept_ref, outer_ref, held, moved,
):
    planes, orient, _ = alone_ref.shape
    matrix = m_ref[...]
    first, second = boltzmann(first_ref[...]), boltzmann(second_ref[...])
    core = core_ref[0]
    mine, other = (block[:4] + block[4:8] for block in (ref[0, orient:].astype(F32) for ref in (mine_ref, other_ref)))
    other = (other[2:4], other[0:2])
    mine = (mine[0:2], mine[2:4])
    low = [jnp.where(core == 0, mine[k], other[k]) for k in range(2)]
    high = [jnp.where(core == 0, other[k], mine[k]) for k in range(2)]
    beyond = [boltzmann(block[k : k + 1]) for block in (low[0], high[0], low[1], high[1]) for k in range(2)]
    face_drifts(v_ref, mine_ref, other_ref, moved, (0, 1))

    @each_row_block(orient)
    def _(index):
        rows = rows_of(index)
        _, rate_plus, rate_minus = face_parts(v_ref, rows)
        for t in range(edge_ref.shape[2] // LANES):
            edge = edge_ref[0, rows, columns(t)].astype(F32)
            moved[2, rows, columns(t)] = (rate_minus * edge).astype(BF16)
            moved[3, rows, columns(t)] = (rate_plus * edge).astype(BF16)

    squared = first * first
    for p, slot, face_ref in ((0, 1, face_low_ref), (planes - 1, 2, face_high_ref)):
        arrived = squared[p : p + 1] * mix(matrix, moved[slot - 1])
        held[slot] = arrived.astype(BF16)
        face_ref[0] = (alone_ref[p].astype(F32) + arrived).astype(BF16)
    held[0] = (beyond[0] * beyond[0] * mix(matrix, moved[2])).astype(BF16)
    held[3] = (beyond[2] * beyond[2] * mix(matrix, moved[3])).astype(BF16)

    @each_row_block(orient)
    def _(index):
        rows = rows_of(index)
        geo = geometry(v_ref, rows)
        _, rate_plus, rate_minus = face_parts(v_ref, rows)
        below, low, high, above = (load_plane(held, p, rows) for p in range(4))
        face_low, face_high = (load_plane(ref, 0, rows) for ref in (face_low_ref, face_high_ref))

        def onward(rate, tiles):
            return [rate * tile.astype(F32) for tile in tiles]

        store_plane(moved, 0, rows, onward(rate_minus, below))
        store_plane(moved, 1, rows, drift(below, None, face_low, geo))
        store_plane(moved, 2, rows, drift(low, below, None, geo))
        store_plane(moved, 3, rows, onward(rate_plus, low))
        store_plane(moved, 4, rows, onward(rate_minus, high))
        store_plane(moved, 5, rows, drift(high, None, above, geo))
        store_plane(moved, 6, rows, drift(above, face_high, None, geo))
        store_plane(moved, 7, rows, onward(rate_plus, above))

    cross = first * second
    outer = ((0, 0, beyond[1] * beyond[5]), (1, 1, beyond[0] * beyond[4]))
    outer += ((planes + 2, 6, beyond[2] * beyond[6]), (planes + 3, 7, beyond[3] * beyond[7]))
    for p, slot, factor in outer:
        next_ref[p] = (factor * mix(matrix, moved[slot])).astype(BF16)
    slots = {0: 2, 1: 3, planes - 2: 4, planes - 1: 5}
    for p in range(planes):
        kept = later_ref[p]
        if p in slots:
            kept = (kept.astype(F32) + cross[p : p + 1] * mix(matrix, moved[slots[p]])).astype(BF16)
        next_ref[p + 2] = kept
    for p in range(planes // 2):
        sent_ref = (sent_near_ref, sent_far_ref)[p]
        sent_ref[0] = next_ref[2 + (planes - 1) * (1 - core) + (2 * core - 1) * p]
        kept_ref[p] = next_ref[2 + (planes - 1) * core + (1 - 2 * core) * p]
    outer_ref[0:1] = beyond[4] * beyond[4]
    outer_ref[1:2] = beyond[6] * beyond[6]


def middle_kernel(
    core_ref, own_ref, near_ref, far_ref, message_ref, first_ref, second_ref, v_ref, m_ref, out_ref, total_ref, moved
):
    _, orient, cells = own_ref.shape
    planes = first_ref.shape[0]

    def cross_of(depth):
        low, high = (
            boltzmann(first_ref[p : p + 1]) * boltzmann(second_ref[p : p + 1]) for p in (depth, planes - 1 - depth)
        )
        return jnp.where(core_ref[0] == 0, low, high)

    cross = [cross_of(depth) for depth in range(2)]

    @each_row_block(orient)
    def _(index):
        rows = rows_of(index)
        ahead, rate_plus, rate_minus = face_parts(v_ref, rows)
        rate = rate_plus + rate_minus
        for t in range(cells // LANES):
            gained = rate * message_ref[0, rows, columns(t)].astype(F32)
            moved[0, rows, columns(t)] = jnp.where(ahead, gained, 0.0).astype(BF16)
            moved[1, rows, columns(t)] = jnp.where(ahead, 0.0, gained).astype(BF16)

    own_face = own_ref[0].astype(F32) + cross[0] * mix(m_ref[...], moved[0])
    partner_face = near_ref[0].astype(F32) + cross[0] * mix(m_ref[...], moved[1])
    face = jnp.sum(own_face * partner_face, axis=0, keepdims=True)
    total = jnp.zeros((1, 1), F32)
    for p in range(own_ref.shape[0]):
        if p > 0:
            face = jnp.sum(own_ref[p].astype(F32) * far_ref[0].astype(F32), axis=0, keepdims=True)
        met = face / (orient * cross[p])
        out_ref[p : p + 1] = met
        total = total + jnp.sum(met, axis=1, keepdims=True)
    total_ref[...] = jnp.broadcast_to(total, total_ref.shape)


def third_step_kernel(
    held_ref, mine_ref, other_ref, first_ref, second_ref, outer_ref, v_ref, m_ref, next_ref, held, moved
):
    planes, orient, _ = held.shape
    matrix = m_ref[...]
    first, second = boltzmann(first_ref[...]), boltzmann(second_ref[...])
    face_drifts(v_ref, mine_ref, other_ref, moved, (0, 1))
    cross = first * second
    for p in range(planes):
        kept = held_ref[p + 2]
        if p in (0, planes - 1):
            arrived = cross[p : p + 1] * mix(matrix, moved[min(p, 1)])
            kept = (kept.astype(F32) + arrived).astype(BF16)
        held[p] = kept

    @each_row_block(orient)
    def _(index):
        rows = rows_of(index)
        geo = geometry(v_ref, rows)
        loaded = [load_plane(held_ref, p, rows) for p in (0, 1)]
        loaded += [load_plane(held, p, rows) for p in range(planes)]
        loaded += [load_plane(held_ref, p, rows) for p in (planes + 2, planes + 3)]
        for p in range(planes + 2):
            store_plane(moved, p, rows, drift(loaded[p + 1], loaded[p], loaded[p + 2], geo))

    squared = second * second
    factors = [outer_ref[0:1]] + [squared[p : p + 1] for p in range(planes)] + [outer_ref[1:2]]
    for p, factor in enumerate(factors):
        next_ref[p] = (factor * mix(matrix, moved[p])).astype(BF16)


def weight_kernel(core_ref, partner_ref, start_ref, turned_ref, weight_ref, own_ref):
    planes = partner_ref.shape[0]
    core = core_ref[0]
    for p in range(planes):
        weight_ref[p] = mix(turned_ref[...], partner_ref[p]).astype(BF16)
    for p in range(2):
        own_ref[p] = mix(turned_ref[...], start_ref[core * (planes - 1) + p - 2 * p * core]).astype(BF16)


def fold(value):
    return jnp.sum(value.reshape(ROWS // 8, 8, LANES), axis=0)


def pairing_kernel(held_ref, second_ref, v_ref, weight_ref, *refs):
    *partner_refs, out_ref = refs
    planes, orient, cells = weight_ref.shape
    second = boltzmann(second_ref[...])
    tiles = cells // LANES

    def body(index, sums):
        rows = rows_of(index)
        geo = geometry(v_ref, rows)
        loaded = [load_plane(held_ref, p, rows) for p in range(planes + 2)]
        new = []
        for p in range(planes):
            moved_tiles = drift(loaded[p + 1], loaded[p], loaded[p + 2], geo)
            weights = load_plane(weight_ref, p, rows)
            partner = load_plane(partner_refs[p], 0, rows)
            for t in range(tiles):
                last, third = sums[2 * (p * tiles + t)], sums[2 * (p * tiles + t) + 1]
                new.append(last + fold(moved_tiles[t] * weights[t].astype(F32)))
                new.append(third + fold(loaded[p + 1][t].astype(F32) * partner[t].astype(F32)))
        return tuple(new)

    zero = jnp.zeros((8, LANES), F32)
    sums = lax.fori_loop(0, orient // ROWS, body, (zero,) * (2 * planes * tiles), unroll=UNROLL)
    for p in range(planes):
        for t in range(tiles):
            last = jnp.sum(sums[2 * (p * tiles + t)], axis=0, keepdims=True)
            third = jnp.sum(sums[2 * (p * tiles + t) + 1], axis=0, keepdims=True)
            factor = second[p : p + 1, columns(t)]
            out_ref[p : p + 1, columns(t)] = (0.5 * factor * last + third / (factor * factor)) / orient


def last_kernel(
    core_ref, message_ref, weight_ref, own_weight_ref, own_low_ref, own_high_ref, partner_low_ref, partner_high_ref,
    shared_ref, met_ref,    own_ref, partner_ref, v_ref, m_ref, sent_ref, kept_ref, moved, gained,
):
    planes, cells = shared_ref.shape
    orient = m_ref.shape[0]
    tiles = cells // LANES
    core = core_ref[0]
    half = planes // 2
    face = core * (planes - 1)
    inner = face + 1 - 2 * core

    def at_face(ref, depth):
        return jnp.where(core == 0, boltzmann(ref[depth : depth + 1]), boltzmann(ref[planes - 1 - depth : planes - depth]))

    factors = [[at_face(ref, depth) for depth in range(2)] for ref in (partner_ref, own_ref)]

    @each_row_block(orient)
    def _(index):
        rows = rows_of(index)
        ahead, rate_plus, rate_minus = face_parts(v_ref, rows)
        rate = rate_plus + rate_minus
        for t in range(tiles):
            got = rate * message_ref[0, rows, columns(t)].astype(F32)
            moved[0, rows, columns(t)] = jnp.where(ahead, got, 0.0).astype(BF16)
            moved[1, rows, columns(t)] = jnp.where(ahead, 0.0, got).astype(BF16)

    for s in range(2):
        gained[s] = (factors[s][0] * factors[s][0] * mix(m_ref[...], moved[s])).astype(BF16)

    def body(index, sums):
        rows = rows_of(index)
        ahead, rate_plus, rate_minus = face_parts(v_ref, rows)
        rate = rate_plus + rate_minus
        sides = (jnp.where(ahead, rate, 0.0), jnp.where(ahead, 0.0, rate))
        message = load_plane(message_ref, 1, rows)
        new = []
        for s in range(2):
            change = load_plane(gained, s, rows)
            moved_tiles = drift(change, None, None, geometry(v_ref, rows, 1.0 - 2.0 * s))
            if s == 0:
                weights = [load_plane(weight_ref, p, rows) for p in (face, inner)]
            else:
                weights = [load_plane(own_weight_ref, p, rows) for p in (0, 1)]
            pair = ((partner_low_ref, partner_high_ref), (own_low_ref, own_high_ref))[s]
            third = [jnp.where(core == 0, low, high) for low, high in zip(*(load_plane(ref, 0, rows) for ref in pair))]
            for t in range(tiles):
                on_face = moved_tiles[t] + sides[s] * message[t].astype(F32)
                wide = change[t].astype(F32)
                terms = (
                    on_face * weights[0][t].astype(F32),
                    sides[s] * wide * weights[1][t].astype(F32),
                    wide * third[t].astype(F32),
                )
                base = 3 * (s * tiles + t)
                new += [sums[base + k] + fold(term) for k, term in enumerate(terms)]
        return tuple(new)

    zero = jnp.zeros((8, LANES), F32)
    sums = lax.fori_loop(0, orient // ROWS, body, (zero,) * (6 * tiles), unroll=UNROLL)
    for t in range(tiles):
        shares = []
        for s in range(2):
            base = 3 * (s * tiles + t)
            last, onward, third = (jnp.sum(sums[base + k], axis=0, keepdims=True) / orient for k in range(3))
            near, far = (factors[s][depth][:, columns(t)] for depth in range(2))
            shares.append((0.5 * near * last + third / (near * near), 0.5 * far * onward))
        for p in range(planes):
            at = slice(p, p + 1), columns(t)
            mine = core == (0 if p < half else 1)
            depth = min(p, planes - 1 - p)
            met = jnp.where(mine, 0.5 * met_ref[depth : depth + 1, columns(t)], 0.0)
            sent, kept = shared_ref[at] + met, met
            if depth < 2:
                sent = sent + jnp.where(mine, shares[0][depth], 0.0)
                kept = kept + jnp.where(mine, shares[1][depth], 0.0)
            sent_ref[at] = sent
            kept_ref[at] = kept


def split_outputs(outs):
    low, high, state, near, far, kept, outer = outs
    return (low, high), state, (near, far), kept, outer


def kernel_call(kernel, outs, scratch, args):
    vmem = pl.BlockSpec(memory_space=pltpu.VMEM)
    smem = pl.BlockSpec(memory_space=pltpu.SMEM)
    return pl.pallas_call(
        kernel,
        out_shape=outs,
        in_specs=[smem if arg.dtype == jnp.int32 else vmem for arg in args],
        out_specs=jax.tree.map(lambda _: vmem, outs),
        scratch_shapes=[pltpu.VMEM(*s) if len(s) == 2 else pltpu.VMEM(s, BF16) for s in scratch],
        compiler_params=pltpu.CompilerParams(vmem_limit_bytes=12 << 20),
        cost_estimate=pl.CostEstimate(flops=0, bytes_accessed=0, transcendentals=0),
    )(*args)


def shards(fields, end_weights, directions, analysis, synthesis, decay_rates):
    device = lax.axis_index("space")
    core = device % 2
    planes, cells = fields.shape
    orient = end_weights.shape[0]
    plane_index = device // 2 * planes + lax.broadcasted_iota(jnp.int32, (planes, 1), 0)
    ramp = slope * plane_index.astype(F32) / (planes * lax.axis_size("space") // 2)
    own = fields + ramp
    partner = swap_species(fields) + ramp

    wide = lambda extra: jax.ShapeDtypeStruct((planes + extra, orient, cells), BF16)
    slab, plane = wide(0), wide(1 - planes)
    face = core ^ (1 - device // 2 % 2)
    core_word = jnp.reshape(face, (1,)).astype(jnp.int32)
    species_word = jnp.reshape(core, (1,)).astype(jnp.int32)
    start = jnp.transpose(end_weights, (1, 0, 2))
    spread, edge0, coded = kernel_call(
        prologue_kernel,
        (jax.ShapeDtypeStruct((4, orient, LANES), F32), plane, jax.ShapeDtypeStruct((16, cells), BF16)),
        (((16, cells), F32),),
        (core_word, species_word, directions, start, own, partner),
    )
    matrix, turned = kernel_call(
        matrix_kernel,
        (jax.ShapeDtypeStruct((orient, orient), BF16),) * 2,
        (),
        (synthesis, decay_rates[None], analysis),
    )
    other0, matrix = lax.optimization_barrier((swap_species(edge0), matrix))
    message0 = kernel_call(
        first_message_kernel,
        jax.ShapeDtypeStruct((1, orient + 16, cells), BF16),
        (),
        (edge0, other0, coded, spread),
    )

    def message(blocks, others):
        shape = jax.ShapeDtypeStruct((len(blocks), orient + PAD_ROWS, cells), BF16)
        return kernel_call(message_kernel, shape, (), (*blocks, *others, spread))

    start, _ = lax.optimization_barrier((start, message0))
    arrived0 = exchange_faces(message0)
    alone, edges1, *inner = kernel_call(
        first_alone_kernel,
        (slab, plane) + (plane,) * (planes - 2),
        (slab.shape, slab.shape),
        (start, own, spread, matrix),
    )
    weights, own_weights = kernel_call(
        weight_kernel, (slab, wide(2 - planes)), (), (core_word, swap_species(start), start, turned)
    )
    others1, weights, *partner_inner = lax.optimization_barrier(
        (swap_species(edges1), weights, *map(swap_species, inner))
    )
    message1 = kernel_call(
        first_message_kernel,
        jax.ShapeDtypeStruct((1, orient + 16 * PAD, cells), BF16),
        (),
        (edges1, others1, *[coded] * PAD, spread),
    )
    state, *_ = lax.optimization_barrier((alone, message1, weights))
    later, edges2, edges3 = kernel_call(
        next_alone_kernel, (slab, plane, plane), (slab.shape, slab.shape), (state, own, partner, spread, matrix)
    )
    edges2, edges3, arrived0 = lax.optimization_barrier((edges2, edges3, arrived0))
    message2 = message([edges2, edges3], [swap_species(edges2), swap_species(edges3)])
    arrived = [exchange_faces(message1), exchange_faces(message2)]
    crossed0 = swap_species(arrived0)

    alone, *_ = lax.optimization_barrier((alone, message1, message2))
    half = planes // 2
    faces, second_state, sent_half, kept_half, outer = split_outputs(
        kernel_call(
            second_step_kernel,
            (plane, plane, wide(4), plane, plane, wide(half - planes), jax.ShapeDtypeStruct((2, cells), F32)),
            ((4, orient, cells), (8, orient, cells)),
            (core_word, alone, later, edge0, arrived0, crossed0, own, partner, spread, matrix),
        )
    )
    arrived1, second_state = lax.optimization_barrier((arrived[0], second_state))
    *moving, _ = lax.optimization_barrier((*sent_half, arrived1))
    *partner_half, crossed1 = lax.optimization_barrier((*map(swap_species, moving), swap_species(arrived1)))
    density = jax.ShapeDtypeStruct((planes, cells), F32)
    met, partition = kernel_call(
        middle_kernel,
        (jax.ShapeDtypeStruct((half, cells), F32), density),
        ((2, orient, cells),),
        (core_word, kept_half, *partner_half, arrived1, own, partner, spread, matrix),
    )
    count = lax.axis_size("space")

    def received(value, distance, after):
        block = lax.ppermute(value, "space", [(i, i ^ distance) for i in range(count)])
        return lax.optimization_barrier((block, after))

    def gathered(value, distance, after):
        block, after = received(value, distance, after)
        return kernel_call(add_kernel, density, (), (value, block)), after

    *faces, second_state, _ = lax.optimization_barrier((*faces, second_state, met))
    partner_faces = [swap_species(block) for block in faces]
    third_state = kernel_call(
        third_step_kernel,
        wide(2),
        (slab.shape, wide(2).shape),
        (second_state, arrived1, crossed1, own, partner, outer, spread, matrix),
    )
    partition, third_state = gathered(partition, 4, third_state)
    third_state, _ = lax.optimization_barrier((third_state, partition))
    shared = kernel_call(
        pairing_kernel,
        density,
        (),
        (third_state, partner, spread, weights, partner_faces[0], *partner_inner, partner_faces[1]),
    )
    distance = 8
    while distance < count // 2:
        partition, shared = gathered(partition, distance, shared)
        distance *= 2
    block, shared = received(partition, distance, shared)
    triple = jax.ShapeDtypeStruct((3 * planes, cells), F32)
    partition = kernel_call(add_wide_kernel, triple, (), (partition, block))
    arrived2, shared, _ = lax.optimization_barrier((arrived[1], shared, partition))
    beside = [lax.ppermute(partition, "space", [(i, i ^ near) for i in range(count)]) for near in (2, 3, 1)]
    sent, kept = kernel_call(
        last_kernel,
        (density, density),
        ((2, orient, cells), (2, orient, cells)),
        (
            core_word, arrived2, weights, own_weights, *faces, *partner_faces, shared, met,
            own, partner, spread, matrix,
        ),
    )
    return kernel_call(
        functools.partial(divide_kernel, count // 2 * planes * cells),
        density,
        (),
        (kept, swap_species(sent), partition, *beside),
    )


def solution(mesh):
    return jax.shard_map(
        shards,
        mesh=mesh,
        in_specs=(P(("runs", "space"), None), P(None, ("runs", "space"), None), P(), P(), P(), P()),
        out_specs=P(("runs", "space"), None),
        check_vma=False,
    )
```

```python
import functools

import jax
import jax.numpy as jnp
from jax import lax
from jax.experimental import pallas as pl
from jax.experimental.pallas import tpu as pltpu
from jax.sharding import PartitionSpec as P

NZ = 16
STEPS = 4
LANES = 128
ROWS = 16
UNROLL = 16
PAD = 2
PAD_ROWS = 32

courant = 0.3
slope = 0.6

BF16 = jnp.bfloat16
F32 = jnp.float32


def swap_species(block):
    count = lax.axis_size("space")
    return lax.ppermute(block, "space", [(i ^ 1, i) for i in range(count)])


def exchange_faces(block):
    count = lax.axis_size("space")
    route = []
    for slab in range(count // 2):
        beside = ((slab + 1) ^ 1) - 1
        route += [(2 * slab, 2 * (slab ^ 1)), (2 * slab + 1, 2 * beside % count + 1)]
    return lax.ppermute(block, "space", route)


def rows_of(index):
    return pl.ds(pl.multiple_of(index * ROWS, ROWS), ROWS)


def each_row_block(orient):
    def run(body):
        def step(index, carry):
            body(index)
            return carry

        lax.fori_loop(0, orient // ROWS, step, 0, unroll=UNROLL)

    return run


def columns(tile):
    return slice(LANES * tile, LANES * (tile + 1))


def geometry(v_ref, rows, sign=1.0):
    lane = lax.broadcasted_iota(jnp.int32, (ROWS, LANES), 1)
    vx, vy, vz = (sign * v_ref[c, rows, :] for c in range(3))
    narrow = vx.astype(BF16)
    plus_x, narrow_plus, plus_y, plus_z = vx > 0, narrow > jnp.zeros_like(narrow), vy > 0, vz > 0
    rate_x, rate_y, rate_z = (courant * jnp.abs(t) for t in (vx, vy, vz))
    stay = 1.0 - (rate_x + rate_y + rate_z)
    z_from = (lane & (LANES - NZ)) | (jnp.where(plus_z, lane - 1, lane + 1) & (NZ - 1))
    y_from = jnp.where(plus_y, lane - NZ, lane + NZ) & (LANES - 1)
    y_edge = jnp.where(plus_y, lane, LANES - 1 - lane) < NZ
    return plus_x, narrow_plus, plus_y, stay, rate_x, rate_y, rate_z, z_from, y_from, y_edge


def pick(tile, index):
    return jnp.take_along_axis(tile, index, axis=1, mode="promise_in_bounds")


def load_plane(ref, plane, rows):
    return [ref[plane, rows, columns(t)] for t in range(ref.shape[2] // LANES)]


def drift(center, before, after, geo):
    plus_x, narrow_plus, plus_y, stay, rate_x, rate_y, rate_z, z_from, y_from, y_edge = geo
    tiles = len(center)
    center = [tile.astype(F32) for tile in center]
    turned = [pick(tile, y_from) for tile in center]
    moved = []
    for t in range(tiles):
        total = stay * center[t]
        if before is not None and after is not None:
            total = total + rate_x * jnp.where(narrow_plus, before[t], after[t]).astype(F32)
        elif before is not None:
            total = total + jnp.where(plus_x, rate_x, 0.0) * before[t].astype(F32)
        elif after is not None:
            total = total + jnp.where(plus_x, 0.0, rate_x) * after[t].astype(F32)
        over = jnp.where(plus_y, turned[t - 1], turned[(t + 1) % tiles])
        total = total + rate_y * jnp.where(y_edge, over, turned[t])
        total = total + rate_z * pick(center[t], z_from)
        moved.append(total)
    return moved


def store_plane(ref, plane, rows, tiles):
    for t, tile in enumerate(tiles):
        ref[plane, rows, columns(t)] = tile.astype(ref.dtype)


def mix(matrix, moved):
    return jnp.dot(matrix, moved, preferred_element_type=F32)


def boltzmann(field):
    return jnp.exp(-0.5 * field)


def prologue_kernel(
    core_ref, species_ref, directions_ref, start_ref, fields_ref, partner_ref, spread_ref, edge_ref, coded_ref, near
):
    sign = 1.0 - 2.0 * species_ref[0].astype(F32)
    toward = sign * (1.0 - 2.0 * core_ref[0].astype(F32))
    planes, orient, cells = start_ref.shape
    low = boltzmann(fields_ref[0:1])
    high = boltzmann(fields_ref[fields_ref.shape[0] - 1 :])
    for c in range(4):
        row = directions_ref[c % 3 : c % 3 + 1]
        column = jnp.broadcast_to(row, (LANES, orient)).T
        spread_ref[c] = (toward if c == 3 else sign) * column

    @each_row_block(orient)
    def _(index):
        rows = rows_of(index)
        plus_x = spread_ref[0, rows, :] > 0
        for t in range(cells // LANES):
            at = rows, columns(t)
            chosen = jnp.where(
                plus_x,
                high[:, columns(t)] * start_ref[planes - 1, *at].astype(F32),
                low[:, columns(t)] * start_ref[0, *at].astype(F32),
            )
            edge_ref[0, *at] = chosen.astype(BF16)

    near[...] = jnp.zeros_like(near)
    for s, ref in enumerate((fields_ref, partner_ref)):
        for depth in range(2):
            high_row, low_row = (ref[p : p + 1] for p in (planes - 1 - depth, depth))
            row = jnp.where(core_ref[0] == 1, high_row, low_row)
            coarse = row.astype(BF16).astype(F32)
            at = 2 * s + depth
            near[at : at + 1] = coarse
            near[at + 4 : at + 5] = row - coarse
    coded_ref[...] = near[...].astype(BF16)


def matrix_kernel(synthesis_ref, decay_ref, analysis_ref, out_ref, turned_ref):
    rest = synthesis_ref[...].astype(F32) * decay_ref[...]
    total = jnp.full(out_ref.shape, 1.0 / out_ref.shape[1], F32)
    for _ in range(3):
        part = rest.astype(BF16)
        rest = rest - part.astype(F32)
        total = total + jnp.dot(part, analysis_ref[...], preferred_element_type=F32)
    out_ref[...] = total.astype(BF16)
    turned_ref[...] = total.T.astype(BF16)


def add_kernel(one_ref, two_ref, out_ref):
    out_ref[...] = one_ref[...] + two_ref[...]


def join_kernel(sent_ref, one_ref, two_ref, out_ref):
    planes = sent_ref.shape[0]
    out_ref[:planes] = sent_ref[...]
    out_ref[planes:] = one_ref[...] + two_ref[...]


def divide_kernel(cells, kept_ref, mine_ref, arrived_ref, out_ref):
    planes = kept_ref.shape[0]
    total = mine_ref[planes:] + arrived_ref[planes:]
    out_ref[...] = (kept_ref[...] + arrived_ref[:planes]) * (cells / total)


def message_kernel(*refs):
    count = (len(refs) - 2) // 2
    v_ref, out_ref = refs[-2:]
    orient, cells = refs[0].shape[1:]

    @each_row_block(orient)
    def _(index):
        rows = rows_of(index)
        narrow = v_ref[3, rows, :].astype(BF16)
        leaves = narrow < jnp.zeros_like(narrow)
        for p in range(count):
            for t in range(cells // LANES):
                at = 0, rows, columns(t)
                out_ref[p, rows, columns(t)] = jnp.where(leaves, refs[p][at], refs[count + p][at])

    if count > 1:
        out_ref[:, orient:] = jnp.zeros_like(out_ref[:, orient:])


def first_message_kernel(mine_ref, other_ref, *refs):
    *coded_refs, v_ref, out_ref = refs
    message_kernel(mine_ref, other_ref, v_ref, out_ref)
    orient = mine_ref.shape[1]
    for k, ref in enumerate(coded_refs):
        out_ref[0, orient + 16 * k : orient + 16 * (k + 1)] = ref[...]


def write_edge(edges_ref, step, faces, rows, v_ref):
    narrow = v_ref[0, rows, :].astype(BF16)
    plus_x = narrow > jnp.zeros_like(narrow)
    for t in range(len(faces[0])):
        edges_ref[step, rows, columns(t)] = jnp.where(plus_x, faces[-1][t], faces[0][t])


def alone_step(source_ref, moved, targets, v_ref, edges_ref, step):
    planes, orient, _ = source_ref.shape

    @each_row_block(orient)
    def _(index):
        rows = rows_of(index)
        geo = geometry(v_ref, rows)
        loaded = [load_plane(source_ref, p, rows) for p in range(planes)]
        if edges_ref is not None:
            write_edge(edges_ref, step, loaded, rows, v_ref)
        for p in targets:
            before = loaded[p - 1] if p > 0 else None
            after = loaded[p + 1] if p < planes - 1 else None
            store_plane(moved, p, rows, drift(loaded[p], before, after, geo))


def first_alone_kernel(start_ref, first_ref, v_ref, m_ref, out_ref, edges_ref, *refs):
    *inner_refs, held, moved = refs
    planes, orient, _ = start_ref.shape
    first = boltzmann(first_ref[...])
    for p in range(planes):
        held[p] = (first[p : p + 1] * start_ref[p].astype(F32)).astype(BF16)
    alone_step(held, moved, range(planes), v_ref, None, 0)
    for p in (0, planes - 1, *range(1, planes - 1)):
        state = (first[p : p + 1] * first[p : p + 1] * mix(m_ref[...], moved[p])).astype(BF16)
        out_ref[p] = state
        if 0 < p < planes - 1:
            inner_refs[p - 1][0] = state

    @each_row_block(orient)
    def _(index):
        rows = rows_of(index)
        write_edge(edges_ref, 0, [load_plane(out_ref, p, rows) for p in (0, planes - 1)], rows, v_ref)


def next_alone_kernel(
    state_ref, first_ref, second_ref, v_ref, m_ref, out_ref, edges2_ref, edges3_ref, held, moved
):
    planes, orient, _ = state_ref.shape
    first = boltzmann(first_ref[...])
    second = boltzmann(second_ref[...])
    alone_step(state_ref, moved, range(planes), v_ref, None, 0)
    for p in range(planes):
        out_ref[p] = (first[p : p + 1] * second[p : p + 1] * mix(m_ref[...], moved[p])).astype(BF16)
    alone_step(out_ref, moved, (0, planes - 1), v_ref, edges2_ref, 0)
    for p in (0, planes - 1):
        held[p] = (second[p : p + 1] * second[p : p + 1] * mix(m_ref[...], moved[p])).astype(BF16)

    @each_row_block(orient)
    def _(index):
        rows = rows_of(index)
        write_edge(edges3_ref, 0, [load_plane(held, p, rows) for p in (0, planes - 1)], rows, v_ref)


def face_parts(v_ref, rows):
    vx = v_ref[0, rows, :]
    rate = courant * jnp.abs(vx)
    return v_ref[3, rows, :] > 0, jnp.where(vx > 0, rate, 0.0), jnp.where(vx > 0, 0.0, rate)


def face_drifts(v_ref, mine_ref, other_ref, moved, slots):
    @each_row_block(v_ref.shape[1])
    def _(index):
        rows = rows_of(index)
        ahead, rate_plus, rate_minus = face_parts(v_ref, rows)
        for t in range(mine_ref.shape[2] // LANES):
            mine = mine_ref[0, rows, columns(t)].astype(F32)
            other = other_ref[0, rows, columns(t)].astype(F32)
            face = jnp.where(ahead, mine, other)
            moved[slots[0], rows, columns(t)] = (rate_plus * face).astype(BF16)
            moved[slots[1], rows, columns(t)] = (rate_minus * face).astype(BF16)


def second_step_kernel(
    core_ref, alone_ref, later_ref, edge_ref, mine_ref, other_ref, first_ref, second_ref, v_ref, m_ref,
    face_low_ref, face_high_ref, next_ref, sent_near_ref, sent_far_ref, kept_ref, outer_ref, held, moved,
):
    planes, orient, _ = alone_ref.shape
    matrix = m_ref[...]
    first, second = boltzmann(first_ref[...]), boltzmann(second_ref[...])
    core = core_ref[0]
    mine, other = (block[:4] + block[4:8] for block in (ref[0, orient:].astype(F32) for ref in (mine_ref, other_ref)))
    other = (other[2:4], other[0:2])
    mine = (mine[0:2], mine[2:4])
    low = [jnp.where(core == 0, mine[k], other[k]) for k in range(2)]
    high = [jnp.where(core == 0, other[k], mine[k]) for k in range(2)]
    beyond = [boltzmann(block[k : k + 1]) for block in (low[0], high[0], low[1], high[1]) for k in range(2)]
    face_drifts(v_ref, mine_ref, other_ref, moved, (0, 1))

    @each_row_block(orient)
    def _(index):
        rows = rows_of(index)
        _, rate_plus, rate_minus = face_parts(v_ref, rows)
        for t in range(edge_ref.shape[2] // LANES):
            edge = edge_ref[0, rows, columns(t)].astype(F32)
            moved[2, rows, columns(t)] = (rate_minus * edge).astype(BF16)
            moved[3, rows, columns(t)] = (rate_plus * edge).astype(BF16)

    squared = first * first
    for p, slot, face_ref in ((0, 1, face_low_ref), (planes - 1, 2, face_high_ref)):
        arrived = squared[p : p + 1] * mix(matrix, moved[slot - 1])
        held[slot] = arrived.astype(BF16)
        face_ref[0] = (alone_ref[p].astype(F32) + arrived).astype(BF16)
    held[0] = (beyond[0] * beyond[0] * mix(matrix, moved[2])).astype(BF16)
    held[3] = (beyond[2] * beyond[2] * mix(matrix, moved[3])).astype(BF16)

    @each_row_block(orient)
    def _(index):
        rows = rows_of(index)
        geo = geometry(v_ref, rows)
        _, rate_plus, rate_minus = face_parts(v_ref, rows)
        below, low, high, above = (load_plane(held, p, rows) for p in range(4))
        face_low, face_high = (load_plane(ref, 0, rows) for ref in (face_low_ref, face_high_ref))

        def onward(rate, tiles):
            return [rate * tile.astype(F32) for tile in tiles]

        store_plane(moved, 0, rows, onward(rate_minus, below))
        store_plane(moved, 1, rows, drift(below, None, face_low, geo))
        store_plane(moved, 2, rows, drift(low, below, None, geo))
        store_plane(moved, 3, rows, onward(rate_plus, low))
        store_plane(moved, 4, rows, onward(rate_minus, high))
        store_plane(moved, 5, rows, drift(high, None, above, geo))
        store_plane(moved, 6, rows, drift(above, face_high, None, geo))
        store_plane(moved, 7, rows, onward(rate_plus, above))

    cross = first * second
    outer = ((0, 0, beyond[1] * beyond[5]), (1, 1, beyond[0] * beyond[4]))
    outer += ((planes + 2, 6, beyond[2] * beyond[6]), (planes + 3, 7, beyond[3] * beyond[7]))
    for p, slot, factor in outer:
        next_ref[p] = (factor * mix(matrix, moved[slot])).astype(BF16)
    slots = {0: 2, 1: 3, planes - 2: 4, planes - 1: 5}
    for p in range(planes):
        kept = later_ref[p]
        if p in slots:
            kept = (kept.astype(F32) + cross[p : p + 1] * mix(matrix, moved[slots[p]])).astype(BF16)
        next_ref[p + 2] = kept
    for p in range(planes // 2):
        sent_ref = (sent_near_ref, sent_far_ref)[p]
        sent_ref[0] = next_ref[2 + (planes - 1) * (1 - core) + (2 * core - 1) * p]
        kept_ref[p] = next_ref[2 + (planes - 1) * core + (1 - 2 * core) * p]
    outer_ref[0:1] = beyond[4] * beyond[4]
    outer_ref[1:2] = beyond[6] * beyond[6]


def middle_kernel(
    core_ref, own_ref, near_ref, far_ref, message_ref, first_ref, second_ref, v_ref, m_ref, out_ref, total_ref, moved
):
    _, orient, cells = own_ref.shape
    planes = first_ref.shape[0]

    def cross_of(depth):
        low, high = (
            boltzmann(first_ref[p : p + 1]) * boltzmann(second_ref[p : p + 1]) for p in (depth, planes - 1 - depth)
        )
        return jnp.where(core_ref[0] == 0, low, high)

    cross = [cross_of(depth) for depth in range(2)]

    @each_row_block(orient)
    def _(index):
        rows = rows_of(index)
        ahead, rate_plus, rate_minus = face_parts(v_ref, rows)
        rate = rate_plus + rate_minus
        for t in range(cells // LANES):
            gained = rate * message_ref[0, rows, columns(t)].astype(F32)
            moved[0, rows, columns(t)] = jnp.where(ahead, gained, 0.0).astype(BF16)
            moved[1, rows, columns(t)] = jnp.where(ahead, 0.0, gained).astype(BF16)

    own_face = own_ref[0].astype(F32) + cross[0] * mix(m_ref[...], moved[0])
    partner_face = near_ref[0].astype(F32) + cross[0] * mix(m_ref[...], moved[1])
    face = jnp.sum(own_face * partner_face, axis=0, keepdims=True)
    total = jnp.zeros((1, 1), F32)
    for p in range(own_ref.shape[0]):
        if p > 0:
            face = jnp.sum(own_ref[p].astype(F32) * far_ref[0].astype(F32), axis=0, keepdims=True)
        met = face / (orient * cross[p])
        out_ref[p : p + 1] = met
        total = total + jnp.sum(met, axis=1, keepdims=True)
    total_ref[...] = jnp.broadcast_to(total, total_ref.shape)


def third_step_kernel(
    held_ref, mine_ref, other_ref, first_ref, second_ref, outer_ref, v_ref, m_ref, next_ref, held, moved
):
    planes, orient, _ = held.shape
    matrix = m_ref[...]
    first, second = boltzmann(first_ref[...]), boltzmann(second_ref[...])
    face_drifts(v_ref, mine_ref, other_ref, moved, (0, 1))
    cross = first * second
    for p in range(planes):
        kept = held_ref[p + 2]
        if p in (0, planes - 1):
            arrived = cross[p : p + 1] * mix(matrix, moved[min(p, 1)])
            kept = (kept.astype(F32) + arrived).astype(BF16)
        held[p] = kept

    @each_row_block(orient)
    def _(index):
        rows = rows_of(index)
        geo = geometry(v_ref, rows)
        loaded = [load_plane(held_ref, p, rows) for p in (0, 1)]
        loaded += [load_plane(held, p, rows) for p in range(planes)]
        loaded += [load_plane(held_ref, p, rows) for p in (planes + 2, planes + 3)]
        for p in range(planes + 2):
            store_plane(moved, p, rows, drift(loaded[p + 1], loaded[p], loaded[p + 2], geo))

    squared = second * second
    factors = [outer_ref[0:1]] + [squared[p : p + 1] for p in range(planes)] + [outer_ref[1:2]]
    for p, factor in enumerate(factors):
        next_ref[p] = (factor * mix(matrix, moved[p])).astype(BF16)


def weight_kernel(core_ref, partner_ref, start_ref, turned_ref, weight_ref, own_ref):
    planes = partner_ref.shape[0]
    core = core_ref[0]
    for p in range(planes):
        weight_ref[p] = mix(turned_ref[...], partner_ref[p]).astype(BF16)
    for p in range(2):
        own_ref[p] = mix(turned_ref[...], start_ref[core * (planes - 1) + p - 2 * p * core]).astype(BF16)


def fold(value):
    return jnp.sum(value.reshape(ROWS // 8, 8, LANES), axis=0)


def pairing_kernel(held_ref, second_ref, v_ref, weight_ref, *refs):
    *partner_refs, out_ref = refs
    planes, orient, cells = weight_ref.shape
    second = boltzmann(second_ref[...])
    tiles = cells // LANES

    def body(index, sums):
        rows = rows_of(index)
        geo = geometry(v_ref, rows)
        loaded = [load_plane(held_ref, p, rows) for p in range(planes + 2)]
        new = []
        for p in range(planes):
            moved_tiles = drift(loaded[p + 1], loaded[p], loaded[p + 2], geo)
            weights = load_plane(weight_ref, p, rows)
            partner = load_plane(partner_refs[p], 0, rows)
            for t in range(tiles):
                last, third = sums[2 * (p * tiles + t)], sums[2 * (p * tiles + t) + 1]
                new.append(last + fold(moved_tiles[t] * weights[t].astype(F32)))
                new.append(third + fold(loaded[p + 1][t].astype(F32) * partner[t].astype(F32)))
        return tuple(new)

    zero = jnp.zeros((8, LANES), F32)
    sums = lax.fori_loop(0, orient // ROWS, body, (zero,) * (2 * planes * tiles), unroll=UNROLL)
    for p in range(planes):
        for t in range(tiles):
            last = jnp.sum(sums[2 * (p * tiles + t)], axis=0, keepdims=True)
            third = jnp.sum(sums[2 * (p * tiles + t) + 1], axis=0, keepdims=True)
            factor = second[p : p + 1, columns(t)]
            out_ref[p : p + 1, columns(t)] = (0.5 * factor * last + third / (factor * factor)) / orient


def last_kernel(
    core_ref, message_ref, weight_ref, own_weight_ref, own_low_ref, own_high_ref, partner_low_ref, partner_high_ref,
    shared_ref, met_ref,    own_ref, partner_ref, v_ref, m_ref, sent_ref, kept_ref, moved, gained,
):
    planes, cells = shared_ref.shape
    orient = m_ref.shape[0]
    tiles = cells // LANES
    core = core_ref[0]
    half = planes // 2
    face = core * (planes - 1)
    inner = face + 1 - 2 * core

    def at_face(ref, depth):
        return jnp.where(core == 0, boltzmann(ref[depth : depth + 1]), boltzmann(ref[planes - 1 - depth : planes - depth]))

    factors = [[at_face(ref, depth) for depth in range(2)] for ref in (partner_ref, own_ref)]

    @each_row_block(orient)
    def _(index):
        rows = rows_of(index)
        ahead, rate_plus, rate_minus = face_parts(v_ref, rows)
        rate = rate_plus + rate_minus
        for t in range(tiles):
            got = rate * message_ref[0, rows, columns(t)].astype(F32)
            moved[0, rows, columns(t)] = jnp.where(ahead, got, 0.0).astype(BF16)
            moved[1, rows, columns(t)] = jnp.where(ahead, 0.0, got).astype(BF16)

    for s in range(2):
        gained[s] = (factors[s][0] * factors[s][0] * mix(m_ref[...], moved[s])).astype(BF16)

    def body(index, sums):
        rows = rows_of(index)
        ahead, rate_plus, rate_minus = face_parts(v_ref, rows)
        rate = rate_plus + rate_minus
        sides = (jnp.where(ahead, rate, 0.0), jnp.where(ahead, 0.0, rate))
        message = load_plane(message_ref, 1, rows)
        new = []
        for s in range(2):
            change = load_plane(gained, s, rows)
            moved_tiles = drift(change, None, None, geometry(v_ref, rows, 1.0 - 2.0 * s))
            if s == 0:
                weights = [load_plane(weight_ref, p, rows) for p in (face, inner)]
            else:
                weights = [load_plane(own_weight_ref, p, rows) for p in (0, 1)]
            pair = ((partner_low_ref, partner_high_ref), (own_low_ref, own_high_ref))[s]
            third = [jnp.where(core == 0, low, high) for low, high in zip(*(load_plane(ref, 0, rows) for ref in pair))]
            for t in range(tiles):
                on_face = moved_tiles[t] + sides[s] * message[t].astype(F32)
                wide = change[t].astype(F32)
                terms = (
                    on_face * weights[0][t].astype(F32),
                    sides[s] * wide * weights[1][t].astype(F32),
                    wide * third[t].astype(F32),
                )
                base = 3 * (s * tiles + t)
                new += [sums[base + k] + fold(term) for k, term in enumerate(terms)]
        return tuple(new)

    zero = jnp.zeros((8, LANES), F32)
    sums = lax.fori_loop(0, orient // ROWS, body, (zero,) * (6 * tiles), unroll=UNROLL)
    for t in range(tiles):
        shares = []
        for s in range(2):
            base = 3 * (s * tiles + t)
            last, onward, third = (jnp.sum(sums[base + k], axis=0, keepdims=True) / orient for k in range(3))
            near, far = (factors[s][depth][:, columns(t)] for depth in range(2))
            shares.append((0.5 * near * last + third / (near * near), 0.5 * far * onward))
        for p in range(planes):
            at = slice(p, p + 1), columns(t)
            mine = core == (0 if p < half else 1)
            depth = min(p, planes - 1 - p)
            met = jnp.where(mine, 0.5 * met_ref[depth : depth + 1, columns(t)], 0.0)
            sent, kept = shared_ref[at] + met, met
            if depth < 2:
                sent = sent + jnp.where(mine, shares[0][depth], 0.0)
                kept = kept + jnp.where(mine, shares[1][depth], 0.0)
            sent_ref[at] = sent
            kept_ref[at] = kept


def split_outputs(outs):
    low, high, state, near, far, kept, outer = outs
    return (low, high), state, (near, far), kept, outer


def kernel_call(kernel, outs, scratch, args):
    vmem = pl.BlockSpec(memory_space=pltpu.VMEM)
    smem = pl.BlockSpec(memory_space=pltpu.SMEM)
    return pl.pallas_call(
        kernel,
        out_shape=outs,
        in_specs=[smem if arg.dtype == jnp.int32 else vmem for arg in args],
        out_specs=jax.tree.map(lambda _: vmem, outs),
        scratch_shapes=[pltpu.VMEM(*s) if len(s) == 2 else pltpu.VMEM(s, BF16) for s in scratch],
        compiler_params=pltpu.CompilerParams(vmem_limit_bytes=12 << 20),
        cost_estimate=pl.CostEstimate(flops=0, bytes_accessed=0, transcendentals=0),
    )(*args)


def shards(fields, end_weights, directions, analysis, synthesis, decay_rates):
    device = lax.axis_index("space")
    core = device % 2
    planes, cells = fields.shape
    orient = end_weights.shape[0]
    plane_index = device // 2 * planes + lax.broadcasted_iota(jnp.int32, (planes, 1), 0)
    ramp = slope * plane_index.astype(F32) / (planes * lax.axis_size("space") // 2)
    own = fields + ramp
    partner = swap_species(fields) + ramp

    wide = lambda extra: jax.ShapeDtypeStruct((planes + extra, orient, cells), BF16)
    slab, plane = wide(0), wide(1 - planes)
    face = core ^ (1 - device // 2 % 2)
    core_word = jnp.reshape(face, (1,)).astype(jnp.int32)
    species_word = jnp.reshape(core, (1,)).astype(jnp.int32)
    start = jnp.transpose(end_weights, (1, 0, 2))
    spread, edge0, coded = kernel_call(
        prologue_kernel,
        (jax.ShapeDtypeStruct((4, orient, LANES), F32), plane, jax.ShapeDtypeStruct((16, cells), BF16)),
        (((16, cells), F32),),
        (core_word, species_word, directions, start, own, partner),
    )
    matrix, turned = kernel_call(
        matrix_kernel,
        (jax.ShapeDtypeStruct((orient, orient), BF16),) * 2,
        (),
        (synthesis, decay_rates[None], analysis),
    )
    other0, matrix = lax.optimization_barrier((swap_species(edge0), matrix))
    message0 = kernel_call(
        first_message_kernel,
        jax.ShapeDtypeStruct((1, orient + 16, cells), BF16),
        (),
        (edge0, other0, coded, spread),
    )

    def message(blocks, others):
        shape = jax.ShapeDtypeStruct((len(blocks), orient + PAD_ROWS, cells), BF16)
        return kernel_call(message_kernel, shape, (), (*blocks, *others, spread))

    start, _ = lax.optimization_barrier((start, message0))
    arrived0 = exchange_faces(message0)
    alone, edges1, *inner = kernel_call(
        first_alone_kernel,
        (slab, plane) + (plane,) * (planes - 2),
        (slab.shape, slab.shape),
        (start, own, spread, matrix),
    )
    weights, own_weights = kernel_call(
        weight_kernel, (slab, wide(2 - planes)), (), (core_word, swap_species(start), start, turned)
    )
    others1, weights, *partner_inner = lax.optimization_barrier(
        (swap_species(edges1), weights, *map(swap_species, inner))
    )
    message1 = kernel_call(
        first_message_kernel,
        jax.ShapeDtypeStruct((1, orient + 16 * PAD, cells), BF16),
        (),
        (edges1, others1, *[coded] * PAD, spread),
    )
    state, *_ = lax.optimization_barrier((alone, message1, weights))
    later, edges2, edges3 = kernel_call(
        next_alone_kernel, (slab, plane, plane), (slab.shape, slab.shape), (state, own, partner, spread, matrix)
    )
    edges2, edges3, arrived0 = lax.optimization_barrier((edges2, edges3, arrived0))
    message2 = message([edges2, edges3], [swap_species(edges2), swap_species(edges3)])
    arrived = [exchange_faces(message1), exchange_faces(message2)]
    crossed0 = swap_species(arrived0)

    alone, *_ = lax.optimization_barrier((alone, message1, message2))
    half = planes // 2
    faces, second_state, sent_half, kept_half, outer = split_outputs(
        kernel_call(
            second_step_kernel,
            (plane, plane, wide(4), plane, plane, wide(half - planes), jax.ShapeDtypeStruct((2, cells), F32)),
            ((4, orient, cells), (8, orient, cells)),
            (core_word, alone, later, edge0, arrived0, crossed0, own, partner, spread, matrix),
        )
    )
    arrived1, second_state = lax.optimization_barrier((arrived[0], second_state))
    *moving, _ = lax.optimization_barrier((*sent_half, arrived1))
    partner_half = [swap_species(block) for block in moving]
    density = jax.ShapeDtypeStruct((planes, cells), F32)
    met, partition = kernel_call(
        middle_kernel,
        (jax.ShapeDtypeStruct((half, cells), F32), density),
        ((2, orient, cells),),
        (core_word, kept_half, *partner_half, arrived1, own, partner, spread, matrix),
    )
    count = lax.axis_size("space")

    def received(value, distance, after):
        block = lax.ppermute(value, "space", [(i, i ^ distance) for i in range(count)])
        return lax.optimization_barrier((block, after))

    def gathered(value, distance, after):
        block, after = received(value, distance, after)
        return kernel_call(add_kernel, density, (), (value, block)), after

    *faces, second_state, late, _ = lax.optimization_barrier((*faces, second_state, arrived1, met))
    crossed1 = swap_species(late)
    partner_faces = [swap_species(block) for block in faces]
    third_state = kernel_call(
        third_step_kernel,
        wide(2),
        (slab.shape, wide(2).shape),
        (second_state, arrived1, crossed1, own, partner, outer, spread, matrix),
    )
    partition, third_state = gathered(partition, 4, third_state)
    third_state, _ = lax.optimization_barrier((third_state, partition))
    shared = kernel_call(
        pairing_kernel,
        density,
        (),
        (third_state, partner, spread, weights, partner_faces[0], *partner_inner, partner_faces[1]),
    )
    distance = 8
    while distance < count:
        partition, shared = gathered(partition, distance, shared)
        distance *= 2
    arrived2, shared, _ = lax.optimization_barrier((arrived[1], shared, partition))
    sent, kept = kernel_call(
        last_kernel,
        (density, density),
        ((2, orient, cells), (2, orient, cells)),
        (
            core_word, arrived2, weights, own_weights, *faces, *partner_faces, shared, met,
            own, partner, spread, matrix,
        ),
    )
    beside, sent = received(partition, 2, sent)
    joined = kernel_call(
        join_kernel, jax.ShapeDtypeStruct((2 * planes, cells), F32), (), (sent, partition, beside)
    )
    return kernel_call(
        functools.partial(divide_kernel, count // 2 * planes * cells),
        density,
        (),
        (kept, joined, swap_species(joined)),
    )


def solution(mesh):
    return jax.shard_map(
        shards,
        mesh=mesh,
        in_specs=(P(("runs", "space"), None), P(None, ("runs", "space"), None), P(), P(), P(), P()),
        out_specs=P(("runs", "space"), None),
        check_vma=False,
    )
```

```python
import functools

import jax
import jax.numpy as jnp
from jax import lax
from jax.experimental import pallas as pl
from jax.experimental.pallas import tpu as pltpu
from jax.sharding import PartitionSpec as P

NZ = 16
STEPS = 4
LANES = 128
ROWS = 16
UNROLL = 16
PAD = 2
PAD_ROWS = 32

courant = 0.3
slope = 0.6

BF16 = jnp.bfloat16
F32 = jnp.float32


def swap_species(block):
    count = lax.axis_size("space")
    return lax.ppermute(block, "space", [(i ^ 1, i) for i in range(count)])


def exchange_faces(block):
    count = lax.axis_size("space")
    route = []
    for slab in range(count // 2):
        beside = ((slab + 1) ^ 1) - 1
        route += [(2 * slab, 2 * (slab ^ 1)), (2 * slab + 1, 2 * beside % count + 1)]
    return lax.ppermute(block, "space", route)


def rows_of(index):
    return pl.ds(pl.multiple_of(index * ROWS, ROWS), ROWS)


def each_row_block(orient):
    def run(body):
        def step(index, carry):
            body(index)
            return carry

        lax.fori_loop(0, orient // ROWS, step, 0, unroll=UNROLL)

    return run


def columns(tile):
    return slice(LANES * tile, LANES * (tile + 1))


def geometry(v_ref, rows, sign=1.0):
    lane = lax.broadcasted_iota(jnp.int32, (ROWS, LANES), 1)
    vx, vy, vz = (sign * v_ref[c, rows, :] for c in range(3))
    narrow = vx.astype(BF16)
    plus_x, narrow_plus, plus_y, plus_z = vx > 0, narrow > jnp.zeros_like(narrow), vy > 0, vz > 0
    rate_x, rate_y, rate_z = (courant * jnp.abs(t) for t in (vx, vy, vz))
    stay = 1.0 - (rate_x + rate_y + rate_z)
    z_from = (lane & (LANES - NZ)) | (jnp.where(plus_z, lane - 1, lane + 1) & (NZ - 1))
    y_from = jnp.where(plus_y, lane - NZ, lane + NZ) & (LANES - 1)
    y_edge = jnp.where(plus_y, lane, LANES - 1 - lane) < NZ
    return plus_x, narrow_plus, plus_y, stay, rate_x, rate_y, rate_z, z_from, y_from, y_edge


def pick(tile, index):
    return jnp.take_along_axis(tile, index, axis=1, mode="promise_in_bounds")


def load_plane(ref, plane, rows):
    return [ref[plane, rows, columns(t)] for t in range(ref.shape[2] // LANES)]


def drift(center, before, after, geo):
    plus_x, narrow_plus, plus_y, stay, rate_x, rate_y, rate_z, z_from, y_from, y_edge = geo
    tiles = len(center)
    center = [tile.astype(F32) for tile in center]
    turned = [pick(tile, y_from) for tile in center]
    moved = []
    for t in range(tiles):
        total = stay * center[t]
        if before is not None and after is not None:
            total = total + rate_x * jnp.where(narrow_plus, before[t], after[t]).astype(F32)
        elif before is not None:
            total = total + jnp.where(plus_x, rate_x, 0.0) * before[t].astype(F32)
        elif after is not None:
            total = total + jnp.where(plus_x, 0.0, rate_x) * after[t].astype(F32)
        over = jnp.where(plus_y, turned[t - 1], turned[(t + 1) % tiles])
        total = total + rate_y * jnp.where(y_edge, over, turned[t])
        total = total + rate_z * pick(center[t], z_from)
        moved.append(total)
    return moved


def store_plane(ref, plane, rows, tiles):
    for t, tile in enumerate(tiles):
        ref[plane, rows, columns(t)] = tile.astype(ref.dtype)


def mix(matrix, moved):
    return jnp.dot(matrix, moved, preferred_element_type=F32)


def boltzmann(field):
    return jnp.exp(-0.5 * field)


def prologue_kernel(
    core_ref, species_ref, directions_ref, start_ref, fields_ref, partner_ref, spread_ref, edge_ref, coded_ref, near
):
    sign = 1.0 - 2.0 * species_ref[0].astype(F32)
    toward = sign * (1.0 - 2.0 * core_ref[0].astype(F32))
    planes, orient, cells = start_ref.shape
    low = boltzmann(fields_ref[0:1])
    high = boltzmann(fields_ref[fields_ref.shape[0] - 1 :])
    for c in range(4):
        row = directions_ref[c % 3 : c % 3 + 1]
        column = jnp.broadcast_to(row, (LANES, orient)).T
        spread_ref[c] = (toward if c == 3 else sign) * column

    @each_row_block(orient)
    def _(index):
        rows = rows_of(index)
        plus_x = spread_ref[0, rows, :] > 0
        for t in range(cells // LANES):
            at = rows, columns(t)
            chosen = jnp.where(
                plus_x,
                high[:, columns(t)] * start_ref[planes - 1, *at].astype(F32),
                low[:, columns(t)] * start_ref[0, *at].astype(F32),
            )
            edge_ref[0, *at] = chosen.astype(BF16)

    near[...] = jnp.zeros_like(near)
    for s, ref in enumerate((fields_ref, partner_ref)):
        for depth in range(2):
            high_row, low_row = (ref[p : p + 1] for p in (planes - 1 - depth, depth))
            row = jnp.where(core_ref[0] == 1, high_row, low_row)
            coarse = row.astype(BF16).astype(F32)
            at = 2 * s + depth
            near[at : at + 1] = coarse
            near[at + 4 : at + 5] = row - coarse
    coded_ref[...] = near[...].astype(BF16)


def matrix_kernel(synthesis_ref, decay_ref, analysis_ref, out_ref, turned_ref):
    rest = synthesis_ref[...].astype(F32) * decay_ref[...]
    total = jnp.full(out_ref.shape, 1.0 / out_ref.shape[1], F32)
    for _ in range(3):
        part = rest.astype(BF16)
        rest = rest - part.astype(F32)
        total = total + jnp.dot(part, analysis_ref[...], preferred_element_type=F32)
    out_ref[...] = total.astype(BF16)
    turned_ref[...] = total.T.astype(BF16)


def add_kernel(one_ref, two_ref, out_ref):
    out_ref[...] = one_ref[...] + two_ref[...]


def join_kernel(sent_ref, one_ref, two_ref, out_ref):
    planes = sent_ref.shape[0]
    out_ref[:planes] = sent_ref[...]
    out_ref[planes:] = one_ref[...] + two_ref[...]


def divide_kernel(cells, kept_ref, mine_ref, arrived_ref, out_ref):
    planes = kept_ref.shape[0]
    total = mine_ref[planes:] + arrived_ref[planes:]
    out_ref[...] = (kept_ref[...] + arrived_ref[:planes]) * (cells / total)


def message_kernel(*refs):
    count = (len(refs) - 2) // 2
    v_ref, out_ref = refs[-2:]
    orient, cells = refs[0].shape[1:]

    @each_row_block(orient)
    def _(index):
        rows = rows_of(index)
        narrow = v_ref[3, rows, :].astype(BF16)
        leaves = narrow < jnp.zeros_like(narrow)
        for p in range(count):
            for t in range(cells // LANES):
                at = 0, rows, columns(t)
                out_ref[p, rows, columns(t)] = jnp.where(leaves, refs[p][at], refs[count + p][at])

    if count > 1:
        out_ref[:, orient:] = jnp.zeros_like(out_ref[:, orient:])


def first_message_kernel(mine_ref, other_ref, *refs):
    *coded_refs, v_ref, out_ref = refs
    message_kernel(mine_ref, other_ref, v_ref, out_ref)
    orient = mine_ref.shape[1]
    for k, ref in enumerate(coded_refs):
        out_ref[0, orient + 16 * k : orient + 16 * (k + 1)] = ref[...]


def write_edge(edges_ref, step, faces, rows, v_ref):
    narrow = v_ref[0, rows, :].astype(BF16)
    plus_x = narrow > jnp.zeros_like(narrow)
    for t in range(len(faces[0])):
        edges_ref[step, rows, columns(t)] = jnp.where(plus_x, faces[-1][t], faces[0][t])


def alone_step(source_ref, moved, targets, v_ref, edges_ref, step):
    planes, orient, _ = source_ref.shape

    @each_row_block(orient)
    def _(index):
        rows = rows_of(index)
        geo = geometry(v_ref, rows)
        loaded = [load_plane(source_ref, p, rows) for p in range(planes)]
        if edges_ref is not None:
            write_edge(edges_ref, step, loaded, rows, v_ref)
        for p in targets:
            before = loaded[p - 1] if p > 0 else None
            after = loaded[p + 1] if p < planes - 1 else None
            store_plane(moved, p, rows, drift(loaded[p], before, after, geo))


def first_alone_kernel(start_ref, first_ref, v_ref, m_ref, out_ref, edges_ref, *refs):
    *inner_refs, held, moved = refs
    planes, orient, _ = start_ref.shape
    first = boltzmann(first_ref[...])
    for p in range(planes):
        held[p] = (first[p : p + 1] * start_ref[p].astype(F32)).astype(BF16)
    alone_step(held, moved, range(planes), v_ref, None, 0)
    for p in (0, planes - 1, *range(1, planes - 1)):
        state = (first[p : p + 1] * first[p : p + 1] * mix(m_ref[...], moved[p])).astype(BF16)
        out_ref[p] = state
        if 0 < p < planes - 1:
            inner_refs[p - 1][0] = state

    @each_row_block(orient)
    def _(index):
        rows = rows_of(index)
        write_edge(edges_ref, 0, [load_plane(out_ref, p, rows) for p in (0, planes - 1)], rows, v_ref)


def next_alone_kernel(
    state_ref, first_ref, second_ref, v_ref, m_ref, out_ref, edges2_ref, edges3_ref, held, moved
):
    planes, orient, _ = state_ref.shape
    first = boltzmann(first_ref[...])
    second = boltzmann(second_ref[...])
    alone_step(state_ref, moved, range(planes), v_ref, None, 0)
    for p in range(planes):
        out_ref[p] = (first[p : p + 1] * second[p : p + 1] * mix(m_ref[...], moved[p])).astype(BF16)
    alone_step(out_ref, moved, (0, planes - 1), v_ref, edges2_ref, 0)
    for p in (0, planes - 1):
        held[p] = (second[p : p + 1] * second[p : p + 1] * mix(m_ref[...], moved[p])).astype(BF16)

    @each_row_block(orient)
    def _(index):
        rows = rows_of(index)
        write_edge(edges3_ref, 0, [load_plane(held, p, rows) for p in (0, planes - 1)], rows, v_ref)


def face_parts(v_ref, rows):
    vx = v_ref[0, rows, :]
    rate = courant * jnp.abs(vx)
    return v_ref[3, rows, :] > 0, jnp.where(vx > 0, rate, 0.0), jnp.where(vx > 0, 0.0, rate)


def face_drifts(v_ref, mine_ref, other_ref, moved, slots):
    @each_row_block(v_ref.shape[1])
    def _(index):
        rows = rows_of(index)
        ahead, rate_plus, rate_minus = face_parts(v_ref, rows)
        for t in range(mine_ref.shape[2] // LANES):
            mine = mine_ref[0, rows, columns(t)].astype(F32)
            other = other_ref[0, rows, columns(t)].astype(F32)
            face = jnp.where(ahead, mine, other)
            moved[slots[0], rows, columns(t)] = (rate_plus * face).astype(BF16)
            moved[slots[1], rows, columns(t)] = (rate_minus * face).astype(BF16)


def second_step_kernel(
    core_ref, alone_ref, later_ref, edge_ref, mine_ref, other_ref, first_ref, second_ref, v_ref, m_ref,
    face_low_ref, face_high_ref, next_ref, sent_near_ref, sent_far_ref, kept_ref, outer_ref, held, moved,
):
    planes, orient, _ = alone_ref.shape
    matrix = m_ref[...]
    first, second = boltzmann(first_ref[...]), boltzmann(second_ref[...])
    core = core_ref[0]
    mine, other = (block[:4] + block[4:8] for block in (ref[0, orient:].astype(F32) for ref in (mine_ref, other_ref)))
    other = (other[2:4], other[0:2])
    mine = (mine[0:2], mine[2:4])
    low = [jnp.where(core == 0, mine[k], other[k]) for k in range(2)]
    high = [jnp.where(core == 0, other[k], mine[k]) for k in range(2)]
    beyond = [boltzmann(block[k : k + 1]) for block in (low[0], high[0], low[1], high[1]) for k in range(2)]
    face_drifts(v_ref, mine_ref, other_ref, moved, (0, 1))

    @each_row_block(orient)
    def _(index):
        rows = rows_of(index)
        _, rate_plus, rate_minus = face_parts(v_ref, rows)
        for t in range(edge_ref.shape[2] // LANES):
            edge = edge_ref[0, rows, columns(t)].astype(F32)
            moved[2, rows, columns(t)] = (rate_minus * edge).astype(BF16)
            moved[3, rows, columns(t)] = (rate_plus * edge).astype(BF16)

    squared = first * first
    for p, slot, face_ref in ((0, 1, face_low_ref), (planes - 1, 2, face_high_ref)):
        arrived = squared[p : p + 1] * mix(matrix, moved[slot - 1])
        held[slot] = arrived.astype(BF16)
        face_ref[0] = (alone_ref[p].astype(F32) + arrived).astype(BF16)
    held[0] = (beyond[0] * beyond[0] * mix(matrix, moved[2])).astype(BF16)
    held[3] = (beyond[2] * beyond[2] * mix(matrix, moved[3])).astype(BF16)

    @each_row_block(orient)
    def _(index):
        rows = rows_of(index)
        geo = geometry(v_ref, rows)
        _, rate_plus, rate_minus = face_parts(v_ref, rows)
        below, low, high, above = (load_plane(held, p, rows) for p in range(4))
        face_low, face_high = (load_plane(ref, 0, rows) for ref in (face_low_ref, face_high_ref))

        def onward(rate, tiles):
            return [rate * tile.astype(F32) for tile in tiles]

        store_plane(moved, 0, rows, onward(rate_minus, below))
        store_plane(moved, 1, rows, drift(below, None, face_low, geo))
        store_plane(moved, 2, rows, drift(low, below, None, geo))
        store_plane(moved, 3, rows, onward(rate_plus, low))
        store_plane(moved, 4, rows, onward(rate_minus, high))
        store_plane(moved, 5, rows, drift(high, None, above, geo))
        store_plane(moved, 6, rows, drift(above, face_high, None, geo))
        store_plane(moved, 7, rows, onward(rate_plus, above))

    cross = first * second
    outer = ((0, 0, beyond[1] * beyond[5]), (1, 1, beyond[0] * beyond[4]))
    outer += ((planes + 2, 6, beyond[2] * beyond[6]), (planes + 3, 7, beyond[3] * beyond[7]))
    for p, slot, factor in outer:
        next_ref[p] = (factor * mix(matrix, moved[slot])).astype(BF16)
    slots = {0: 2, 1: 3, planes - 2: 4, planes - 1: 5}
    for p in range(planes):
        kept = later_ref[p]
        if p in slots:
            kept = (kept.astype(F32) + cross[p : p + 1] * mix(matrix, moved[slots[p]])).astype(BF16)
        next_ref[p + 2] = kept
    for p in range(planes // 2):
        sent_ref = (sent_near_ref, sent_far_ref)[p]
        sent_ref[0] = next_ref[2 + (planes - 1) * (1 - core) + (2 * core - 1) * p]
        kept_ref[p] = next_ref[2 + (planes - 1) * core + (1 - 2 * core) * p]
    outer_ref[0:1] = beyond[4] * beyond[4]
    outer_ref[1:2] = beyond[6] * beyond[6]


def middle_kernel(
    core_ref, own_ref, near_ref, far_ref, message_ref, first_ref, second_ref, v_ref, m_ref, out_ref, total_ref, moved
):
    _, orient, cells = own_ref.shape
    planes = first_ref.shape[0]

    def cross_of(depth):
        low, high = (
            boltzmann(first_ref[p : p + 1]) * boltzmann(second_ref[p : p + 1]) for p in (depth, planes - 1 - depth)
        )
        return jnp.where(core_ref[0] == 0, low, high)

    cross = [cross_of(depth) for depth in range(2)]

    @each_row_block(orient)
    def _(index):
        rows = rows_of(index)
        ahead, rate_plus, rate_minus = face_parts(v_ref, rows)
        rate = rate_plus + rate_minus
        for t in range(cells // LANES):
            gained = rate * message_ref[0, rows, columns(t)].astype(F32)
            moved[0, rows, columns(t)] = jnp.where(ahead, gained, 0.0).astype(BF16)
            moved[1, rows, columns(t)] = jnp.where(ahead, 0.0, gained).astype(BF16)

    own_face = own_ref[0].astype(F32) + cross[0] * mix(m_ref[...], moved[0])
    partner_face = near_ref[0].astype(F32) + cross[0] * mix(m_ref[...], moved[1])
    face = jnp.sum(own_face * partner_face, axis=0, keepdims=True)
    total = jnp.zeros((1, 1), F32)
    for p in range(own_ref.shape[0]):
        if p > 0:
            face = jnp.sum(own_ref[p].astype(F32) * far_ref[0].astype(F32), axis=0, keepdims=True)
        met = face / (orient * cross[p])
        out_ref[p : p + 1] = met
        total = total + jnp.sum(met, axis=1, keepdims=True)
    total_ref[...] = jnp.broadcast_to(total, total_ref.shape)


def third_step_kernel(
    held_ref, mine_ref, other_ref, first_ref, second_ref, outer_ref, v_ref, m_ref, next_ref, held, moved
):
    planes, orient, _ = held.shape
    matrix = m_ref[...]
    first, second = boltzmann(first_ref[...]), boltzmann(second_ref[...])
    face_drifts(v_ref, mine_ref, other_ref, moved, (0, 1))
    cross = first * second
    for p in range(planes):
        kept = held_ref[p + 2]
        if p in (0, planes - 1):
            arrived = cross[p : p + 1] * mix(matrix, moved[min(p, 1)])
            kept = (kept.astype(F32) + arrived).astype(BF16)
        held[p] = kept

    @each_row_block(orient)
    def _(index):
        rows = rows_of(index)
        geo = geometry(v_ref, rows)
        loaded = [load_plane(held_ref, p, rows) for p in (0, 1)]
        loaded += [load_plane(held, p, rows) for p in range(planes)]
        loaded += [load_plane(held_ref, p, rows) for p in (planes + 2, planes + 3)]
        for p in range(planes + 2):
            store_plane(moved, p, rows, drift(loaded[p + 1], loaded[p], loaded[p + 2], geo))

    squared = second * second
    factors = [outer_ref[0:1]] + [squared[p : p + 1] for p in range(planes)] + [outer_ref[1:2]]
    for p, factor in enumerate(factors):
        next_ref[p] = (factor * mix(matrix, moved[p])).astype(BF16)


def weight_kernel(core_ref, partner_ref, start_ref, turned_ref, weight_ref, own_ref):
    planes = partner_ref.shape[0]
    core = core_ref[0]
    for p in range(planes):
        weight_ref[p] = mix(turned_ref[...], partner_ref[p]).astype(BF16)
    for p in range(2):
        own_ref[p] = mix(turned_ref[...], start_ref[core * (planes - 1) + p - 2 * p * core]).astype(BF16)


def fold(value):
    return jnp.sum(value.reshape(ROWS // 8, 8, LANES), axis=0)


def pairing_kernel(held_ref, second_ref, v_ref, weight_ref, *refs):
    *partner_refs, out_ref = refs
    planes, orient, cells = weight_ref.shape
    second = boltzmann(second_ref[...])
    tiles = cells // LANES

    def body(index, sums):
        rows = rows_of(index)
        geo = geometry(v_ref, rows)
        loaded = [load_plane(held_ref, p, rows) for p in range(planes + 2)]
        new = []
        for p in range(planes):
            moved_tiles = drift(loaded[p + 1], loaded[p], loaded[p + 2], geo)
            weights = load_plane(weight_ref, p, rows)
            partner = load_plane(partner_refs[p], 0, rows)
            for t in range(tiles):
                last, third = sums[2 * (p * tiles + t)], sums[2 * (p * tiles + t) + 1]
                new.append(last + fold(moved_tiles[t] * weights[t].astype(F32)))
                new.append(third + fold(loaded[p + 1][t].astype(F32) * partner[t].astype(F32)))
        return tuple(new)

    zero = jnp.zeros((8, LANES), F32)
    sums = lax.fori_loop(0, orient // ROWS, body, (zero,) * (2 * planes * tiles), unroll=UNROLL)
    for p in range(planes):
        for t in range(tiles):
            last = jnp.sum(sums[2 * (p * tiles + t)], axis=0, keepdims=True)
            third = jnp.sum(sums[2 * (p * tiles + t) + 1], axis=0, keepdims=True)
            factor = second[p : p + 1, columns(t)]
            out_ref[p : p + 1, columns(t)] = (0.5 * factor * last + third / (factor * factor)) / orient


def last_kernel(
    core_ref, message_ref, weight_ref, own_weight_ref, own_low_ref, own_high_ref, partner_low_ref, partner_high_ref,
    shared_ref, met_ref,    own_ref, partner_ref, v_ref, m_ref, sent_ref, kept_ref, moved, gained,
):
    planes, cells = shared_ref.shape
    orient = m_ref.shape[0]
    tiles = cells // LANES
    core = core_ref[0]
    half = planes // 2
    face = core * (planes - 1)
    inner = face + 1 - 2 * core

    def at_face(ref, depth):
        return jnp.where(core == 0, boltzmann(ref[depth : depth + 1]), boltzmann(ref[planes - 1 - depth : planes - depth]))

    factors = [[at_face(ref, depth) for depth in range(2)] for ref in (partner_ref, own_ref)]

    @each_row_block(orient)
    def _(index):
        rows = rows_of(index)
        ahead, rate_plus, rate_minus = face_parts(v_ref, rows)
        rate = rate_plus + rate_minus
        for t in range(tiles):
            got = rate * message_ref[0, rows, columns(t)].astype(F32)
            moved[0, rows, columns(t)] = jnp.where(ahead, got, 0.0).astype(BF16)
            moved[1, rows, columns(t)] = jnp.where(ahead, 0.0, got).astype(BF16)

    for s in range(2):
        gained[s] = (factors[s][0] * factors[s][0] * mix(m_ref[...], moved[s])).astype(BF16)

    def body(index, sums):
        rows = rows_of(index)
        ahead, rate_plus, rate_minus = face_parts(v_ref, rows)
        rate = rate_plus + rate_minus
        sides = (jnp.where(ahead, rate, 0.0), jnp.where(ahead, 0.0, rate))
        message = load_plane(message_ref, 1, rows)
        new = []
        for s in range(2):
            change = load_plane(gained, s, rows)
            moved_tiles = drift(change, None, None, geometry(v_ref, rows, 1.0 - 2.0 * s))
            if s == 0:
                weights = [load_plane(weight_ref, p, rows) for p in (face, inner)]
            else:
                weights = [load_plane(own_weight_ref, p, rows) for p in (0, 1)]
            pair = ((partner_low_ref, partner_high_ref), (own_low_ref, own_high_ref))[s]
            third = [jnp.where(core == 0, low, high) for low, high in zip(*(load_plane(ref, 0, rows) for ref in pair))]
            for t in range(tiles):
                on_face = moved_tiles[t] + sides[s] * message[t].astype(F32)
                wide = change[t].astype(F32)
                terms = (
                    on_face * weights[0][t].astype(F32),
                    sides[s] * wide * weights[1][t].astype(F32),
                    wide * third[t].astype(F32),
                )
                base = 3 * (s * tiles + t)
                new += [sums[base + k] + fold(term) for k, term in enumerate(terms)]
        return tuple(new)

    zero = jnp.zeros((8, LANES), F32)
    sums = lax.fori_loop(0, orient // ROWS, body, (zero,) * (6 * tiles), unroll=UNROLL)
    for t in range(tiles):
        shares = []
        for s in range(2):
            base = 3 * (s * tiles + t)
            last, onward, third = (jnp.sum(sums[base + k], axis=0, keepdims=True) / orient for k in range(3))
            near, far = (factors[s][depth][:, columns(t)] for depth in range(2))
            shares.append((0.5 * near * last + third / (near * near), 0.5 * far * onward))
        for p in range(planes):
            at = slice(p, p + 1), columns(t)
            mine = core == (0 if p < half else 1)
            depth = min(p, planes - 1 - p)
            met = jnp.where(mine, 0.5 * met_ref[depth : depth + 1, columns(t)], 0.0)
            sent, kept = shared_ref[at] + met, met
            if depth < 2:
                sent = sent + jnp.where(mine, shares[0][depth], 0.0)
                kept = kept + jnp.where(mine, shares[1][depth], 0.0)
            sent_ref[at] = sent
            kept_ref[at] = kept


def split_outputs(outs):
    low, high, state, near, far, kept, outer = outs
    return (low, high), state, (near, far), kept, outer


def kernel_call(kernel, outs, scratch, args):
    vmem = pl.BlockSpec(memory_space=pltpu.VMEM)
    smem = pl.BlockSpec(memory_space=pltpu.SMEM)
    return pl.pallas_call(
        kernel,
        out_shape=outs,
        in_specs=[smem if arg.dtype == jnp.int32 else vmem for arg in args],
        out_specs=jax.tree.map(lambda _: vmem, outs),
        scratch_shapes=[pltpu.VMEM(*s) if len(s) == 2 else pltpu.VMEM(s, BF16) for s in scratch],
        compiler_params=pltpu.CompilerParams(vmem_limit_bytes=12 << 20),
        cost_estimate=pl.CostEstimate(flops=0, bytes_accessed=0, transcendentals=0),
    )(*args)


def shards(fields, end_weights, directions, analysis, synthesis, decay_rates):
    device = lax.axis_index("space")
    core = device % 2
    planes, cells = fields.shape
    orient = end_weights.shape[0]
    plane_index = device // 2 * planes + lax.broadcasted_iota(jnp.int32, (planes, 1), 0)
    ramp = slope * plane_index.astype(F32) / (planes * lax.axis_size("space") // 2)
    own = fields + ramp
    partner = swap_species(fields) + ramp

    wide = lambda extra: jax.ShapeDtypeStruct((planes + extra, orient, cells), BF16)
    slab, plane = wide(0), wide(1 - planes)
    face = core ^ (1 - device // 2 % 2)
    core_word = jnp.reshape(face, (1,)).astype(jnp.int32)
    species_word = jnp.reshape(core, (1,)).astype(jnp.int32)
    start = jnp.transpose(end_weights, (1, 0, 2))
    spread, edge0, coded = kernel_call(
        prologue_kernel,
        (jax.ShapeDtypeStruct((4, orient, LANES), F32), plane, jax.ShapeDtypeStruct((16, cells), BF16)),
        (((16, cells), F32),),
        (core_word, species_word, directions, start, own, partner),
    )
    matrix, turned = kernel_call(
        matrix_kernel,
        (jax.ShapeDtypeStruct((orient, orient), BF16),) * 2,
        (),
        (synthesis, decay_rates[None], analysis),
    )
    other0, matrix = lax.optimization_barrier((swap_species(edge0), matrix))
    message0 = kernel_call(
        first_message_kernel,
        jax.ShapeDtypeStruct((1, orient + 16, cells), BF16),
        (),
        (edge0, other0, coded, spread),
    )

    def message(blocks, others):
        shape = jax.ShapeDtypeStruct((len(blocks), orient + PAD_ROWS, cells), BF16)
        return kernel_call(message_kernel, shape, (), (*blocks, *others, spread))

    start, _ = lax.optimization_barrier((start, message0))
    arrived0 = exchange_faces(message0)
    alone, edges1, *inner = kernel_call(
        first_alone_kernel,
        (slab, plane) + (plane,) * (planes - 2),
        (slab.shape, slab.shape),
        (start, own, spread, matrix),
    )
    weights, own_weights = kernel_call(
        weight_kernel, (slab, wide(2 - planes)), (), (core_word, swap_species(start), start, turned)
    )
    others1, weights = lax.optimization_barrier((swap_species(edges1), weights))
    partner_inner = [swap_species(block) for block in inner]
    message1 = kernel_call(
        first_message_kernel,
        jax.ShapeDtypeStruct((1, orient + 16 * PAD, cells), BF16),
        (),
        (edges1, others1, *[coded] * PAD, spread),
    )
    state, *_ = lax.optimization_barrier((alone, message1, weights))
    later, edges2, edges3 = kernel_call(
        next_alone_kernel, (slab, plane, plane), (slab.shape, slab.shape), (state, own, partner, spread, matrix)
    )
    edges2, edges3, arrived0, *partner_inner = lax.optimization_barrier((edges2, edges3, arrived0, *partner_inner))
    message2 = message([edges2, edges3], [swap_species(edges2), swap_species(edges3)])
    arrived = [exchange_faces(message1), exchange_faces(message2)]
    crossed0 = swap_species(arrived0)

    alone, *_ = lax.optimization_barrier((alone, message1, message2))
    half = planes // 2
    faces, second_state, sent_half, kept_half, outer = split_outputs(
        kernel_call(
            second_step_kernel,
            (plane, plane, wide(4), plane, plane, wide(half - planes), jax.ShapeDtypeStruct((2, cells), F32)),
            ((4, orient, cells), (8, orient, cells)),
            (core_word, alone, later, edge0, arrived0, crossed0, own, partner, spread, matrix),
        )
    )
    arrived1, second_state = lax.optimization_barrier((arrived[0], second_state))
    *moving, _ = lax.optimization_barrier((*sent_half, arrived1))
    *partner_half, crossed1 = lax.optimization_barrier((*map(swap_species, moving), swap_species(arrived1)))
    density = jax.ShapeDtypeStruct((planes, cells), F32)
    met, partition = kernel_call(
        middle_kernel,
        (jax.ShapeDtypeStruct((half, cells), F32), density),
        ((2, orient, cells),),
        (core_word, kept_half, *partner_half, arrived1, own, partner, spread, matrix),
    )
    count = lax.axis_size("space")

    def received(value, distance, after):
        block = lax.ppermute(value, "space", [(i, i ^ distance) for i in range(count)])
        return lax.optimization_barrier((block, after))

    def gathered(value, distance, after):
        block, after = received(value, distance, after)
        return kernel_call(add_kernel, density, (), (value, block)), after

    *faces, second_state, _ = lax.optimization_barrier((*faces, second_state, met))
    partner_faces = [swap_species(block) for block in faces]
    third_state = kernel_call(
        third_step_kernel,
        wide(2),
        (slab.shape, wide(2).shape),
        (second_state, arrived1, crossed1, own, partner, outer, spread, matrix),
    )
    partition, third_state = gathered(partition, 4, third_state)
    third_state, _ = lax.optimization_barrier((third_state, partition))
    shared = kernel_call(
        pairing_kernel,
        density,
        (),
        (third_state, partner, spread, weights, partner_faces[0], *partner_inner, partner_faces[1]),
    )
    distance = 8
    while distance < count:
        partition, shared = gathered(partition, distance, shared)
        distance *= 2
    arrived2, shared, _ = lax.optimization_barrier((arrived[1], shared, partition))
    sent, kept = kernel_call(
        last_kernel,
        (density, density),
        ((2, orient, cells), (2, orient, cells)),
        (
            core_word, arrived2, weights, own_weights, *faces, *partner_faces, shared, met,
            own, partner, spread, matrix,
        ),
    )
    beside, sent = received(partition, 2, sent)
    joined = kernel_call(
        join_kernel, jax.ShapeDtypeStruct((2 * planes, cells), F32), (), (sent, partition, beside)
    )
    return kernel_call(
        functools.partial(divide_kernel, count // 2 * planes * cells),
        density,
        (),
        (kept, joined, swap_species(joined)),
    )


def solution(mesh):
    return jax.shard_map(
        shards,
        mesh=mesh,
        in_specs=(P(("runs", "space"), None), P(None, ("runs", "space"), None), P(), P(), P(), P()),
        out_specs=P(("runs", "space"), None),
        check_vma=False,
    )
```
